32 devices in a mesh: seq: 8 (over z, y), tp: 4 (over x, core).
Axes of the slice: x: 2, y: 2, z: 4, core: 2. Of those that a mesh axis runs over, the one named last changes fastest.
Arguments:
- residual: bfloat16 [2048, 2048], P('seq', 'tp'), may hold values from -6 to 6
- query_vectors: bfloat16 [2048, 2048], P('seq', 'tp'), may hold values from -6 to 6
- key_vectors: bfloat16 [2048, 2048], P('seq', 'tp'), may hold values from -6 to 6
- value_vectors: bfloat16 [2048, 2048], P('seq', 'tp'), may hold values from -6 to 6
- log_decay: float32 [16, 2048], P('tp', 'seq'), may hold values from -1 to 0, as said below
- norm_gain: float32 [2048], P('tp'), may hold values from 0.5 to 1.5
- out_weight: bfloat16 [2048, 2048], P('tp'), may hold values from -0.125 to 0.125
Outputs:
- mixed: bfloat16 [2048, 2048], P('seq', 'tp')
The draws below stay inside these ranges and needn't reach their ends.
Inputs may be any that keep to these rules, and one draw needn't show every extreme that they name: `log_decay`: Log-decays are never positive.
All inputs are finite; a program needn't handle non-finite values.
Results may differ from the reference program's by a relative error of at most 0.005.
Values may be sent and summed in bfloat16 or wider, within the bound.
No kernel may reach another device: no remote copies, remote signals or barrier semaphores. Data moves between devices by JAX's collectives and lax.ppermute only.
A program may use at most 128 MiB of HBM per device.

```python
import math
import jax
import jax.numpy as jnp
from jax import lax

D = 2048
HEADS = 16
HEAD_DIM = 128
GROUP = 256
TOK_DEV = 256
TOKENS = 2048


def draw_log_decay(key, part):
    subkeys = jax.random.split(key, 8)
    fast_share = 0.5
    fast_heads = jax.random.uniform(subkeys[0], (HEADS, 1)) < fast_share
    fast_rate = jnp.exp(jax.random.uniform(subkeys[1], (HEADS, 1), minval=math.log(1.0 / 50.0), maxval=math.log(1.0 / 30.0)))
    slow_rate = jax.random.uniform(subkeys[2], (HEADS, 1), minval=4.0, maxval=12.0) / TOKENS
    reference_speed_factor = jnp.where(fast_heads, fast_rate, slow_rate)
    processor_scaling_factor = jnp.exp(jax.random.uniform(subkeys[3], (HEADS, TOKENS // TOK_DEV), minval=-0.5, maxval=0.5))
    processor_scaling_factor = jnp.repeat(processor_scaling_factor, TOK_DEV, axis=1)
    texture_coarseness = jax.random.uniform(subkeys[4], (HEADS, TOKENS), minval=0.5, maxval=1.5)
    first_place = jax.random.randint(subkeys[5], (HEADS, 1, 1), 0, TOKENS)
    offset = jax.random.randint(subkeys[7], (HEADS, 1, 1), 1, TOKENS)
    sequence_indices = jnp.concatenate([first_place, (first_place + offset) % TOKENS], axis=1)
    stack_tiers = jnp.log(jax.random.uniform(subkeys[6], (HEADS, 2, 1), minval=0.5, maxval=0.8))
    location_entries = jnp.arange(TOKENS, dtype=jnp.int32)[None, None, :]
    spike_occurrences = jnp.sum(jnp.where(location_entries == sequence_indices, stack_tiers, 0.0), axis=1)
    return (spike_occurrences - reference_speed_factor * processor_scaling_factor * texture_coarseness).astype(jnp.float32)


def block_levels(stream_key, dims, cuts, low, high):
    gain = 1.0
    for axis_at, parts in cuts:
        draws = jax.random.uniform(jax.random.fold_in(jax.random.fold_in(stream_key, 6), axis_at), (parts,), jnp.float32, low / len(cuts), high / len(cuts))
        gain = gain * jnp.repeat(jnp.exp(draws), dims[axis_at] // parts).reshape((-1,) + (1,) * (len(dims) - 1 - axis_at))
    return gain


def bell_draw(stream_key, shape, spread, limit, shards=(), kind=jnp.bfloat16):
    values = jax.random.normal(stream_key, shape, jnp.float32) * spread
    if len(shards) > 0:
        values = block_levels(stream_key, shape, shards, -0.22, 0.18) * values
    return jnp.clip(values, min=-limit, max=limit).astype(kind)


def setup_inputs(seed: int = 0) -> dict:
    seeds = jax.random.split(jax.random.key(seed), 8)
    return {
        "residual": bell_draw(seeds[0], (TOKENS, D), 1.0, 6.0, ((0, 8), (1, 4))),
        "query_vectors": bell_draw(seeds[1], (TOKENS, HEADS * HEAD_DIM), 1.0, 6.0, ((0, 8), (1, 4))),
        "key_vectors": bell_draw(seeds[2], (TOKENS, HEADS * HEAD_DIM), 1.0, 6.0, ((0, 8), (1, 4))),
        "value_vectors": bell_draw(seeds[3], (TOKENS, HEADS * HEAD_DIM), 1.0, 6.0, ((0, 8), (1, 4))),
        "log_decay": draw_log_decay(jax.random.fold_in(seeds[7], 71), 0),
        "norm_gain": jnp.clip(1.0 + 0.1 * jax.random.normal(seeds[5], (HEADS * HEAD_DIM,), jnp.float32), 0.5, 1.5),
        "out_weight": bell_draw(seeds[6], (HEADS * HEAD_DIM, D), (HEADS * HEAD_DIM) ** -0.5, 0.125, ((0, 4),)),
    }


def reference(residual, query_vectors, key_vectors, value_vectors, log_decay, norm_gain, out_weight):
    tokens = residual.shape[0]
    blocks = tokens // GROUP
    block_shape = (blocks, GROUP, HEADS, HEAD_DIM)
    queries = query_vectors.reshape(block_shape)
    key_blocks = key_vectors.reshape(block_shape)
    value_blocks = value_vectors.reshape(block_shape)
    decays = log_decay.reshape(HEADS, blocks, GROUP).transpose(1, 0, 2)
    score_scale = HEAD_DIM ** (-0.5)
    causal = jnp.tril(jnp.ones((GROUP, GROUP), dtype=bool))
    highest = lax.Precision.HIGHEST

    def advance_group(carried_state, inputs):
        query_block, key_block, value_block, decay_block = inputs
        query_float = query_block.astype(jnp.float32)
        key_float = key_block.astype(jnp.float32)
        value_float = value_block.astype(jnp.float32)
        within = jnp.cumsum(decay_block, axis=1)
        scores = jnp.einsum('thd,shd->hts', query_float, key_float, precision=highest) * score_scale
        decay_gaps = within[:, :, None] - within[:, None, :]
        weights = jnp.where(causal, jnp.exp(decay_gaps), 0.0)
        score_probs = (scores * weights).astype(jnp.bfloat16)
        intra_part = jnp.einsum('hts,shd->thd', score_probs.astype(jnp.float32), value_float, precision=highest)
        inter_part = jnp.einsum('thd,hde->the', query_float, carried_state, precision=highest)
        inter_part = inter_part * (jnp.exp(within).T[:, :, None] * score_scale)
        tail_decay = jnp.exp(within[:, -1:] - within)
        weighted = (key_float * tail_decay.T[:, :, None]).astype(jnp.bfloat16)
        update = jnp.einsum('shd,she->hde', weighted.astype(jnp.float32), value_float, precision=highest)
        carried_state = carried_state * jnp.exp(within[:, -1])[:, None, None] + update
        return (carried_state, intra_part + inter_part)
    initial = jnp.zeros((HEADS, HEAD_DIM, HEAD_DIM), jnp.float32)
    final_state, attended = lax.scan(advance_group, initial, (queries, key_blocks, value_blocks, decays))
    attended = attended.reshape(tokens, HEADS, HEAD_DIM)
    mean_square = lax.optimization_barrier(jnp.mean(attended * attended, axis=-1, keepdims=True))
    normed = attended / jnp.sqrt(mean_square + 1e-06)
    normed = (normed.reshape(tokens, HEADS * HEAD_DIM) * norm_gain).astype(jnp.bfloat16)
    projected = jnp.dot(normed, out_weight, preferred_element_type=jnp.float32)
    return (residual.astype(jnp.float32) + projected).astype(jnp.bfloat16)
```

```python
import functools

import jax
import jax.numpy as jnp
from jax import lax
from jax.experimental import pallas as pl
from jax.experimental.pallas import tpu as pltpu
from jax.sharding import PartitionSpec as P

HEAD_DIM = 128
GROUP = 256
SCALE = HEAD_DIM ** (-0.5)
F32 = jnp.float32
BF16 = jnp.bfloat16
VMEM = pl.BlockSpec(memory_space=pltpu.VMEM)
DECAY_ROWS = 16


def head(ref, h):
    return ref[:, h * HEAD_DIM : (h + 1) * HEAD_DIM]


def contract(a, b, dims, **kwargs):
    return lax.dot_general(a, b, ((dims[0], dims[1]), ((), ())), **kwargs)


def positions():
    shape = (GROUP, GROUP)
    return lax.broadcasted_iota(jnp.int32, shape, 0), lax.broadcasted_iota(jnp.int32, shape, 1)


def state_kernel(heads, devices, decay_ref, key_ref, value_ref, out_ref):
    decays = decay_ref[...]
    row, col = positions()
    later = jnp.where(col > row, 1.0, 0.0).astype(F32)
    tail = jnp.exp(
        contract(
            later, decays, ((1,), (1,)),
            precision=lax.Precision.HIGHEST, preferred_element_type=F32,
        )
    )
    whole = jnp.exp(jnp.sum(decays, axis=1, keepdims=True))
    rows = heads * HEAD_DIM // devices
    per_head = HEAD_DIM // rows
    padded = out_ref.shape[1] - DECAY_ROWS
    for h in range(heads):
        weighted = (head(key_ref, h).astype(F32) * tail[:, h : h + 1]).astype(BF16)
        update = contract(
            weighted, head(value_ref, h), ((0,), (0,)), preferred_element_type=F32
        ).astype(BF16)
        wide = jnp.broadcast_to(whole[h : h + 1, :], (DECAY_ROWS // 2, HEAD_DIM))
        coarse = wide.astype(BF16).astype(F32)
        decay_rows = jnp.concatenate([coarse, wide - coarse], axis=0).astype(BF16)
        for i in range(per_head):
            piece = update[i * rows : (i + 1) * rows]
            if padded > rows:
                piece = jnp.concatenate(
                    [piece, jnp.zeros((padded - rows, HEAD_DIM), BF16)], axis=0
                )
            out_ref[h * per_head + i, :padded, :] = piece
            out_ref[h * per_head + i, padded:, :] = decay_rows


def intra_kernel(heads, decay_ref, query_ref, key_ref, value_ref, out_ref, own_ref):
    decays = decay_ref[...]
    row, col = positions()
    causal = col <= row
    upto = jnp.where(causal, 1.0, 0.0).astype(F32)
    exact = dict(precision=lax.Precision.HIGHEST, preferred_element_type=F32)
    down = contract(upto, decays, ((1,), (1,)), **exact)
    across = contract(decays, upto, ((1,), (1,)), **exact)
    own_ref[...] = jnp.exp(down) * SCALE
    for h in range(heads):
        scores = contract(
            head(query_ref, h), head(key_ref, h), ((1,), (1,)), preferred_element_type=F32
        )
        gaps = down[:, h : h + 1] - across[h : h + 1, :]
        weights = jnp.where(causal, jnp.exp(gaps), 0.0)
        probs = (scores * SCALE * weights).astype(BF16)
        out_ref[:, h * HEAD_DIM : (h + 1) * HEAD_DIM] = jnp.dot(
            probs, head(value_ref, h), preferred_element_type=F32
        )


def mix_kernel(devices, rows, received_ref, out_ref):
    padded = received_ref.shape[1] - DECAY_ROWS
    half = DECAY_ROWS // 2
    held = jnp.zeros((out_ref.shape[1], HEAD_DIM), F32)
    for m in range(devices):
        out_ref[m] = held.astype(BF16)
        if m < devices - 1:
            decay_rows = received_ref[m, padded:, :].astype(F32)
            decay = (decay_rows[:half] + decay_rows[half:])[:1]
            held = held * decay + received_ref[m, :padded, :].astype(F32)


def project_kernel(
    heads, tp, query_ref, incoming_ref, intra_ref, own_ref, gain_ref, weight_ref,
    mine_ref, near_ref, far_mine_ref, far_near_ref,
):
    me = lax.axis_index("tp")
    parts = []
    for h in range(heads):
        state = incoming_ref[h * HEAD_DIM : (h + 1) * HEAD_DIM, :]
        inter = jnp.dot(head(query_ref, h), state, preferred_element_type=F32)
        attended = head(intra_ref, h) + own_ref[:, h : h + 1] * inter
        mean_square = jnp.mean(attended * attended, axis=-1, keepdims=True)
        normed = attended * lax.rsqrt(mean_square + 1e-06)
        gain = gain_ref[:, h * HEAD_DIM : (h + 1) * HEAD_DIM]
        parts.append((normed * gain).astype(BF16))
    normed = jnp.concatenate(parts, axis=1)
    width = weight_ref.shape[1] // tp

    def share(step):
        other = me ^ step
        columns = pl.ds(pl.multiple_of(other * width, width), width)
        return jnp.dot(normed, weight_ref[:, columns], preferred_element_type=F32)

    far_near_ref[...] = share(3).astype(BF16)
    far_mine_ref[...] = share(2)
    near_ref[...] = share(1).astype(BF16)
    mine_ref[...] = share(0)


def cost(flops, moved):
    return pl.CostEstimate(flops=flops, bytes_accessed=moved, transcendentals=0)


def on_device(
    residual, query_vectors, key_vectors, value_vectors, log_decay, norm_gain, out_weight
):
    tokens, width = residual.shape
    heads = log_decay.shape[0]
    devices = lax.axis_size("seq")
    tp = lax.axis_size("tp")
    rows = heads * HEAD_DIM // devices
    padded = -(-rows // 16) * 16
    limit = pltpu.CompilerParams(vmem_limit_bytes=24 * 1024 * 1024)

    sent = pl.pallas_call(
        functools.partial(state_kernel, heads, devices),
        out_shape=jax.ShapeDtypeStruct((devices, padded + DECAY_ROWS, HEAD_DIM), BF16),
        in_specs=[VMEM] * 3,
        out_specs=VMEM,
        compiler_params=limit,
        name="states",
    )(log_decay, key_vectors, value_vectors)
    received = lax.all_to_all(sent, "seq", split_axis=0, concat_axis=0, tiled=True)
    intra, own = pl.pallas_call(
        functools.partial(intra_kernel, heads),
        out_shape=(
            jax.ShapeDtypeStruct((tokens, heads * HEAD_DIM), F32),
            jax.ShapeDtypeStruct((tokens, heads), F32),
        ),
        in_specs=[VMEM] * 4,
        out_specs=(VMEM, VMEM),
        compiler_params=limit,
        cost_estimate=cost(4 * tokens * tokens * heads * HEAD_DIM, 2_000_000),
        name="intra",
    )(log_decay, query_vectors, key_vectors, value_vectors)
    mixed = pl.pallas_call(
        functools.partial(mix_kernel, devices, rows),
        out_shape=jax.ShapeDtypeStruct((devices, padded, HEAD_DIM), BF16),
        in_specs=[VMEM],
        out_specs=VMEM,
        compiler_params=limit,
        name="mix",
    )(received)
    incoming = lax.all_to_all(mixed, "seq", split_axis=0, concat_axis=0, tiled=True)
    incoming = incoming[:, :rows, :].reshape(heads * HEAD_DIM, HEAD_DIM)
    out_width = out_weight.shape[1] // tp
    mine, near, far_mine, far_near = pl.pallas_call(
        functools.partial(project_kernel, heads, tp),
        out_shape=tuple(
            jax.ShapeDtypeStruct((tokens, out_width), kind) for kind in (F32, BF16, F32, BF16)
        ),
        in_specs=[VMEM] * 6,
        out_specs=(VMEM,) * 4,
        compiler_params=limit,
        name="project",
    )(query_vectors, incoming, intra, own, norm_gain.reshape(1, -1), out_weight)
    near_pairs = [(i, i ^ 1) for i in range(tp)]
    far_pairs = [(i, i ^ 2) for i in range(tp)]
    far_near = lax.ppermute(far_near, "tp", near_pairs)
    near = lax.ppermute(near, "tp", near_pairs)
    far = lax.ppermute((far_mine + far_near.astype(F32)).astype(BF16), "tp", far_pairs)
    total = residual.astype(F32) + (mine + near.astype(F32)) + far.astype(F32)
    return total.astype(BF16)


def solution(mesh):
    return jax.shard_map(
        on_device,
        mesh=mesh,
        in_specs=(
            P("seq", "tp"),
            P("seq", "tp"),
            P("seq", "tp"),
            P("seq", "tp"),
            P("tp", "seq"),
            P("tp"),
            P("tp", None),
        ),
        out_specs=P("seq", "tp"),
        check_vma=False,
    )
```

```python
import functools

import jax
import jax.numpy as jnp
from jax import lax
from jax.experimental import pallas as pl
from jax.experimental.pallas import tpu as pltpu
from jax.sharding import PartitionSpec as P

HEAD_DIM = 128
GROUP = 256
SCALE = HEAD_DIM ** (-0.5)
F32 = jnp.float32
BF16 = jnp.bfloat16
VMEM = pl.BlockSpec(memory_space=pltpu.VMEM)
HBM = pl.BlockSpec(memory_space=pltpu.HBM)
DECAY_ROWS = 16
MESSAGE = (HEAD_DIM + DECAY_ROWS, HEAD_DIM)
PARAMS = pltpu.CompilerParams(vmem_limit_bytes=24 * 1024 * 1024)


def columns(h):
    return slice(h * HEAD_DIM, (h + 1) * HEAD_DIM)


def head_columns(h):
    return pl.ds(pl.multiple_of(h * HEAD_DIM, HEAD_DIM), HEAD_DIM)


def contract(a, b, dims, **kwargs):
    return lax.dot_general(
        a, b, ((dims[0], dims[1]), ((), ())), preferred_element_type=F32, **kwargs
    )


def positions():
    shape = (GROUP, GROUP)
    return lax.broadcasted_iota(jnp.int32, shape, 0), lax.broadcasted_iota(jnp.int32, shape, 1)


def decay_to_rows(decay):
    wide = jnp.broadcast_to(decay, (DECAY_ROWS // 2, HEAD_DIM))
    coarse = wide.astype(BF16).astype(F32)
    return jnp.concatenate([coarse, wide - coarse], axis=0).astype(BF16)


def rows_to_decay(message):
    rows = message[HEAD_DIM:, :].astype(F32)
    return (rows[: DECAY_ROWS // 2] + rows[DECAY_ROWS // 2 :])[:1]


def place(members):
    return lax.rem(lax.axis_index("seq"), members)


def state_kernel(heads, *refs):
    sources, outs, held = refs[:5], refs[5 : 5 + heads], refs[5 + heads : 10 + heads]
    sems = refs[10 + heads]
    decay_ref, key_ref, value_ref = held[:3]
    copies = [
        pltpu.make_async_copy(source, target, sems.at[i])
        for i, (source, target) in enumerate(zip(sources, held))
    ]
    for copy in copies:
        copy.start()
    me = place(heads)
    row, col = positions()
    later = jnp.where(col > row, 1.0, 0.0).astype(F32)
    copies[0].wait()
    decays = decay_ref[...]
    tail = jnp.exp(contract(later, decays, ((1,), (1,)), precision=lax.Precision.HIGHEST))
    whole = jnp.exp(jnp.sum(decays, axis=1, keepdims=True))
    lane = lax.broadcasted_iota(jnp.int32, tail.shape, 1)
    line = lax.broadcasted_iota(jnp.int32, whole.shape, 0)
    copies[1].wait()
    copies[2].wait()
    for step in range(heads):
        h = me ^ step
        factor = jnp.sum(jnp.where(lane == h, tail, 0.0), axis=1, keepdims=True)
        decay = jnp.sum(jnp.where(line == h, whole, 0.0), axis=0, keepdims=True)
        weighted = (key_ref[:, head_columns(h)].astype(F32) * factor).astype(BF16)
        update = contract(weighted, value_ref[:, head_columns(h)], ((0,), (0,)))
        outs[step][:HEAD_DIM, :] = update.astype(BF16)
        outs[step][HEAD_DIM:, :] = decay_to_rows(decay)
    for copy in copies[3:]:
        copy.wait()


def intra_kernel(
    heads, decay_ref, query_ref, key_ref, value_ref, out_ref, own_ref
):
    row, col = positions()
    causal = col <= row
    upto = jnp.where(causal, 1.0, 0.0).astype(F32)
    decays = decay_ref[...]
    down = contract(upto, decays, ((1,), (1,)), precision=lax.Precision.HIGHEST)
    across = contract(decays, upto, ((1,), (1,)), precision=lax.Precision.HIGHEST)
    own_ref[...] = jnp.exp(down) * SCALE
    for h in range(heads):
        at = columns(h)
        scores = contract(query_ref[:, at], key_ref[:, at], ((1,), (1,)))
        gaps = down[:, h : h + 1] - across[h : h + 1, :]
        weights = jnp.where(causal, jnp.exp(gaps), 0.0)
        probs = (scores * SCALE * weights).astype(BF16)
        out_ref[:, at] = jnp.dot(probs, value_ref[:, at], preferred_element_type=F32)


def gather_kernel(heads, after_ref, *refs):
    received, (prefix_ref, decay_ref, total_ref, held_ref) = refs[:heads], refs[heads:]
    me = place(heads)
    for step in range(heads):
        held_ref[me ^ step] = received[step][...]
    held = jnp.zeros((HEAD_DIM, HEAD_DIM), F32)
    through = jnp.ones((1, HEAD_DIM), F32)
    for m in range(heads):
        prefix_ref[m] = held
        decay_ref[m] = jnp.broadcast_to(through, decay_ref.shape[1:])
        message = held_ref[m]
        decay = rows_to_decay(message)
        held = held * decay + message[:HEAD_DIM, :].astype(F32)
        through = through * decay
    total_ref[:HEAD_DIM, :] = held.astype(BF16)
    total_ref[HEAD_DIM:, :] = decay_to_rows(through)


def scatter_kernel(heads, prefix_ref, decay_ref, earlier_ref, *outs):
    me = place(heads)
    earlier = earlier_ref[:HEAD_DIM, :].astype(F32)
    for step in range(heads):
        m = me ^ step
        outs[step][...] = (prefix_ref[m] + decay_ref[m][:1] * earlier).astype(BF16)


def norm_kernel(heads, query_ref, intra_ref, own_ref, gain_ref, *refs):
    received, (out_ref, state_ref) = refs[:heads], refs[heads:]
    me = place(heads)
    for step in range(heads):
        state_ref[me ^ step] = received[step][...]
    for h in range(heads):
        at = columns(h)
        inter = jnp.dot(query_ref[:, at], state_ref[h], preferred_element_type=F32)
        attended = intra_ref[:, at] + own_ref[:, h : h + 1] * inter
        mean_square = jnp.mean(attended * attended, axis=-1, keepdims=True)
        normed = attended * lax.rsqrt(mean_square + 1e-06)
        out_ref[:, at] = (normed * gain_ref[:, at]).astype(BF16)


def share(step, tp, mine_ref, other_ref, weight_ref, other_weight_ref):
    width = weight_ref.shape[1] // tp
    target = lax.axis_index("tp") ^ step
    at = pl.ds(pl.multiple_of(target * width, width), width)
    return jnp.dot(mine_ref[...], weight_ref[:, at], preferred_element_type=F32) + jnp.dot(
        other_ref[...], other_weight_ref[:, at], preferred_element_type=F32
    )


def far_kernel(tp, mine_ref, other_ref, weight_ref, other_weight_ref, out_ref):
    out_ref[...] = share(2, tp, mine_ref, other_ref, weight_ref, other_weight_ref).astype(BF16)


def near_kernel(tp, mine_ref, other_ref, weight_ref, other_weight_ref, residual_ref, out_ref):
    near = share(0, tp, mine_ref, other_ref, weight_ref, other_weight_ref)
    out_ref[...] = residual_ref[...].astype(F32) + near


def cost(flops, moved):
    return pl.CostEstimate(flops=flops, bytes_accessed=moved, transcendentals=0)


def earlier_groups(total, members, devices):
    groups = devices // members

    def shift(message, by):
        pairs = [(i, i + by * members) for i in range(devices - by * members)]
        return lax.ppermute(message, "seq", pairs)

    held = shift(total, 1)
    by = 1
    while by < groups - 1:
        before = shift(held, by)
        decay = rows_to_decay(held)
        state = held[:HEAD_DIM].astype(F32) + decay * before[:HEAD_DIM].astype(F32)
        through = decay_to_rows(decay * rows_to_decay(before))
        held = jnp.concatenate([state.astype(BF16), through], axis=0)
        by *= 2
    return held


def on_device(
    residual, query_vectors, key_vectors, value_vectors, log_decay, norm_gain, out_weight
):
    tokens, width = residual.shape
    heads = log_decay.shape[0]
    devices = lax.axis_size("seq")
    tp = lax.axis_size("tp")
    wide = (tokens, heads * HEAD_DIM)
    near_pairs = [(i, i ^ 1) for i in range(tp)]
    far_pairs = [(i, i ^ 2) for i in range(tp)]

    def exchange(pieces):
        moved = [
            lax.ppermute(pieces[step], "seq", [(i, i ^ step) for i in range(devices)])
            for step in range(1, heads)
        ]
        return [pieces[0]] + moved

    arguments = (log_decay, key_vectors, value_vectors, query_vectors, norm_gain.reshape(1, -1))
    *states, decays, keys, values, queries, gain = pl.pallas_call(
        functools.partial(state_kernel, heads),
        out_shape=(jax.ShapeDtypeStruct(MESSAGE, BF16),) * heads
        + tuple(jax.ShapeDtypeStruct(a.shape, a.dtype) for a in arguments),
        in_specs=[HBM] * 5,
        out_specs=(VMEM,) * (heads + 5),
        scratch_shapes=[pltpu.SemaphoreType.DMA((5,))],
        compiler_params=PARAMS,
        name="states",
    )(*(pltpu.with_memory_space_constraint(a, pltpu.HBM) for a in arguments))
    gathered = exchange(states)
    other_weight = lax.ppermute(out_weight, "tp", near_pairs)
    intra, own = pl.pallas_call(
        functools.partial(intra_kernel, heads),
        out_shape=(
            jax.ShapeDtypeStruct(wide, F32),
            jax.ShapeDtypeStruct((tokens, heads), F32),
        ),
        in_specs=[VMEM] * 4,
        out_specs=(VMEM,) * 2,
        compiler_params=PARAMS,
        cost_estimate=cost(4 * tokens * tokens * heads * HEAD_DIM, 2_000_000),
        name="intra",
    )(decays, queries, keys, values)
    prefix, through, total = pl.pallas_call(
        functools.partial(gather_kernel, heads),
        out_shape=(
            jax.ShapeDtypeStruct((heads, HEAD_DIM, HEAD_DIM), F32),
            jax.ShapeDtypeStruct((heads, 8, HEAD_DIM), F32),
            jax.ShapeDtypeStruct(MESSAGE, BF16),
        ),
        in_specs=[VMEM] * (heads + 1),
        out_specs=(VMEM,) * 3,
        scratch_shapes=[pltpu.VMEM((heads,) + MESSAGE, BF16)],
        compiler_params=PARAMS,
        name="gather_states",
    )(own, *gathered)
    earlier = earlier_groups(total, heads, devices)
    starts = pl.pallas_call(
        functools.partial(scatter_kernel, heads),
        out_shape=(jax.ShapeDtypeStruct((HEAD_DIM, HEAD_DIM), BF16),) * heads,
        in_specs=[VMEM] * 3,
        out_specs=(VMEM,) * heads,
        compiler_params=PARAMS,
        name="scatter_states",
    )(prefix, through, earlier)
    incoming = exchange(starts)
    normed = pl.pallas_call(
        functools.partial(norm_kernel, heads),
        out_shape=jax.ShapeDtypeStruct(wide, BF16),
        in_specs=[VMEM] * (4 + heads),
        out_specs=VMEM,
        scratch_shapes=[pltpu.VMEM((heads, HEAD_DIM, HEAD_DIM), BF16)],
        compiler_params=PARAMS,
        name="norm",
    )(queries, intra, own, gain, *incoming)
    other_normed = lax.ppermute(normed, "tp", near_pairs)
    out_width = out_weight.shape[1] // tp
    operands = (normed, other_normed, out_weight, other_weight)
    far = pl.pallas_call(
        functools.partial(far_kernel, tp),
        out_shape=jax.ShapeDtypeStruct((tokens, out_width), BF16),
        in_specs=[VMEM] * 4,
        out_specs=VMEM,
        compiler_params=PARAMS,
        name="project_far",
    )(*operands)
    far = lax.ppermute(far, "tp", far_pairs)
    near = pl.pallas_call(
        functools.partial(near_kernel, tp),
        out_shape=jax.ShapeDtypeStruct((tokens, out_width), F32),
        in_specs=[VMEM] * 5,
        out_specs=VMEM,
        compiler_params=PARAMS,
        cost_estimate=cost(4 * tokens * width * heads * HEAD_DIM, 2_000_000),
        name="project_near",
    )(*operands, residual)
    return (near + far.astype(F32)).astype(BF16)


def solution(mesh):
    return jax.shard_map(
        on_device,
        mesh=mesh,
        in_specs=(
            P("seq", "tp"),
            P("seq", "tp"),
            P("seq", "tp"),
            P("seq", "tp"),
            P("tp", "seq"),
            P("tp"),
            P("tp", None),
        ),
        out_specs=P("seq", "tp"),
        check_vma=False,
    )
```

```python
import functools

import jax
import jax.numpy as jnp
from jax import lax
from jax.experimental import pallas as pl
from jax.experimental.pallas import tpu as pltpu
from jax.sharding import PartitionSpec as P

HEAD_DIM = 128
GROUP = 256
SCALE = HEAD_DIM ** (-0.5)
F32 = jnp.float32
BF16 = jnp.bfloat16
VMEM = pl.BlockSpec(memory_space=pltpu.VMEM)
HBM = pl.BlockSpec(memory_space=pltpu.HBM)
DECAY_ROWS = 16
PARAMS = pltpu.CompilerParams(vmem_limit_bytes=24 * 1024 * 1024)


def columns(h):
    return slice(h * HEAD_DIM, (h + 1) * HEAD_DIM)


def head_columns(h):
    return pl.ds(pl.multiple_of(h * HEAD_DIM, HEAD_DIM), HEAD_DIM)


def contract(a, b, dims, **kwargs):
    return lax.dot_general(
        a, b, ((dims[0], dims[1]), ((), ())), preferred_element_type=F32, **kwargs
    )


def positions():
    shape = (GROUP, GROUP)
    return lax.broadcasted_iota(jnp.int32, shape, 0), lax.broadcasted_iota(jnp.int32, shape, 1)


def decay_to_rows(decay):
    wide = jnp.broadcast_to(decay, (DECAY_ROWS // 2, HEAD_DIM))
    coarse = wide.astype(BF16).astype(F32)
    return jnp.concatenate([coarse, wide - coarse], axis=0).astype(BF16)


def rows_to_decay(rows):
    rows = rows.astype(F32)
    return (rows[: DECAY_ROWS // 2] + rows[DECAY_ROWS // 2 :])[:1]


def state_rows(h):
    return slice(h * HEAD_DIM, (h + 1) * HEAD_DIM)


def decay_rows(heads, h):
    return slice(heads * HEAD_DIM + h * DECAY_ROWS, heads * HEAD_DIM + (h + 1) * DECAY_ROWS)


def side():
    return lax.rem(lax.axis_index("seq"), 2)


def state_kernel(half, *refs):
    sources, outs, held, sems = refs[:5], refs[5:7], refs[7:12], refs[12]
    decay_ref, key_ref, value_ref = held[:3]
    copies = [
        pltpu.make_async_copy(source, target, sems.at[i])
        for i, (source, target) in enumerate(zip(sources, held))
    ]
    for copy in copies:
        copy.start()
    me = side()
    row, col = positions()
    later = jnp.where(col > row, 1.0, 0.0).astype(F32)
    copies[0].wait()
    decays = decay_ref[...]
    tail = jnp.exp(contract(later, decays, ((1,), (1,)), precision=lax.Precision.HIGHEST))
    whole = jnp.exp(jnp.sum(decays, axis=1, keepdims=True))
    lane = lax.broadcasted_iota(jnp.int32, tail.shape, 1)
    line = lax.broadcasted_iota(jnp.int32, whole.shape, 0)
    copies[1].wait()
    copies[2].wait()
    for out_ref, owner in zip(outs, (1 - me, me)):
        for j in range(half):
            h = owner * half + j
            factor = jnp.sum(jnp.where(lane == h, tail, 0.0), axis=1, keepdims=True)
            decay = jnp.sum(jnp.where(line == h, whole, 0.0), axis=0, keepdims=True)
            weighted = (key_ref[:, head_columns(h)].astype(F32) * factor).astype(BF16)
            update = contract(weighted, value_ref[:, head_columns(h)], ((0,), (0,)))
            out_ref[state_rows(j), :] = update.astype(BF16)
            out_ref[decay_rows(half, j), :] = decay_to_rows(decay)
    for copy in copies[3:]:
        copy.wait()


def intra_kernel(
    heads, decay_ref, query_ref, key_ref, value_ref, out_ref, own_ref
):
    row, col = positions()
    causal = col <= row
    upto = jnp.where(causal, 1.0, 0.0).astype(F32)
    decays = decay_ref[...]
    down = contract(upto, decays, ((1,), (1,)), precision=lax.Precision.HIGHEST)
    across = contract(decays, upto, ((1,), (1,)), precision=lax.Precision.HIGHEST)
    own_ref[...] = jnp.exp(down) * SCALE
    for h in range(heads):
        at = columns(h)
        scores = contract(query_ref[:, at], key_ref[:, at], ((1,), (1,)))
        gaps = down[:, h : h + 1] - across[h : h + 1, :]
        weights = jnp.where(causal, jnp.exp(gaps), 0.0)
        probs = (scores * SCALE * weights).astype(BF16)
        out_ref[:, at] = jnp.dot(probs, value_ref[:, at], preferred_element_type=F32)


def pair_kernel(
    half, after_ref, mine_ref, other_ref, total_ref, through_ref, first_ref, decay_ref, sent_ref
):
    second = side() == 1
    for j in range(half):
        at = state_rows(j)
        mine, other = mine_ref[at, :].astype(F32), other_ref[at, :].astype(F32)
        mine_decay = rows_to_decay(mine_ref[decay_rows(half, j), :])
        other_decay = rows_to_decay(other_ref[decay_rows(half, j), :])
        first = jnp.where(second, other, mine)
        first_decay = jnp.where(second, other_decay, mine_decay)
        last_decay = jnp.where(second, mine_decay, other_decay)
        total = first * last_decay + jnp.where(second, mine, other)
        total_ref[at, :] = total
        sent_ref[at, :] = total.astype(BF16)
        first_ref[at, :] = first
        rows = slice(j * 8, (j + 1) * 8)
        through_ref[rows, :] = jnp.broadcast_to(first_decay * last_decay, (8, HEAD_DIM))
        decay_ref[rows, :] = jnp.broadcast_to(first_decay, (8, HEAD_DIM))


def chain_kernel(half, total_ref, through_ref, received_ref, out_ref):
    for j in range(half):
        at = state_rows(j)
        through = through_ref[j * 8 : j * 8 + 1, :]
        held = total_ref[at, :] + through * received_ref[at, :].astype(F32)
        out_ref[at, :] = held.astype(BF16)


def start_kernel(half, first_ref, decay_ref, *refs):
    received, (mine_ref, other_ref) = refs[:-2], refs[-2:]
    second = side() == 1
    for j in range(half):
        at = state_rows(j)
        earlier = received[0][at, :].astype(F32)
        for ref in received[1:]:
            earlier = earlier + ref[at, :].astype(F32)
        decay = decay_ref[j * 8 : j * 8 + 1, :]
        last = (first_ref[at, :] + decay * earlier).astype(BF16)
        first = earlier.astype(BF16)
        mine_ref[at, :] = jnp.where(second, last, first)
        other_ref[at, :] = jnp.where(second, first, last)


def norm_kernel(
    heads, query_ref, intra_ref, own_ref, gain_ref, mine_ref, other_ref, out_ref, state_ref
):
    me = side()
    state_ref[me] = mine_ref[...]
    state_ref[1 - me] = other_ref[...]
    half = heads // 2
    for h in range(heads):
        at = columns(h)
        state = state_ref[h // half, state_rows(h % half), :]
        inter = jnp.dot(query_ref[:, at], state, preferred_element_type=F32)
        attended = intra_ref[:, at] + own_ref[:, h : h + 1] * inter
        mean_square = jnp.mean(attended * attended, axis=-1, keepdims=True)
        normed = attended * lax.rsqrt(mean_square + 1e-06)
        out_ref[:, at] = (normed * gain_ref[:, at]).astype(BF16)


def share(step, tp, mine_ref, other_ref, weight_ref, other_weight_ref):
    width = weight_ref.shape[1] // tp
    target = lax.axis_index("tp") ^ step
    at = pl.ds(pl.multiple_of(target * width, width), width)
    return jnp.dot(mine_ref[...], weight_ref[:, at], preferred_element_type=F32) + jnp.dot(
        other_ref[...], other_weight_ref[:, at], preferred_element_type=F32
    )


def far_kernel(tp, mine_ref, other_ref, weight_ref, other_weight_ref, out_ref):
    out_ref[...] = share(2, tp, mine_ref, other_ref, weight_ref, other_weight_ref).astype(BF16)


def near_kernel(tp, mine_ref, other_ref, weight_ref, other_weight_ref, residual_ref, out_ref):
    near = share(0, tp, mine_ref, other_ref, weight_ref, other_weight_ref)
    out_ref[...] = residual_ref[...].astype(F32) + near


def cost(flops, moved):
    return pl.CostEstimate(flops=flops, bytes_accessed=moved, transcendentals=0)


def earlier_pairs(total, through, sent, half, devices):
    pairs = devices // 2
    if pairs <= 4:
        received = []
        for step in range(pairs - 1):
            hop = [(2 * step + i, 2 * step + 2 + i) for i in range(2)]
            received.append(lax.ppermute(sent, "seq", hop))
            if step < pairs - 2:
                sent = pl.pallas_call(
                    functools.partial(chain_kernel, half),
                    out_shape=jax.ShapeDtypeStruct(sent.shape, BF16),
                    in_specs=[VMEM] * 3,
                    out_specs=VMEM,
                    compiler_params=PARAMS,
                    name="chain",
                )(total, through, received[-1])
        return received

    def shift(message, by):
        moves = [(i, i + 2 * by) for i in range(devices - 2 * by)]
        return lax.ppermute(message, "seq", moves)

    factor = jnp.repeat(through[::8], HEAD_DIM, axis=0)
    state, factor = shift(sent, 1).astype(F32), shift(factor, 1)
    by = 1
    while by < pairs - 1:
        state = state + factor * shift(state.astype(BF16), by).astype(F32)
        factor = factor * shift(factor, by)
        by *= 2
    return [state.astype(BF16)]


def on_device(
    residual, query_vectors, key_vectors, value_vectors, log_decay, norm_gain, out_weight
):
    tokens, width = residual.shape
    heads = log_decay.shape[0]
    devices = lax.axis_size("seq")
    tp = lax.axis_size("tp")
    wide = (tokens, heads * HEAD_DIM)
    near_pairs = [(i, i ^ 1) for i in range(tp)]
    far_pairs = [(i, i ^ 2) for i in range(tp)]

    arguments = (log_decay, key_vectors, value_vectors, query_vectors, norm_gain.reshape(1, -1))
    half = heads // 2
    message = jax.ShapeDtypeStruct((half * (HEAD_DIM + DECAY_ROWS), HEAD_DIM), BF16)
    side_pairs = [(i, i ^ 1) for i in range(devices)]
    outgoing, kept, decays, keys, values, queries, gain = pl.pallas_call(
        functools.partial(state_kernel, half),
        out_shape=(message, message)
        + tuple(jax.ShapeDtypeStruct(a.shape, a.dtype) for a in arguments),
        in_specs=[HBM] * 5,
        out_specs=(VMEM,) * 7,
        scratch_shapes=[pltpu.SemaphoreType.DMA((5,))],
        compiler_params=PARAMS,
        name="states",
    )(*(pltpu.with_memory_space_constraint(a, pltpu.HBM) for a in arguments))
    gathered = lax.ppermute(outgoing, "seq", side_pairs)
    intra, own = pl.pallas_call(
        functools.partial(intra_kernel, heads),
        out_shape=(
            jax.ShapeDtypeStruct(wide, F32),
            jax.ShapeDtypeStruct((tokens, heads), F32),
        ),
        in_specs=[VMEM] * 4,
        out_specs=(VMEM,) * 2,
        compiler_params=PARAMS,
        cost_estimate=cost(4 * tokens * tokens * heads * HEAD_DIM, 2_000_000),
        name="intra",
    )(decays, queries, keys, values)
    other_weight = lax.ppermute(out_weight, "tp", near_pairs)
    states = (half * HEAD_DIM, HEAD_DIM)
    factors = jax.ShapeDtypeStruct((half * 8, HEAD_DIM), F32)
    total, through, first, first_decay, sent = pl.pallas_call(
        functools.partial(pair_kernel, half),
        out_shape=(
            jax.ShapeDtypeStruct(states, F32),
            factors,
            jax.ShapeDtypeStruct(states, F32),
            factors,
            jax.ShapeDtypeStruct(states, BF16),
        ),
        in_specs=[VMEM] * 3,
        out_specs=(VMEM,) * 5,
        compiler_params=PARAMS,
        name="pair_states",
    )(own, kept, gathered)
    earlier = earlier_pairs(total, through, sent, half, devices)
    mine, other = pl.pallas_call(
        functools.partial(start_kernel, half),
        out_shape=(jax.ShapeDtypeStruct(states, BF16),) * 2,
        in_specs=[VMEM] * (2 + len(earlier)),
        out_specs=(VMEM,) * 2,
        compiler_params=PARAMS,
        name="start_states",
    )(first, first_decay, *earlier)
    other = lax.ppermute(other, "seq", side_pairs)
    normed = pl.pallas_call(
        functools.partial(norm_kernel, heads),
        out_shape=jax.ShapeDtypeStruct(wide, BF16),
        in_specs=[VMEM] * 6,
        out_specs=VMEM,
        scratch_shapes=[pltpu.VMEM((2,) + states, BF16)],
        compiler_params=PARAMS,
        name="norm",
    )(queries, intra, own, gain, mine, other)
    other_normed = lax.ppermute(normed, "tp", near_pairs)
    out_width = out_weight.shape[1] // tp
    operands = (normed, other_normed, out_weight, other_weight)
    far = pl.pallas_call(
        functools.partial(far_kernel, tp),
        out_shape=jax.ShapeDtypeStruct((tokens, out_width), BF16),
        in_specs=[VMEM] * 4,
        out_specs=VMEM,
        compiler_params=PARAMS,
        name="project_far",
    )(*operands)
    far = lax.ppermute(far, "tp", far_pairs)
    near = pl.pallas_call(
        functools.partial(near_kernel, tp),
        out_shape=jax.ShapeDtypeStruct((tokens, out_width), F32),
        in_specs=[VMEM] * 5,
        out_specs=VMEM,
        compiler_params=PARAMS,
        cost_estimate=cost(4 * tokens * width * heads * HEAD_DIM, 2_000_000),
        name="project_near",
    )(*operands, residual)
    return (near + far.astype(F32)).astype(BF16)


def solution(mesh):
    return jax.shard_map(
        on_device,
        mesh=mesh,
        in_specs=(
            P("seq", "tp"),
            P("seq", "tp"),
            P("seq", "tp"),
            P("seq", "tp"),
            P("tp", "seq"),
            P("tp"),
            P("tp", None),
        ),
        out_specs=P("seq", "tp"),
        check_vma=False,
    )
```

```python
import functools

import jax
import jax.numpy as jnp
from jax import lax
from jax.experimental import pallas as pl
from jax.experimental.pallas import tpu as pltpu
from jax.sharding import PartitionSpec as P

HEAD_DIM = 128
GROUP = 256
SCALE = HEAD_DIM ** (-0.5)
F32 = jnp.float32
BF16 = jnp.bfloat16
VMEM = pl.BlockSpec(memory_space=pltpu.VMEM)
HBM = pl.BlockSpec(memory_space=pltpu.HBM)
DECAY_ROWS = 16
PARAMS = pltpu.CompilerParams(vmem_limit_bytes=24 * 1024 * 1024)


def columns(h):
    return slice(h * HEAD_DIM, (h + 1) * HEAD_DIM)


def head_columns(h):
    return pl.ds(pl.multiple_of(h * HEAD_DIM, HEAD_DIM), HEAD_DIM)


def contract(a, b, dims, **kwargs):
    return lax.dot_general(
        a, b, ((dims[0], dims[1]), ((), ())), preferred_element_type=F32, **kwargs
    )


def positions():
    shape = (GROUP, GROUP)
    return lax.broadcasted_iota(jnp.int32, shape, 0), lax.broadcasted_iota(jnp.int32, shape, 1)


def decay_to_rows(decay):
    wide = jnp.broadcast_to(decay, (DECAY_ROWS // 2, HEAD_DIM))
    coarse = wide.astype(BF16).astype(F32)
    return jnp.concatenate([coarse, wide - coarse], axis=0).astype(BF16)


def rows_to_decay(rows):
    rows = rows.astype(F32)
    return (rows[: DECAY_ROWS // 2] + rows[DECAY_ROWS // 2 :])[:1]


def state_rows(h):
    return slice(h * HEAD_DIM, (h + 1) * HEAD_DIM)


def decay_rows(heads, h):
    return slice(heads * HEAD_DIM + h * DECAY_ROWS, heads * HEAD_DIM + (h + 1) * DECAY_ROWS)


def side():
    return lax.rem(lax.axis_index("seq"), 2)


def state_kernel(half, *refs):
    sources, outs, held, sems = refs[:5], refs[5:7], refs[7:12], refs[12]
    decay_ref, key_ref, value_ref = held[:3]
    copies = [
        pltpu.make_async_copy(source, target, sems.at[i])
        for i, (source, target) in enumerate(zip(sources, held))
    ]
    for copy in copies:
        copy.start()
    me = side()
    row, col = positions()
    later = jnp.where(col > row, 1.0, 0.0).astype(F32)
    copies[0].wait()
    decays = decay_ref[...]
    tail = jnp.exp(contract(later, decays, ((1,), (1,)), precision=lax.Precision.HIGHEST))
    whole = jnp.exp(jnp.sum(decays, axis=1, keepdims=True))
    lane = lax.broadcasted_iota(jnp.int32, tail.shape, 1)
    line = lax.broadcasted_iota(jnp.int32, whole.shape, 0)
    copies[1].wait()
    copies[2].wait()
    for out_ref, owner in zip(outs, (1 - me, me)):
        for j in range(half):
            h = owner * half + j
            factor = jnp.sum(jnp.where(lane == h, tail, 0.0), axis=1, keepdims=True)
            decay = jnp.sum(jnp.where(line == h, whole, 0.0), axis=0, keepdims=True)
            weighted = (key_ref[:, head_columns(h)].astype(F32) * factor).astype(BF16)
            update = contract(weighted, value_ref[:, head_columns(h)], ((0,), (0,)))
            out_ref[state_rows(j), :] = update.astype(BF16)
            out_ref[decay_rows(half, j), :] = decay_to_rows(decay)
    for copy in copies[3:]:
        copy.wait()


def intra_kernel(
    heads, decay_ref, query_ref, key_ref, value_ref, out_ref, own_ref
):
    row, col = positions()
    causal = col <= row
    upto = jnp.where(causal, 1.0, 0.0).astype(F32)
    decays = decay_ref[...]
    down = contract(upto, decays, ((1,), (1,)), precision=lax.Precision.HIGHEST)
    across = contract(decays, upto, ((1,), (1,)), precision=lax.Precision.HIGHEST)
    own_ref[...] = jnp.exp(down) * SCALE
    for h in range(heads):
        at = columns(h)
        scores = contract(query_ref[:, at], key_ref[:, at], ((1,), (1,)))
        gaps = down[:, h : h + 1] - across[h : h + 1, :]
        weights = jnp.where(causal, jnp.exp(gaps), 0.0)
        probs = (scores * SCALE * weights).astype(BF16)
        out_ref[:, at] = jnp.dot(probs, value_ref[:, at], preferred_element_type=F32)


def pair_kernel(
    half, after_ref, mine_ref, other_ref, total_ref, through_ref, first_ref, decay_ref, sent_ref
):
    second = side() == 1
    for j in range(half):
        at = state_rows(j)
        mine, other = mine_ref[at, :].astype(F32), other_ref[at, :].astype(F32)
        mine_decay = rows_to_decay(mine_ref[decay_rows(half, j), :])
        other_decay = rows_to_decay(other_ref[decay_rows(half, j), :])
        first = jnp.where(second, other, mine)
        first_decay = jnp.where(second, other_decay, mine_decay)
        last_decay = jnp.where(second, mine_decay, other_decay)
        total = first * last_decay + jnp.where(second, mine, other)
        total_ref[at, :] = total
        sent_ref[at, :] = total.astype(BF16)
        sent_ref[decay_rows(half, j), :] = decay_to_rows(first_decay * last_decay)
        first_ref[at, :] = first
        rows = slice(j * 8, (j + 1) * 8)
        through_ref[rows, :] = jnp.broadcast_to(first_decay * last_decay, (8, HEAD_DIM))
        decay_ref[rows, :] = jnp.broadcast_to(first_decay, (8, HEAD_DIM))


def rank():
    return lax.axis_index("seq") // 2


def lower_kernel(half, total_ref, through_ref, received_ref, out_ref):
    second = lax.rem(rank(), 2) == 1
    for j in range(half):
        at = state_rows(j)
        mine, other = total_ref[at, :], received_ref[at, :].astype(F32)
        mine_decay = through_ref[j * 8 : j * 8 + 1, :]
        other_decay = rows_to_decay(received_ref[decay_rows(half, j), :])
        first = jnp.where(second, other, mine)
        last = jnp.where(second, mine, other)
        decay = jnp.where(second, mine_decay, other_decay)
        out_ref[at, :] = (first * decay + last).astype(BF16)


def earlier_kernel(half, low_ref, high_ref, lower_ref, out_ref):
    me = rank()
    for j in range(half):
        at = state_rows(j)
        low, high = low_ref[at, :], high_ref[at, :].astype(F32)
        lower = lower_ref[at, :]
        decay = rows_to_decay(high_ref[decay_rows(half, j), :])
        last = (high + decay * lower.astype(F32)).astype(BF16)
        upper = jnp.where(me == 2, lower, last)
        out_ref[at, :] = jnp.where(me >= 2, upper, jnp.where(me == 1, low, jnp.zeros_like(low)))


def start_kernel(half, first_ref, decay_ref, earlier_ref, mine_ref, other_ref):
    second = side() == 1
    for j in range(half):
        at = state_rows(j)
        earlier = earlier_ref[at, :].astype(F32)
        decay = decay_ref[j * 8 : j * 8 + 1, :]
        last = (first_ref[at, :] + decay * earlier).astype(BF16)
        first = earlier.astype(BF16)
        mine_ref[at, :] = jnp.where(second, last, first)
        other_ref[at, :] = jnp.where(second, first, last)


def norm_kernel(
    heads, query_ref, intra_ref, own_ref, gain_ref, mine_ref, other_ref, out_ref, state_ref
):
    me = side()
    state_ref[me] = mine_ref[...]
    state_ref[1 - me] = other_ref[...]
    half = heads // 2
    for h in range(heads):
        at = columns(h)
        state = state_ref[h // half, state_rows(h % half), :]
        inter = jnp.dot(query_ref[:, at], state, preferred_element_type=F32)
        attended = intra_ref[:, at] + own_ref[:, h : h + 1] * inter
        mean_square = jnp.mean(attended * attended, axis=-1, keepdims=True)
        normed = attended * lax.rsqrt(mean_square + 1e-06)
        out_ref[:, at] = (normed * gain_ref[:, at]).astype(BF16)


def share(step, tp, mine_ref, other_ref, weight_ref, other_weight_ref):
    width = weight_ref.shape[1] // tp
    target = lax.axis_index("tp") ^ step
    at = pl.ds(pl.multiple_of(target * width, width), width)
    return jnp.dot(mine_ref[...], weight_ref[:, at], preferred_element_type=F32) + jnp.dot(
        other_ref[...], other_weight_ref[:, at], preferred_element_type=F32
    )


def far_kernel(tp, mine_ref, other_ref, weight_ref, other_weight_ref, out_ref):
    out_ref[...] = share(2, tp, mine_ref, other_ref, weight_ref, other_weight_ref).astype(BF16)


def near_kernel(tp, mine_ref, other_ref, weight_ref, other_weight_ref, residual_ref, out_ref):
    near = share(0, tp, mine_ref, other_ref, weight_ref, other_weight_ref)
    out_ref[...] = residual_ref[...].astype(F32) + near


def cost(flops, moved):
    return pl.CostEstimate(flops=flops, bytes_accessed=moved, transcendentals=0)


def earlier_pairs(total, through, sent, half, devices):
    pairs = devices // 2
    shape = jax.ShapeDtypeStruct(total.shape, BF16)
    if pairs == 4:

        def swap(message, partner):
            moves = [(2 * i + y, 2 * partner[i] + y) for i in range(4) for y in range(2)]
            return lax.ppermute(message, "seq", moves)

        low = swap(sent, (1, 0, 2, 3))
        high = swap(sent, (0, 1, 3, 2))
        lower = pl.pallas_call(
            functools.partial(lower_kernel, half),
            out_shape=shape,
            in_specs=[VMEM] * 3,
            out_specs=VMEM,
            compiler_params=PARAMS,
            name="lower_states",
        )(total, through, low)
        lower = swap(lower, (2, 3, 0, 1))
        return pl.pallas_call(
            functools.partial(earlier_kernel, half),
            out_shape=shape,
            in_specs=[VMEM] * 3,
            out_specs=VMEM,
            compiler_params=PARAMS,
            name="earlier_states",
        )(low, high, lower)

    def shift(message, by):
        moves = [(i, i + 2 * by) for i in range(devices - 2 * by)]
        return lax.ppermute(message, "seq", moves)

    factor = jnp.repeat(through[::8], HEAD_DIM, axis=0)
    state, factor = shift(total.astype(BF16), 1).astype(F32), shift(factor, 1)
    by = 1
    while by < pairs - 1:
        state = state + factor * shift(state.astype(BF16), by).astype(F32)
        factor = factor * shift(factor, by)
        by *= 2
    return state.astype(BF16)


def on_device(
    residual, query_vectors, key_vectors, value_vectors, log_decay, norm_gain, out_weight
):
    tokens, width = residual.shape
    heads = log_decay.shape[0]
    devices = lax.axis_size("seq")
    tp = lax.axis_size("tp")
    wide = (tokens, heads * HEAD_DIM)
    near_pairs = [(i, i ^ 1) for i in range(tp)]
    far_pairs = [(i, i ^ 2) for i in range(tp)]

    arguments = (log_decay, key_vectors, value_vectors, query_vectors, norm_gain.reshape(1, -1))
    half = heads // 2
    message = jax.ShapeDtypeStruct((half * (HEAD_DIM + DECAY_ROWS), HEAD_DIM), BF16)
    side_pairs = [(i, i ^ 1) for i in range(devices)]
    outgoing, kept, decays, keys, values, queries, gain = pl.pallas_call(
        functools.partial(state_kernel, half),
        out_shape=(message, message)
        + tuple(jax.ShapeDtypeStruct(a.shape, a.dtype) for a in arguments),
        in_specs=[HBM] * 5,
        out_specs=(VMEM,) * 7,
        scratch_shapes=[pltpu.SemaphoreType.DMA((5,))],
        compiler_params=PARAMS,
        name="states",
    )(*(pltpu.with_memory_space_constraint(a, pltpu.HBM) for a in arguments))
    gathered = lax.ppermute(outgoing, "seq", side_pairs)
    intra, own = pl.pallas_call(
        functools.partial(intra_kernel, heads),
        out_shape=(
            jax.ShapeDtypeStruct(wide, F32),
            jax.ShapeDtypeStruct((tokens, heads), F32),
        ),
        in_specs=[VMEM] * 4,
        out_specs=(VMEM,) * 2,
        compiler_params=PARAMS,
        cost_estimate=cost(4 * tokens * tokens * heads * HEAD_DIM, 2_000_000),
        name="intra",
    )(decays, queries, keys, values)
    other_weight = lax.ppermute(out_weight, "tp", near_pairs)
    states = (half * HEAD_DIM, HEAD_DIM)
    factors = jax.ShapeDtypeStruct((half * 8, HEAD_DIM), F32)
    total, through, first, first_decay, sent = pl.pallas_call(
        functools.partial(pair_kernel, half),
        out_shape=(
            jax.ShapeDtypeStruct(states, F32),
            factors,
            jax.ShapeDtypeStruct(states, F32),
            factors,
            message,
        ),
        in_specs=[VMEM] * 3,
        out_specs=(VMEM,) * 5,
        compiler_params=PARAMS,
        name="pair_states",
    )(own, kept, gathered)
    earlier = earlier_pairs(total, through, sent, half, devices)
    mine, other = pl.pallas_call(
        functools.partial(start_kernel, half),
        out_shape=(jax.ShapeDtypeStruct(states, BF16),) * 2,
        in_specs=[VMEM] * 3,
        out_specs=(VMEM,) * 2,
        compiler_params=PARAMS,
        name="start_states",
    )(first, first_decay, earlier)
    other = lax.ppermute(other, "seq", side_pairs)
    normed = pl.pallas_call(
        functools.partial(norm_kernel, heads),
        out_shape=jax.ShapeDtypeStruct(wide, BF16),
        in_specs=[VMEM] * 6,
        out_specs=VMEM,
        scratch_shapes=[pltpu.VMEM((2,) + states, BF16)],
        compiler_params=PARAMS,
        name="norm",
    )(queries, intra, own, gain, mine, other)
    other_normed = lax.ppermute(normed, "tp", near_pairs)
    out_width = out_weight.shape[1] // tp
    operands = (normed, other_normed, out_weight, other_weight)
    far = pl.pallas_call(
        functools.partial(far_kernel, tp),
        out_shape=jax.ShapeDtypeStruct((tokens, out_width), BF16),
        in_specs=[VMEM] * 4,
        out_specs=VMEM,
        compiler_params=PARAMS,
        name="project_far",
    )(*operands)
    far = lax.ppermute(far, "tp", far_pairs)
    near = pl.pallas_call(
        functools.partial(near_kernel, tp),
        out_shape=jax.ShapeDtypeStruct((tokens, out_width), F32),
        in_specs=[VMEM] * 5,
        out_specs=VMEM,
        compiler_params=PARAMS,
        cost_estimate=cost(4 * tokens * width * heads * HEAD_DIM, 2_000_000),
        name="project_near",
    )(*operands, residual)
    return (near + far.astype(F32)).astype(BF16)


def solution(mesh):
    return jax.shard_map(
        on_device,
        mesh=mesh,
        in_specs=(
            P("seq", "tp"),
            P("seq", "tp"),
            P("seq", "tp"),
            P("seq", "tp"),
            P("tp", "seq"),
            P("tp"),
            P("tp", None),
        ),
        out_specs=P("seq", "tp"),
        check_vma=False,
    )
```

```python
import functools

import jax
import jax.numpy as jnp
from jax import lax
from jax.experimental import pallas as pl
from jax.experimental.pallas import tpu as pltpu
from jax.sharding import PartitionSpec as P

HEAD_DIM = 128
GROUP = 256
SCALE = HEAD_DIM ** (-0.5)
F32 = jnp.float32
BF16 = jnp.bfloat16
VMEM = pl.BlockSpec(memory_space=pltpu.VMEM)
HBM = pl.BlockSpec(memory_space=pltpu.HBM)
DECAY_ROWS = 16
PARAMS = pltpu.CompilerParams(vmem_limit_bytes=24 * 1024 * 1024)


def columns(h):
    return slice(h * HEAD_DIM, (h + 1) * HEAD_DIM)


def head_columns(h):
    return pl.ds(pl.multiple_of(h * HEAD_DIM, HEAD_DIM), HEAD_DIM)


def state_rows(h):
    return slice(h * HEAD_DIM, (h + 1) * HEAD_DIM)


def contract(a, b, dims):
    return lax.dot_general(a, b, ((dims[0], dims[1]), ((), ())), preferred_element_type=F32)


def positions():
    shape = (GROUP, GROUP)
    return lax.broadcasted_iota(jnp.int32, shape, 0), lax.broadcasted_iota(jnp.int32, shape, 1)


def three_terms(values):
    first = values.astype(BF16).astype(F32)
    second = (values - first).astype(BF16).astype(F32)
    third = values - first - second
    return jnp.concatenate([first, second, third], axis=0).astype(BF16)


def sums_down(mask, decays):
    heads = decays.shape[0]
    terms = contract(mask, three_terms(decays), ((1,), (1,)))
    return terms[:, :heads] + terms[:, heads : 2 * heads] + terms[:, 2 * heads :]


def sums_across(mask, decays):
    heads = decays.shape[0]
    terms = contract(three_terms(decays), mask, ((1,), (1,)))
    return terms[:heads] + terms[heads : 2 * heads] + terms[2 * heads :]


def decays_to_rows(decays):
    each = DECAY_ROWS // (2 * len(decays))
    wide = jnp.concatenate([jnp.broadcast_to(d, (each, HEAD_DIM)) for d in decays], axis=0)
    coarse = wide.astype(BF16).astype(F32)
    return jnp.concatenate([coarse, wide - coarse], axis=0).astype(BF16)


def rows_to_decays(message_ref, half):
    rows = message_ref[half * HEAD_DIM :, :].astype(F32)
    each = DECAY_ROWS // (2 * half)
    both = rows[: DECAY_ROWS // 2] + rows[DECAY_ROWS // 2 :]
    return [both[j * each : j * each + 1] for j in range(half)]


def side():
    return lax.rem(lax.axis_index("seq"), 2)


def pick(owner, values, half, axis):
    low = lax.slice_in_dim(values, 0, half, axis=axis)
    high = lax.slice_in_dim(values, half, 2 * half, axis=axis)
    return jnp.where(owner == 0, low, high)


def write_states(owner, half, decay_ref, key_ref, value_ref, out_ref):
    row, col = positions()
    later = jnp.where(col > row, 1.0, 0.0).astype(BF16)
    decays = decay_ref[...]
    tail = pick(owner, jnp.exp(sums_down(later, decays)), half, 1)
    whole = pick(owner, jnp.exp(jnp.sum(decays, axis=1, keepdims=True)), half, 0)
    for j in range(half):
        at = head_columns(owner * half + j)
        weighted = (key_ref[:, at].astype(F32) * tail[:, j : j + 1]).astype(BF16)
        update = contract(weighted, value_ref[:, at], ((0,), (0,)))
        out_ref[state_rows(j), :] = update.astype(BF16)
    out_ref[half * HEAD_DIM :, :] = decays_to_rows([whole[j : j + 1] for j in range(half)])


def outgoing_kernel(half, *refs):
    sources, out_ref, held, sems = refs[:5], refs[5], refs[6:11], refs[11]
    copies = [
        pltpu.make_async_copy(source, target, sems.at[i])
        for i, (source, target) in enumerate(zip(sources, held))
    ]
    for copy in copies:
        copy.start()
    for copy in copies[:3]:
        copy.wait()
    write_states(1 - side(), half, *held[:3], out_ref)
    for copy in copies[3:]:
        copy.wait()


def local_kernel(
    heads, decay_ref, query_ref, key_ref, value_ref, intra_ref, own_ref, kept_ref
):
    row, col = positions()
    causal = col <= row
    upto = jnp.where(causal, 1.0, 0.0).astype(BF16)
    decays = decay_ref[...]
    down = sums_down(upto, decays)
    across = sums_across(upto, decays)
    own_ref[...] = jnp.exp(down) * SCALE
    write_states(side(), heads // 2, decay_ref, key_ref, value_ref, kept_ref)
    for h in range(heads):
        at = columns(h)
        scores = contract(query_ref[:, at], key_ref[:, at], ((1,), (1,)))
        gaps = down[:, h : h + 1] - across[h : h + 1, :]
        weights = jnp.where(causal, jnp.exp(gaps), 0.0)
        probs = (scores * SCALE * weights).astype(BF16)
        intra_ref[:, at] = jnp.dot(probs, value_ref[:, at], preferred_element_type=F32)


def pair_kernel(
    half, mine_ref, other_ref, total_ref, through_ref, first_ref, decay_ref, sent_ref
):
    second = side() == 1
    mine_decays, other_decays = rows_to_decays(mine_ref, half), rows_to_decays(other_ref, half)
    throughs = []
    for j in range(half):
        at = state_rows(j)
        mine, other = mine_ref[at, :].astype(F32), other_ref[at, :].astype(F32)
        first = jnp.where(second, other, mine)
        first_decay = jnp.where(second, other_decays[j], mine_decays[j])
        last_decay = jnp.where(second, mine_decays[j], other_decays[j])
        total = first * last_decay + jnp.where(second, mine, other)
        total_ref[at, :] = total
        sent_ref[at, :] = total.astype(BF16)
        first_ref[at, :] = first
        through = first_decay * last_decay
        throughs.append(through)
        rows = slice(j * 8, (j + 1) * 8)
        through_ref[rows, :] = jnp.broadcast_to(through, (8, HEAD_DIM))
        decay_ref[rows, :] = jnp.broadcast_to(first_decay, (8, HEAD_DIM))
    sent_ref[half * HEAD_DIM :, :] = decays_to_rows(throughs)


def rank():
    return lax.axis_index("seq") // 2


def both_kernel(half, total_ref, through_ref, received_ref, out_ref):
    second = lax.rem(rank(), 2) == 1
    other_decays = rows_to_decays(received_ref, half)
    for j in range(half):
        at = state_rows(j)
        mine, other = total_ref[at, :], received_ref[at, :].astype(F32)
        mine_decay = through_ref[j * 8 : j * 8 + 1, :]
        first = jnp.where(second, other, mine)
        last = jnp.where(second, mine, other)
        decay = jnp.where(second, mine_decay, other_decays[j])
        out_ref[at, :] = (first * decay + last).astype(BF16)


def write_starts(half, first_ref, decay_ref, earlier, mine_ref, other_ref):
    second = side() == 1
    for j in range(half):
        at = state_rows(j)
        decay = decay_ref[j * 8 : j * 8 + 1, :]
        last = (first_ref[at, :] + decay * earlier[j]).astype(BF16)
        first = earlier[j].astype(BF16)
        mine_ref[at, :] = jnp.where(second, last, first)
        other_ref[at, :] = jnp.where(second, first, last)


def start_kernel(half, first_ref, decay_ref, earlier_ref, mine_ref, other_ref):
    earlier = [earlier_ref[state_rows(j), :].astype(F32) for j in range(half)]
    write_starts(half, first_ref, decay_ref, earlier, mine_ref, other_ref)


def start_of_four_kernel(
    half, first_ref, decay_ref, near_ref, far_ref, mine_ref, other_ref
):
    me = rank()
    second, upper = lax.rem(me, 2) == 1, me >= 2
    near_decays = rows_to_decays(near_ref, half)
    earlier = []
    for j in range(half):
        at = state_rows(j)
        far = jnp.where(upper, far_ref[at, :].astype(F32), 0.0)
        passed = near_ref[at, :].astype(F32) + near_decays[j] * far
        earlier.append(jnp.where(second, passed, far))
    write_starts(half, first_ref, decay_ref, earlier, mine_ref, other_ref)


def norm_kernel(
    heads, rows, query_ref, intra_ref, own_ref, gain_ref, mine_ref, other_ref, out_ref, state_ref
):
    me = side()
    state_ref[me] = mine_ref[...]
    state_ref[1 - me] = other_ref[...]
    half = heads // 2
    for h in range(heads):
        at = columns(h)
        state = state_ref[h // half, state_rows(h % half), :]
        inter = jnp.dot(query_ref[rows, at], state, preferred_element_type=F32)
        attended = intra_ref[rows, at] + own_ref[rows, h : h + 1] * inter
        mean_square = jnp.mean(attended * attended, axis=-1, keepdims=True)
        normed = attended * lax.rsqrt(mean_square + 1e-06)
        out_ref[:, at] = (normed * gain_ref[:, at]).astype(BF16)


def share(step, tp, mine_ref, other_ref, weight_ref, other_weight_ref):
    width = weight_ref.shape[1] // tp
    target = lax.axis_index("tp") ^ step
    at = pl.ds(pl.multiple_of(target * width, width), width)
    return jnp.dot(mine_ref[...], weight_ref[:, at], preferred_element_type=F32) + jnp.dot(
        other_ref[...], other_weight_ref[:, at], preferred_element_type=F32
    )


def far_kernel(tp, mine_ref, other_ref, weight_ref, other_weight_ref, out_ref):
    out_ref[...] = share(2, tp, mine_ref, other_ref, weight_ref, other_weight_ref).astype(BF16)


def near_kernel(tp, chunks, residual_ref, weight_ref, other_weight_ref, *refs):
    out_ref = refs[-1]
    for i, rows in enumerate(chunks):
        near = share(0, tp, refs[2 * i], refs[2 * i + 1], weight_ref, other_weight_ref)
        out_ref[rows, :] = residual_ref[rows, :].astype(F32) + near


def last_kernel(chunks, near_ref, *refs):
    far, (out_hbm, out_ref, sems) = refs[: len(chunks)], refs[len(chunks) :]
    copies = []
    for i, rows in enumerate(chunks):
        out_ref[rows, :] = (near_ref[rows, :] + far[i][...].astype(F32)).astype(BF16)
        copies.append(
            pltpu.make_async_copy(out_ref.at[rows, :], out_hbm.at[rows, :], sems.at[i])
        )
        copies[-1].start()
    for copy in copies:
        copy.wait()


def call(kernel, out_shape, in_specs, name, out_specs=None, scratch=(), cost=None):
    single = isinstance(out_shape, jax.ShapeDtypeStruct)
    if out_specs is None:
        out_specs = VMEM if single else (VMEM,) * len(out_shape)
    if cost is not None:
        cost = pl.CostEstimate(flops=cost, bytes_accessed=2_000_000, transcendentals=0)
    return pl.pallas_call(
        kernel,
        out_shape=out_shape,
        in_specs=in_specs,
        out_specs=out_specs,
        scratch_shapes=scratch,
        compiler_params=PARAMS,
        cost_estimate=cost,
        name=name,
    )


def start_states(total, through, sent, first, first_decay, half, devices):
    pairs = devices // 2
    state = jax.ShapeDtypeStruct(total.shape, BF16)
    if pairs == 4:

        def swap(message, step):
            return lax.ppermute(message, "seq", [(i, i ^ step) for i in range(devices)])

        near = swap(sent, 2)
        both = call(functools.partial(both_kernel, half), state, [VMEM] * 3, "both_pairs")(
            total, through, near
        )
        far = swap(both, 4)
        kernel = functools.partial(start_of_four_kernel, half)
        return call(kernel, (state, state), [VMEM] * 4, "start_states")(
            first, first_decay, near, far
        )

    def shift(message, by):
        moves = [(i, i + 2 * by) for i in range(devices - 2 * by)]
        return lax.ppermute(message, "seq", moves)

    factor = jnp.repeat(through[::8], HEAD_DIM, axis=0)
    held, factor = shift(total.astype(BF16), 1).astype(F32), shift(factor, 1)
    by = 1
    while by < pairs - 1:
        held = held + factor * shift(held.astype(BF16), by).astype(F32)
        factor = factor * shift(factor, by)
        by *= 2
    kernel = functools.partial(start_kernel, half)
    return call(kernel, (state, state), [VMEM] * 3, "start_states")(
        first, first_decay, held.astype(BF16)
    )


def on_device(
    residual, query_vectors, key_vectors, value_vectors, log_decay, norm_gain, out_weight
):
    tokens, width = residual.shape
    heads = log_decay.shape[0]
    half = heads // 2
    devices = lax.axis_size("seq")
    tp = lax.axis_size("tp")
    wide = (tokens, heads * HEAD_DIM)
    near_pairs = [(i, i ^ 1) for i in range(tp)]
    far_pairs = [(i, i ^ 2) for i in range(tp)]
    side_pairs = [(i, i ^ 1) for i in range(devices)]
    shape = jax.ShapeDtypeStruct
    message = shape((half * HEAD_DIM + DECAY_ROWS, HEAD_DIM), BF16)
    states = (half * HEAD_DIM, HEAD_DIM)
    factors = shape((half * 8, HEAD_DIM), F32)

    other_weight = lax.ppermute(out_weight, "tp", near_pairs)
    arguments = (log_decay, key_vectors, value_vectors, query_vectors, norm_gain.reshape(1, -1))
    outgoing, decays, keys, values, queries, gain = call(
        functools.partial(outgoing_kernel, half),
        (message,) + tuple(shape(a.shape, a.dtype) for a in arguments),
        [HBM] * 5,
        "outgoing_states",
        scratch=[pltpu.SemaphoreType.DMA((5,))],
    )(*(pltpu.with_memory_space_constraint(a, pltpu.HBM) for a in arguments))
    received = lax.ppermute(outgoing, "seq", side_pairs)
    intra, own, kept = call(
        functools.partial(local_kernel, heads),
        (shape(wide, F32), shape((tokens, heads), F32), message),
        [VMEM] * 4,
        "local",
        cost=4 * tokens * tokens * heads * HEAD_DIM,
    )(decays, queries, keys, values)
    total, through, first, first_decay, sent = call(
        functools.partial(pair_kernel, half),
        (shape(states, F32), factors, shape(states, F32), factors, message),
        [VMEM] * 2,
        "pair_states",
    )(kept, received)
    mine, other = start_states(total, through, sent, first, first_decay, half, devices)
    other = lax.ppermute(other, "seq", side_pairs)

    chunks = [slice(0, tokens // 2), slice(tokens // 2, tokens)]
    out_width = out_weight.shape[1] // tp
    normed, far = [], []
    for i, rows in enumerate(chunks):
        part = call(
            functools.partial(norm_kernel, heads, rows),
            shape((rows.stop - rows.start, heads * HEAD_DIM), BF16),
            [VMEM] * 6,
            f"norm_{i}",
            scratch=[pltpu.VMEM((2,) + states, BF16)],
        )(queries, intra, own, gain, mine, other)
        normed.append((part, lax.ppermute(part, "tp", near_pairs)))
    for i, rows in enumerate(chunks):
        part = call(
            functools.partial(far_kernel, tp),
            shape((rows.stop - rows.start, out_width), BF16),
            [VMEM] * 4,
            f"project_far_{i}",
        )(*normed[i], out_weight, other_weight)
        far.append(lax.ppermute(part, "tp", far_pairs))
    near = call(
        functools.partial(near_kernel, tp, chunks),
        shape((tokens, out_width), F32),
        [VMEM] * (3 + 2 * len(chunks)),
        "project_near",
        cost=4 * tokens * width * heads * HEAD_DIM,
    )(residual, out_weight, other_weight, *(a for pair in normed for a in pair))
    return call(
        functools.partial(last_kernel, chunks),
        shape((tokens, out_width), BF16),
        [VMEM] * (1 + len(chunks)),
        "add",
        out_specs=HBM,
        scratch=[
            pltpu.VMEM((tokens, out_width), BF16),
            pltpu.SemaphoreType.DMA((len(chunks),)),
        ],
    )(near, *far)


def solution(mesh):
    return jax.shard_map(
        on_device,
        mesh=mesh,
        in_specs=(
            P("seq", "tp"),
            P("seq", "tp"),
            P("seq", "tp"),
            P("seq", "tp"),
            P("tp", "seq"),
            P("tp"),
            P("tp", None),
        ),
        out_specs=P("seq", "tp"),
        check_vma=False,
    )
```

```python
import functools

import jax
import jax.numpy as jnp
from jax import lax
from jax.experimental import pallas as pl
from jax.experimental.pallas import tpu as pltpu
from jax.sharding import PartitionSpec as P

HEAD_DIM = 128
GROUP = 256
SCALE = HEAD_DIM ** (-0.5)
F32 = jnp.float32
BF16 = jnp.bfloat16
VMEM = pl.BlockSpec(memory_space=pltpu.VMEM)
HBM = pl.BlockSpec(memory_space=pltpu.HBM)
DECAY_ROWS = 16
PARAMS = pltpu.CompilerParams(vmem_limit_bytes=24 * 1024 * 1024)


def columns(h):
    return slice(h * HEAD_DIM, (h + 1) * HEAD_DIM)


def head_columns(h):
    return pl.ds(pl.multiple_of(h * HEAD_DIM, HEAD_DIM), HEAD_DIM)


def state_rows(h):
    return slice(h * HEAD_DIM, (h + 1) * HEAD_DIM)


def contract(a, b, dims):
    return lax.dot_general(a, b, ((dims[0], dims[1]), ((), ())), preferred_element_type=F32)


def positions():
    shape = (GROUP, GROUP)
    return lax.broadcasted_iota(jnp.int32, shape, 0), lax.broadcasted_iota(jnp.int32, shape, 1)


def three_terms(values):
    first = values.astype(BF16).astype(F32)
    second = (values - first).astype(BF16).astype(F32)
    third = values - first - second
    return jnp.concatenate([first, second, third], axis=0).astype(BF16)


def sums_down(mask, decays):
    heads = decays.shape[0]
    terms = contract(mask, three_terms(decays), ((1,), (1,)))
    return terms[:, :heads] + terms[:, heads : 2 * heads] + terms[:, 2 * heads :]


def sums_across(mask, decays):
    heads = decays.shape[0]
    terms = contract(three_terms(decays), mask, ((1,), (1,)))
    return terms[:heads] + terms[heads : 2 * heads] + terms[2 * heads :]


def decays_to_rows(decays):
    each = DECAY_ROWS // (2 * len(decays))
    wide = jnp.concatenate([jnp.broadcast_to(d, (each, HEAD_DIM)) for d in decays], axis=0)
    coarse = wide.astype(BF16).astype(F32)
    return jnp.concatenate([coarse, wide - coarse], axis=0).astype(BF16)


def rows_to_decays(message_ref, half):
    rows = message_ref[half * HEAD_DIM :, :].astype(F32)
    each = DECAY_ROWS // (2 * half)
    both = rows[: DECAY_ROWS // 2] + rows[DECAY_ROWS // 2 :]
    return [both[j * each : j * each + 1] for j in range(half)]


def side():
    return lax.rem(lax.axis_index("seq"), 2)


def pick(owner, values, half, axis):
    low = lax.slice_in_dim(values, 0, half, axis=axis)
    high = lax.slice_in_dim(values, half, 2 * half, axis=axis)
    return jnp.where(owner == 0, low, high)


def state_factors(owner, half, later, decay_ref):
    decays = decay_ref[...]
    tail = pick(owner, jnp.exp(sums_down(later, decays)), half, 1)
    whole = pick(owner, jnp.exp(jnp.sum(decays, axis=1, keepdims=True)), half, 0)
    return tail, whole


def write_states(owner, half, tail, whole, key_ref, value_ref, out_ref):
    for j in range(half):
        at = head_columns(owner * half + j)
        weighted = (key_ref[:, at].astype(F32) * tail[:, j : j + 1]).astype(BF16)
        update = contract(weighted, value_ref[:, at], ((0,), (0,)))
        out_ref[state_rows(j), :] = update.astype(BF16)
    out_ref[half * HEAD_DIM :, :] = decays_to_rows([whole[j : j + 1] for j in range(half)])


def outgoing_kernel(half, *refs):
    sources, out_ref, held, sems = refs[:5], refs[5], refs[6:11], refs[11]
    me = side()
    width = half * HEAD_DIM

    def part(i, owner):
        at = pl.ds(pl.multiple_of(owner * width, width), width)
        return sources[i].at[:, at], held[i].at[:, at]

    whole = [(sources[i], held[i]) for i in range(5)]
    moves = [whole[0], part(1, 1 - me), part(2, 1 - me)]
    moves += [part(1, me), part(2, me), whole[3], whole[4]]
    copies = [
        pltpu.make_async_copy(source, target, sems.at[i])
        for i, (source, target) in enumerate(moves)
    ]
    for copy in copies:
        copy.start()
    row, col = positions()
    later = jnp.where(col > row, 1.0, 0.0).astype(BF16)
    copies[0].wait()
    factors = state_factors(1 - me, half, later, held[0])
    for copy in copies[1:3]:
        copy.wait()
    write_states(1 - me, half, *factors, *held[1:3], out_ref)
    for copy in copies[3:]:
        copy.wait()


def local_kernel(
    heads, decay_ref, query_ref, key_ref, value_ref, intra_ref, own_ref, kept_ref
):
    row, col = positions()
    causal = col <= row
    upto = jnp.where(causal, 1.0, 0.0).astype(BF16)
    decays = decay_ref[...]
    down = sums_down(upto, decays)
    across = sums_across(upto, decays)
    own_ref[...] = jnp.exp(down) * SCALE
    later = jnp.where(causal, 0.0, 1.0).astype(BF16)
    factors = state_factors(side(), heads // 2, later, decay_ref)
    write_states(side(), heads // 2, *factors, key_ref, value_ref, kept_ref)
    for h in range(heads):
        at = columns(h)
        scores = contract(query_ref[:, at], key_ref[:, at], ((1,), (1,)))
        gaps = down[:, h : h + 1] - across[h : h + 1, :]
        weights = jnp.where(causal, jnp.exp(gaps), 0.0)
        probs = (scores * SCALE * weights).astype(BF16)
        intra_ref[:, at] = jnp.dot(probs, value_ref[:, at], preferred_element_type=F32)


def pair_kernel(
    half, mine_ref, other_ref, total_ref, through_ref, first_ref, decay_ref, sent_ref
):
    second = side() == 1
    mine_decays, other_decays = rows_to_decays(mine_ref, half), rows_to_decays(other_ref, half)
    throughs = []
    for j in range(half):
        at = state_rows(j)
        mine, other = mine_ref[at, :].astype(F32), other_ref[at, :].astype(F32)
        first = jnp.where(second, other, mine)
        first_decay = jnp.where(second, other_decays[j], mine_decays[j])
        last_decay = jnp.where(second, mine_decays[j], other_decays[j])
        total = first * last_decay + jnp.where(second, mine, other)
        total_ref[at, :] = total
        sent_ref[at, :] = total.astype(BF16)
        first_ref[at, :] = first
        through = first_decay * last_decay
        throughs.append(through)
        rows = slice(j * 8, (j + 1) * 8)
        through_ref[rows, :] = jnp.broadcast_to(through, (8, HEAD_DIM))
        decay_ref[rows, :] = jnp.broadcast_to(first_decay, (8, HEAD_DIM))
    sent_ref[half * HEAD_DIM :, :] = decays_to_rows(throughs)


def rank():
    return lax.axis_index("seq") // 2


def both_kernel(half, total_ref, through_ref, received_ref, out_ref):
    second = lax.rem(rank(), 2) == 1
    other_decays = rows_to_decays(received_ref, half)
    for j in range(half):
        at = state_rows(j)
        mine, other = total_ref[at, :], received_ref[at, :].astype(F32)
        mine_decay = through_ref[j * 8 : j * 8 + 1, :]
        first = jnp.where(second, other, mine)
        last = jnp.where(second, mine, other)
        decay = jnp.where(second, mine_decay, other_decays[j])
        out_ref[at, :] = (first * decay + last).astype(BF16)


def write_starts(half, first_ref, decay_ref, earlier, mine_ref, other_ref):
    second = side() == 1
    for j in range(half):
        at = state_rows(j)
        decay = decay_ref[j * 8 : j * 8 + 1, :]
        last = (first_ref[at, :] + decay * earlier[j]).astype(BF16)
        first = earlier[j].astype(BF16)
        mine_ref[at, :] = jnp.where(second, last, first)
        other_ref[at, :] = jnp.where(second, first, last)


def start_kernel(half, first_ref, decay_ref, earlier_ref, mine_ref, other_ref):
    earlier = [earlier_ref[state_rows(j), :].astype(F32) for j in range(half)]
    write_starts(half, first_ref, decay_ref, earlier, mine_ref, other_ref)


def start_of_four_kernel(
    half, first_ref, decay_ref, near_ref, far_ref, mine_ref, other_ref
):
    me = rank()
    second, upper = lax.rem(me, 2) == 1, me >= 2
    near_decays = rows_to_decays(near_ref, half)
    earlier = []
    for j in range(half):
        at = state_rows(j)
        far = jnp.where(upper, far_ref[at, :].astype(F32), 0.0)
        passed = near_ref[at, :].astype(F32) + near_decays[j] * far
        earlier.append(jnp.where(second, passed, far))
    write_starts(half, first_ref, decay_ref, earlier, mine_ref, other_ref)


def norm_kernel(
    heads, rows, query_ref, intra_ref, own_ref, gain_ref, mine_ref, other_ref, out_ref, state_ref
):
    me = side()
    state_ref[me] = mine_ref[...]
    state_ref[1 - me] = other_ref[...]
    half = heads // 2
    for h in range(heads):
        at = columns(h)
        state = state_ref[h // half, state_rows(h % half), :]
        inter = jnp.dot(query_ref[rows, at], state, preferred_element_type=F32)
        attended = intra_ref[rows, at] + own_ref[rows, h : h + 1] * inter
        mean_square = jnp.mean(attended * attended, axis=-1, keepdims=True)
        normed = attended * lax.rsqrt(mean_square + 1e-06)
        out_ref[:, at] = (normed * gain_ref[:, at]).astype(BF16)


def share(step, tp, mine_ref, other_ref, weight_ref, other_weight_ref):
    width = weight_ref.shape[1] // tp
    target = lax.axis_index("tp") ^ step
    at = pl.ds(pl.multiple_of(target * width, width), width)
    return jnp.dot(mine_ref[...], weight_ref[:, at], preferred_element_type=F32) + jnp.dot(
        other_ref[...], other_weight_ref[:, at], preferred_element_type=F32
    )


def far_kernel(tp, mine_ref, other_ref, weight_ref, other_weight_ref, out_ref):
    out_ref[...] = share(2, tp, mine_ref, other_ref, weight_ref, other_weight_ref).astype(BF16)


def near_kernel(tp, chunks, residual_ref, weight_ref, other_weight_ref, *refs):
    out_ref = refs[-1]
    for i, rows in enumerate(chunks):
        near = share(0, tp, refs[2 * i], refs[2 * i + 1], weight_ref, other_weight_ref)
        out_ref[rows, :] = residual_ref[rows, :].astype(F32) + near


def add_kernel(rows, near_ref, far_ref, *refs):
    out_hbm, out_ref, sem = refs[-3:]
    out_ref[...] = (near_ref[rows, :] + far_ref[...].astype(F32)).astype(BF16)
    copy = pltpu.make_async_copy(out_ref, out_hbm.at[rows, :], sem)
    copy.start()
    copy.wait()


def call(kernel, out_shape, in_specs, name, out_specs=None, scratch=(), cost=0, aliases={}):
    single = isinstance(out_shape, jax.ShapeDtypeStruct)
    if out_specs is None:
        out_specs = VMEM if single else (VMEM,) * len(out_shape)
    cost = pl.CostEstimate(
        flops=cost, bytes_accessed=2_000_000 if cost else 0, transcendentals=0
    )
    return pl.pallas_call(
        kernel,
        out_shape=out_shape,
        in_specs=in_specs,
        out_specs=out_specs,
        scratch_shapes=scratch,
        input_output_aliases=aliases,
        compiler_params=PARAMS,
        cost_estimate=cost,
        name=name,
    )


def start_states(total, through, sent, first, first_decay, half, devices):
    pairs = devices // 2
    state = jax.ShapeDtypeStruct(total.shape, BF16)
    if pairs == 4:

        def swap(message, step):
            return lax.ppermute(message, "seq", [(i, i ^ step) for i in range(devices)])

        near = swap(sent, 2)
        both = call(functools.partial(both_kernel, half), state, [VMEM] * 3, "both_pairs")(
            total, through, near
        )
        far = swap(both, 4)
        kernel = functools.partial(start_of_four_kernel, half)
        return call(kernel, (state, state), [VMEM] * 4, "start_states")(
            first, first_decay, near, far
        )

    def shift(message, by):
        moves = [(i, i + 2 * by) for i in range(devices - 2 * by)]
        return lax.ppermute(message, "seq", moves)

    factor = jnp.repeat(through[::8], HEAD_DIM, axis=0)
    held, factor = shift(total.astype(BF16), 1).astype(F32), shift(factor, 1)
    by = 1
    while by < pairs - 1:
        held = held + factor * shift(held.astype(BF16), by).astype(F32)
        factor = factor * shift(factor, by)
        by *= 2
    kernel = functools.partial(start_kernel, half)
    return call(kernel, (state, state), [VMEM] * 3, "start_states")(
        first, first_decay, held.astype(BF16)
    )


def on_device(
    residual, query_vectors, key_vectors, value_vectors, log_decay, norm_gain, out_weight
):
    tokens, width = residual.shape
    heads = log_decay.shape[0]
    half = heads // 2
    devices = lax.axis_size("seq")
    tp = lax.axis_size("tp")
    wide = (tokens, heads * HEAD_DIM)
    near_pairs = [(i, i ^ 1) for i in range(tp)]
    far_pairs = [(i, i ^ 2) for i in range(tp)]
    side_pairs = [(i, i ^ 1) for i in range(devices)]
    shape = jax.ShapeDtypeStruct
    message = shape((half * HEAD_DIM + DECAY_ROWS, HEAD_DIM), BF16)
    states = (half * HEAD_DIM, HEAD_DIM)
    factors = shape((half * 8, HEAD_DIM), F32)

    other_weight = lax.ppermute(out_weight, "tp", near_pairs)
    arguments = (log_decay, key_vectors, value_vectors, query_vectors, norm_gain.reshape(1, -1))
    outgoing, decays, keys, values, queries, gain = call(
        functools.partial(outgoing_kernel, half),
        (message,) + tuple(shape(a.shape, a.dtype) for a in arguments),
        [HBM] * 5,
        "outgoing_states",
        scratch=[pltpu.SemaphoreType.DMA((7,))],
    )(*(pltpu.with_memory_space_constraint(a, pltpu.HBM) for a in arguments))
    received = lax.ppermute(outgoing, "seq", side_pairs)
    intra, own, kept = call(
        functools.partial(local_kernel, heads),
        (shape(wide, F32), shape((tokens, heads), F32), message),
        [VMEM] * 4,
        "local",
        cost=4 * tokens * tokens * heads * HEAD_DIM,
    )(decays, queries, keys, values)
    total, through, first, first_decay, sent = call(
        functools.partial(pair_kernel, half),
        (shape(states, F32), factors, shape(states, F32), factors, message),
        [VMEM] * 2,
        "pair_states",
    )(kept, received)
    mine, other = start_states(total, through, sent, first, first_decay, half, devices)
    other = lax.ppermute(other, "seq", side_pairs)

    chunks = [slice(0, tokens // 4), slice(tokens // 4, tokens)]
    out_width = out_weight.shape[1] // tp
    normed, far = [], []
    for i, rows in enumerate(chunks):
        count = rows.stop - rows.start
        part = call(
            functools.partial(norm_kernel, heads, rows),
            shape((count, heads * HEAD_DIM), BF16),
            [VMEM] * 6,
            f"norm_{i}",
            scratch=[pltpu.VMEM((2,) + states, BF16)],
        )(queries, intra, own, gain, mine, other)
        normed += [part, lax.ppermute(part, "tp", near_pairs)]
        part = call(
            functools.partial(far_kernel, tp),
            shape((count, out_width), BF16),
            [VMEM] * 4,
            f"project_far_{i}",
        )(*normed[-2:], out_weight, other_weight)
        far.append(lax.ppermute(part, "tp", far_pairs))
    near = call(
        functools.partial(near_kernel, tp, chunks),
        shape((tokens, out_width), F32),
        [VMEM] * (3 + len(normed)),
        "project_near",
    )(residual, out_weight, other_weight, *normed)
    out = []
    for i, rows in enumerate(chunks):
        out = [
            call(
                functools.partial(add_kernel, rows),
                shape((tokens, out_width), BF16),
                [VMEM, VMEM] + [HBM] * len(out),
                f"add_{i}",
                out_specs=HBM,
                scratch=[
                    pltpu.VMEM((rows.stop - rows.start, out_width), BF16),
                    pltpu.SemaphoreType.DMA,
                ],
                aliases={2: 0} if out else {},
            )(near, far[i], *out)
        ]
    return out[0]


def solution(mesh):
    return jax.shard_map(
        on_device,
        mesh=mesh,
        in_specs=(
            P("seq", "tp"),
            P("seq", "tp"),
            P("seq", "tp"),
            P("seq", "tp"),
            P("tp", "seq"),
            P("tp"),
            P("tp", None),
        ),
        out_specs=P("seq", "tp"),
        check_vma=False,
    )
```

```python
import functools

import jax
import jax.numpy as jnp
from jax import lax
from jax.experimental import pallas as pl
from jax.experimental.pallas import tpu as pltpu
from jax.sharding import PartitionSpec as P

HEAD_DIM = 128
GROUP = 256
SCALE = HEAD_DIM ** (-0.5)
F32 = jnp.float32
BF16 = jnp.bfloat16
VMEM = pl.BlockSpec(memory_space=pltpu.VMEM)
HBM = pl.BlockSpec(memory_space=pltpu.HBM)
DECAY_ROWS = 16
MESSAGE = (HEAD_DIM + DECAY_ROWS, HEAD_DIM)
PARAMS = pltpu.CompilerParams(vmem_limit_bytes=24 * 1024 * 1024)


def columns(h):
    return slice(h * HEAD_DIM, (h + 1) * HEAD_DIM)


def contract(a, b, dims):
    return lax.dot_general(a, b, ((dims[0], dims[1]), ((), ())), preferred_element_type=F32)


def positions():
    shape = (GROUP, GROUP)
    return lax.broadcasted_iota(jnp.int32, shape, 0), lax.broadcasted_iota(jnp.int32, shape, 1)


def three_terms(values):
    first = values.astype(BF16).astype(F32)
    second = (values - first).astype(BF16).astype(F32)
    third = values - first - second
    return jnp.concatenate([first, second, third], axis=0).astype(BF16)


def sums_down(mask, decays):
    heads = decays.shape[0]
    terms = contract(mask, three_terms(decays), ((1,), (1,)))
    return terms[:, :heads] + terms[:, heads : 2 * heads] + terms[:, 2 * heads :]


def sums_across(mask, decays):
    heads = decays.shape[0]
    terms = contract(three_terms(decays), mask, ((1,), (1,)))
    return terms[:heads] + terms[heads : 2 * heads] + terms[2 * heads :]


def decay_to_rows(decay):
    wide = jnp.broadcast_to(decay, (DECAY_ROWS // 2, HEAD_DIM))
    coarse = wide.astype(BF16).astype(F32)
    return jnp.concatenate([coarse, wide - coarse], axis=0).astype(BF16)


def rows_to_decay(message):
    rows = message[HEAD_DIM:, :].astype(F32)
    return (rows[: DECAY_ROWS // 2] + rows[DECAY_ROWS // 2 :])[:1]


def state_kernel(heads, *refs):
    sources, out_ref, held, sems = refs[:5], refs[5], refs[6:11], refs[11]
    copies = [
        pltpu.make_async_copy(source, target, sems.at[i])
        for i, (source, target) in enumerate(zip(sources, held))
    ]
    for copy in copies:
        copy.start()
    decay_ref, key_ref, value_ref = held[:3]
    row, col = positions()
    later = jnp.where(col > row, 1.0, 0.0).astype(BF16)
    copies[0].wait()
    decays = decay_ref[...]
    tail = jnp.exp(sums_across(later, decays))
    whole = jnp.exp(jnp.sum(decays, axis=1, keepdims=True))
    copies[1].wait()
    copies[2].wait()
    for h in range(heads):
        at = columns(h)
        weighted = (key_ref[:, at].T.astype(F32) * tail[h : h + 1, :]).astype(BF16)
        update = jnp.dot(weighted, value_ref[:, at], preferred_element_type=F32)
        out_ref[h, :HEAD_DIM, :] = update.astype(BF16)
        out_ref[h, HEAD_DIM:, :] = decay_to_rows(whole[h : h + 1])
    for copy in copies[3:]:
        copy.wait()


def local_kernel(heads, decay_ref, query_ref, key_ref, value_ref, intra_ref, own_ref):
    row, col = positions()
    causal = col <= row
    upto = jnp.where(causal, 1.0, 0.0).astype(BF16)
    decays = decay_ref[...]
    down = sums_down(upto, decays)
    across = sums_across(upto, decays)
    own_ref[...] = jnp.exp(down) * SCALE
    for h in range(heads):
        at = columns(h)
        scores = contract(query_ref[:, at], key_ref[:, at], ((1,), (1,)))
        gaps = down[:, h : h + 1] - across[h : h + 1, :]
        weights = jnp.where(causal, jnp.exp(gaps), 0.0)
        probs = (scores * SCALE * weights).astype(BF16)
        intra_ref[:, at] = jnp.dot(probs, value_ref[:, at], preferred_element_type=F32)


def gather_kernel(members, received_ref, prefix_ref, decay_ref, total_ref):
    held = jnp.zeros((HEAD_DIM, HEAD_DIM), F32)
    through = jnp.ones((1, HEAD_DIM), F32)
    for m in range(members):
        prefix_ref[m] = held
        decay_ref[m] = jnp.broadcast_to(through, decay_ref.shape[1:])
        message = received_ref[m]
        decay = rows_to_decay(message)
        held = held * decay + message[:HEAD_DIM, :].astype(F32)
        through = through * decay
    total_ref[:HEAD_DIM, :] = held.astype(BF16)
    total_ref[HEAD_DIM:, :] = decay_to_rows(through)


def scatter_kernel(members, swapped, prefix_ref, decay_ref, earlier_ref, out_ref):
    earlier = earlier_ref[:HEAD_DIM, :].astype(F32)
    if swapped:
        earlier = jnp.where(lax.axis_index("seq") >= members, earlier, 0.0)
    for m in range(members):
        out_ref[m] = (prefix_ref[m] + decay_ref[m][:1] * earlier).astype(BF16)


def norm_kernel(heads, rows, query_ref, intra_ref, own_ref, gain_ref, state_ref, out_ref):
    for h in range(heads):
        at = columns(h)
        inter = jnp.dot(query_ref[rows, at], state_ref[h], preferred_element_type=F32)
        attended = intra_ref[rows, at] + own_ref[rows, h : h + 1] * inter
        mean_square = jnp.mean(attended * attended, axis=-1, keepdims=True)
        normed = attended * lax.rsqrt(mean_square + 1e-06)
        out_ref[:, at] = (normed * gain_ref[:, at]).astype(BF16)


def share(step, tp, mine_ref, other_ref, weight_ref, other_weight_ref):
    width = weight_ref.shape[1] // tp
    target = lax.axis_index("tp") ^ step
    at = pl.ds(pl.multiple_of(target * width, width), width)
    return jnp.dot(mine_ref[...], weight_ref[:, at], preferred_element_type=F32) + jnp.dot(
        other_ref[...], other_weight_ref[:, at], preferred_element_type=F32
    )


def far_kernel(tp, mine_ref, other_ref, weight_ref, other_weight_ref, out_ref):
    out_ref[...] = share(2, tp, mine_ref, other_ref, weight_ref, other_weight_ref).astype(BF16)


def near_kernel(tp, chunks, residual_ref, weight_ref, other_weight_ref, *refs):
    out_ref = refs[-1]
    for i, rows in enumerate(chunks):
        near = share(0, tp, refs[2 * i], refs[2 * i + 1], weight_ref, other_weight_ref)
        out_ref[rows, :] = residual_ref[rows, :].astype(F32) + near


def add_kernel(chunks, near_ref, *refs):
    far, (out_hbm, out_ref, sems) = refs[: len(chunks)], refs[len(chunks) :]
    copies = []
    for i, rows in enumerate(chunks):
        out_ref[rows, :] = (near_ref[rows, :] + far[i][...].astype(F32)).astype(BF16)
        copies.append(
            pltpu.make_async_copy(out_ref.at[rows, :], out_hbm.at[rows, :], sems.at[i])
        )
        copies[-1].start()
    for copy in copies:
        copy.wait()


def call(kernel, out_shape, in_specs, name, out_specs=None, scratch=(), cost=0):
    single = isinstance(out_shape, jax.ShapeDtypeStruct)
    if out_specs is None:
        out_specs = VMEM if single else (VMEM,) * len(out_shape)
    cost = pl.CostEstimate(
        flops=cost, bytes_accessed=2_000_000 if cost else 0, transcendentals=0
    )
    return pl.pallas_call(
        kernel,
        out_shape=out_shape,
        in_specs=in_specs,
        out_specs=out_specs,
        scratch_shapes=scratch,
        compiler_params=PARAMS,
        cost_estimate=cost,
        name=name,
    )


def earlier_groups(total, members, devices):
    groups = devices // members
    if groups == 2:
        return lax.ppermute(total, "seq", [(i, i ^ members) for i in range(devices)])

    def shift(message, by):
        moves = [(i, i + by * members) for i in range(devices - by * members)]
        return lax.ppermute(message, "seq", moves)

    held = shift(total, 1)
    by = 1
    while by < groups - 1:
        before = shift(held, by)
        decay = rows_to_decay(held)
        state = held[:HEAD_DIM].astype(F32) + decay * before[:HEAD_DIM].astype(F32)
        through = decay_to_rows(decay * rows_to_decay(before))
        held = jnp.concatenate([state.astype(BF16), through], axis=0)
        by *= 2
    return held


def on_device(
    residual, query_vectors, key_vectors, value_vectors, log_decay, norm_gain, out_weight
):
    tokens, width = residual.shape
    heads = log_decay.shape[0]
    devices = lax.axis_size("seq")
    tp = lax.axis_size("tp")
    wide = (tokens, heads * HEAD_DIM)
    near_pairs = [(i, i ^ 1) for i in range(tp)]
    far_pairs = [(i, i ^ 2) for i in range(tp)]
    groups = [list(range(i, i + heads)) for i in range(0, devices, heads)]
    shape = jax.ShapeDtypeStruct

    def exchange(messages):
        return lax.all_to_all(
            messages, "seq", split_axis=0, concat_axis=0, axis_index_groups=groups, tiled=True
        )

    other_weight = lax.ppermute(out_weight, "tp", near_pairs)
    arguments = (log_decay, key_vectors, value_vectors, query_vectors, norm_gain.reshape(1, -1))
    states, decays, keys, values, queries, gain = call(
        functools.partial(state_kernel, heads),
        (shape((heads,) + MESSAGE, BF16),) + tuple(shape(a.shape, a.dtype) for a in arguments),
        [HBM] * 5,
        "states",
        scratch=[pltpu.SemaphoreType.DMA((5,))],
    )(*(pltpu.with_memory_space_constraint(a, pltpu.HBM) for a in arguments))
    received = exchange(states)
    intra, own = call(
        functools.partial(local_kernel, heads),
        (shape(wide, F32), shape((tokens, heads), F32)),
        [VMEM] * 4,
        "local",
        cost=4 * tokens * tokens * heads * HEAD_DIM,
    )(decays, queries, keys, values)
    prefix, through, total = call(
        functools.partial(gather_kernel, heads),
        (
            shape((heads, HEAD_DIM, HEAD_DIM), F32),
            shape((heads, 8, HEAD_DIM), F32),
            shape(MESSAGE, BF16),
        ),
        [VMEM],
        "gather_states",
    )(received)
    earlier = earlier_groups(total, heads, devices)
    starts = call(
        functools.partial(scatter_kernel, heads, len(groups) == 2),
        shape((heads, HEAD_DIM, HEAD_DIM), BF16),
        [VMEM] * 3,
        "scatter_states",
    )(prefix, through, earlier)
    incoming = exchange(starts)

    chunks = [slice(0, tokens // 2), slice(tokens // 2, tokens)]
    out_width = out_weight.shape[1] // tp
    normed, far = [], []
    for i, rows in enumerate(chunks):
        part = call(
            functools.partial(norm_kernel, heads, rows),
            shape((rows.stop - rows.start, heads * HEAD_DIM), BF16),
            [VMEM] * 5,
            f"norm_{i}",
        )(queries, intra, own, gain, incoming)
        normed.append((part, lax.ppermute(part, "tp", near_pairs)))
    for i, rows in enumerate(chunks):
        part = call(
            functools.partial(far_kernel, tp),
            shape((rows.stop - rows.start, out_width), BF16),
            [VMEM] * 4,
            f"project_far_{i}",
        )(*normed[i], out_weight, other_weight)
        far.append(lax.ppermute(part, "tp", far_pairs))
    near = call(
        functools.partial(near_kernel, tp, chunks),
        shape((tokens, out_width), F32),
        [VMEM] * (3 + 2 * len(chunks)),
        "project_near",
    )(residual, out_weight, other_weight, *(a for pair in normed for a in pair))
    return call(
        functools.partial(add_kernel, chunks),
        shape((tokens, out_width), BF16),
        [VMEM] * (1 + len(chunks)),
        "add",
        out_specs=HBM,
        scratch=[
            pltpu.VMEM((tokens, out_width), BF16),
            pltpu.SemaphoreType.DMA((len(chunks),)),
        ],
    )(near, *far)


def solution(mesh):
    return jax.shard_map(
        on_device,
        mesh=mesh,
        in_specs=(
            P("seq", "tp"),
            P("seq", "tp"),
            P("seq", "tp"),
            P("seq", "tp"),
            P("tp", "seq"),
            P("tp"),
            P("tp", None),
        ),
        out_specs=P("seq", "tp"),
        check_vma=False,
    )
```

```python
import functools

import jax
import jax.numpy as jnp
from jax import lax
from jax.experimental import pallas as pl
from jax.experimental.pallas import tpu as pltpu
from jax.sharding import PartitionSpec as P

HEAD_DIM = 128
GROUP = 256
SCALE = HEAD_DIM ** (-0.5)
F32 = jnp.float32
BF16 = jnp.bfloat16
VMEM = pl.BlockSpec(memory_space=pltpu.VMEM)
HBM = pl.BlockSpec(memory_space=pltpu.HBM)
DECAY_ROWS = 16
MESSAGE = (HEAD_DIM + DECAY_ROWS, HEAD_DIM)
PARAMS = pltpu.CompilerParams(vmem_limit_bytes=24 * 1024 * 1024)


def columns(h):
    return slice(h * HEAD_DIM, (h + 1) * HEAD_DIM)


def head_columns(h):
    return pl.ds(pl.multiple_of(h * HEAD_DIM, HEAD_DIM), HEAD_DIM)


def place(members):
    return lax.rem(lax.axis_index("seq"), members)


def contract(a, b, dims):
    return lax.dot_general(a, b, ((dims[0], dims[1]), ((), ())), preferred_element_type=F32)


def positions():
    shape = (GROUP, GROUP)
    return lax.broadcasted_iota(jnp.int32, shape, 0), lax.broadcasted_iota(jnp.int32, shape, 1)


def three_terms(values):
    first = values.astype(BF16).astype(F32)
    second = (values - first).astype(BF16).astype(F32)
    third = values - first - second
    return jnp.concatenate([first, second, third], axis=0).astype(BF16)


def sums_down(mask, decays):
    heads = decays.shape[0]
    terms = contract(mask, three_terms(decays), ((1,), (1,)))
    return terms[:, :heads] + terms[:, heads : 2 * heads] + terms[:, 2 * heads :]


def sums_across(mask, decays):
    heads = decays.shape[0]
    terms = contract(three_terms(decays), mask, ((1,), (1,)))
    return terms[:heads] + terms[heads : 2 * heads] + terms[2 * heads :]


def decay_to_rows(decay):
    wide = jnp.broadcast_to(decay, (DECAY_ROWS // 2, HEAD_DIM))
    coarse = wide.astype(BF16).astype(F32)
    return jnp.concatenate([coarse, wide - coarse], axis=0).astype(BF16)


def rows_to_decay(message):
    rows = message[HEAD_DIM:, :].astype(F32)
    return (rows[: DECAY_ROWS // 2] + rows[DECAY_ROWS // 2 :])[:1]


def write_state(h, tail, whole, key_ref, value_ref, out_ref):
    at = head_columns(h)
    factor = jnp.sum(jnp.where(row_is(tail, h), tail, 0.0), axis=0, keepdims=True)
    decay = jnp.sum(jnp.where(row_is(whole, h), whole, 0.0), axis=0, keepdims=True)
    weighted = (key_ref[:, at].T.astype(F32) * factor).astype(BF16)
    update = jnp.dot(weighted, value_ref[:, at], preferred_element_type=F32)
    out_ref[:HEAD_DIM, :] = update.astype(BF16)
    out_ref[HEAD_DIM:, :] = decay_to_rows(decay)


def row_is(values, h):
    return lax.broadcasted_iota(jnp.int32, values.shape, 0) == h


def state_factors(later, decays):
    tail = jnp.exp(sums_across(later, decays))
    whole = jnp.exp(jnp.sum(decays, axis=1, keepdims=True))
    return tail, whole


def state_kernel(steps, heads, *refs):
    sources, outs = refs[:5], refs[5 : 5 + len(steps)]
    held, sems = refs[5 + len(steps) : 10 + len(steps)], refs[-1]
    copies = [
        pltpu.make_async_copy(source, target, sems.at[i])
        for i, (source, target) in enumerate(zip(sources, held))
    ]
    for copy in copies:
        copy.start()
    decay_ref, key_ref, value_ref = held[:3]
    row, col = positions()
    later = jnp.where(col > row, 1.0, 0.0).astype(BF16)
    copies[0].wait()
    factors = state_factors(later, decay_ref[...])
    copies[1].wait()
    copies[2].wait()
    for step, out_ref in zip(steps, outs):
        write_state(place(heads) ^ step, *factors, key_ref, value_ref, out_ref)
    for copy in copies[3:]:
        copy.wait()


def local_kernel(
    heads, decay_ref, query_ref, key_ref, value_ref, intra_ref, own_ref, kept_ref
):
    row, col = positions()
    causal = col <= row
    upto = jnp.where(causal, 1.0, 0.0).astype(BF16)
    later = jnp.where(causal, 0.0, 1.0).astype(BF16)
    decays = decay_ref[...]
    write_state(place(heads), *state_factors(later, decays), key_ref, value_ref, kept_ref)
    down = sums_down(upto, decays)
    across = sums_across(upto, decays)
    own_ref[...] = jnp.exp(down) * SCALE
    for h in range(heads):
        at = columns(h)
        scores = contract(query_ref[:, at], key_ref[:, at], ((1,), (1,)))
        gaps = down[:, h : h + 1] - across[h : h + 1, :]
        weights = jnp.where(causal, jnp.exp(gaps), 0.0)
        probs = (scores * SCALE * weights).astype(BF16)
        intra_ref[:, at] = jnp.dot(probs, value_ref[:, at], preferred_element_type=F32)


def gather_kernel(steps, members, *refs):
    received, (prefix_ref, decay_ref, total_ref, held_ref) = refs[: len(steps)], refs[len(steps) :]
    me = place(members)
    for step, message_ref in zip(steps, received):
        held_ref[me ^ step] = message_ref[...]
    held = jnp.zeros((HEAD_DIM, HEAD_DIM), F32)
    through = jnp.ones((1, HEAD_DIM), F32)
    for m in range(members):
        prefix_ref[m] = held
        decay_ref[m] = jnp.broadcast_to(through, decay_ref.shape[1:])
        message = held_ref[m]
        decay = rows_to_decay(message)
        held = held * decay + message[:HEAD_DIM, :].astype(F32)
        through = through * decay
    total_ref[:HEAD_DIM, :] = held.astype(BF16)
    total_ref[HEAD_DIM:, :] = decay_to_rows(through)


def scatter_kernel(steps, members, swapped, prefix_ref, decay_ref, earlier_ref, *outs):
    earlier = earlier_ref[:HEAD_DIM, :].astype(F32)
    if swapped:
        earlier = jnp.where(lax.axis_index("seq") >= members, earlier, 0.0)
    for step, out_ref in zip(steps, outs):
        m = place(members) ^ step
        out_ref[...] = (prefix_ref[m] + decay_ref[m][:1] * earlier).astype(BF16)


def norm_kernel(steps, heads, rows, query_ref, intra_ref, own_ref, gain_ref, *refs):
    received, (out_ref, state_ref) = refs[: len(steps)], refs[len(steps) :]
    me = place(heads)
    for step, message_ref in zip(steps, received):
        state_ref[me ^ step] = message_ref[...]
    for h in range(heads):
        at = columns(h)
        inter = jnp.dot(query_ref[rows, at], state_ref[h], preferred_element_type=F32)
        attended = intra_ref[rows, at] + own_ref[rows, h : h + 1] * inter
        mean_square = jnp.mean(attended * attended, axis=-1, keepdims=True)
        normed = attended * lax.rsqrt(mean_square + 1e-06)
        out_ref[:, at] = (normed * gain_ref[:, at]).astype(BF16)


def share(step, tp, mine_ref, other_ref, weight_ref, other_weight_ref):
    width = weight_ref.shape[1] // tp
    target = lax.axis_index("tp") ^ step
    at = pl.ds(pl.multiple_of(target * width, width), width)
    return jnp.dot(mine_ref[...], weight_ref[:, at], preferred_element_type=F32) + jnp.dot(
        other_ref[...], other_weight_ref[:, at], preferred_element_type=F32
    )


def far_kernel(tp, mine_ref, other_ref, weight_ref, other_weight_ref, out_ref):
    out_ref[...] = share(2, tp, mine_ref, other_ref, weight_ref, other_weight_ref).astype(BF16)


def near_kernel(tp, chunks, residual_ref, weight_ref, other_weight_ref, *refs):
    out_ref = refs[-1]
    for i, rows in enumerate(chunks):
        near = share(0, tp, refs[2 * i], refs[2 * i + 1], weight_ref, other_weight_ref)
        out_ref[rows, :] = residual_ref[rows, :].astype(F32) + near


def add_kernel(chunks, near_ref, *refs):
    far, (out_hbm, out_ref, sems) = refs[: len(chunks)], refs[len(chunks) :]
    copies = []
    for i, rows in enumerate(chunks):
        out_ref[rows, :] = (near_ref[rows, :] + far[i][...].astype(F32)).astype(BF16)
        copies.append(
            pltpu.make_async_copy(out_ref.at[rows, :], out_hbm.at[rows, :], sems.at[i])
        )
        copies[-1].start()
    for copy in copies:
        copy.wait()


def call(kernel, out_shape, in_specs, name, out_specs=None, scratch=(), cost=0):
    single = isinstance(out_shape, jax.ShapeDtypeStruct)
    if out_specs is None:
        out_specs = VMEM if single else (VMEM,) * len(out_shape)
    cost = pl.CostEstimate(
        flops=cost, bytes_accessed=2_000_000 if cost else 0, transcendentals=0
    )
    return pl.pallas_call(
        kernel,
        out_shape=out_shape,
        in_specs=in_specs,
        out_specs=out_specs,
        scratch_shapes=scratch,
        compiler_params=PARAMS,
        cost_estimate=cost,
        name=name,
    )


def earlier_groups(total, members, devices):
    groups = devices // members
    if groups == 2:
        return lax.ppermute(total, "seq", [(i, i ^ members) for i in range(devices)])

    def shift(message, by):
        moves = [(i, i + by * members) for i in range(devices - by * members)]
        return lax.ppermute(message, "seq", moves)

    held = shift(total, 1)
    by = 1
    while by < groups - 1:
        before = shift(held, by)
        decay = rows_to_decay(held)
        state = held[:HEAD_DIM].astype(F32) + decay * before[:HEAD_DIM].astype(F32)
        through = decay_to_rows(decay * rows_to_decay(before))
        held = jnp.concatenate([state.astype(BF16), through], axis=0)
        by *= 2
    return held


def on_device(
    residual, query_vectors, key_vectors, value_vectors, log_decay, norm_gain, out_weight
):
    tokens, width = residual.shape
    heads = log_decay.shape[0]
    devices = lax.axis_size("seq")
    tp = lax.axis_size("tp")
    wide = (tokens, heads * HEAD_DIM)
    near_pairs = [(i, i ^ 1) for i in range(tp)]
    far_pairs = [(i, i ^ 2) for i in range(tp)]
    shape = jax.ShapeDtypeStruct
    steps = [heads - 1, *range(1, heads - 1), 0]

    def exchange(messages):
        moved = []
        for step, message in zip(steps, messages):
            pairs = [(i, i ^ step) for i in range(devices)]
            moved.append(lax.ppermute(message, "seq", pairs) if step else message)
        return moved

    other_weight = lax.ppermute(out_weight, "tp", near_pairs)
    arguments = (log_decay, key_vectors, value_vectors, query_vectors, norm_gain.reshape(1, -1))
    *states, decays, keys, values, queries, gain = call(
        functools.partial(state_kernel, steps[:-1], heads),
        (shape(MESSAGE, BF16),) * (heads - 1)
        + tuple(shape(a.shape, a.dtype) for a in arguments),
        [HBM] * 5,
        "states",
        scratch=[pltpu.SemaphoreType.DMA((5,))],
    )(*(pltpu.with_memory_space_constraint(a, pltpu.HBM) for a in arguments))
    received = exchange(states)
    intra, own, kept = call(
        functools.partial(local_kernel, heads),
        (shape(wide, F32), shape((tokens, heads), F32), shape(MESSAGE, BF16)),
        [VMEM] * 4,
        "local",
        cost=4 * tokens * tokens * heads * HEAD_DIM,
    )(decays, queries, keys, values)
    prefix, through, total = call(
        functools.partial(gather_kernel, steps, heads),
        (
            shape((heads, HEAD_DIM, HEAD_DIM), F32),
            shape((heads, 8, HEAD_DIM), F32),
            shape(MESSAGE, BF16),
        ),
        [VMEM] * heads,
        "gather_states",
        scratch=[pltpu.VMEM((heads,) + MESSAGE, BF16)],
    )(*received, kept)
    earlier = earlier_groups(total, heads, devices)
    starts = call(
        functools.partial(scatter_kernel, steps, heads, devices == 2 * heads),
        (shape((HEAD_DIM, HEAD_DIM), BF16),) * heads,
        [VMEM] * 3,
        "scatter_states",
    )(prefix, through, earlier)
    incoming = exchange(starts)

    chunks = [slice(0, tokens // 2), slice(tokens // 2, tokens)]
    out_width = out_weight.shape[1] // tp
    normed, far = [], []
    for i, rows in enumerate(chunks):
        part = call(
            functools.partial(norm_kernel, steps, heads, rows),
            shape((rows.stop - rows.start, heads * HEAD_DIM), BF16),
            [VMEM] * (4 + heads),
            f"norm_{i}",
            scratch=[pltpu.VMEM((heads, HEAD_DIM, HEAD_DIM), BF16)],
        )(queries, intra, own, gain, *incoming)
        normed.append((part, lax.ppermute(part, "tp", near_pairs)))
    for i, rows in enumerate(chunks):
        part = call(
            functools.partial(far_kernel, tp),
            shape((rows.stop - rows.start, out_width), BF16),
            [VMEM] * 4,
            f"project_far_{i}",
        )(*normed[i], out_weight, other_weight)
        far.append(lax.ppermute(part, "tp", far_pairs))
    near = call(
        functools.partial(near_kernel, tp, chunks),
        shape((tokens, out_width), F32),
        [VMEM] * (3 + 2 * len(chunks)),
        "project_near",
    )(residual, out_weight, other_weight, *(a for pair in normed for a in pair))
    return call(
        functools.partial(add_kernel, chunks),
        shape((tokens, out_width), BF16),
        [VMEM] * (1 + len(chunks)),
        "add",
        out_specs=HBM,
        scratch=[
            pltpu.VMEM((tokens, out_width), BF16),
            pltpu.SemaphoreType.DMA((len(chunks),)),
        ],
    )(near, *far)


def solution(mesh):
    return jax.shard_map(
        on_device,
        mesh=mesh,
        in_specs=(
            P("seq", "tp"),
            P("seq", "tp"),
            P("seq", "tp"),
            P("seq", "tp"),
            P("tp", "seq"),
            P("tp"),
            P("tp", None),
        ),
        out_specs=P("seq", "tp"),
        check_vma=False,
    )
```

```python
import functools

import jax
import jax.numpy as jnp
from jax import lax
from jax.experimental import pallas as pl
from jax.experimental.pallas import tpu as pltpu
from jax.sharding import PartitionSpec as P

HEAD_DIM = 128
GROUP = 256
SCALE = HEAD_DIM ** (-0.5)
F32 = jnp.float32
BF16 = jnp.bfloat16
VMEM = pl.BlockSpec(memory_space=pltpu.VMEM)
HBM = pl.BlockSpec(memory_space=pltpu.HBM)
DECAY_ROWS = 16
MESSAGE = (HEAD_DIM + DECAY_ROWS, HEAD_DIM)
PARAMS = pltpu.CompilerParams(vmem_limit_bytes=24 * 1024 * 1024)


def columns(h):
    return slice(h * HEAD_DIM, (h + 1) * HEAD_DIM)


def head_columns(h):
    return pl.ds(pl.multiple_of(h * HEAD_DIM, HEAD_DIM), HEAD_DIM)


def place(members):
    return lax.rem(lax.axis_index("seq"), members)


def contract(a, b, dims):
    return lax.dot_general(a, b, ((dims[0], dims[1]), ((), ())), preferred_element_type=F32)


def positions():
    shape = (GROUP, GROUP)
    return lax.broadcasted_iota(jnp.int32, shape, 0), lax.broadcasted_iota(jnp.int32, shape, 1)


def three_terms(values):
    first = values.astype(BF16).astype(F32)
    second = (values - first).astype(BF16).astype(F32)
    third = values - first - second
    return jnp.concatenate([first, second, third], axis=0).astype(BF16)


def sums_down(mask, decays):
    heads = decays.shape[0]
    terms = contract(mask, three_terms(decays), ((1,), (1,)))
    return terms[:, :heads] + terms[:, heads : 2 * heads] + terms[:, 2 * heads :]


def sums_across(mask, decays):
    heads = decays.shape[0]
    terms = contract(three_terms(decays), mask, ((1,), (1,)))
    return terms[:heads] + terms[heads : 2 * heads] + terms[2 * heads :]


def decay_to_rows(decay):
    wide = jnp.broadcast_to(decay, (DECAY_ROWS // 2, HEAD_DIM))
    coarse = wide.astype(BF16).astype(F32)
    return jnp.concatenate([coarse, wide - coarse], axis=0).astype(BF16)


def rows_to_decay(message):
    rows = message[HEAD_DIM:, :].astype(F32)
    return (rows[: DECAY_ROWS // 2] + rows[DECAY_ROWS // 2 :])[:1]


def write_state(h, tail, whole, key_ref, value_ref, out_ref):
    at = head_columns(h)
    factor = jnp.sum(jnp.where(row_is(tail, h), tail, 0.0), axis=0, keepdims=True)
    decay = jnp.sum(jnp.where(row_is(whole, h), whole, 0.0), axis=0, keepdims=True)
    weighted = (key_ref[:, at].T.astype(F32) * factor).astype(BF16)
    update = jnp.dot(weighted, value_ref[:, at], preferred_element_type=F32)
    out_ref[:HEAD_DIM, :] = update.astype(BF16)
    out_ref[HEAD_DIM:, :] = decay_to_rows(decay)


def row_is(values, h):
    return lax.broadcasted_iota(jnp.int32, values.shape, 0) == h


def state_factors(later, decays):
    tail = jnp.exp(sums_across(later, decays))
    whole = jnp.exp(jnp.sum(decays, axis=1, keepdims=True))
    return tail, whole


def state_kernel(steps, heads, *refs):
    sources, outs = refs[:5], refs[5 : 5 + len(steps)]
    held, sems = refs[5 + len(steps) : 10 + len(steps)], refs[-1]
    copies = [
        pltpu.make_async_copy(source, target, sems.at[i])
        for i, (source, target) in enumerate(zip(sources, held))
    ]
    for copy in copies:
        copy.start()
    decay_ref, key_ref, value_ref = held[:3]
    row, col = positions()
    later = jnp.where(col > row, 1.0, 0.0).astype(BF16)
    copies[0].wait()
    factors = state_factors(later, decay_ref[...])
    copies[1].wait()
    copies[2].wait()
    for step, out_ref in zip(steps, outs):
        write_state(place(heads) ^ step, *factors, key_ref, value_ref, out_ref)
    for copy in copies[3:]:
        copy.wait()


def local_kernel(
    heads, decay_ref, query_ref, key_ref, value_ref, intra_ref, own_ref, kept_ref
):
    row, col = positions()
    causal = col <= row
    upto = jnp.where(causal, 1.0, 0.0).astype(BF16)
    later = jnp.where(causal, 0.0, 1.0).astype(BF16)
    decays = decay_ref[...]
    write_state(place(heads), *state_factors(later, decays), key_ref, value_ref, kept_ref)
    down = sums_down(upto, decays)
    across = sums_across(upto, decays)
    own_ref[...] = jnp.exp(down) * SCALE
    for h in range(heads):
        at = columns(h)
        scores = contract(query_ref[:, at], key_ref[:, at], ((1,), (1,)))
        gaps = down[:, h : h + 1] - across[h : h + 1, :]
        weights = jnp.where(causal, jnp.exp(gaps), 0.0)
        probs = (scores * SCALE * weights).astype(BF16)
        intra_ref[:, at] = jnp.dot(probs, value_ref[:, at], preferred_element_type=F32)


def gather_kernel(steps, members, *refs):
    received, (prefix_ref, decay_ref, total_ref, held_ref) = refs[: len(steps)], refs[len(steps) :]
    me = place(members)
    for step, message_ref in zip(steps, received):
        held_ref[me ^ step] = message_ref[...]
    held = jnp.zeros((HEAD_DIM, HEAD_DIM), F32)
    through = jnp.ones((1, HEAD_DIM), F32)
    for m in range(members):
        prefix_ref[m] = held
        decay_ref[m] = jnp.broadcast_to(through, decay_ref.shape[1:])
        message = held_ref[m]
        decay = rows_to_decay(message)
        held = held * decay + message[:HEAD_DIM, :].astype(F32)
        through = through * decay
    total_ref[:HEAD_DIM, :] = held.astype(BF16)
    if total_ref.shape == MESSAGE:
        total_ref[HEAD_DIM:, :] = decay_to_rows(through)


def scatter_kernel(steps, members, swapped, prefix_ref, decay_ref, earlier_ref, *outs):
    earlier = earlier_ref[:HEAD_DIM, :].astype(F32)
    if swapped:
        earlier = jnp.where(lax.axis_index("seq") >= members, earlier, 0.0)
    for step, out_ref in zip(steps, outs):
        m = place(members) ^ step
        out_ref[...] = (prefix_ref[m] + decay_ref[m][:1] * earlier).astype(BF16)


def norm_kernel(steps, heads, rows, query_ref, intra_ref, own_ref, gain_ref, *refs):
    received, (out_ref, state_ref) = refs[: len(steps)], refs[-2:]
    me = place(heads)
    for step, message_ref in zip(steps, received):
        state_ref[me ^ step] = message_ref[...]
    for h in range(heads):
        at = columns(h)
        inter = jnp.dot(query_ref[rows, at], state_ref[h], preferred_element_type=F32)
        attended = intra_ref[rows, at] + own_ref[rows, h : h + 1] * inter
        mean_square = jnp.mean(attended * attended, axis=-1, keepdims=True)
        normed = attended * lax.rsqrt(mean_square + 1e-06)
        out_ref[:, at] = (normed * gain_ref[:, at]).astype(BF16)


def share(step, tp, mine_ref, other_ref, weight_ref, other_weight_ref):
    width = weight_ref.shape[1] // tp
    target = lax.axis_index("tp") ^ step
    at = pl.ds(pl.multiple_of(target * width, width), width)
    return jnp.dot(mine_ref[...], weight_ref[:, at], preferred_element_type=F32) + jnp.dot(
        other_ref[...], other_weight_ref[:, at], preferred_element_type=F32
    )


def far_kernel(tp, mine_ref, other_ref, weight_ref, other_weight_ref, out_ref):
    out_ref[...] = share(2, tp, mine_ref, other_ref, weight_ref, other_weight_ref).astype(BF16)


def near_kernel(tp, chunks, residual_ref, weight_ref, other_weight_ref, *refs):
    out_ref = refs[-1]
    for i, rows in enumerate(chunks):
        near = share(0, tp, refs[2 * i], refs[2 * i + 1], weight_ref, other_weight_ref)
        out_ref[rows, :] = residual_ref[rows, :].astype(F32) + near


def add_kernel(chunks, near_ref, *refs):
    far, (out_hbm, out_ref, sems) = refs[: len(chunks)], refs[len(chunks) :]
    copies = []
    for i, rows in enumerate(chunks):
        out_ref[rows, :] = (near_ref[rows, :] + far[i][...].astype(F32)).astype(BF16)
        copies.append(
            pltpu.make_async_copy(out_ref.at[rows, :], out_hbm.at[rows, :], sems.at[i])
        )
        copies[-1].start()
    for copy in copies:
        copy.wait()


def call(kernel, out_shape, in_specs, name, out_specs=None, scratch=(), cost=0):
    single = isinstance(out_shape, jax.ShapeDtypeStruct)
    if out_specs is None:
        out_specs = VMEM if single else (VMEM,) * len(out_shape)
    cost = pl.CostEstimate(
        flops=cost, bytes_accessed=2_000_000 if cost else 0, transcendentals=0
    )
    return pl.pallas_call(
        kernel,
        out_shape=out_shape,
        in_specs=in_specs,
        out_specs=out_specs,
        scratch_shapes=scratch,
        compiler_params=PARAMS,
        cost_estimate=cost,
        name=name,
    )


def earlier_groups(total, members, devices):
    groups = devices // members
    if groups == 2:
        pairs = [(i, i ^ members) for i in range(devices)]
        return lax.ppermute(total, "seq", pairs)

    def shift(message, by):
        moves = [(i, i + by * members) for i in range(devices - by * members)]
        return lax.ppermute(message, "seq", moves)

    held = shift(total, 1)
    by = 1
    while by < groups - 1:
        before = shift(held, by)
        decay = rows_to_decay(held)
        state = held[:HEAD_DIM].astype(F32) + decay * before[:HEAD_DIM].astype(F32)
        through = decay_to_rows(decay * rows_to_decay(before))
        held = jnp.concatenate([state.astype(BF16), through], axis=0)
        by *= 2
    return held


def on_device(
    residual, query_vectors, key_vectors, value_vectors, log_decay, norm_gain, out_weight
):
    tokens, width = residual.shape
    heads = log_decay.shape[0]
    devices = lax.axis_size("seq")
    tp = lax.axis_size("tp")
    wide = (tokens, heads * HEAD_DIM)
    near_pairs = [(i, i ^ 1) for i in range(tp)]
    far_pairs = [(i, i ^ 2) for i in range(tp)]
    shape = jax.ShapeDtypeStruct
    steps = [heads - 1, *range(1, heads - 1), 0]

    def exchange(messages):
        moved = []
        for step, message in zip(steps, messages):
            pairs = [(i, i ^ step) for i in range(devices)]
            moved.append(lax.ppermute(message, "seq", pairs) if step else message)
        return moved

    other_weight = lax.ppermute(out_weight, "tp", near_pairs)
    arguments = (log_decay, key_vectors, value_vectors, query_vectors, norm_gain.reshape(1, -1))
    *states, decays, keys, values, queries, gain = call(
        functools.partial(state_kernel, steps[:-1], heads),
        (shape(MESSAGE, BF16),) * (heads - 1)
        + tuple(shape(a.shape, a.dtype) for a in arguments),
        [HBM] * 5,
        "states",
        scratch=[pltpu.SemaphoreType.DMA((5,))],
    )(*(pltpu.with_memory_space_constraint(a, pltpu.HBM) for a in arguments))
    received = exchange(states)
    intra, own, kept = call(
        functools.partial(local_kernel, heads),
        (shape(wide, F32), shape((tokens, heads), F32), shape(MESSAGE, BF16)),
        [VMEM] * 4,
        "local",
        cost=4 * tokens * tokens * heads * HEAD_DIM,
    )(decays, queries, keys, values)
    prefix, through, total = call(
        functools.partial(gather_kernel, steps, heads),
        (
            shape((heads, HEAD_DIM, HEAD_DIM), F32),
            shape((heads, 8, HEAD_DIM), F32),
            shape((HEAD_DIM, HEAD_DIM) if devices == 2 * heads else MESSAGE, BF16),
        ),
        [VMEM] * heads,
        "gather_states",
        scratch=[pltpu.VMEM((heads,) + MESSAGE, BF16)],
    )(*received, kept)
    earlier = earlier_groups(total, heads, devices)
    starts = call(
        functools.partial(scatter_kernel, steps, heads, devices == 2 * heads),
        (shape((HEAD_DIM, HEAD_DIM), BF16),) * heads,
        [VMEM] * 3,
        "scatter_states",
    )(prefix, through, earlier)
    incoming = exchange(starts)

    first = tokens * 3 // 8
    chunks = [slice(0, first), slice(first, tokens)]
    out_width = out_weight.shape[1] // tp
    normed, far, ahead = [], [], []
    for i, rows in enumerate(chunks):
        part = call(
            functools.partial(norm_kernel, steps, heads, rows),
            shape((rows.stop - rows.start, heads * HEAD_DIM), BF16),
            [VMEM] * (4 + heads + len(ahead)),
            f"norm_{i}",
            scratch=[pltpu.VMEM((heads, HEAD_DIM, HEAD_DIM), BF16)],
        )(queries, intra, own, gain, *incoming, *ahead)
        normed.append((part, lax.ppermute(part, "tp", near_pairs)))
        part = call(
            functools.partial(far_kernel, tp),
            shape((rows.stop - rows.start, out_width), BF16),
            [VMEM] * 4,
            f"project_far_{i}",
        )(*normed[i], out_weight, other_weight)
        far.append(lax.ppermute(part, "tp", far_pairs))
        ahead = [part]
    near = call(
        functools.partial(near_kernel, tp, chunks),
        shape((tokens, out_width), F32),
        [VMEM] * (3 + 2 * len(chunks)),
        "project_near",
    )(residual, out_weight, other_weight, *(a for pair in normed for a in pair))
    return call(
        functools.partial(add_kernel, chunks),
        shape((tokens, out_width), BF16),
        [VMEM] * (1 + len(chunks)),
        "add",
        out_specs=HBM,
        scratch=[
            pltpu.VMEM((tokens, out_width), BF16),
            pltpu.SemaphoreType.DMA((len(chunks),)),
        ],
    )(near, *far)


def solution(mesh):
    return jax.shard_map(
        on_device,
        mesh=mesh,
        in_specs=(
            P("seq", "tp"),
            P("seq", "tp"),
            P("seq", "tp"),
            P("seq", "tp"),
            P("tp", "seq"),
            P("tp"),
            P("tp", None),
        ),
        out_specs=P("seq", "tp"),
        check_vma=False,
    )
```

```python
import functools

import jax
import jax.numpy as jnp
from jax import lax
from jax.experimental import pallas as pl
from jax.experimental.pallas import tpu as pltpu
from jax.sharding import PartitionSpec as P

HEAD_DIM = 128
GROUP = 256
SCALE = HEAD_DIM ** (-0.5)
F32 = jnp.float32
BF16 = jnp.bfloat16
VMEM = pl.BlockSpec(memory_space=pltpu.VMEM)
HBM = pl.BlockSpec(memory_space=pltpu.HBM)
DECAY_ROWS = 16
MEMBERS = 4
PARAMS = pltpu.CompilerParams(vmem_limit_bytes=24 * 1024 * 1024)


def state_rows(j):
    return slice(j * HEAD_DIM, (j + 1) * HEAD_DIM)


def place():
    return lax.rem(lax.axis_index("seq"), MEMBERS)


def side():
    return lax.rem(lax.axis_index("seq"), 2)


def half_at(owner, size):
    return pl.ds(pl.multiple_of(owner * size, size), size)


def pick(owner, values, axis):
    half = values.shape[axis] // 2
    low = lax.slice_in_dim(values, 0, half, axis=axis)
    high = lax.slice_in_dim(values, half, 2 * half, axis=axis)
    return jnp.where(owner == 0, low, high)


def contract(a, b):
    return lax.dot_general(a, b, (((1,), (1,)), ((), ())), preferred_element_type=F32)


def positions():
    shape = (GROUP, GROUP)
    return lax.broadcasted_iota(jnp.int32, shape, 0), lax.broadcasted_iota(jnp.int32, shape, 1)


def three_terms(values):
    first = values.astype(BF16).astype(F32)
    second = (values - first).astype(BF16).astype(F32)
    third = values - first - second
    return jnp.concatenate([first, second, third], axis=0).astype(BF16)


def sums_down(mask, decays):
    heads = decays.shape[0]
    terms = contract(mask, three_terms(decays))
    return terms[:, :heads] + terms[:, heads : 2 * heads] + terms[:, 2 * heads :]


def sums_across(mask, decays):
    heads = decays.shape[0]
    terms = contract(three_terms(decays), mask)
    return terms[:heads] + terms[heads : 2 * heads] + terms[2 * heads :]


def decays_to_rows(decays):
    each = DECAY_ROWS // (2 * len(decays))
    wide = jnp.concatenate([jnp.broadcast_to(d, (each, HEAD_DIM)) for d in decays], axis=0)
    coarse = wide.astype(BF16).astype(F32)
    return jnp.concatenate([coarse, wide - coarse], axis=0).astype(BF16)


def rows_to_decays(rows, half):
    rows = rows.astype(F32)
    each = DECAY_ROWS // (2 * half)
    both = rows[: DECAY_ROWS // 2] + rows[DECAY_ROWS // 2 :]
    return [both[j * each : j * each + 1] for j in range(half)]


def state_kernel(half, *refs):
    sources, outs, held, sems = refs[:5], refs[5:7], refs[7:12], refs[12]
    copies = [
        pltpu.make_async_copy(source, target, sems.at[i])
        for i, (source, target) in enumerate(zip(sources, held))
    ]
    for copy in copies:
        copy.start()
    decay_ref, key_ref, value_ref = held[:3]
    me = side()
    row, col = positions()
    later = jnp.where(col > row, 1.0, 0.0).astype(BF16)
    copies[0].wait()
    decays = decay_ref[...]
    tail = jnp.exp(sums_across(later, decays))
    whole = jnp.exp(jnp.sum(decays, axis=1, keepdims=True))
    copies[1].wait()
    copies[2].wait()
    for owner, out_ref in zip((1 - me, me), outs):
        factors, totals = pick(owner, tail, 0), pick(owner, whole, 0)
        for j in range(half):
            at = half_at(owner * half + j, HEAD_DIM)
            weighted = (key_ref[:, at].T.astype(F32) * factors[j : j + 1, :]).astype(BF16)
            update = jnp.dot(weighted, value_ref[:, at], preferred_element_type=F32)
            out_ref[state_rows(j), :] = update.astype(BF16)
        out_ref[half * HEAD_DIM :, :] = decays_to_rows([totals[j : j + 1] for j in range(half)])
    for copy in copies[3:]:
        copy.wait()


def local_kernel(heads, decay_ref, query_ref, key_ref, value_ref, intra_ref, own_ref):
    row, col = positions()
    causal = col <= row
    upto = jnp.where(causal, 1.0, 0.0).astype(BF16)
    decays = decay_ref[...]
    down = sums_down(upto, decays)
    across = sums_across(upto, decays)
    own_ref[...] = jnp.exp(down) * SCALE
    for h in range(heads):
        at = slice(h * HEAD_DIM, (h + 1) * HEAD_DIM)
        scores = contract(query_ref[:, at], key_ref[:, at])
        gaps = down[:, h : h + 1] - across[h : h + 1, :]
        weights = jnp.where(causal, jnp.exp(gaps), 0.0)
        probs = (scores * SCALE * weights).astype(BF16)
        intra_ref[:, at] = jnp.dot(probs, value_ref[:, at], preferred_element_type=F32)


def gather_kernel(half, steps, *refs):
    received, (before_ref, through_ref, total_ref, held_ref) = refs[: len(steps)], refs[len(steps) :]
    me = place()
    for step, message_ref in zip(steps, received):
        held_ref[me ^ step] = message_ref[...]
    second = me >= 2
    decays = [rows_to_decays(held_ref[m, half * HEAD_DIM :, :], half) for m in range(MEMBERS)]
    totals = []
    for j in range(half):
        at = state_rows(j)
        held = [jnp.zeros((HEAD_DIM, HEAD_DIM), F32)]
        through = [jnp.ones((1, HEAD_DIM), F32)]
        for m in range(MEMBERS):
            held.append(held[m] * decays[m][j] + held_ref[m, at, :].astype(F32))
            through.append(through[m] * decays[m][j])
        for i in range(2):
            before_ref[i, at, :] = jnp.where(second, held[2 + i], held[i])
            factor = jnp.where(second, through[2 + i], through[i])
            rows = slice(j * 8, (j + 1) * 8)
            through_ref[i, rows, :] = jnp.broadcast_to(factor, (8, HEAD_DIM))
        total_ref[at, :] = held[MEMBERS].astype(BF16)
        totals.append(through[MEMBERS])
    if total_ref.shape[0] > half * HEAD_DIM:
        total_ref[half * HEAD_DIM :, :] = decays_to_rows(totals)


def start_kernel(half, swapped, before_ref, through_ref, earlier_ref, _, mine_ref, other_ref):
    second = side() == 1
    other_ref[half * HEAD_DIM :, :] = jnp.zeros((DECAY_ROWS, HEAD_DIM), BF16)
    for j in range(half):
        at = state_rows(j)
        earlier = earlier_ref[at, :].astype(F32)
        if swapped:
            earlier = jnp.where(lax.axis_index("seq") >= MEMBERS, earlier, 0.0)
        first, last = [
            (before_ref[i, at, :] + through_ref[i, j * 8 : j * 8 + 1, :] * earlier).astype(BF16)
            for i in range(2)
        ]
        mine_ref[at, :] = jnp.where(second, last, first)
        other_ref[at, :] = jnp.where(second, first, last)


def norm_kernel(half, mine, rows, query_ref, intra_ref, own_ref, gain_ref, state_ref, *refs):
    out_ref = refs[-1]
    owner = side() if mine else 1 - side()
    own = pick(owner, own_ref[rows, :], 1)
    for j in range(half):
        at = half_at(owner * half + j, HEAD_DIM)
        inter = jnp.dot(query_ref[rows, at], state_ref[state_rows(j), :], preferred_element_type=F32)
        attended = intra_ref[rows, at] + own[:, j : j + 1] * inter
        mean_square = jnp.mean(attended * attended, axis=-1, keepdims=True)
        normed = attended * lax.rsqrt(mean_square + 1e-06)
        out_ref[:, j * HEAD_DIM : (j + 1) * HEAD_DIM] = (normed * gain_ref[:, at]).astype(BF16)


def share(mine, step, tp, pair, weight_ref, other_weight_ref):
    rows, width = weight_ref.shape[0] // 2, weight_ref.shape[1] // tp
    at = (
        half_at(side() if mine else 1 - side(), rows),
        half_at(lax.axis_index("tp") ^ step, width),
    )
    return jnp.dot(pair[0][...], weight_ref[at], preferred_element_type=F32) + jnp.dot(
        pair[1][...], other_weight_ref[at], preferred_element_type=F32
    )


def far_mine_kernel(tp, chunks, weight_ref, other_weight_ref, *refs):
    for i, rows in enumerate(chunks):
        pair = refs[2 * i : 2 * i + 2]
        refs[-1][rows, :] = share(True, 2, tp, pair, weight_ref, other_weight_ref)


def far_kernel(tp, rows, begun_ref, mine_ref, other_ref, weight_ref, other_weight_ref, out_ref):
    rest = share(False, 2, tp, (mine_ref, other_ref), weight_ref, other_weight_ref)
    out_ref[...] = (begun_ref[rows, :] + rest).astype(BF16)


def near_kernel(tp, chunks, residual_ref, weight_ref, other_weight_ref, *refs):
    weights, out_ref = (weight_ref, other_weight_ref), refs[-1]
    for i, rows in enumerate(chunks):
        mine, rest = refs[4 * i : 4 * i + 2], refs[4 * i + 2 : 4 * i + 4]
        near = share(True, 0, tp, mine, *weights) + share(False, 0, tp, rest, *weights)
        out_ref[rows, :] = residual_ref[rows, :].astype(F32) + near


def add_kernel(chunks, near_ref, *refs):
    far, (out_hbm, out_ref, sems) = refs[: len(chunks)], refs[len(chunks) :]
    copies = []
    for i, rows in enumerate(chunks):
        out_ref[rows, :] = (near_ref[rows, :] + far[i][...].astype(F32)).astype(BF16)
        copies.append(
            pltpu.make_async_copy(out_ref.at[rows, :], out_hbm.at[rows, :], sems.at[i])
        )
        copies[-1].start()
    for copy in copies:
        copy.wait()


def call(kernel, out_shape, in_specs, name, out_specs=None, scratch=(), cost=0):
    single = isinstance(out_shape, jax.ShapeDtypeStruct)
    if out_specs is None:
        out_specs = VMEM if single else (VMEM,) * len(out_shape)
    cost = pl.CostEstimate(
        flops=cost, bytes_accessed=2_000_000 if cost else 0, transcendentals=0
    )
    return pl.pallas_call(
        kernel,
        out_shape=out_shape,
        in_specs=in_specs,
        out_specs=out_specs,
        scratch_shapes=scratch,
        compiler_params=PARAMS,
        cost_estimate=cost,
        name=name,
    )


def earlier_groups(total, half, devices):
    groups = devices // MEMBERS
    if groups == 2:
        return lax.ppermute(total, "seq", [(i, i ^ MEMBERS) for i in range(devices)])

    def shift(message, by):
        moves = [(i, i + by * MEMBERS) for i in range(devices - by * MEMBERS)]
        return lax.ppermute(message, "seq", moves)

    rows = half * HEAD_DIM
    held = shift(total, 1)
    by = 1
    while by < groups - 1:
        before = shift(held, by)
        decays = rows_to_decays(held[rows:], half)
        factor = jnp.concatenate([jnp.broadcast_to(d, (HEAD_DIM, HEAD_DIM)) for d in decays])
        state = held[:rows].astype(F32) + factor * before[:rows].astype(F32)
        through = [a * b for a, b in zip(decays, rows_to_decays(before[rows:], half))]
        held = jnp.concatenate([state.astype(BF16), decays_to_rows(through)], axis=0)
        by *= 2
    return held


def on_device(
    residual, query_vectors, key_vectors, value_vectors, log_decay, norm_gain, out_weight
):
    tokens, width = residual.shape
    heads = log_decay.shape[0]
    half = heads // 2
    devices = lax.axis_size("seq")
    tp = lax.axis_size("tp")
    wide = (tokens, heads * HEAD_DIM)
    states = (half * HEAD_DIM, HEAD_DIM)
    near_pairs = [(i, i ^ 1) for i in range(tp)]
    far_pairs = [(i, i ^ 2) for i in range(tp)]
    shape = jax.ShapeDtypeStruct
    message = shape((half * HEAD_DIM + DECAY_ROWS, HEAD_DIM), BF16)

    def swap(piece, step):
        return lax.ppermute(piece, "seq", [(i, i ^ step) for i in range(devices)])

    other_weight = lax.ppermute(out_weight, "tp", near_pairs)
    arguments = (log_decay, key_vectors, value_vectors, query_vectors, norm_gain.reshape(1, -1))
    theirs, mine, decays, keys, values, queries, gain = call(
        functools.partial(state_kernel, half),
        (message, message) + tuple(shape(a.shape, a.dtype) for a in arguments),
        [HBM] * 5,
        "states",
        scratch=[pltpu.SemaphoreType.DMA((5,))],
    )(*(pltpu.with_memory_space_constraint(a, pltpu.HBM) for a in arguments))
    steps = (3, 1, 2, 0)
    received = [swap(theirs, 3), swap(theirs, 1), swap(mine, 2), mine]
    intra, own = call(
        functools.partial(local_kernel, heads),
        (shape(wide, F32), shape((tokens, heads), F32)),
        [VMEM] * 4,
        "local",
        cost=4 * tokens * tokens * heads * HEAD_DIM,
    )(decays, queries, keys, values)
    before, through, total = call(
        functools.partial(gather_kernel, half, steps),
        (
            shape((2,) + states, F32),
            shape((2, half * 8, HEAD_DIM), F32),
            shape(states, BF16) if devices == 2 * MEMBERS else message,
        ),
        [VMEM] * len(steps),
        "gather_states",
        scratch=[pltpu.VMEM((MEMBERS,) + message.shape, BF16)],
    )(*received)
    earlier = earlier_groups(total, half, devices)
    state, other_state = call(
        functools.partial(start_kernel, half, devices == 2 * MEMBERS),
        (shape(states, BF16), message),
        [VMEM] * 4,
        "start_states",
    )(before, through, earlier, own)
    other_state = swap(other_state, 1)

    def normed(name, rows, mine, state, *ahead):
        part = call(
            functools.partial(norm_kernel, half, mine, rows),
            shape((rows.stop - rows.start, half * HEAD_DIM), BF16),
            [VMEM] * (5 + len(ahead)),
            name,
        )(queries, intra, own, gain, state, *ahead)
        return part, lax.ppermute(part, "tp", near_pairs)

    out_width = out_weight.shape[1] // tp
    weights = (out_weight, other_weight)
    chunks = [slice(0, tokens // 2), slice(tokens // 2, tokens)]
    begun = [normed(f"norm_mine_{i}", rows, True, state) for i, rows in enumerate(chunks)]
    far_begun = call(
        functools.partial(far_mine_kernel, tp, chunks),
        shape((tokens, out_width), F32),
        [VMEM] * (2 + 2 * len(chunks)),
        "project_far_mine",
    )(*weights, *(a for pair in begun for a in pair))
    parts = [
        normed(f"norm_{i}", rows, False, other_state, far_begun) for i, rows in enumerate(chunks)
    ]
    far = []
    for i, rows in enumerate(chunks):
        part = call(
            functools.partial(far_kernel, tp, rows),
            shape((rows.stop - rows.start, out_width), BF16),
            [VMEM] * 5,
            f"project_far_{i}",
        )(far_begun, *parts[i], *weights)
        far.append(lax.ppermute(part, "tp", far_pairs))
    near = call(
        functools.partial(near_kernel, tp, chunks),
        shape((tokens, out_width), F32),
        [VMEM] * (3 + 4 * len(chunks)),
        "project_near",
    )(residual, *weights, *(a for i in range(len(chunks)) for a in begun[i] + parts[i]))
    return call(
        functools.partial(add_kernel, chunks),
        shape((tokens, out_width), BF16),
        [VMEM] * (1 + len(chunks)),
        "add",
        out_specs=HBM,
        scratch=[
            pltpu.VMEM((tokens, out_width), BF16),
            pltpu.SemaphoreType.DMA((len(chunks),)),
        ],
    )(near, *far)


def solution(mesh):
    return jax.shard_map(
        on_device,
        mesh=mesh,
        in_specs=(
            P("seq", "tp"),
            P("seq", "tp"),
            P("seq", "tp"),
            P("seq", "tp"),
            P("tp", "seq"),
            P("tp"),
            P("tp", None),
        ),
        out_specs=P("seq", "tp"),
        check_vma=False,
    )
```

```python
import functools

import jax
import jax.numpy as jnp
from jax import lax
from jax.experimental import pallas as pl
from jax.experimental.pallas import tpu as pltpu
from jax.sharding import PartitionSpec as P

HEAD_DIM = 128
GROUP = 256
SCALE = HEAD_DIM ** (-0.5)
F32 = jnp.float32
BF16 = jnp.bfloat16
VMEM = pl.BlockSpec(memory_space=pltpu.VMEM)
HBM = pl.BlockSpec(memory_space=pltpu.HBM)
DECAY_ROWS = 16
MEMBERS = 4
PARAMS = pltpu.CompilerParams(vmem_limit_bytes=24 * 1024 * 1024)


def state_rows(j):
    return slice(j * HEAD_DIM, (j + 1) * HEAD_DIM)


def place():
    return lax.rem(lax.axis_index("seq"), MEMBERS)


def side():
    return lax.rem(lax.axis_index("seq"), 2)


def half_at(owner, size):
    return pl.ds(pl.multiple_of(owner * size, size), size)


def pick(owner, values, axis):
    half = values.shape[axis] // 2
    low = lax.slice_in_dim(values, 0, half, axis=axis)
    high = lax.slice_in_dim(values, half, 2 * half, axis=axis)
    return jnp.where(owner == 0, low, high)


def contract(a, b):
    return lax.dot_general(a, b, (((1,), (1,)), ((), ())), preferred_element_type=F32)


def positions():
    shape = (GROUP, GROUP)
    return lax.broadcasted_iota(jnp.int32, shape, 0), lax.broadcasted_iota(jnp.int32, shape, 1)


def three_terms(values):
    first = values.astype(BF16).astype(F32)
    second = (values - first).astype(BF16).astype(F32)
    third = values - first - second
    return jnp.concatenate([first, second, third], axis=0).astype(BF16)


def sums_down(mask, decays):
    heads = decays.shape[0]
    terms = contract(mask, three_terms(decays))
    return terms[:, :heads] + terms[:, heads : 2 * heads] + terms[:, 2 * heads :]


def sums_across(mask, decays):
    heads = decays.shape[0]
    terms = contract(three_terms(decays), mask)
    return terms[:heads] + terms[heads : 2 * heads] + terms[2 * heads :]


def decays_to_rows(decays):
    each = DECAY_ROWS // (2 * len(decays))
    wide = jnp.concatenate([jnp.broadcast_to(d, (each, HEAD_DIM)) for d in decays], axis=0)
    coarse = wide.astype(BF16).astype(F32)
    return jnp.concatenate([coarse, wide - coarse], axis=0).astype(BF16)


def rows_to_decays(rows, count):
    rows = rows.astype(F32)
    each = DECAY_ROWS // (2 * count)
    both = rows[: DECAY_ROWS // 2] + rows[DECAY_ROWS // 2 :]
    return [both[j * each : j * each + 1] for j in range(count)]


def state_kernel(half, *refs):
    sources, outs, held, sems = refs[:5], refs[5:7], refs[7:12], refs[12]
    copies = [
        pltpu.make_async_copy(source, target, sems.at[i])
        for i, (source, target) in enumerate(zip(sources, held))
    ]
    for copy in copies:
        copy.start()
    decay_ref, key_ref, value_ref = held[:3]
    me = side()
    row, col = positions()
    later = jnp.where(col > row, 1.0, 0.0).astype(BF16)
    copies[0].wait()
    decays = decay_ref[...]
    tail = jnp.exp(sums_across(later, decays))
    whole = jnp.exp(jnp.sum(decays, axis=1, keepdims=True))
    copies[1].wait()
    copies[2].wait()
    decay_rows = decays_to_rows([whole[h : h + 1] for h in range(2 * half)])
    for owner, out_ref in zip((1 - me, me), outs):
        factors = pick(owner, tail, 0)
        for j in range(half):
            at = half_at(owner * half + j, HEAD_DIM)
            weighted = (key_ref[:, at].T.astype(F32) * factors[j : j + 1, :]).astype(BF16)
            update = jnp.dot(weighted, value_ref[:, at], preferred_element_type=F32)
            out_ref[state_rows(j), :] = update.astype(BF16)
        out_ref[half * HEAD_DIM :, :] = decay_rows
    for copy in copies[3:]:
        copy.wait()


def local_kernel(heads, decay_ref, query_ref, key_ref, value_ref, intra_ref, own_ref):
    row, col = positions()
    causal = col <= row
    upto = jnp.where(causal, 1.0, 0.0).astype(BF16)
    decays = decay_ref[...]
    down = sums_down(upto, decays)
    across = sums_across(upto, decays)
    own_ref[...] = jnp.exp(down) * SCALE
    for h in range(heads):
        at = slice(h * HEAD_DIM, (h + 1) * HEAD_DIM)
        scores = contract(query_ref[:, at], key_ref[:, at])
        gaps = down[:, h : h + 1] - across[h : h + 1, :]
        weights = jnp.where(causal, jnp.exp(gaps), 0.0)
        probs = (scores * SCALE * weights).astype(BF16)
        intra_ref[:, at] = jnp.dot(probs, value_ref[:, at], preferred_element_type=F32)


def gather_kernel(half, steps, *refs):
    received, (before_ref, mine_ref, sent_ref, through_ref, total_ref, held_ref) = (
        refs[: len(steps)],
        refs[len(steps) :],
    )
    me, upper = place(), side() == 1
    for step, message_ref in zip(steps, received):
        held_ref[me ^ step] = message_ref[...]
    later_pair = me >= 2
    decays = [rows_to_decays(held_ref[m, half * HEAD_DIM :, :], 2 * half) for m in range(MEMBERS)]
    totals = []
    for j in range(2 * half):
        low, high = (j, half + j) if j < half else (j, j - half)
        decay = [jnp.where(upper, d[high], d[low]) for d in decays]
        through = [jnp.ones((1, HEAD_DIM), F32)]
        for m in range(MEMBERS):
            through.append(through[m] * decay[m])
        first, last = [jnp.where(later_pair, through[2 + i], through[i]) for i in range(2)]
        factor = jnp.where(upper, last, first)
        through_ref[j * 8 : (j + 1) * 8, :] = jnp.broadcast_to(factor, (8, HEAD_DIM))
        if j >= half:
            continue
        at = state_rows(j)
        held = [jnp.zeros((HEAD_DIM, HEAD_DIM), F32)]
        for m in range(MEMBERS):
            held.append(held[m] * decay[m] + held_ref[m, at, :].astype(F32))
        first, last = [jnp.where(later_pair, held[2 + i], held[i]) for i in range(2)]
        before = jnp.where(upper, last, first)
        before_ref[at, :] = before
        mine_ref[at, :] = before.astype(BF16)
        sent_ref[at, :] = jnp.where(upper, first, last).astype(BF16)
        total_ref[at, :] = held[MEMBERS].astype(BF16)
        totals.append(through[MEMBERS])
    total_ref[half * HEAD_DIM :, :] = decays_to_rows(totals)


def start_kernel(half, mine, before_ref, through_ref, earlier_ref, *refs):
    for j in range(half):
        at, row = state_rows(j), 8 * (j if mine else half + j)
        earlier = through_ref[row : row + 1, :] * earlier_ref[at, :].astype(F32)
        refs[-1][at, :] = (before_ref[at, :].astype(F32) + earlier).astype(BF16)


def norm_kernel(half, mine, rows, query_ref, intra_ref, own_ref, gain_ref, state_ref, out_ref):
    owner = side() if mine else 1 - side()
    own = pick(owner, own_ref[rows, :], 1)
    for j in range(half):
        at = half_at(owner * half + j, HEAD_DIM)
        inter = jnp.dot(query_ref[rows, at], state_ref[state_rows(j), :], preferred_element_type=F32)
        attended = intra_ref[rows, at] + own[:, j : j + 1] * inter
        mean_square = jnp.mean(attended * attended, axis=-1, keepdims=True)
        normed = attended * lax.rsqrt(mean_square + 1e-06)
        out_ref[:, j * HEAD_DIM : (j + 1) * HEAD_DIM] = (normed * gain_ref[:, at]).astype(BF16)


def share(mine, step, tp, pair, weight_ref, other_weight_ref):
    rows, width = weight_ref.shape[0] // 2, weight_ref.shape[1] // tp
    at = (
        half_at(side() if mine else 1 - side(), rows),
        half_at(lax.axis_index("tp") ^ step, width),
    )
    return jnp.dot(pair[0][...], weight_ref[at], preferred_element_type=F32) + jnp.dot(
        pair[1][...], other_weight_ref[at], preferred_element_type=F32
    )


def far_mine_kernel(tp, chunks, weight_ref, other_weight_ref, *refs):
    for i, rows in enumerate(chunks):
        pair = refs[2 * i : 2 * i + 2]
        refs[-1][rows, :] = share(True, 2, tp, pair, weight_ref, other_weight_ref)


def far_kernel(tp, rows, begun_ref, mine_ref, other_ref, weight_ref, other_weight_ref, out_ref):
    rest = share(False, 2, tp, (mine_ref, other_ref), weight_ref, other_weight_ref)
    out_ref[...] = (begun_ref[rows, :] + rest).astype(BF16)


def near_kernel(tp, chunks, residual_ref, weight_ref, other_weight_ref, *refs):
    weights, out_ref = (weight_ref, other_weight_ref), refs[-1]
    for i, rows in enumerate(chunks):
        mine, rest = refs[4 * i : 4 * i + 2], refs[4 * i + 2 : 4 * i + 4]
        near = share(True, 0, tp, mine, *weights) + share(False, 0, tp, rest, *weights)
        out_ref[rows, :] = residual_ref[rows, :].astype(F32) + near


def add_kernel(chunks, near_ref, *refs):
    far, (out_hbm, out_ref, sems) = refs[: len(chunks)], refs[len(chunks) :]
    copies = []
    for i, rows in enumerate(chunks):
        out_ref[rows, :] = (near_ref[rows, :] + far[i][...].astype(F32)).astype(BF16)
        copies.append(
            pltpu.make_async_copy(out_ref.at[rows, :], out_hbm.at[rows, :], sems.at[i])
        )
        copies[-1].start()
    for copy in copies:
        copy.wait()


def call(kernel, out_shape, in_specs, name, out_specs=None, scratch=(), cost=0):
    single = isinstance(out_shape, jax.ShapeDtypeStruct)
    if out_specs is None:
        out_specs = VMEM if single else (VMEM,) * len(out_shape)
    cost = pl.CostEstimate(
        flops=cost, bytes_accessed=2_000_000 if cost else 0, transcendentals=0
    )
    return pl.pallas_call(
        kernel,
        out_shape=out_shape,
        in_specs=in_specs,
        out_specs=out_specs,
        scratch_shapes=scratch,
        compiler_params=PARAMS,
        cost_estimate=cost,
        name=name,
    )


def earlier_groups(total, half, devices):
    groups = devices // MEMBERS
    if groups == 2:
        return lax.ppermute(total, "seq", [(i, i ^ MEMBERS) for i in range(devices)])

    def shift(message, by):
        moves = [(i, i + by * MEMBERS) for i in range(devices - by * MEMBERS)]
        return lax.ppermute(message, "seq", moves)

    rows = half * HEAD_DIM
    held = shift(total, 1)
    by = 1
    while by < groups - 1:
        before = shift(held, by)
        decays = rows_to_decays(held[rows:], half)
        factor = jnp.concatenate([jnp.broadcast_to(d, (HEAD_DIM, HEAD_DIM)) for d in decays])
        state = held[:rows].astype(F32) + factor * before[:rows].astype(F32)
        through = [a * b for a, b in zip(decays, rows_to_decays(before[rows:], half))]
        held = jnp.concatenate([state.astype(BF16), decays_to_rows(through)], axis=0)
        by *= 2
    return held


def on_device(
    residual, query_vectors, key_vectors, value_vectors, log_decay, norm_gain, out_weight
):
    tokens, width = residual.shape
    heads = log_decay.shape[0]
    half = heads // 2
    devices = lax.axis_size("seq")
    tp = lax.axis_size("tp")
    wide = (tokens, heads * HEAD_DIM)
    states = (half * HEAD_DIM, HEAD_DIM)
    near_pairs = [(i, i ^ 1) for i in range(tp)]
    far_pairs = [(i, i ^ 2) for i in range(tp)]
    shape = jax.ShapeDtypeStruct
    message = shape((half * HEAD_DIM + DECAY_ROWS, HEAD_DIM), BF16)

    def swap(piece, step):
        return lax.ppermute(piece, "seq", [(i, i ^ step) for i in range(devices)])

    other_weight = lax.ppermute(out_weight, "tp", near_pairs)
    arguments = (log_decay, key_vectors, value_vectors, query_vectors, norm_gain.reshape(1, -1))
    theirs, mine, decays, keys, values, queries, gain = call(
        functools.partial(state_kernel, half),
        (message, message) + tuple(shape(a.shape, a.dtype) for a in arguments),
        [HBM] * 5,
        "states",
        scratch=[pltpu.SemaphoreType.DMA((5,))],
    )(*(pltpu.with_memory_space_constraint(a, pltpu.HBM) for a in arguments))
    steps = (3, 1, 2, 0)
    received = [swap(theirs, 3), swap(theirs, 1), swap(mine, 2), mine]
    intra, own = call(
        functools.partial(local_kernel, heads),
        (shape(wide, F32), shape((tokens, heads), F32)),
        [VMEM] * 4,
        "local",
        cost=4 * tokens * tokens * heads * HEAD_DIM,
    )(decays, queries, keys, values)
    state = shape(states, BF16)
    before, mine, sent, through, total = call(
        functools.partial(gather_kernel, half, steps),
        (shape(states, F32), state, state, shape((heads * 8, HEAD_DIM), F32), message),
        [VMEM] * len(steps),
        "gather_states",
        scratch=[pltpu.VMEM((MEMBERS,) + message.shape, BF16)],
    )(*received)
    earlier = earlier_groups(total, half, devices)
    inside = swap(sent, 1)

    def normed(name, rows, mine, state):
        part = call(
            functools.partial(norm_kernel, half, mine, rows),
            shape((rows.stop - rows.start, half * HEAD_DIM), BF16),
            [VMEM] * 5,
            name,
        )(queries, intra, own, gain, state)
        return part, lax.ppermute(part, "tp", near_pairs)

    out_width = out_weight.shape[1] // tp
    weights = (out_weight, other_weight)
    chunks = [slice(0, tokens // 2), slice(tokens // 2, tokens)]

    def finish(state, other_state_behind):
        begun = [normed(f"norm_mine_{i}", rows, True, state) for i, rows in enumerate(chunks)]
        far_begun = call(
            functools.partial(far_mine_kernel, tp, chunks),
            shape((tokens, out_width), F32),
            [VMEM] * (2 + 2 * len(chunks)),
            "project_far_mine",
        )(*weights, *(a for pair in begun for a in pair))
        other_state = other_state_behind(far_begun)
        parts = [normed(f"norm_{i}", rows, False, other_state) for i, rows in enumerate(chunks)]
        far = []
        for i, rows in enumerate(chunks):
            part = call(
                functools.partial(far_kernel, tp, rows),
                shape((rows.stop - rows.start, out_width), BF16),
                [VMEM] * 5,
                f"project_far_{i}",
            )(far_begun, *parts[i], *weights)
            far.append(lax.ppermute(part, "tp", far_pairs))
        near = call(
            functools.partial(near_kernel, tp, chunks),
            shape((tokens, out_width), F32),
            [VMEM] * (3 + 4 * len(chunks)),
            "project_near",
        )(residual, *weights, *(a for i in range(len(chunks)) for a in begun[i] + parts[i]))
        return call(
            functools.partial(add_kernel, chunks),
            pltpu.HBM((tokens, out_width), BF16),
            [VMEM] * (1 + len(chunks)),
            "add",
            out_specs=HBM,
            scratch=[
                pltpu.VMEM((tokens, out_width), BF16),
                pltpu.SemaphoreType.DMA((len(chunks),)),
            ],
        )(near, *far)

    def first_group():
        return finish(mine, lambda begun: inside)

    def later_group():
        swapped = swap(earlier, 1)
        start = functools.partial(start_kernel, half)
        my_start = call(functools.partial(start, True), state, [VMEM] * 3, "start_mine")
        other_start = call(functools.partial(start, False), state, [VMEM] * 4, "start_other")
        return finish(
            my_start(before, through, earlier),
            lambda begun: other_start(inside, through, swapped, begun),
        )

    return lax.cond(lax.axis_index("seq") < MEMBERS, first_group, later_group)


def solution(mesh):
    return jax.shard_map(
        on_device,
        mesh=mesh,
        in_specs=(
            P("seq", "tp"),
            P("seq", "tp"),
            P("seq", "tp"),
            P("seq", "tp"),
            P("tp", "seq"),
            P("tp"),
            P("tp", None),
        ),
        out_specs=P("seq", "tp"),
        check_vma=False,
    )
```

```python
import functools

import jax
import jax.numpy as jnp
from jax import lax
from jax.experimental import pallas as pl
from jax.experimental.pallas import tpu as pltpu
from jax.sharding import PartitionSpec as P

HEAD_DIM = 128
GROUP = 256
SCALE = HEAD_DIM ** (-0.5)
F32 = jnp.float32
BF16 = jnp.bfloat16
VMEM = pl.BlockSpec(memory_space=pltpu.VMEM)
HBM = pl.BlockSpec(memory_space=pltpu.HBM)
DECAY_ROWS = 16
MEMBERS = 4
PARAMS = pltpu.CompilerParams(vmem_limit_bytes=24 * 1024 * 1024)


def state_rows(j):
    return slice(j * HEAD_DIM, (j + 1) * HEAD_DIM)


def place():
    return lax.rem(lax.axis_index("seq"), MEMBERS)


def side():
    return lax.rem(lax.axis_index("seq"), 2)


def half_at(owner, size):
    return pl.ds(pl.multiple_of(owner * size, size), size)


def pick(owner, values, axis):
    half = values.shape[axis] // 2
    low = lax.slice_in_dim(values, 0, half, axis=axis)
    high = lax.slice_in_dim(values, half, 2 * half, axis=axis)
    return jnp.where(owner == 0, low, high)


def contract(a, b):
    return lax.dot_general(a, b, (((1,), (1,)), ((), ())), preferred_element_type=F32)


def positions():
    shape = (GROUP, GROUP)
    return lax.broadcasted_iota(jnp.int32, shape, 0), lax.broadcasted_iota(jnp.int32, shape, 1)


def three_terms(values):
    first = values.astype(BF16).astype(F32)
    second = (values - first).astype(BF16).astype(F32)
    third = values - first - second
    return jnp.concatenate([first, second, third], axis=0).astype(BF16)


def sums_down(mask, decays):
    heads = decays.shape[0]
    terms = contract(mask, three_terms(decays))
    return terms[:, :heads] + terms[:, heads : 2 * heads] + terms[:, 2 * heads :]


def sums_across(mask, decays):
    heads = decays.shape[0]
    terms = contract(three_terms(decays), mask)
    return terms[:heads] + terms[heads : 2 * heads] + terms[2 * heads :]


def decays_to_rows(decays):
    each = DECAY_ROWS // (2 * len(decays))
    wide = jnp.concatenate([jnp.broadcast_to(d, (each, HEAD_DIM)) for d in decays], axis=0)
    coarse = wide.astype(BF16).astype(F32)
    return jnp.concatenate([coarse, wide - coarse], axis=0).astype(BF16)


def rows_to_decays(rows, count):
    rows = rows.astype(F32)
    each = DECAY_ROWS // (2 * count)
    both = rows[: DECAY_ROWS // 2] + rows[DECAY_ROWS // 2 :]
    return [both[j * each : j * each + 1] for j in range(count)]


def state_kernel(half, *refs):
    sources, outs, held, sems = refs[:5], refs[5:7], refs[7:12], refs[12]
    copies = [
        pltpu.make_async_copy(source, target, sems.at[i])
        for i, (source, target) in enumerate(zip(sources, held))
    ]
    for copy in copies:
        copy.start()
    decay_ref, key_ref, value_ref = held[:3]
    me = side()
    row, col = positions()
    later = jnp.where(col > row, 1.0, 0.0).astype(BF16)
    copies[0].wait()
    decays = decay_ref[...]
    tail = jnp.exp(sums_across(later, decays))
    whole = jnp.exp(jnp.sum(decays, axis=1, keepdims=True))
    copies[1].wait()
    copies[2].wait()
    decay_rows = decays_to_rows([whole[h : h + 1] for h in range(2 * half)])
    for owner, out_ref in zip((1 - me, me), outs):
        factors = pick(owner, tail, 0)
        for j in range(half):
            at = half_at(owner * half + j, HEAD_DIM)
            weighted = (key_ref[:, at].T.astype(F32) * factors[j : j + 1, :]).astype(BF16)
            update = jnp.dot(weighted, value_ref[:, at], preferred_element_type=F32)
            out_ref[state_rows(j), :] = update.astype(BF16)
        out_ref[half * HEAD_DIM :, :] = decay_rows
    for copy in copies[3:]:
        copy.wait()


def local_kernel(
    heads, decay_ref, query_ref, key_ref, value_ref, weight_hbm, other_weight_hbm,
    intra_ref, own_ref, weight_ref, other_weight_ref, sems,
):
    copies = [
        pltpu.make_async_copy(weight_hbm, weight_ref, sems.at[0]),
        pltpu.make_async_copy(other_weight_hbm, other_weight_ref, sems.at[1]),
    ]
    for copy in copies:
        copy.start()
    row, col = positions()
    causal = col <= row
    upto = jnp.where(causal, 1.0, 0.0).astype(BF16)
    decays = decay_ref[...]
    down = sums_down(upto, decays)
    across = sums_across(upto, decays)
    own_ref[...] = jnp.exp(down) * SCALE
    for h in range(heads):
        at = slice(h * HEAD_DIM, (h + 1) * HEAD_DIM)
        scores = contract(query_ref[:, at], key_ref[:, at])
        gaps = down[:, h : h + 1] - across[h : h + 1, :]
        weights = jnp.where(causal, jnp.exp(gaps), 0.0)
        probs = (scores * SCALE * weights).astype(BF16)
        intra_ref[:, at] = jnp.dot(probs, value_ref[:, at], preferred_element_type=F32)
    for copy in copies:
        copy.wait()


def gather_kernel(half, steps, *refs):
    received, (before_ref, mine_ref, sent_ref, through_ref, total_ref, held_ref) = (
        refs[: len(steps)],
        refs[len(steps) :],
    )
    me, upper = place(), side() == 1
    for step, message_ref in zip(steps, received):
        held_ref[me ^ step] = message_ref[...]
    later_pair = me >= 2
    decays = [rows_to_decays(held_ref[m, half * HEAD_DIM :, :], 2 * half) for m in range(MEMBERS)]
    totals = []
    for j in range(2 * half):
        low, high = (j, half + j) if j < half else (j, j - half)
        decay = [jnp.where(upper, d[high], d[low]) for d in decays]
        through = [jnp.ones((1, HEAD_DIM), F32)]
        for m in range(MEMBERS):
            through.append(through[m] * decay[m])
        first, last = [jnp.where(later_pair, through[2 + i], through[i]) for i in range(2)]
        factor = jnp.where(upper, last, first)
        through_ref[j * 8 : (j + 1) * 8, :] = jnp.broadcast_to(factor, (8, HEAD_DIM))
        if j >= half:
            continue
        at = state_rows(j)
        held = [jnp.zeros((HEAD_DIM, HEAD_DIM), F32)]
        for m in range(MEMBERS):
            held.append(held[m] * decay[m] + held_ref[m, at, :].astype(F32))
        first, last = [jnp.where(later_pair, held[2 + i], held[i]) for i in range(2)]
        before = jnp.where(upper, last, first)
        before_ref[at, :] = before
        mine_ref[at, :] = before.astype(BF16)
        sent_ref[at, :] = jnp.where(upper, first, last).astype(BF16)
        total_ref[at, :] = held[MEMBERS].astype(BF16)
        totals.append(through[MEMBERS])
    total_ref[half * HEAD_DIM :, :] = decays_to_rows(totals)


def start_kernel(half, mine, before_ref, through_ref, earlier_ref, *refs):
    for j in range(half):
        at, row = state_rows(j), 8 * (j if mine else half + j)
        earlier = through_ref[row : row + 1, :] * earlier_ref[at, :].astype(F32)
        refs[-1][at, :] = (before_ref[at, :].astype(F32) + earlier).astype(BF16)


def norm_kernel(half, mine, rows, query_ref, intra_ref, own_ref, gain_ref, state_ref, out_ref):
    owner = side() if mine else 1 - side()
    own = pick(owner, own_ref[rows, :], 1)
    for j in range(half):
        at = half_at(owner * half + j, HEAD_DIM)
        inter = jnp.dot(query_ref[rows, at], state_ref[state_rows(j), :], preferred_element_type=F32)
        attended = intra_ref[rows, at] + own[:, j : j + 1] * inter
        mean_square = jnp.mean(attended * attended, axis=-1, keepdims=True)
        normed = attended * lax.rsqrt(mean_square + 1e-06)
        out_ref[:, j * HEAD_DIM : (j + 1) * HEAD_DIM] = (normed * gain_ref[:, at]).astype(BF16)


def share(mine, step, tp, pair, weight_ref, other_weight_ref):
    rows, width = weight_ref.shape[0] // 2, weight_ref.shape[1] // tp
    at = (
        half_at(side() if mine else 1 - side(), rows),
        half_at(lax.axis_index("tp") ^ step, width),
    )
    return jnp.dot(pair[0][...], weight_ref[at], preferred_element_type=F32) + jnp.dot(
        pair[1][...], other_weight_ref[at], preferred_element_type=F32
    )


def far_mine_kernel(tp, chunks, weight_ref, other_weight_ref, *refs):
    for i, rows in enumerate(chunks):
        pair = refs[2 * i : 2 * i + 2]
        refs[-1][rows, :] = share(True, 2, tp, pair, weight_ref, other_weight_ref)


def far_kernel(tp, rows, begun_ref, mine_ref, other_ref, weight_ref, other_weight_ref, out_ref):
    rest = share(False, 2, tp, (mine_ref, other_ref), weight_ref, other_weight_ref)
    out_ref[...] = (begun_ref[rows, :] + rest).astype(BF16)


def near_kernel(tp, chunks, residual_ref, weight_ref, other_weight_ref, *refs):
    weights, out_ref = (weight_ref, other_weight_ref), refs[-1]
    for i, rows in enumerate(chunks):
        mine, rest = refs[4 * i : 4 * i + 2], refs[4 * i + 2 : 4 * i + 4]
        near = share(True, 0, tp, mine, *weights) + share(False, 0, tp, rest, *weights)
        out_ref[rows, :] = residual_ref[rows, :].astype(F32) + near


def add_kernel(chunks, near_ref, *refs):
    far, (out_hbm, out_ref, sems) = refs[: len(chunks)], refs[len(chunks) :]
    copies = []
    for i, rows in enumerate(chunks):
        out_ref[rows, :] = (near_ref[rows, :] + far[i][...].astype(F32)).astype(BF16)
        copies.append(
            pltpu.make_async_copy(out_ref.at[rows, :], out_hbm.at[rows, :], sems.at[i])
        )
        copies[-1].start()
    for copy in copies:
        copy.wait()


def call(kernel, out_shape, in_specs, name, out_specs=None, scratch=(), cost=0):
    single = isinstance(out_shape, jax.ShapeDtypeStruct)
    if out_specs is None:
        out_specs = VMEM if single else (VMEM,) * len(out_shape)
    cost = pl.CostEstimate(
        flops=cost, bytes_accessed=2_000_000 if cost else 0, transcendentals=0
    )
    return pl.pallas_call(
        kernel,
        out_shape=out_shape,
        in_specs=in_specs,
        out_specs=out_specs,
        scratch_shapes=scratch,
        compiler_params=PARAMS,
        cost_estimate=cost,
        name=name,
    )


def earlier_groups(total, half, devices):
    groups = devices // MEMBERS
    if groups == 2:
        return lax.ppermute(total, "seq", [(i, i ^ MEMBERS) for i in range(devices)])

    def shift(message, by):
        moves = [(i, i + by * MEMBERS) for i in range(devices - by * MEMBERS)]
        return lax.ppermute(message, "seq", moves)

    rows = half * HEAD_DIM
    held = shift(total, 1)
    by = 1
    while by < groups - 1:
        before = shift(held, by)
        decays = rows_to_decays(held[rows:], half)
        factor = jnp.concatenate([jnp.broadcast_to(d, (HEAD_DIM, HEAD_DIM)) for d in decays])
        state = held[:rows].astype(F32) + factor * before[:rows].astype(F32)
        through = [a * b for a, b in zip(decays, rows_to_decays(before[rows:], half))]
        held = jnp.concatenate([state.astype(BF16), decays_to_rows(through)], axis=0)
        by *= 2
    return held


def on_device(
    residual, query_vectors, key_vectors, value_vectors, log_decay, norm_gain, out_weight
):
    tokens, width = residual.shape
    heads = log_decay.shape[0]
    half = heads // 2
    devices = lax.axis_size("seq")
    tp = lax.axis_size("tp")
    wide = (tokens, heads * HEAD_DIM)
    states = (half * HEAD_DIM, HEAD_DIM)
    near_pairs = [(i, i ^ 1) for i in range(tp)]
    far_pairs = [(i, i ^ 2) for i in range(tp)]
    shape = jax.ShapeDtypeStruct
    message = shape((half * HEAD_DIM + DECAY_ROWS, HEAD_DIM), BF16)

    def swap(piece, step):
        return lax.ppermute(piece, "seq", [(i, i ^ step) for i in range(devices)])

    other_weight = lax.ppermute(out_weight, "tp", near_pairs)
    arguments = (log_decay, key_vectors, value_vectors, query_vectors, norm_gain.reshape(1, -1))
    theirs, mine, decays, keys, values, queries, gain = call(
        functools.partial(state_kernel, half),
        (message, message) + tuple(shape(a.shape, a.dtype) for a in arguments),
        [HBM] * 5,
        "states",
        scratch=[pltpu.SemaphoreType.DMA((5,))],
    )(*(pltpu.with_memory_space_constraint(a, pltpu.HBM) for a in arguments))
    steps = (3, 1, 2, 0)
    received = [swap(theirs, 3), swap(theirs, 1), swap(mine, 2), mine]
    state = shape(states, BF16)
    before, mine, sent, through, total = call(
        functools.partial(gather_kernel, half, steps),
        (shape(states, F32), state, state, shape((heads * 8, HEAD_DIM), F32), message),
        [VMEM] * len(steps),
        "gather_states",
        scratch=[pltpu.VMEM((MEMBERS,) + message.shape, BF16)],
    )(*received)
    earlier = earlier_groups(total, half, devices)
    inside = swap(sent, 1)
    intra, own, *weights = call(
        functools.partial(local_kernel, heads),
        (shape(wide, F32), shape((tokens, heads), F32))
        + (pltpu.VMEM(out_weight.shape, BF16),) * 2,
        [VMEM] * 4 + [HBM, pl.BlockSpec(memory_space=pl.ANY)],
        "local",
        scratch=[pltpu.SemaphoreType.DMA((2,))],
        cost=4 * tokens * tokens * heads * HEAD_DIM,
    )(
        decays, queries, keys, values,
        pltpu.with_memory_space_constraint(out_weight, pltpu.HBM), other_weight,
    )

    def normed(name, rows, mine, state):
        part = call(
            functools.partial(norm_kernel, half, mine, rows),
            shape((rows.stop - rows.start, half * HEAD_DIM), BF16),
            [VMEM] * 5,
            name,
        )(queries, intra, own, gain, state)
        return part, lax.ppermute(part, "tp", near_pairs)

    out_width = out_weight.shape[1] // tp
    chunks = [slice(0, tokens // 2), slice(tokens // 2, tokens)]

    def finish(state, other_state_behind):
        begun = [normed(f"norm_mine_{i}", rows, True, state) for i, rows in enumerate(chunks)]
        far_begun = call(
            functools.partial(far_mine_kernel, tp, chunks),
            shape((tokens, out_width), F32),
            [VMEM] * (2 + 2 * len(chunks)),
            "project_far_mine",
        )(*weights, *(a for pair in begun for a in pair))
        other_state = other_state_behind(far_begun)
        parts = [normed(f"norm_{i}", rows, False, other_state) for i, rows in enumerate(chunks)]
        far = []
        for i, rows in enumerate(chunks):
            part = call(
                functools.partial(far_kernel, tp, rows),
                shape((rows.stop - rows.start, out_width), BF16),
                [VMEM] * 5,
                f"project_far_{i}",
            )(far_begun, *parts[i], *weights)
            far.append(lax.ppermute(part, "tp", far_pairs))
        near = call(
            functools.partial(near_kernel, tp, chunks),
            shape((tokens, out_width), F32),
            [VMEM] * (3 + 4 * len(chunks)),
            "project_near",
        )(residual, *weights, *(a for i in range(len(chunks)) for a in begun[i] + parts[i]))
        return call(
            functools.partial(add_kernel, chunks),
            pltpu.HBM((tokens, out_width), BF16),
            [VMEM] * (1 + len(chunks)),
            "add",
            out_specs=HBM,
            scratch=[
                pltpu.VMEM((tokens, out_width), BF16),
                pltpu.SemaphoreType.DMA((len(chunks),)),
            ],
        )(near, *far)

    def first_group():
        return finish(mine, lambda begun: inside)

    def later_group():
        swapped = swap(earlier, 1)
        start = functools.partial(start_kernel, half)
        my_start = call(functools.partial(start, True), state, [VMEM] * 3, "start_mine")
        other_start = call(functools.partial(start, False), state, [VMEM] * 4, "start_other")
        return finish(
            my_start(before, through, earlier),
            lambda begun: other_start(inside, through, swapped, begun),
        )

    return lax.cond(lax.axis_index("seq") < MEMBERS, first_group, later_group)


def solution(mesh):
    return jax.shard_map(
        on_device,
        mesh=mesh,
        in_specs=(
            P("seq", "tp"),
            P("seq", "tp"),
            P("seq", "tp"),
            P("seq", "tp"),
            P("tp", "seq"),
            P("tp"),
            P("tp", None),
        ),
        out_specs=P("seq", "tp"),
        check_vma=False,
    )
```

```python
import functools

import jax
import jax.numpy as jnp
from jax import lax
from jax.experimental import pallas as pl
from jax.experimental.pallas import tpu as pltpu
from jax.sharding import PartitionSpec as P

HEAD_DIM = 128
GROUP = 256
SCALE = HEAD_DIM ** (-0.5)
F32 = jnp.float32
BF16 = jnp.bfloat16
VMEM = pl.BlockSpec(memory_space=pltpu.VMEM)
HBM = pl.BlockSpec(memory_space=pltpu.HBM)
DECAY_ROWS = 16
MEMBERS = 4
PARAMS = pltpu.CompilerParams(vmem_limit_bytes=24 * 1024 * 1024)


def state_rows(j):
    return slice(j * HEAD_DIM, (j + 1) * HEAD_DIM)


def place():
    return lax.rem(lax.axis_index("seq"), MEMBERS)


def side():
    return lax.rem(lax.axis_index("seq"), 2)


def half_at(owner, size):
    return pl.ds(pl.multiple_of(owner * size, size), size)


def pick(owner, values, axis):
    half = values.shape[axis] // 2
    low = lax.slice_in_dim(values, 0, half, axis=axis)
    high = lax.slice_in_dim(values, half, 2 * half, axis=axis)
    return jnp.where(owner == 0, low, high)


def contract(a, b):
    return lax.dot_general(a, b, (((1,), (1,)), ((), ())), preferred_element_type=F32)


def positions():
    shape = (GROUP, GROUP)
    return lax.broadcasted_iota(jnp.int32, shape, 0), lax.broadcasted_iota(jnp.int32, shape, 1)


def three_terms(values):
    first = values.astype(BF16).astype(F32)
    second = (values - first).astype(BF16).astype(F32)
    third = values - first - second
    return jnp.concatenate([first, second, third], axis=0).astype(BF16)


def sums_down(mask, decays):
    heads = decays.shape[0]
    terms = contract(mask, three_terms(decays))
    return terms[:, :heads] + terms[:, heads : 2 * heads] + terms[:, 2 * heads :]


def sums_across(mask, decays):
    heads = decays.shape[0]
    terms = contract(three_terms(decays), mask)
    return terms[:heads] + terms[heads : 2 * heads] + terms[2 * heads :]


def decays_to_rows(decays):
    each = DECAY_ROWS // (2 * len(decays))
    wide = jnp.concatenate([jnp.broadcast_to(d, (each, HEAD_DIM)) for d in decays], axis=0)
    coarse = wide.astype(BF16).astype(F32)
    return jnp.concatenate([coarse, wide - coarse], axis=0).astype(BF16)


def rows_to_decays(rows, count):
    rows = rows.astype(F32)
    each = DECAY_ROWS // (2 * count)
    both = rows[: DECAY_ROWS // 2] + rows[DECAY_ROWS // 2 :]
    return [both[j * each : j * each + 1] for j in range(count)]


def state_kernel(half, *refs):
    sources, outs, held, sems = refs[:5], refs[5:7], refs[7:12], refs[12]
    copies = [
        pltpu.make_async_copy(source, target, sems.at[i])
        for i, (source, target) in enumerate(zip(sources, held))
    ]
    for copy in copies:
        copy.start()
    decay_ref, key_ref, value_ref = held[:3]
    me = side()
    row, col = positions()
    later = jnp.where(col > row, 1.0, 0.0).astype(BF16)
    copies[0].wait()
    decays = decay_ref[...]
    tail = jnp.exp(sums_across(later, decays))
    whole = jnp.exp(jnp.sum(decays, axis=1, keepdims=True))
    copies[1].wait()
    copies[2].wait()
    decay_rows = decays_to_rows([whole[h : h + 1] for h in range(2 * half)])
    for owner, out_ref in zip((1 - me, me), outs):
        factors = pick(owner, tail, 0)
        for j in range(half):
            at = half_at(owner * half + j, HEAD_DIM)
            weighted = (key_ref[:, at].T.astype(F32) * factors[j : j + 1, :]).astype(BF16)
            update = jnp.dot(weighted, value_ref[:, at], preferred_element_type=F32)
            out_ref[state_rows(j), :] = update.astype(BF16)
        out_ref[half * HEAD_DIM :, :] = decay_rows
    for copy in copies[3:]:
        copy.wait()


def fetch_columns(step, weights, held, sems):
    copies = []
    for i, (weight, ref) in enumerate(zip(weights, held)):
        at = half_at(lax.axis_index("tp") ^ step, ref.shape[1])
        copies.append(pltpu.make_async_copy(weight.at[:, at], ref, sems.at[i]))
        copies[-1].start()
    return copies


def local_kernel(
    heads, decay_ref, query_ref, key_ref, value_ref, weight_hbm, other_weight_hbm,
    intra_ref, own_ref, weight_ref, other_weight_ref, other_near_hbm, sems, near_sem,
):
    copies = fetch_columns(2, (weight_hbm, other_weight_hbm), (weight_ref, other_weight_ref), sems)
    copies += fetch_columns(0, (other_weight_hbm,), (other_near_hbm,), near_sem)
    row, col = positions()
    causal = col <= row
    upto = jnp.where(causal, 1.0, 0.0).astype(BF16)
    decays = decay_ref[...]
    down = sums_down(upto, decays)
    across = sums_across(upto, decays)
    own_ref[...] = jnp.exp(down) * SCALE
    for h in range(heads):
        at = slice(h * HEAD_DIM, (h + 1) * HEAD_DIM)
        scores = contract(query_ref[:, at], key_ref[:, at])
        gaps = down[:, h : h + 1] - across[h : h + 1, :]
        weights = jnp.where(causal, jnp.exp(gaps), 0.0)
        probs = (scores * SCALE * weights).astype(BF16)
        intra_ref[:, at] = jnp.dot(probs, value_ref[:, at], preferred_element_type=F32)
    for copy in copies:
        copy.wait()


def gather_kernel(half, steps, *refs):
    received, (before_ref, mine_ref, sent_ref, through_ref, total_ref, held_ref) = (
        refs[: len(steps)],
        refs[len(steps) :],
    )
    me, upper = place(), side() == 1
    for step, message_ref in zip(steps, received):
        held_ref[me ^ step] = message_ref[...]
    later_pair = me >= 2
    decays = [rows_to_decays(held_ref[m, half * HEAD_DIM :, :], 2 * half) for m in range(MEMBERS)]
    totals = []
    for j in range(2 * half):
        low, high = (j, half + j) if j < half else (j, j - half)
        decay = [jnp.where(upper, d[high], d[low]) for d in decays]
        through = [jnp.ones((1, HEAD_DIM), F32)]
        for m in range(MEMBERS):
            through.append(through[m] * decay[m])
        first, last = [jnp.where(later_pair, through[2 + i], through[i]) for i in range(2)]
        factor = jnp.where(upper, last, first)
        through_ref[j * 8 : (j + 1) * 8, :] = jnp.broadcast_to(factor, (8, HEAD_DIM))
        if j >= half:
            continue
        at = state_rows(j)
        held = [jnp.zeros((HEAD_DIM, HEAD_DIM), F32)]
        for m in range(MEMBERS):
            held.append(held[m] * decay[m] + held_ref[m, at, :].astype(F32))
        first, last = [jnp.where(later_pair, held[2 + i], held[i]) for i in range(2)]
        before = jnp.where(upper, last, first)
        before_ref[at, :] = before
        mine_ref[at, :] = before.astype(BF16)
        sent_ref[at, :] = jnp.where(upper, first, last).astype(BF16)
        total_ref[at, :] = held[MEMBERS].astype(BF16)
        totals.append(through[MEMBERS])
    total_ref[half * HEAD_DIM :, :] = decays_to_rows(totals)


def start_kernel(half, mine, before_ref, through_ref, earlier_ref, *refs):
    for j in range(half):
        at, row = state_rows(j), 8 * (j if mine else half + j)
        earlier = through_ref[row : row + 1, :] * earlier_ref[at, :].astype(F32)
        refs[-1][at, :] = (before_ref[at, :].astype(F32) + earlier).astype(BF16)


def norm_kernel(half, mine, rows, query_ref, intra_ref, own_ref, gain_ref, state_ref, out_ref):
    owner = side() if mine else 1 - side()
    own = pick(owner, own_ref[rows, :], 1)
    for j in range(half):
        at = half_at(owner * half + j, HEAD_DIM)
        inter = jnp.dot(query_ref[rows, at], state_ref[state_rows(j), :], preferred_element_type=F32)
        attended = intra_ref[rows, at] + own[:, j : j + 1] * inter
        mean_square = jnp.mean(attended * attended, axis=-1, keepdims=True)
        normed = attended * lax.rsqrt(mean_square + 1e-06)
        out_ref[:, j * HEAD_DIM : (j + 1) * HEAD_DIM] = (normed * gain_ref[:, at]).astype(BF16)


def share(mine, pair, weight_ref, other_weight_ref):
    rows = weight_ref.shape[0] // 2
    at = half_at(side() if mine else 1 - side(), rows)
    return jnp.dot(pair[0][...], weight_ref[at, :], preferred_element_type=F32) + jnp.dot(
        pair[1][...], other_weight_ref[at, :], preferred_element_type=F32
    )


def far_mine_kernel(chunks, weight_ref, other_weight_ref, *refs):
    for i, rows in enumerate(chunks):
        pair = refs[2 * i : 2 * i + 2]
        refs[-1][rows, :] = share(True, pair, weight_ref, other_weight_ref)


def far_kernel(rows, begun_ref, mine_ref, other_ref, weight_ref, other_weight_ref, out_ref):
    rest = share(False, (mine_ref, other_ref), weight_ref, other_weight_ref)
    out_ref[...] = (begun_ref[rows, :] + rest).astype(BF16)


def near_kernel(chunks, residual_ref, weight_hbm, other_weight_hbm, *refs):
    pairs, (out_ref, weight_ref, other_weight_ref, sems) = refs[:-4], refs[-4:]
    weights = (weight_ref, other_weight_ref)
    copies = fetch_columns(0, (weight_hbm,), (weight_ref,), sems)
    copies.append(pltpu.make_async_copy(other_weight_hbm, other_weight_ref, sems.at[1]))
    copies[1].start()
    for copy in copies:
        copy.wait()
    for i, rows in enumerate(chunks):
        mine, rest = pairs[4 * i : 4 * i + 2], pairs[4 * i + 2 : 4 * i + 4]
        near = share(True, mine, *weights) + share(False, rest, *weights)
        out_ref[rows, :] = residual_ref[rows, :].astype(F32) + near


def add_kernel(chunks, near_ref, *refs):
    far, (out_hbm, out_ref, sems) = refs[: len(chunks)], refs[len(chunks) :]
    copies = []
    for i, rows in enumerate(chunks):
        out_ref[rows, :] = (near_ref[rows, :] + far[i][...].astype(F32)).astype(BF16)
        copies.append(
            pltpu.make_async_copy(out_ref.at[rows, :], out_hbm.at[rows, :], sems.at[i])
        )
        copies[-1].start()
    for copy in copies:
        copy.wait()


def call(kernel, out_shape, in_specs, name, out_specs=None, scratch=(), cost=0):
    single = isinstance(out_shape, jax.ShapeDtypeStruct)
    if out_specs is None:
        out_specs = VMEM if single else (VMEM,) * len(out_shape)
    cost = pl.CostEstimate(
        flops=cost, bytes_accessed=2_000_000 if cost else 0, transcendentals=0
    )
    return pl.pallas_call(
        kernel,
        out_shape=out_shape,
        in_specs=in_specs,
        out_specs=out_specs,
        scratch_shapes=scratch,
        compiler_params=PARAMS,
        cost_estimate=cost,
        name=name,
    )


def earlier_groups(total, half, devices):
    groups = devices // MEMBERS
    if groups == 2:
        return lax.ppermute(total, "seq", [(i, i ^ MEMBERS) for i in range(devices)])

    def shift(message, by):
        moves = [(i, i + by * MEMBERS) for i in range(devices - by * MEMBERS)]
        return lax.ppermute(message, "seq", moves)

    rows = half * HEAD_DIM
    held = shift(total, 1)
    by = 1
    while by < groups - 1:
        before = shift(held, by)
        decays = rows_to_decays(held[rows:], half)
        factor = jnp.concatenate([jnp.broadcast_to(d, (HEAD_DIM, HEAD_DIM)) for d in decays])
        state = held[:rows].astype(F32) + factor * before[:rows].astype(F32)
        through = [a * b for a, b in zip(decays, rows_to_decays(before[rows:], half))]
        held = jnp.concatenate([state.astype(BF16), decays_to_rows(through)], axis=0)
        by *= 2
    return held


def on_device(
    residual, query_vectors, key_vectors, value_vectors, log_decay, norm_gain, out_weight
):
    tokens, width = residual.shape
    heads = log_decay.shape[0]
    half = heads // 2
    devices = lax.axis_size("seq")
    tp = lax.axis_size("tp")
    wide = (tokens, heads * HEAD_DIM)
    out_width = out_weight.shape[1] // tp
    states = (half * HEAD_DIM, HEAD_DIM)
    near_pairs = [(i, i ^ 1) for i in range(tp)]
    far_pairs = [(i, i ^ 2) for i in range(tp)]
    shape = jax.ShapeDtypeStruct
    message = shape((half * HEAD_DIM + DECAY_ROWS, HEAD_DIM), BF16)

    def swap(piece, step):
        return lax.ppermute(piece, "seq", [(i, i ^ step) for i in range(devices)])

    other_weight = lax.ppermute(out_weight, "tp", near_pairs)
    weight = pltpu.with_memory_space_constraint(out_weight, pltpu.HBM)
    arguments = (log_decay, key_vectors, value_vectors, query_vectors, norm_gain.reshape(1, -1))
    theirs, mine, decays, keys, values, queries, gain = call(
        functools.partial(state_kernel, half),
        (message, message) + tuple(shape(a.shape, a.dtype) for a in arguments),
        [HBM] * 5,
        "states",
        scratch=[pltpu.SemaphoreType.DMA((5,))],
    )(*(pltpu.with_memory_space_constraint(a, pltpu.HBM) for a in arguments))
    steps = (3, 1, 2, 0)
    received = [swap(theirs, 3), swap(theirs, 1), swap(mine, 2), mine]
    state = shape(states, BF16)
    before, mine, sent, through, total = call(
        functools.partial(gather_kernel, half, steps),
        (shape(states, F32), state, state, shape((heads * 8, HEAD_DIM), F32), message),
        [VMEM] * len(steps),
        "gather_states",
        scratch=[pltpu.VMEM((MEMBERS,) + message.shape, BF16)],
    )(*received)
    earlier = earlier_groups(total, half, devices)
    inside = swap(sent, 1)
    block = (out_weight.shape[0], out_width)
    intra, own, *weights, other_near = call(
        functools.partial(local_kernel, heads),
        (shape(wide, F32), shape((tokens, heads), F32))
        + (pltpu.VMEM(block, BF16),) * 2
        + (pltpu.HBM(block, BF16),),
        [VMEM] * 4 + [HBM, pl.BlockSpec(memory_space=pl.ANY)],
        "local",
        out_specs=(VMEM,) * 4 + (HBM,),
        scratch=[pltpu.SemaphoreType.DMA((2,)), pltpu.SemaphoreType.DMA((1,))],
        cost=4 * tokens * tokens * heads * HEAD_DIM,
    )(decays, queries, keys, values, weight, other_weight)

    def normed(name, rows, mine, state):
        part = call(
            functools.partial(norm_kernel, half, mine, rows),
            shape((rows.stop - rows.start, half * HEAD_DIM), BF16),
            [VMEM] * 5,
            name,
        )(queries, intra, own, gain, state)
        return part, lax.ppermute(part, "tp", near_pairs)

    chunks = [slice(0, tokens // 2), slice(tokens // 2, tokens)]

    def finish(state, other_state_behind):
        begun = [normed(f"norm_mine_{i}", rows, True, state) for i, rows in enumerate(chunks)]
        far_begun = call(
            functools.partial(far_mine_kernel, chunks),
            shape((tokens, out_width), F32),
            [VMEM] * (2 + 2 * len(chunks)),
            "project_far_mine",
        )(*weights, *(a for pair in begun for a in pair))
        other_state = other_state_behind(far_begun)
        parts = [normed(f"norm_{i}", rows, False, other_state) for i, rows in enumerate(chunks)]
        far = []
        for i, rows in enumerate(chunks):
            part = call(
                functools.partial(far_kernel, rows),
                shape((rows.stop - rows.start, out_width), BF16),
                [VMEM] * 5,
                f"project_far_{i}",
            )(far_begun, *parts[i], *weights)
            far.append(lax.ppermute(part, "tp", far_pairs))
        near = call(
            functools.partial(near_kernel, chunks),
            shape((tokens, out_width), F32),
            [VMEM, HBM, HBM] + [VMEM] * (4 * len(chunks)),
            "project_near",
            scratch=[
                pltpu.VMEM(block, BF16),
                pltpu.VMEM(block, BF16),
                pltpu.SemaphoreType.DMA((2,)),
            ],
        )(residual, weight, other_near, *(a for i in range(len(chunks)) for a in begun[i] + parts[i]))
        return call(
            functools.partial(add_kernel, chunks),
            pltpu.HBM((tokens, out_width), BF16),
            [VMEM] * (1 + len(chunks)),
            "add",
            out_specs=HBM,
            scratch=[
                pltpu.VMEM((tokens, out_width), BF16),
                pltpu.SemaphoreType.DMA((len(chunks),)),
            ],
        )(near, *far)

    def first_group():
        return finish(mine, lambda begun: inside)

    def later_group():
        swapped = swap(earlier, 1)
        start = functools.partial(start_kernel, half)
        my_start = call(functools.partial(start, True), state, [VMEM] * 3, "start_mine")
        other_start = call(functools.partial(start, False), state, [VMEM] * 4, "start_other")
        return finish(
            my_start(before, through, earlier),
            lambda begun: other_start(inside, through, swapped, begun),
        )

    return lax.cond(lax.axis_index("seq") < MEMBERS, first_group, later_group)


def solution(mesh):
    return jax.shard_map(
        on_device,
        mesh=mesh,
        in_specs=(
            P("seq", "tp"),
            P("seq", "tp"),
            P("seq", "tp"),
            P("seq", "tp"),
            P("tp", "seq"),
            P("tp"),
            P("tp", None),
        ),
        out_specs=P("seq", "tp"),
        check_vma=False,
    )
```

```python
import functools

import jax
import jax.numpy as jnp
from jax import lax
from jax.experimental import pallas as pl
from jax.experimental.pallas import tpu as pltpu
from jax.sharding import PartitionSpec as P

HEAD_DIM = 128
GROUP = 256
SCALE = HEAD_DIM ** (-0.5)
F32 = jnp.float32
BF16 = jnp.bfloat16
VMEM = pl.BlockSpec(memory_space=pltpu.VMEM)
HBM = pl.BlockSpec(memory_space=pltpu.HBM)
DECAY_ROWS = 16
MEMBERS = 4
PARAMS = pltpu.CompilerParams(vmem_limit_bytes=24 * 1024 * 1024)


def state_rows(j):
    return slice(j * HEAD_DIM, (j + 1) * HEAD_DIM)


def place():
    return lax.rem(lax.axis_index("seq"), MEMBERS)


def side():
    return lax.rem(lax.axis_index("seq"), 2)


def half_at(owner, size):
    return pl.ds(pl.multiple_of(owner * size, size), size)


def pick(owner, values, axis):
    half = values.shape[axis] // 2
    low = lax.slice_in_dim(values, 0, half, axis=axis)
    high = lax.slice_in_dim(values, half, 2 * half, axis=axis)
    return jnp.where(owner == 0, low, high)


def contract(a, b):
    return lax.dot_general(a, b, (((1,), (1,)), ((), ())), preferred_element_type=F32)


def positions():
    shape = (GROUP, GROUP)
    return lax.broadcasted_iota(jnp.int32, shape, 0), lax.broadcasted_iota(jnp.int32, shape, 1)


def three_terms(values):
    first = values.astype(BF16).astype(F32)
    second = (values - first).astype(BF16).astype(F32)
    third = values - first - second
    return jnp.concatenate([first, second, third], axis=0).astype(BF16)


def sums_down(mask, decays):
    heads = decays.shape[0]
    terms = contract(mask, three_terms(decays))
    return terms[:, :heads] + terms[:, heads : 2 * heads] + terms[:, 2 * heads :]


def sums_across(mask, decays):
    heads = decays.shape[0]
    terms = contract(three_terms(decays), mask)
    return terms[:heads] + terms[heads : 2 * heads] + terms[2 * heads :]


def decays_to_rows(decays):
    each = DECAY_ROWS // (2 * len(decays))
    wide = jnp.concatenate([jnp.broadcast_to(d, (each, HEAD_DIM)) for d in decays], axis=0)
    coarse = wide.astype(BF16).astype(F32)
    return jnp.concatenate([coarse, wide - coarse], axis=0).astype(BF16)


def rows_to_decays(rows, count):
    rows = rows.astype(F32)
    each = DECAY_ROWS // (2 * count)
    both = rows[: DECAY_ROWS // 2] + rows[DECAY_ROWS // 2 :]
    return [both[j * each : j * each + 1] for j in range(count)]


def state_kernel(half, *refs):
    sources, outs, held, sems = refs[:5], refs[5:7], refs[7:12], refs[12]
    copies = [
        pltpu.make_async_copy(source, target, sems.at[i])
        for i, (source, target) in enumerate(zip(sources, held))
    ]
    for copy in copies:
        copy.start()
    decay_ref, key_ref, value_ref = held[:3]
    me = side()
    row, col = positions()
    later = jnp.where(col > row, 1.0, 0.0).astype(BF16)
    copies[0].wait()
    decays = decay_ref[...]
    tail = jnp.exp(sums_across(later, decays))
    whole = jnp.exp(jnp.sum(decays, axis=1, keepdims=True))
    copies[1].wait()
    copies[2].wait()
    decay_rows = decays_to_rows([whole[h : h + 1] for h in range(2 * half)])
    for owner, out_ref in zip((1 - me, me), outs):
        factors = pick(owner, tail, 0)
        for j in range(half):
            at = half_at(owner * half + j, HEAD_DIM)
            weighted = (key_ref[:, at].T.astype(F32) * factors[j : j + 1, :]).astype(BF16)
            update = jnp.dot(weighted, value_ref[:, at], preferred_element_type=F32)
            out_ref[state_rows(j), :] = update.astype(BF16)
        out_ref[half * HEAD_DIM :, :] = decay_rows
    for copy in copies[3:]:
        copy.wait()


def local_kernel(
    heads, decay_ref, query_ref, key_ref, value_ref, weight_hbm, other_weight_hbm,
    intra_ref, own_ref, *refs,
):
    outs, sems = refs[:4], refs[4]
    copies = []
    for i, out in enumerate(outs):
        at = half_at(lax.axis_index("tp") ^ (2 if i < 2 else 0), out.shape[1])
        weight = other_weight_hbm if i % 2 else weight_hbm
        copies.append(pltpu.make_async_copy(weight.at[:, at], out, sems.at[i]))
        copies[i].start()
    row, col = positions()
    causal = col <= row
    upto = jnp.where(causal, 1.0, 0.0).astype(BF16)
    decays = decay_ref[...]
    down = sums_down(upto, decays)
    across = sums_across(upto, decays)
    own_ref[...] = jnp.exp(down) * SCALE
    for h in range(heads):
        at = slice(h * HEAD_DIM, (h + 1) * HEAD_DIM)
        scores = contract(query_ref[:, at], key_ref[:, at])
        gaps = down[:, h : h + 1] - across[h : h + 1, :]
        weights = jnp.where(causal, jnp.exp(gaps), 0.0)
        probs = (scores * SCALE * weights).astype(BF16)
        intra_ref[:, at] = jnp.dot(probs, value_ref[:, at], preferred_element_type=F32)
    for copy in copies:
        copy.wait()


def gather_kernel(half, steps, *refs):
    received, (before_ref, mine_ref, sent_ref, through_ref, total_ref, held_ref) = (
        refs[: len(steps)],
        refs[len(steps) :],
    )
    me, upper = place(), side() == 1
    for step, message_ref in zip(steps, received):
        held_ref[me ^ step] = message_ref[...]
    later_pair = me >= 2
    decays = [rows_to_decays(held_ref[m, half * HEAD_DIM :, :], 2 * half) for m in range(MEMBERS)]
    totals = []
    for j in range(2 * half):
        low, high = (j, half + j) if j < half else (j, j - half)
        decay = [jnp.where(upper, d[high], d[low]) for d in decays]
        through = [jnp.ones((1, HEAD_DIM), F32)]
        for m in range(MEMBERS):
            through.append(through[m] * decay[m])
        first, last = [jnp.where(later_pair, through[2 + i], through[i]) for i in range(2)]
        factor = jnp.where(upper, last, first)
        through_ref[j * 8 : (j + 1) * 8, :] = jnp.broadcast_to(factor, (8, HEAD_DIM))
        if j >= half:
            continue
        at = state_rows(j)
        held = [jnp.zeros((HEAD_DIM, HEAD_DIM), F32)]
        for m in range(MEMBERS):
            held.append(held[m] * decay[m] + held_ref[m, at, :].astype(F32))
        first, last = [jnp.where(later_pair, held[2 + i], held[i]) for i in range(2)]
        before = jnp.where(upper, last, first)
        before_ref[at, :] = before
        mine_ref[at, :] = before.astype(BF16)
        sent_ref[at, :] = jnp.where(upper, first, last).astype(BF16)
        total_ref[at, :] = held[MEMBERS].astype(BF16)
        totals.append(through[MEMBERS])
    total_ref[half * HEAD_DIM :, :] = decays_to_rows(totals)


def start_kernel(half, mine, before_ref, through_ref, earlier_ref, *refs):
    for j in range(half):
        at, row = state_rows(j), 8 * (j if mine else half + j)
        earlier = through_ref[row : row + 1, :] * earlier_ref[at, :].astype(F32)
        refs[-1][at, :] = (before_ref[at, :].astype(F32) + earlier).astype(BF16)


def norm_kernel(half, mine, rows, query_ref, intra_ref, own_ref, gain_ref, state_ref, out_ref):
    owner = side() if mine else 1 - side()
    own = pick(owner, own_ref[rows, :], 1)
    for j in range(half):
        at = half_at(owner * half + j, HEAD_DIM)
        inter = jnp.dot(query_ref[rows, at], state_ref[state_rows(j), :], preferred_element_type=F32)
        attended = intra_ref[rows, at] + own[:, j : j + 1] * inter
        mean_square = jnp.mean(attended * attended, axis=-1, keepdims=True)
        normed = attended * lax.rsqrt(mean_square + 1e-06)
        out_ref[:, j * HEAD_DIM : (j + 1) * HEAD_DIM] = (normed * gain_ref[:, at]).astype(BF16)


def share(mine, pair, weight_ref, other_weight_ref):
    rows = weight_ref.shape[0] // 2
    at = half_at(side() if mine else 1 - side(), rows)
    return jnp.dot(pair[0][...], weight_ref[at, :], preferred_element_type=F32) + jnp.dot(
        pair[1][...], other_weight_ref[at, :], preferred_element_type=F32
    )


def far_mine_kernel(chunks, weight_ref, other_weight_ref, *refs):
    for i, rows in enumerate(chunks):
        pair = refs[2 * i : 2 * i + 2]
        refs[-1][rows, :] = share(True, pair, weight_ref, other_weight_ref)


def far_kernel(rows, begun_ref, mine_ref, other_ref, weight_ref, other_weight_ref, out_ref):
    rest = share(False, (mine_ref, other_ref), weight_ref, other_weight_ref)
    out_ref[...] = (begun_ref[rows, :] + rest).astype(BF16)


def near_kernel(chunks, residual_ref, weight_ref, other_weight_ref, *refs):
    weights, out_ref = (weight_ref, other_weight_ref), refs[-1]
    for i, rows in enumerate(chunks):
        mine, rest = refs[4 * i : 4 * i + 2], refs[4 * i + 2 : 4 * i + 4]
        near = share(True, mine, *weights) + share(False, rest, *weights)
        out_ref[rows, :] = residual_ref[rows, :].astype(F32) + near


def add_kernel(chunks, near_ref, *refs):
    far, (out_hbm, out_ref, sems) = refs[: len(chunks)], refs[len(chunks) :]
    copies = []
    for i, rows in enumerate(chunks):
        out_ref[rows, :] = (near_ref[rows, :] + far[i][...].astype(F32)).astype(BF16)
        copies.append(
            pltpu.make_async_copy(out_ref.at[rows, :], out_hbm.at[rows, :], sems.at[i])
        )
        copies[-1].start()
    for copy in copies:
        copy.wait()


def call(kernel, out_shape, in_specs, name, out_specs=None, scratch=(), cost=0):
    single = isinstance(out_shape, jax.ShapeDtypeStruct)
    if out_specs is None:
        out_specs = VMEM if single else (VMEM,) * len(out_shape)
    cost = pl.CostEstimate(
        flops=cost, bytes_accessed=2_000_000 if cost else 0, transcendentals=0
    )
    return pl.pallas_call(
        kernel,
        out_shape=out_shape,
        in_specs=in_specs,
        out_specs=out_specs,
        scratch_shapes=scratch,
        compiler_params=PARAMS,
        cost_estimate=cost,
        name=name,
    )


def earlier_groups(total, half, devices):
    groups = devices // MEMBERS
    if groups == 2:
        return lax.ppermute(total, "seq", [(i, i ^ MEMBERS) for i in range(devices)])

    def shift(message, by):
        moves = [(i, i + by * MEMBERS) for i in range(devices - by * MEMBERS)]
        return lax.ppermute(message, "seq", moves)

    rows = half * HEAD_DIM
    held = shift(total, 1)
    by = 1
    while by < groups - 1:
        before = shift(held, by)
        decays = rows_to_decays(held[rows:], half)
        factor = jnp.concatenate([jnp.broadcast_to(d, (HEAD_DIM, HEAD_DIM)) for d in decays])
        state = held[:rows].astype(F32) + factor * before[:rows].astype(F32)
        through = [a * b for a, b in zip(decays, rows_to_decays(before[rows:], half))]
        held = jnp.concatenate([state.astype(BF16), decays_to_rows(through)], axis=0)
        by *= 2
    return held


def on_device(
    residual, query_vectors, key_vectors, value_vectors, log_decay, norm_gain, out_weight
):
    tokens, width = residual.shape
    heads = log_decay.shape[0]
    half = heads // 2
    devices = lax.axis_size("seq")
    tp = lax.axis_size("tp")
    wide = (tokens, heads * HEAD_DIM)
    out_width = out_weight.shape[1] // tp
    states = (half * HEAD_DIM, HEAD_DIM)
    near_pairs = [(i, i ^ 1) for i in range(tp)]
    far_pairs = [(i, i ^ 2) for i in range(tp)]
    shape = jax.ShapeDtypeStruct
    message = shape((half * HEAD_DIM + DECAY_ROWS, HEAD_DIM), BF16)

    def swap(piece, step):
        return lax.ppermute(piece, "seq", [(i, i ^ step) for i in range(devices)])

    other_weight = lax.ppermute(out_weight, "tp", near_pairs)
    weight = pltpu.with_memory_space_constraint(out_weight, pltpu.HBM)
    arguments = (log_decay, key_vectors, value_vectors, query_vectors, norm_gain.reshape(1, -1))
    theirs, mine, decays, keys, values, queries, gain = call(
        functools.partial(state_kernel, half),
        (message, message) + tuple(shape(a.shape, a.dtype) for a in arguments),
        [HBM] * 5,
        "states",
        scratch=[pltpu.SemaphoreType.DMA((5,))],
    )(*(pltpu.with_memory_space_constraint(a, pltpu.HBM) for a in arguments))
    steps = (3, 1, 2, 0)
    received = [swap(theirs, 3), swap(theirs, 1), swap(mine, 2), mine]
    state = shape(states, BF16)
    before, mine, sent, through, total = call(
        functools.partial(gather_kernel, half, steps),
        (shape(states, F32), state, state, shape((heads * 8, HEAD_DIM), F32), message),
        [VMEM] * len(steps),
        "gather_states",
        scratch=[pltpu.VMEM((MEMBERS,) + message.shape, BF16)],
    )(*received)
    earlier = earlier_groups(total, half, devices)
    inside = swap(sent, 1)
    block = pltpu.HBM((out_weight.shape[0], out_width), BF16)
    intra, own, *blocks = call(
        functools.partial(local_kernel, heads),
        (shape(wide, F32), shape((tokens, heads), F32)) + (block,) * 4,
        [VMEM] * 4 + [HBM, pl.BlockSpec(memory_space=pl.ANY)],
        "local",
        out_specs=(VMEM,) * 2 + (HBM,) * 4,
        scratch=[pltpu.SemaphoreType.DMA((4,))],
        cost=4 * tokens * tokens * heads * HEAD_DIM,
    )(decays, queries, keys, values, weight, other_weight)
    far_weights, near_weights = blocks[:2], blocks[2:]

    def normed(name, rows, mine, state):
        part = call(
            functools.partial(norm_kernel, half, mine, rows),
            shape((rows.stop - rows.start, half * HEAD_DIM), BF16),
            [VMEM] * 5,
            name,
        )(queries, intra, own, gain, state)
        return part, lax.ppermute(part, "tp", near_pairs)

    chunks = [slice(0, tokens // 2), slice(tokens // 2, tokens)]

    def finish(state, other_state_behind):
        begun = [normed(f"norm_mine_{i}", rows, True, state) for i, rows in enumerate(chunks)]
        far_begun = call(
            functools.partial(far_mine_kernel, chunks),
            shape((tokens, out_width), F32),
            [VMEM] * (2 + 2 * len(chunks)),
            "project_far_mine",
        )(*far_weights, *(a for pair in begun for a in pair))
        other_state = other_state_behind(far_begun)
        parts = [normed(f"norm_{i}", rows, False, other_state) for i, rows in enumerate(chunks)]
        far = []
        for i, rows in enumerate(chunks):
            part = call(
                functools.partial(far_kernel, rows),
                shape((rows.stop - rows.start, out_width), BF16),
                [VMEM] * 5,
                f"project_far_{i}",
            )(far_begun, *parts[i], *far_weights)
            far.append(lax.ppermute(part, "tp", far_pairs))
        near = call(
            functools.partial(near_kernel, chunks),
            shape((tokens, out_width), F32),
            [VMEM] * (3 + 4 * len(chunks)),
            "project_near",
        )(residual, *near_weights, *(a for i in range(len(chunks)) for a in begun[i] + parts[i]))
        return call(
            functools.partial(add_kernel, chunks),
            pltpu.HBM((tokens, out_width), BF16),
            [VMEM] * (1 + len(chunks)),
            "add",
            out_specs=HBM,
            scratch=[
                pltpu.VMEM((tokens, out_width), BF16),
                pltpu.SemaphoreType.DMA((len(chunks),)),
            ],
        )(near, *far)

    def first_group():
        return finish(mine, lambda begun: inside)

    def later_group():
        swapped = swap(earlier, 1)
        start = functools.partial(start_kernel, half)
        my_start = call(functools.partial(start, True), state, [VMEM] * 3, "start_mine")
        other_start = call(functools.partial(start, False), state, [VMEM] * 4, "start_other")
        return finish(
            my_start(before, through, earlier),
            lambda begun: other_start(inside, through, swapped, begun),
        )

    return lax.cond(lax.axis_index("seq") < MEMBERS, first_group, later_group)


def solution(mesh):
    return jax.shard_map(
        on_device,
        mesh=mesh,
        in_specs=(
            P("seq", "tp"),
            P("seq", "tp"),
            P("seq", "tp"),
            P("seq", "tp"),
            P("tp", "seq"),
            P("tp"),
            P("tp", None),
        ),
        out_specs=P("seq", "tp"),
        check_vma=False,
    )
```

```python
import functools

import jax
import jax.numpy as jnp
from jax import lax
from jax.experimental import pallas as pl
from jax.experimental.pallas import tpu as pltpu
from jax.sharding import PartitionSpec as P

HEAD_DIM = 128
GROUP = 256
SCALE = HEAD_DIM ** (-0.5)
F32 = jnp.float32
BF16 = jnp.bfloat16
VMEM = pl.BlockSpec(memory_space=pltpu.VMEM)
HBM = pl.BlockSpec(memory_space=pltpu.HBM)
DECAY_ROWS = 16
MEMBERS = 4
PARAMS = pltpu.CompilerParams(vmem_limit_bytes=24 * 1024 * 1024)


def state_rows(j):
    return slice(j * HEAD_DIM, (j + 1) * HEAD_DIM)


def place():
    return lax.rem(lax.axis_index("seq"), MEMBERS)


def side():
    return lax.rem(lax.axis_index("seq"), 2)


def half_at(owner, size):
    return pl.ds(pl.multiple_of(owner * size, size), size)


def pick(owner, values, axis):
    half = values.shape[axis] // 2
    low = lax.slice_in_dim(values, 0, half, axis=axis)
    high = lax.slice_in_dim(values, half, 2 * half, axis=axis)
    return jnp.where(owner == 0, low, high)


def contract(a, b):
    return lax.dot_general(a, b, (((1,), (1,)), ((), ())), preferred_element_type=F32)


def positions():
    shape = (GROUP, GROUP)
    return lax.broadcasted_iota(jnp.int32, shape, 0), lax.broadcasted_iota(jnp.int32, shape, 1)


def three_terms(values):
    first = values.astype(BF16).astype(F32)
    second = (values - first).astype(BF16).astype(F32)
    third = values - first - second
    return jnp.concatenate([first, second, third], axis=0).astype(BF16)


def sums_down(mask, decays):
    heads = decays.shape[0]
    terms = contract(mask, three_terms(decays))
    return terms[:, :heads] + terms[:, heads : 2 * heads] + terms[:, 2 * heads :]


def sums_across(mask, decays):
    heads = decays.shape[0]
    terms = contract(three_terms(decays), mask)
    return terms[:heads] + terms[heads : 2 * heads] + terms[2 * heads :]


def decays_to_rows(decays):
    each = DECAY_ROWS // (2 * len(decays))
    wide = jnp.concatenate([jnp.broadcast_to(d, (each, HEAD_DIM)) for d in decays], axis=0)
    coarse = wide.astype(BF16).astype(F32)
    return jnp.concatenate([coarse, wide - coarse], axis=0).astype(BF16)


def rows_to_decays(rows, count):
    rows = rows.astype(F32)
    each = DECAY_ROWS // (2 * count)
    both = rows[: DECAY_ROWS // 2] + rows[DECAY_ROWS // 2 :]
    return [both[j * each : j * each + 1] for j in range(count)]


def state_kernel(half, *refs):
    sources, outs, held, sems = refs[:5], refs[5:7], refs[7:12], refs[12]
    copies = [
        pltpu.make_async_copy(source, target, sems.at[i])
        for i, (source, target) in enumerate(zip(sources, held))
    ]
    for copy in copies:
        copy.start()
    decay_ref, key_ref, value_ref = held[:3]
    me = side()
    row, col = positions()
    later = jnp.where(col > row, 1.0, 0.0).astype(BF16)
    copies[0].wait()
    decays = decay_ref[...]
    tail = jnp.exp(sums_across(later, decays))
    whole = jnp.exp(jnp.sum(decays, axis=1, keepdims=True))
    copies[1].wait()
    copies[2].wait()
    decay_rows = decays_to_rows([whole[h : h + 1] for h in range(2 * half)])
    for owner, out_ref in zip((1 - me, me), outs):
        factors = pick(owner, tail, 0)
        for j in range(half):
            at = half_at(owner * half + j, HEAD_DIM)
            weighted = (key_ref[:, at].T.astype(F32) * factors[j : j + 1, :]).astype(BF16)
            update = jnp.dot(weighted, value_ref[:, at], preferred_element_type=F32)
            out_ref[state_rows(j), :] = update.astype(BF16)
        out_ref[half * HEAD_DIM :, :] = decay_rows
    for copy in copies[3:]:
        copy.wait()


def local_kernel(
    heads, decay_ref, query_ref, key_ref, value_ref, weight_hbm, other_weight_hbm,
    intra_ref, own_ref, *refs,
):
    outs, held, sems = refs[:4], refs[4:8], refs[8]
    copies = []
    for i, ref in enumerate(held):
        at = half_at(lax.axis_index("tp") ^ (2 if i < 2 else 0), ref.shape[1])
        weight = other_weight_hbm if i % 2 else weight_hbm
        copies.append(pltpu.make_async_copy(weight.at[:, at], ref, sems.at[0, i]))
        copies[i].start()
    row, col = positions()
    causal = col <= row
    upto = jnp.where(causal, 1.0, 0.0).astype(BF16)
    decays = decay_ref[...]
    down = sums_down(upto, decays)
    across = sums_across(upto, decays)
    own_ref[...] = jnp.exp(down) * SCALE
    for h in range(heads):
        if h == heads - 1:
            for i, ref in enumerate(held):
                copies[i].wait()
                copies[i] = pltpu.make_async_copy(ref, outs[i], sems.at[1, i])
                copies[i].start()
        at = slice(h * HEAD_DIM, (h + 1) * HEAD_DIM)
        scores = contract(query_ref[:, at], key_ref[:, at])
        gaps = down[:, h : h + 1] - across[h : h + 1, :]
        weights = jnp.where(causal, jnp.exp(gaps), 0.0)
        probs = (scores * SCALE * weights).astype(BF16)
        intra_ref[:, at] = jnp.dot(probs, value_ref[:, at], preferred_element_type=F32)
    for copy in copies:
        copy.wait()


def gather_kernel(half, steps, *refs):
    received, (before_ref, mine_ref, sent_ref, through_ref, total_ref, held_ref) = (
        refs[: len(steps)],
        refs[len(steps) :],
    )
    me, upper = place(), side() == 1
    for step, message_ref in zip(steps, received):
        held_ref[me ^ step] = message_ref[...]
    later_pair = me >= 2
    decays = [rows_to_decays(held_ref[m, half * HEAD_DIM :, :], 2 * half) for m in range(MEMBERS)]
    totals = []
    for j in range(2 * half):
        low, high = (j, half + j) if j < half else (j, j - half)
        decay = [jnp.where(upper, d[high], d[low]) for d in decays]
        through = [jnp.ones((1, HEAD_DIM), F32)]
        for m in range(MEMBERS):
            through.append(through[m] * decay[m])
        first, last = [jnp.where(later_pair, through[2 + i], through[i]) for i in range(2)]
        factor = jnp.where(upper, last, first)
        through_ref[j * 8 : (j + 1) * 8, :] = jnp.broadcast_to(factor, (8, HEAD_DIM))
        if j >= half:
            continue
        at = state_rows(j)
        held = [jnp.zeros((HEAD_DIM, HEAD_DIM), F32)]
        for m in range(MEMBERS):
            held.append(held[m] * decay[m] + held_ref[m, at, :].astype(F32))
        first, last = [jnp.where(later_pair, held[2 + i], held[i]) for i in range(2)]
        before = jnp.where(upper, last, first)
        before_ref[at, :] = before
        mine_ref[at, :] = before.astype(BF16)
        sent_ref[at, :] = jnp.where(upper, first, last).astype(BF16)
        total_ref[at, :] = held[MEMBERS].astype(BF16)
        totals.append(through[MEMBERS])
    total_ref[half * HEAD_DIM :, :] = decays_to_rows(totals)


def start_kernel(half, mine, before_ref, through_ref, earlier_ref, *refs):
    for j in range(half):
        at, row = state_rows(j), 8 * (j if mine else half + j)
        earlier = through_ref[row : row + 1, :] * earlier_ref[at, :].astype(F32)
        refs[-1][at, :] = (before_ref[at, :].astype(F32) + earlier).astype(BF16)


def norm_kernel(half, mine, rows, query_ref, intra_ref, own_ref, gain_ref, state_ref, out_ref):
    owner = side() if mine else 1 - side()
    own = pick(owner, own_ref[rows, :], 1)
    for j in range(half):
        at = half_at(owner * half + j, HEAD_DIM)
        inter = jnp.dot(query_ref[rows, at], state_ref[state_rows(j), :], preferred_element_type=F32)
        attended = intra_ref[rows, at] + own[:, j : j + 1] * inter
        mean_square = jnp.mean(attended * attended, axis=-1, keepdims=True)
        normed = attended * lax.rsqrt(mean_square + 1e-06)
        out_ref[:, j * HEAD_DIM : (j + 1) * HEAD_DIM] = (normed * gain_ref[:, at]).astype(BF16)


def share(mine, pair, weight_ref, other_weight_ref):
    rows = weight_ref.shape[0] // 2
    at = half_at(side() if mine else 1 - side(), rows)
    return jnp.dot(pair[0][...], weight_ref[at, :], preferred_element_type=F32) + jnp.dot(
        pair[1][...], other_weight_ref[at, :], preferred_element_type=F32
    )


def far_mine_kernel(chunks, weight_ref, other_weight_ref, *refs):
    for i, rows in enumerate(chunks):
        pair = refs[2 * i : 2 * i + 2]
        refs[-1][rows, :] = share(True, pair, weight_ref, other_weight_ref)


def far_kernel(rows, begun_ref, mine_ref, other_ref, weight_ref, other_weight_ref, out_ref):
    rest = share(False, (mine_ref, other_ref), weight_ref, other_weight_ref)
    out_ref[...] = (begun_ref[rows, :] + rest).astype(BF16)


def near_kernel(chunks, residual_hbm, weight_ref, other_weight_ref, *refs):
    weights, (out_ref, residual_ref, sem) = (weight_ref, other_weight_ref), refs[-3:]
    copy = pltpu.make_async_copy(residual_hbm, residual_ref, sem)
    copy.start()
    copy.wait()
    for i, rows in enumerate(chunks):
        mine, rest = refs[4 * i : 4 * i + 2], refs[4 * i + 2 : 4 * i + 4]
        near = share(True, mine, *weights) + share(False, rest, *weights)
        out_ref[rows, :] = residual_ref[rows, :].astype(F32) + near


def add_kernel(chunks, near_ref, *refs):
    far, (out_hbm, out_ref, sems) = refs[: len(chunks)], refs[len(chunks) :]
    copies = []
    for i, rows in enumerate(chunks):
        out_ref[rows, :] = (near_ref[rows, :] + far[i][...].astype(F32)).astype(BF16)
        copies.append(
            pltpu.make_async_copy(out_ref.at[rows, :], out_hbm.at[rows, :], sems.at[i])
        )
        copies[-1].start()
    for copy in copies:
        copy.wait()


def call(kernel, out_shape, in_specs, name, out_specs=None, scratch=(), cost=0):
    single = isinstance(out_shape, jax.ShapeDtypeStruct)
    if out_specs is None:
        out_specs = VMEM if single else (VMEM,) * len(out_shape)
    cost = pl.CostEstimate(
        flops=cost, bytes_accessed=2_000_000 if cost else 0, transcendentals=0
    )
    return pl.pallas_call(
        kernel,
        out_shape=out_shape,
        in_specs=in_specs,
        out_specs=out_specs,
        scratch_shapes=scratch,
        compiler_params=PARAMS,
        cost_estimate=cost,
        name=name,
    )


def earlier_groups(total, half, devices):
    groups = devices // MEMBERS
    if groups == 2:
        return lax.ppermute(total, "seq", [(i, i ^ MEMBERS) for i in range(devices)])

    def shift(message, by):
        moves = [(i, i + by * MEMBERS) for i in range(devices - by * MEMBERS)]
        return lax.ppermute(message, "seq", moves)

    rows = half * HEAD_DIM
    held = shift(total, 1)
    by = 1
    while by < groups - 1:
        before = shift(held, by)
        decays = rows_to_decays(held[rows:], half)
        factor = jnp.concatenate([jnp.broadcast_to(d, (HEAD_DIM, HEAD_DIM)) for d in decays])
        state = held[:rows].astype(F32) + factor * before[:rows].astype(F32)
        through = [a * b for a, b in zip(decays, rows_to_decays(before[rows:], half))]
        held = jnp.concatenate([state.astype(BF16), decays_to_rows(through)], axis=0)
        by *= 2
    return held


def on_device(
    residual, query_vectors, key_vectors, value_vectors, log_decay, norm_gain, out_weight
):
    tokens, width = residual.shape
    heads = log_decay.shape[0]
    half = heads // 2
    devices = lax.axis_size("seq")
    tp = lax.axis_size("tp")
    wide = (tokens, heads * HEAD_DIM)
    out_width = out_weight.shape[1] // tp
    states = (half * HEAD_DIM, HEAD_DIM)
    near_pairs = [(i, i ^ 1) for i in range(tp)]
    far_pairs = [(i, i ^ 2) for i in range(tp)]
    shape = jax.ShapeDtypeStruct
    message = shape((half * HEAD_DIM + DECAY_ROWS, HEAD_DIM), BF16)

    def swap(piece, step):
        return lax.ppermute(piece, "seq", [(i, i ^ step) for i in range(devices)])

    other_weight = lax.ppermute(out_weight, "tp", near_pairs)
    weight = pltpu.with_memory_space_constraint(out_weight, pltpu.HBM)
    arguments = (log_decay, key_vectors, value_vectors, query_vectors, norm_gain.reshape(1, -1))
    theirs, mine, decays, keys, values, queries, gain = call(
        functools.partial(state_kernel, half),
        (message, message) + tuple(shape(a.shape, a.dtype) for a in arguments),
        [HBM] * 5,
        "states",
        scratch=[pltpu.SemaphoreType.DMA((5,))],
    )(*(pltpu.with_memory_space_constraint(a, pltpu.HBM) for a in arguments))
    steps = (3, 1, 2, 0)
    received = [swap(theirs, 3), swap(theirs, 1), swap(mine, 2), mine]
    state = shape(states, BF16)
    before, mine, sent, through, total = call(
        functools.partial(gather_kernel, half, steps),
        (shape(states, F32), state, state, shape((heads * 8, HEAD_DIM), F32), message),
        [VMEM] * len(steps),
        "gather_states",
        scratch=[pltpu.VMEM((MEMBERS,) + message.shape, BF16)],
    )(*received)
    earlier = earlier_groups(total, half, devices)
    inside = swap(sent, 1)
    block = pltpu.HBM((out_weight.shape[0], out_width), BF16)
    intra, own, *blocks = call(
        functools.partial(local_kernel, heads),
        (shape(wide, F32), shape((tokens, heads), F32)) + (block,) * 4,
        [VMEM] * 4 + [HBM, pl.BlockSpec(memory_space=pl.ANY)],
        "local",
        out_specs=(VMEM,) * 2 + (HBM,) * 4,
        scratch=[pltpu.VMEM(block.shape, BF16)] * 4 + [pltpu.SemaphoreType.DMA((2, 4))],
        cost=4 * tokens * tokens * heads * HEAD_DIM,
    )(decays, queries, keys, values, weight, other_weight)
    far_weights, near_weights = blocks[:2], blocks[2:]

    def normed(name, rows, mine, state):
        part = call(
            functools.partial(norm_kernel, half, mine, rows),
            shape((rows.stop - rows.start, half * HEAD_DIM), BF16),
            [VMEM] * 5,
            name,
        )(queries, intra, own, gain, state)
        return part, lax.ppermute(part, "tp", near_pairs)

    chunks = [slice(0, tokens // 2), slice(tokens // 2, tokens)]

    def finish(state, other_state_behind):
        begun = [normed(f"norm_mine_{i}", rows, True, state) for i, rows in enumerate(chunks)]
        far_begun = call(
            functools.partial(far_mine_kernel, chunks),
            shape((tokens, out_width), F32),
            [VMEM] * (2 + 2 * len(chunks)),
            "project_far_mine",
        )(*far_weights, *(a for pair in begun for a in pair))
        other_state = other_state_behind(far_begun)
        parts = [normed(f"norm_{i}", rows, False, other_state) for i, rows in enumerate(chunks)]
        far = []
        for i, rows in enumerate(chunks):
            part = call(
                functools.partial(far_kernel, rows),
                shape((rows.stop - rows.start, out_width), BF16),
                [VMEM] * 5,
                f"project_far_{i}",
            )(far_begun, *parts[i], *far_weights)
            far.append(lax.ppermute(part, "tp", far_pairs))
        near = call(
            functools.partial(near_kernel, chunks),
            shape((tokens, out_width), F32),
            [HBM] + [VMEM] * (2 + 4 * len(chunks)),
            "project_near",
            scratch=[pltpu.VMEM(residual.shape, BF16), pltpu.SemaphoreType.DMA],
        )(pltpu.with_memory_space_constraint(residual, pltpu.HBM), *near_weights, *(a for i in range(len(chunks)) for a in begun[i] + parts[i]))
        return call(
            functools.partial(add_kernel, chunks),
            pltpu.HBM((tokens, out_width), BF16),
            [VMEM] * (1 + len(chunks)),
            "add",
            out_specs=HBM,
            scratch=[
                pltpu.VMEM((tokens, out_width), BF16),
                pltpu.SemaphoreType.DMA((len(chunks),)),
            ],
        )(near, *far)

    def first_group():
        return finish(mine, lambda begun: inside)

    def later_group():
        swapped = swap(earlier, 1)
        start = functools.partial(start_kernel, half)
        my_start = call(functools.partial(start, True), state, [VMEM] * 3, "start_mine")
        other_start = call(functools.partial(start, False), state, [VMEM] * 4, "start_other")
        return finish(
            my_start(before, through, earlier),
            lambda begun: other_start(inside, through, swapped, begun),
        )

    return lax.cond(lax.axis_index("seq") < MEMBERS, first_group, later_group)


def solution(mesh):
    return jax.shard_map(
        on_device,
        mesh=mesh,
        in_specs=(
            P("seq", "tp"),
            P("seq", "tp"),
            P("seq", "tp"),
            P("seq", "tp"),
            P("tp", "seq"),
            P("tp"),
            P("tp", None),
        ),
        out_specs=P("seq", "tp"),
        check_vma=False,
    )
```

```python
import functools

import jax
import jax.numpy as jnp
from jax import lax
from jax.experimental import pallas as pl
from jax.experimental.pallas import tpu as pltpu
from jax.sharding import PartitionSpec as P

HEAD_DIM = 128
GROUP = 256
SCALE = HEAD_DIM ** (-0.5)
F32 = jnp.float32
BF16 = jnp.bfloat16
VMEM = pl.BlockSpec(memory_space=pltpu.VMEM)
HBM = pl.BlockSpec(memory_space=pltpu.HBM)
DECAY_ROWS = 16
MEMBERS = 4
PARAMS = pltpu.CompilerParams(vmem_limit_bytes=24 * 1024 * 1024)


def state_rows(j):
    return slice(j * HEAD_DIM, (j + 1) * HEAD_DIM)


def place():
    return lax.rem(lax.axis_index("seq"), MEMBERS)


def side():
    return lax.rem(lax.axis_index("seq"), 2)


def half_at(owner, size):
    return pl.ds(pl.multiple_of(owner * size, size), size)


def pick(owner, values, axis):
    half = values.shape[axis] // 2
    low = lax.slice_in_dim(values, 0, half, axis=axis)
    high = lax.slice_in_dim(values, half, 2 * half, axis=axis)
    return jnp.where(owner == 0, low, high)


def contract(a, b):
    return lax.dot_general(a, b, (((1,), (1,)), ((), ())), preferred_element_type=F32)


def positions():
    shape = (GROUP, GROUP)
    return lax.broadcasted_iota(jnp.int32, shape, 0), lax.broadcasted_iota(jnp.int32, shape, 1)


def three_terms(values):
    first = values.astype(BF16).astype(F32)
    second = (values - first).astype(BF16).astype(F32)
    third = values - first - second
    return jnp.concatenate([first, second, third], axis=0).astype(BF16)


def sums_down(mask, decays):
    heads = decays.shape[0]
    terms = contract(mask, three_terms(decays))
    return terms[:, :heads] + terms[:, heads : 2 * heads] + terms[:, 2 * heads :]


def sums_across(mask, decays):
    heads = decays.shape[0]
    terms = contract(three_terms(decays), mask)
    return terms[:heads] + terms[heads : 2 * heads] + terms[2 * heads :]


def decays_to_rows(decays):
    each = DECAY_ROWS // (2 * len(decays))
    wide = jnp.concatenate([jnp.broadcast_to(d, (each, HEAD_DIM)) for d in decays], axis=0)
    coarse = wide.astype(BF16).astype(F32)
    return jnp.concatenate([coarse, wide - coarse], axis=0).astype(BF16)


def rows_to_decays(rows, count):
    rows = rows.astype(F32)
    each = DECAY_ROWS // (2 * count)
    both = rows[: DECAY_ROWS // 2] + rows[DECAY_ROWS // 2 :]
    return [both[j * each : j * each + 1] for j in range(count)]


def state_kernel(half, *refs):
    sources, outs, held, sems = refs[:5], refs[5:7], refs[7:12], refs[12]
    copies = [
        pltpu.make_async_copy(source, target, sems.at[i])
        for i, (source, target) in enumerate(zip(sources, held))
    ]
    for copy in copies:
        copy.start()
    decay_ref, key_ref, value_ref = held[:3]
    me = side()
    row, col = positions()
    later = jnp.where(col > row, 1.0, 0.0).astype(BF16)
    copies[0].wait()
    decays = decay_ref[...]
    tail = jnp.exp(sums_across(later, decays))
    whole = jnp.exp(jnp.sum(decays, axis=1, keepdims=True))
    copies[1].wait()
    copies[2].wait()
    decay_rows = decays_to_rows([whole[h : h + 1] for h in range(2 * half)])
    for owner, out_ref in zip((1 - me, me), outs):
        factors = pick(owner, tail, 0)
        for j in range(half):
            at = half_at(owner * half + j, HEAD_DIM)
            weighted = (key_ref[:, at].T.astype(F32) * factors[j : j + 1, :]).astype(BF16)
            update = jnp.dot(weighted, value_ref[:, at], preferred_element_type=F32)
            out_ref[state_rows(j), :] = update.astype(BF16)
        out_ref[half * HEAD_DIM :, :] = decay_rows
    for copy in copies[3:]:
        copy.wait()


def local_kernel(
    heads, decay_ref, query_ref, key_ref, value_ref, weight_hbm, other_weight_hbm,
    intra_ref, own_ref, *refs,
):
    outs, held, sems = refs[:4], refs[4:8], refs[8]
    copies = []
    for i, ref in enumerate(held):
        at = half_at(lax.axis_index("tp") ^ (2 if i < 2 else 0), ref.shape[1])
        weight = other_weight_hbm if i % 2 else weight_hbm
        copies.append(pltpu.make_async_copy(weight.at[:, at], ref, sems.at[0, i]))
        copies[i].start()
    row, col = positions()
    causal = col <= row
    upto = jnp.where(causal, 1.0, 0.0).astype(BF16)
    decays = decay_ref[...]
    down = sums_down(upto, decays)
    across = sums_across(upto, decays)
    own_ref[...] = jnp.exp(down) * SCALE
    for h in range(heads):
        if h == heads - 1:
            for i, ref in enumerate(held):
                copies[i].wait()
                copies[i] = pltpu.make_async_copy(ref, outs[i], sems.at[1, i])
                copies[i].start()
        at = slice(h * HEAD_DIM, (h + 1) * HEAD_DIM)
        scores = contract(query_ref[:, at], key_ref[:, at])
        gaps = down[:, h : h + 1] - across[h : h + 1, :]
        weights = jnp.where(causal, jnp.exp(gaps), 0.0)
        probs = (scores * SCALE * weights).astype(BF16)
        intra_ref[:, at] = jnp.dot(probs, value_ref[:, at], preferred_element_type=F32)
    for copy in copies:
        copy.wait()


def gather_kernel(half, steps, *refs):
    received, (before_ref, sent_ref, through_ref, total_ref, held_ref) = (
        refs[: len(steps)],
        refs[len(steps) :],
    )
    me, upper = place(), side() == 1
    for step, message_ref in zip(steps, received):
        held_ref[me ^ step] = message_ref[...]
    later_pair = me >= 2
    decays = [rows_to_decays(held_ref[m, half * HEAD_DIM :, :], 2 * half) for m in range(MEMBERS)]
    totals = []
    for j in range(2 * half):
        low, high = (j, half + j) if j < half else (j, j - half)
        decay = [jnp.where(upper, d[high], d[low]) for d in decays]
        through = [jnp.ones((1, HEAD_DIM), F32)]
        for m in range(MEMBERS):
            through.append(through[m] * decay[m])
        first, last = [jnp.where(later_pair, through[2 + i], through[i]) for i in range(2)]
        factor = jnp.where(upper, last, first)
        through_ref[j * 8 : (j + 1) * 8, :] = jnp.broadcast_to(factor, (8, HEAD_DIM))
        if j >= half:
            continue
        at = state_rows(j)
        held = [jnp.zeros((HEAD_DIM, HEAD_DIM), F32)]
        for m in range(MEMBERS):
            held.append(held[m] * decay[m] + held_ref[m, at, :].astype(F32))
        first, last = [jnp.where(later_pair, held[2 + i], held[i]) for i in range(2)]
        before_ref[at, :] = jnp.where(upper, last, first)
        sent_ref[at, :] = jnp.where(upper, first, last).astype(BF16)
        total_ref[at, :] = held[MEMBERS].astype(BF16)
        totals.append(through[MEMBERS])
    total_ref[half * HEAD_DIM :, :] = decays_to_rows(totals)


def start_kernel(half, before_ref, through_ref, inside_ref, earlier_ref, _, *outs):
    mine_ref, rest_ref, factor_ref, sent_ref = outs
    started = lax.axis_index("seq") >= MEMBERS
    for j in range(half):
        at = state_rows(j)
        earlier = jnp.where(started, earlier_ref[at, :].astype(F32), 0.0)
        held = before_ref[at, :] + through_ref[8 * j : 8 * j + 1, :] * earlier
        mine_ref[at, :] = held.astype(BF16)
    rest_ref[...] = inside_ref[...]
    factor_ref[...] = through_ref[8 * half :, :]
    sent_ref[...] = earlier_ref[...]


def start_other_kernel(half, rest_ref, factor_ref, earlier_ref, _, out_ref):
    for j in range(half):
        at = state_rows(j)
        earlier = factor_ref[8 * j : 8 * j + 1, :] * earlier_ref[at, :].astype(F32)
        out_ref[at, :] = (rest_ref[at, :].astype(F32) + earlier).astype(BF16)


def norm_kernel(half, mine, rows, query_ref, intra_ref, own_ref, gain_ref, state_ref, out_ref):
    owner = side() if mine else 1 - side()
    own = pick(owner, own_ref[rows, :], 1)
    for j in range(half):
        at = half_at(owner * half + j, HEAD_DIM)
        inter = jnp.dot(query_ref[rows, at], state_ref[state_rows(j), :], preferred_element_type=F32)
        attended = intra_ref[rows, at] + own[:, j : j + 1] * inter
        mean_square = jnp.mean(attended * attended, axis=-1, keepdims=True)
        normed = attended * lax.rsqrt(mean_square + 1e-06)
        out_ref[:, j * HEAD_DIM : (j + 1) * HEAD_DIM] = (normed * gain_ref[:, at]).astype(BF16)


def share(mine, pair, weight_ref, other_weight_ref):
    rows = weight_ref.shape[0] // 2
    at = half_at(side() if mine else 1 - side(), rows)
    return jnp.dot(pair[0][...], weight_ref[at, :], preferred_element_type=F32) + jnp.dot(
        pair[1][...], other_weight_ref[at, :], preferred_element_type=F32
    )


def far_mine_kernel(chunks, weight_ref, other_weight_ref, *refs):
    for i, rows in enumerate(chunks):
        pair = refs[2 * i : 2 * i + 2]
        refs[-1][rows, :] = share(True, pair, weight_ref, other_weight_ref)


def far_kernel(rows, begun_ref, mine_ref, other_ref, weight_ref, other_weight_ref, out_ref):
    rest = share(False, (mine_ref, other_ref), weight_ref, other_weight_ref)
    out_ref[...] = (begun_ref[rows, :] + rest).astype(BF16)


def near_kernel(chunks, residual_hbm, weight_ref, other_weight_ref, *refs):
    weights, (out_ref, residual_ref, sem) = (weight_ref, other_weight_ref), refs[-3:]
    copy = pltpu.make_async_copy(residual_hbm, residual_ref, sem)
    copy.start()
    copy.wait()
    for i, rows in enumerate(chunks):
        mine, rest = refs[4 * i : 4 * i + 2], refs[4 * i + 2 : 4 * i + 4]
        near = share(True, mine, *weights) + share(False, rest, *weights)
        out_ref[rows, :] = residual_ref[rows, :].astype(F32) + near


def add_kernel(chunks, near_ref, *refs):
    far, (out_hbm, out_ref, sems) = refs[: len(chunks)], refs[len(chunks) :]
    copies = []
    for i, rows in enumerate(chunks):
        out_ref[rows, :] = (near_ref[rows, :] + far[i][...].astype(F32)).astype(BF16)
        copies.append(
            pltpu.make_async_copy(out_ref.at[rows, :], out_hbm.at[rows, :], sems.at[i])
        )
        copies[-1].start()
    for copy in copies:
        copy.wait()


def call(kernel, out_shape, in_specs, name, out_specs=None, scratch=(), cost=0):
    single = isinstance(out_shape, jax.ShapeDtypeStruct)
    if out_specs is None:
        out_specs = VMEM if single else (VMEM,) * len(out_shape)
    cost = pl.CostEstimate(
        flops=cost, bytes_accessed=2_000_000 if cost else 0, transcendentals=0
    )
    return pl.pallas_call(
        kernel,
        out_shape=out_shape,
        in_specs=in_specs,
        out_specs=out_specs,
        scratch_shapes=scratch,
        compiler_params=PARAMS,
        cost_estimate=cost,
        name=name,
    )


def earlier_groups(total, half, devices):
    groups = devices // MEMBERS
    if groups == 2:
        return lax.ppermute(total, "seq", [(i, i ^ MEMBERS) for i in range(devices)])

    def shift(message, by):
        moves = [(i, i + by * MEMBERS) for i in range(devices - by * MEMBERS)]
        return lax.ppermute(message, "seq", moves)

    rows = half * HEAD_DIM
    held = shift(total, 1)
    by = 1
    while by < groups - 1:
        before = shift(held, by)
        decays = rows_to_decays(held[rows:], half)
        factor = jnp.concatenate([jnp.broadcast_to(d, (HEAD_DIM, HEAD_DIM)) for d in decays])
        state = held[:rows].astype(F32) + factor * before[:rows].astype(F32)
        through = [a * b for a, b in zip(decays, rows_to_decays(before[rows:], half))]
        held = jnp.concatenate([state.astype(BF16), decays_to_rows(through)], axis=0)
        by *= 2
    return held


def on_device(
    residual, query_vectors, key_vectors, value_vectors, log_decay, norm_gain, out_weight
):
    tokens, width = residual.shape
    heads = log_decay.shape[0]
    half = heads // 2
    devices = lax.axis_size("seq")
    tp = lax.axis_size("tp")
    wide = (tokens, heads * HEAD_DIM)
    out_width = out_weight.shape[1] // tp
    states = (half * HEAD_DIM, HEAD_DIM)
    near_pairs = [(i, i ^ 1) for i in range(tp)]
    far_pairs = [(i, i ^ 2) for i in range(tp)]
    shape = jax.ShapeDtypeStruct
    message = shape((half * HEAD_DIM + DECAY_ROWS, HEAD_DIM), BF16)

    def swap(piece, step):
        return lax.ppermute(piece, "seq", [(i, i ^ step) for i in range(devices)])

    other_weight = lax.ppermute(out_weight, "tp", near_pairs)
    weight = pltpu.with_memory_space_constraint(out_weight, pltpu.HBM)
    arguments = (log_decay, key_vectors, value_vectors, query_vectors, norm_gain.reshape(1, -1))
    theirs, mine, decays, keys, values, queries, gain = call(
        functools.partial(state_kernel, half),
        (message, message) + tuple(shape(a.shape, a.dtype) for a in arguments),
        [HBM] * 5,
        "states",
        scratch=[pltpu.SemaphoreType.DMA((5,))],
    )(*(pltpu.with_memory_space_constraint(a, pltpu.HBM) for a in arguments))
    steps = (3, 1, 2, 0)
    received = [swap(theirs, 3), swap(theirs, 1), swap(mine, 2), mine]
    state = shape(states, BF16)
    before, sent, through, total = call(
        functools.partial(gather_kernel, half, steps),
        (shape(states, F32), state, shape((heads * 8, HEAD_DIM), F32), message),
        [VMEM] * len(steps),
        "gather_states",
        scratch=[pltpu.VMEM((MEMBERS,) + message.shape, BF16)],
    )(*received)
    earlier = earlier_groups(total, half, devices)
    inside = swap(sent, 1)
    block = pltpu.HBM((out_weight.shape[0], out_width), BF16)
    intra, own, *blocks = call(
        functools.partial(local_kernel, heads),
        (pltpu.VMEM(wide, F32), pltpu.VMEM((tokens, heads), F32)) + (block,) * 4,
        [VMEM] * 4 + [HBM, pl.BlockSpec(memory_space=pl.ANY)],
        "local",
        out_specs=(VMEM,) * 2 + (HBM,) * 4,
        scratch=[pltpu.VMEM(block.shape, BF16)] * 4 + [pltpu.SemaphoreType.DMA((2, 4))],
        cost=4 * tokens * tokens * heads * HEAD_DIM,
    )(decays, queries, keys, values, weight, other_weight)
    far_weights, near_weights = blocks[:2], blocks[2:]
    mine, rest, factor, sent = call(
        functools.partial(start_kernel, half),
        (
            pltpu.VMEM(states, BF16),
            pltpu.VMEM(states, BF16),
            pltpu.VMEM((half * 8, HEAD_DIM), F32),
            pltpu.VMEM(message.shape, BF16),
        ),
        [VMEM] * 5,
        "start_states",
    )(before, through, inside, earlier, own)

    def normed(name, rows, mine, state):
        part = call(
            functools.partial(norm_kernel, half, mine, rows),
            shape((rows.stop - rows.start, half * HEAD_DIM), BF16),
            [VMEM] * 5,
            name,
        )(queries, intra, own, gain, state)
        return part, lax.ppermute(part, "tp", near_pairs)

    chunks = [slice(0, tokens // 2), slice(tokens // 2, tokens)]

    def finish(state, other_state_behind):
        begun = [normed(f"norm_mine_{i}", rows, True, state) for i, rows in enumerate(chunks)]
        far_begun = call(
            functools.partial(far_mine_kernel, chunks),
            shape((tokens, out_width), F32),
            [VMEM] * (2 + 2 * len(chunks)),
            "project_far_mine",
        )(*far_weights, *(a for pair in begun for a in pair))
        other_state = other_state_behind(far_begun)
        parts = [normed(f"norm_{i}", rows, False, other_state) for i, rows in enumerate(chunks)]
        far = []
        for i, rows in enumerate(chunks):
            part = call(
                functools.partial(far_kernel, rows),
                shape((rows.stop - rows.start, out_width), BF16),
                [VMEM] * 5,
                f"project_far_{i}",
            )(far_begun, *parts[i], *far_weights)
            far.append(lax.ppermute(part, "tp", far_pairs))
        near = call(
            functools.partial(near_kernel, chunks),
            shape((tokens, out_width), F32),
            [HBM] + [VMEM] * (2 + 4 * len(chunks)),
            "project_near",
            scratch=[pltpu.VMEM(residual.shape, BF16), pltpu.SemaphoreType.DMA],
        )(pltpu.with_memory_space_constraint(residual, pltpu.HBM), *near_weights, *(a for i in range(len(chunks)) for a in begun[i] + parts[i]))
        return call(
            functools.partial(add_kernel, chunks),
            pltpu.HBM((tokens, out_width), BF16),
            [VMEM] * (1 + len(chunks)),
            "add",
            out_specs=HBM,
            scratch=[
                pltpu.VMEM((tokens, out_width), BF16),
                pltpu.SemaphoreType.DMA((len(chunks),)),
            ],
        )(near, *far)

    def first_group():
        return finish(mine, lambda begun: rest)

    def later_group():
        swapped = swap(sent, 1)
        start = call(functools.partial(start_other_kernel, half), state, [VMEM] * 4, "start_other")
        return finish(mine, lambda begun: start(rest, factor, swapped, begun))

    return lax.cond(lax.axis_index("seq") < MEMBERS, first_group, later_group)


def solution(mesh):
    return jax.shard_map(
        on_device,
        mesh=mesh,
        in_specs=(
            P("seq", "tp"),
            P("seq", "tp"),
            P("seq", "tp"),
            P("seq", "tp"),
            P("tp", "seq"),
            P("tp"),
            P("tp", None),
        ),
        out_specs=P("seq", "tp"),
        check_vma=False,
    )
```

```python
import functools

import jax
import jax.numpy as jnp
from jax import lax
from jax.experimental import pallas as pl
from jax.experimental.pallas import tpu as pltpu
from jax.sharding import PartitionSpec as P

HEAD_DIM = 128
GROUP = 256
SCALE = HEAD_DIM ** (-0.5)
F32 = jnp.float32
BF16 = jnp.bfloat16
VMEM = pl.BlockSpec(memory_space=pltpu.VMEM)
HBM = pl.BlockSpec(memory_space=pltpu.HBM)
DECAY_ROWS = 16
MEMBERS = 4
PARAMS = pltpu.CompilerParams(vmem_limit_bytes=24 * 1024 * 1024)


def state_rows(j):
    return slice(j * HEAD_DIM, (j + 1) * HEAD_DIM)


def place():
    return lax.rem(lax.axis_index("seq"), MEMBERS)


def side():
    return lax.rem(lax.axis_index("seq"), 2)


def half_at(owner, size):
    return pl.ds(pl.multiple_of(owner * size, size), size)


def pick(owner, values, axis):
    half = values.shape[axis] // 2
    low = lax.slice_in_dim(values, 0, half, axis=axis)
    high = lax.slice_in_dim(values, half, 2 * half, axis=axis)
    return jnp.where(owner == 0, low, high)


def contract(a, b):
    return lax.dot_general(a, b, (((1,), (1,)), ((), ())), preferred_element_type=F32)


def positions():
    shape = (GROUP, GROUP)
    return lax.broadcasted_iota(jnp.int32, shape, 0), lax.broadcasted_iota(jnp.int32, shape, 1)


def three_terms(values):
    first = values.astype(BF16).astype(F32)
    second = (values - first).astype(BF16).astype(F32)
    third = values - first - second
    return jnp.concatenate([first, second, third], axis=0).astype(BF16)


def sums_down(mask, decays):
    heads = decays.shape[0]
    terms = contract(mask, three_terms(decays))
    return terms[:, :heads] + terms[:, heads : 2 * heads] + terms[:, 2 * heads :]


def sums_across(mask, decays):
    heads = decays.shape[0]
    terms = contract(three_terms(decays), mask)
    return terms[:heads] + terms[heads : 2 * heads] + terms[2 * heads :]


def decays_to_rows(decays):
    each = DECAY_ROWS // (2 * len(decays))
    wide = jnp.concatenate([jnp.broadcast_to(d, (each, HEAD_DIM)) for d in decays], axis=0)
    coarse = wide.astype(BF16).astype(F32)
    return jnp.concatenate([coarse, wide - coarse], axis=0).astype(BF16)


def rows_to_decays(rows, count):
    rows = rows.astype(F32)
    each = DECAY_ROWS // (2 * count)
    both = rows[: DECAY_ROWS // 2] + rows[DECAY_ROWS // 2 :]
    return [both[j * each : j * each + 1] for j in range(count)]


def state_kernel(half, *refs):
    sources, outs, held, sems = refs[:5], refs[5:7], refs[7:12], refs[12]
    copies = [
        pltpu.make_async_copy(source, target, sems.at[i])
        for i, (source, target) in enumerate(zip(sources, held))
    ]
    for copy in copies:
        copy.start()
    decay_ref, key_ref, value_ref = held[:3]
    me = side()
    row, col = positions()
    later = jnp.where(col > row, 1.0, 0.0).astype(BF16)
    copies[0].wait()
    decays = decay_ref[...]
    tail = jnp.exp(sums_across(later, decays))
    whole = jnp.exp(jnp.sum(decays, axis=1, keepdims=True))
    copies[1].wait()
    copies[2].wait()
    decay_rows = decays_to_rows([whole[h : h + 1] for h in range(2 * half)])
    for owner, out_ref in zip((1 - me, me), outs):
        factors = pick(owner, tail, 0)
        for j in range(half):
            at = half_at(owner * half + j, HEAD_DIM)
            weighted = (key_ref[:, at].T.astype(F32) * factors[j : j + 1, :]).astype(BF16)
            update = jnp.dot(weighted, value_ref[:, at], preferred_element_type=F32)
            out_ref[state_rows(j), :] = update.astype(BF16)
        out_ref[half * HEAD_DIM :, :] = decay_rows
    for copy in copies[3:]:
        copy.wait()


def local_kernel(heads, decay_ref, query_ref, key_ref, value_ref, intra_ref, own_ref):
    row, col = positions()
    causal = col <= row
    upto = jnp.where(causal, 1.0, 0.0).astype(BF16)
    decays = decay_ref[...]
    down = sums_down(upto, decays)
    across = sums_across(upto, decays)
    own_ref[...] = jnp.exp(down) * SCALE
    for h in range(heads):
        at = slice(h * HEAD_DIM, (h + 1) * HEAD_DIM)
        scores = contract(query_ref[:, at], key_ref[:, at])
        gaps = down[:, h : h + 1] - across[h : h + 1, :]
        weights = jnp.where(causal, jnp.exp(gaps), 0.0)
        probs = (scores * SCALE * weights).astype(BF16)
        intra_ref[:, at] = jnp.dot(probs, value_ref[:, at], preferred_element_type=F32)


def gather_kernel(half, steps, *refs):
    received, (before_ref, sent_ref, through_ref, total_ref, held_ref) = (
        refs[: len(steps)],
        refs[len(steps) :],
    )
    me, upper = place(), side() == 1
    for step, message_ref in zip(steps, received):
        held_ref[me ^ step] = message_ref[...]
    later_pair = me >= 2
    decays = [rows_to_decays(held_ref[m, half * HEAD_DIM :, :], 2 * half) for m in range(MEMBERS)]
    totals = []
    for j in range(2 * half):
        low, high = (j, half + j) if j < half else (j, j - half)
        decay = [jnp.where(upper, d[high], d[low]) for d in decays]
        through = [jnp.ones((1, HEAD_DIM), F32)]
        for m in range(MEMBERS):
            through.append(through[m] * decay[m])
        first, last = [jnp.where(later_pair, through[2 + i], through[i]) for i in range(2)]
        factor = jnp.where(upper, last, first)
        through_ref[j * 8 : (j + 1) * 8, :] = jnp.broadcast_to(factor, (8, HEAD_DIM))
        if j >= half:
            continue
        at = state_rows(j)
        held = [jnp.zeros((HEAD_DIM, HEAD_DIM), F32)]
        for m in range(MEMBERS):
            held.append(held[m] * decay[m] + held_ref[m, at, :].astype(F32))
        first, last = [jnp.where(later_pair, held[2 + i], held[i]) for i in range(2)]
        before_ref[at, :] = jnp.where(upper, last, first)
        sent_ref[at, :] = jnp.where(upper, first, last).astype(BF16)
        total_ref[at, :] = held[MEMBERS].astype(BF16)
        totals.append(through[MEMBERS])
    total_ref[half * HEAD_DIM :, :] = decays_to_rows(totals)


def start_kernel(half, before_ref, through_ref, inside_ref, earlier_ref, _, *outs):
    mine_ref, rest_ref, factor_ref, sent_ref = outs
    started = lax.axis_index("seq") >= MEMBERS
    for j in range(half):
        at = state_rows(j)
        earlier = jnp.where(started, earlier_ref[at, :].astype(F32), 0.0)
        held = before_ref[at, :] + through_ref[8 * j : 8 * j + 1, :] * earlier
        mine_ref[at, :] = held.astype(BF16)
    rest_ref[...] = inside_ref[...]
    factor_ref[...] = through_ref[8 * half :, :]
    sent_ref[...] = earlier_ref[...]


def start_other_kernel(half, rest_ref, factor_ref, earlier_ref, _, out_ref):
    for j in range(half):
        at = state_rows(j)
        earlier = factor_ref[8 * j : 8 * j + 1, :] * earlier_ref[at, :].astype(F32)
        out_ref[at, :] = (rest_ref[at, :].astype(F32) + earlier).astype(BF16)


def norm_kernel(half, mine, rows, query_ref, intra_ref, own_ref, gain_ref, state_ref, out_ref):
    owner = side() if mine else 1 - side()
    own = pick(owner, own_ref[rows, :], 1)
    for j in range(half):
        at = half_at(owner * half + j, HEAD_DIM)
        inter = jnp.dot(query_ref[rows, at], state_ref[state_rows(j), :], preferred_element_type=F32)
        attended = intra_ref[rows, at] + own[:, j : j + 1] * inter
        mean_square = jnp.mean(attended * attended, axis=-1, keepdims=True)
        normed = attended * lax.rsqrt(mean_square + 1e-06)
        out_ref[:, j * HEAD_DIM : (j + 1) * HEAD_DIM] = (normed * gain_ref[:, at]).astype(BF16)


def share(mine, pair, weight_ref, other_weight_ref):
    rows = weight_ref.shape[0] // 2
    at = half_at(side() if mine else 1 - side(), rows)
    return jnp.dot(pair[0][...], weight_ref[at, :], preferred_element_type=F32) + jnp.dot(
        pair[1][...], other_weight_ref[at, :], preferred_element_type=F32
    )


def fetch(step, whole, held, sems):
    copies = []
    for i, (weight, ref) in enumerate(zip(whole, held)):
        at = half_at(lax.axis_index("tp") ^ step, ref.shape[1])
        copies.append(pltpu.make_async_copy(weight.at[:, at], ref, sems.at[i]))
        copies[i].start()
    return copies


def fetch_kernel(weight_hbm, other_weight_hbm, _, weight_ref, other_weight_ref, sems):
    for copy in fetch(2, (weight_hbm, other_weight_hbm), (weight_ref, other_weight_ref), sems):
        copy.wait()


def far_mine_kernel(chunks, weight_ref, other_weight_ref, *refs):
    for i, rows in enumerate(chunks):
        pair = refs[2 * i : 2 * i + 2]
        refs[-1][rows, :] = share(True, pair, weight_ref, other_weight_ref)


def far_kernel(rows, begun_ref, mine_ref, other_ref, weight_ref, other_weight_ref, out_ref):
    rest = share(False, (mine_ref, other_ref), weight_ref, other_weight_ref)
    out_ref[...] = (begun_ref[rows, :] + rest).astype(BF16)


def near_kernel(chunks, residual_hbm, weight_hbm, other_weight_hbm, *refs):
    out_ref, residual_ref, *weights, sems = refs[-5:]
    copies = fetch(0, (weight_hbm, other_weight_hbm), weights, sems)
    copies.append(pltpu.make_async_copy(residual_hbm, residual_ref, sems.at[2]))
    copies[2].start()
    for copy in copies:
        copy.wait()
    for i, rows in enumerate(chunks):
        mine, rest = refs[4 * i : 4 * i + 2], refs[4 * i + 2 : 4 * i + 4]
        near = share(True, mine, *weights) + share(False, rest, *weights)
        out_ref[rows, :] = residual_ref[rows, :].astype(F32) + near


def add_kernel(chunks, near_ref, *refs):
    far, (out_hbm, out_ref, sems) = refs[: len(chunks)], refs[len(chunks) :]
    copies = []
    for i, rows in enumerate(chunks):
        out_ref[rows, :] = (near_ref[rows, :] + far[i][...].astype(F32)).astype(BF16)
        copies.append(
            pltpu.make_async_copy(out_ref.at[rows, :], out_hbm.at[rows, :], sems.at[i])
        )
        copies[-1].start()
    for copy in copies:
        copy.wait()


def call(kernel, out_shape, in_specs, name, out_specs=None, scratch=(), cost=0):
    single = isinstance(out_shape, jax.ShapeDtypeStruct)
    if out_specs is None:
        out_specs = VMEM if single else (VMEM,) * len(out_shape)
    cost = pl.CostEstimate(
        flops=cost, bytes_accessed=2_000_000 if cost else 0, transcendentals=0
    )
    return pl.pallas_call(
        kernel,
        out_shape=out_shape,
        in_specs=in_specs,
        out_specs=out_specs,
        scratch_shapes=scratch,
        compiler_params=PARAMS,
        cost_estimate=cost,
        name=name,
    )


def earlier_groups(total, half, devices):
    groups = devices // MEMBERS
    if groups == 2:
        return lax.ppermute(total, "seq", [(i, i ^ MEMBERS) for i in range(devices)])

    def shift(message, by):
        moves = [(i, i + by * MEMBERS) for i in range(devices - by * MEMBERS)]
        return lax.ppermute(message, "seq", moves)

    rows = half * HEAD_DIM
    held = shift(total, 1)
    by = 1
    while by < groups - 1:
        before = shift(held, by)
        decays = rows_to_decays(held[rows:], half)
        factor = jnp.concatenate([jnp.broadcast_to(d, (HEAD_DIM, HEAD_DIM)) for d in decays])
        state = held[:rows].astype(F32) + factor * before[:rows].astype(F32)
        through = [a * b for a, b in zip(decays, rows_to_decays(before[rows:], half))]
        held = jnp.concatenate([state.astype(BF16), decays_to_rows(through)], axis=0)
        by *= 2
    return held


def on_device(
    residual, query_vectors, key_vectors, value_vectors, log_decay, norm_gain, out_weight
):
    tokens, width = residual.shape
    heads = log_decay.shape[0]
    half = heads // 2
    devices = lax.axis_size("seq")
    tp = lax.axis_size("tp")
    wide = (tokens, heads * HEAD_DIM)
    out_width = out_weight.shape[1] // tp
    states = (half * HEAD_DIM, HEAD_DIM)
    near_pairs = [(i, i ^ 1) for i in range(tp)]
    far_pairs = [(i, i ^ 2) for i in range(tp)]
    shape = jax.ShapeDtypeStruct
    message = shape((half * HEAD_DIM + DECAY_ROWS, HEAD_DIM), BF16)

    def swap(piece, step):
        return lax.ppermute(piece, "seq", [(i, i ^ step) for i in range(devices)])

    other_weight = lax.ppermute(out_weight, "tp", near_pairs)
    weight = pltpu.with_memory_space_constraint(out_weight, pltpu.HBM)
    arguments = (log_decay, key_vectors, value_vectors, query_vectors, norm_gain.reshape(1, -1))
    theirs, mine, decays, keys, values, queries, gain = call(
        functools.partial(state_kernel, half),
        (message, message) + tuple(shape(a.shape, a.dtype) for a in arguments),
        [HBM] * 5,
        "states",
        scratch=[pltpu.SemaphoreType.DMA((5,))],
    )(*(pltpu.with_memory_space_constraint(a, pltpu.HBM) for a in arguments))
    steps = (3, 1, 2, 0)
    received = [swap(theirs, 3), swap(theirs, 1), swap(mine, 2), mine]
    state = shape(states, BF16)
    before, sent, through, total = call(
        functools.partial(gather_kernel, half, steps),
        (shape(states, F32), state, shape((heads * 8, HEAD_DIM), F32), message),
        [VMEM] * len(steps),
        "gather_states",
        scratch=[pltpu.VMEM((MEMBERS,) + message.shape, BF16)],
    )(*received)
    earlier = earlier_groups(total, half, devices)
    inside = swap(sent, 1)
    intra, own = call(
        functools.partial(local_kernel, heads),
        (shape(wide, F32), shape((tokens, heads), F32)),
        [VMEM] * 4,
        "local",
        cost=4 * tokens * tokens * heads * HEAD_DIM,
    )(decays, queries, keys, values)
    mine, rest, factor, sent = call(
        functools.partial(start_kernel, half),
        (state, state, shape((half * 8, HEAD_DIM), F32), message),
        [VMEM] * 5,
        "start_states",
    )(before, through, inside, earlier, own)

    def normed(name, rows, mine, state):
        part = call(
            functools.partial(norm_kernel, half, mine, rows),
            shape((rows.stop - rows.start, half * HEAD_DIM), BF16),
            [VMEM] * 5,
            name,
        )(queries, intra, own, gain, state)
        return part, lax.ppermute(part, "tp", near_pairs)

    chunks = [slice(0, tokens // 2), slice(tokens // 2, tokens)]
    block = (out_weight.shape[0], out_width)
    weights = (weight, other_weight)
    weight_specs = [HBM, pl.BlockSpec(memory_space=pl.ANY)]

    def finish(state, other_state_behind):
        begun = [normed(f"norm_mine_{i}", rows, True, state) for i, rows in enumerate(chunks)]
        far_weights = call(
            fetch_kernel,
            (shape(block, BF16),) * 2,
            weight_specs + [VMEM],
            "fetch_far",
            scratch=[pltpu.SemaphoreType.DMA((2,))],
        )(*weights, begun[-1][0])
        far_begun = call(
            functools.partial(far_mine_kernel, chunks),
            shape((tokens, out_width), F32),
            [VMEM] * (2 + 2 * len(chunks)),
            "project_far_mine",
        )(*far_weights, *(a for pair in begun for a in pair))
        other_state = other_state_behind(far_begun)
        parts = [normed(f"norm_{i}", rows, False, other_state) for i, rows in enumerate(chunks)]
        far = []
        for i, rows in enumerate(chunks):
            part = call(
                functools.partial(far_kernel, rows),
                shape((rows.stop - rows.start, out_width), BF16),
                [VMEM] * 5,
                f"project_far_{i}",
            )(far_begun, *parts[i], *far_weights)
            far.append(lax.ppermute(part, "tp", far_pairs))
        near = call(
            functools.partial(near_kernel, chunks),
            shape((tokens, out_width), F32),
            [HBM] + weight_specs + [VMEM] * (4 * len(chunks)),
            "project_near",
            scratch=[
                pltpu.VMEM(residual.shape, BF16),
                pltpu.VMEM(block, BF16),
                pltpu.VMEM(block, BF16),
                pltpu.SemaphoreType.DMA((3,)),
            ],
        )(
            pltpu.with_memory_space_constraint(residual, pltpu.HBM),
            *weights,
            *(a for i in range(len(chunks)) for a in begun[i] + parts[i]),
        )
        return call(
            functools.partial(add_kernel, chunks),
            pltpu.HBM((tokens, out_width), BF16),
            [VMEM] * (1 + len(chunks)),
            "add",
            out_specs=HBM,
            scratch=[
                pltpu.VMEM((tokens, out_width), BF16),
                pltpu.SemaphoreType.DMA((len(chunks),)),
            ],
        )(near, *far)

    def first_group():
        return finish(mine, lambda begun: rest)

    def later_group():
        swapped = swap(sent, 1)
        start = call(functools.partial(start_other_kernel, half), state, [VMEM] * 4, "start_other")
        return finish(mine, lambda begun: start(rest, factor, swapped, begun))

    return lax.cond(lax.axis_index("seq") < MEMBERS, first_group, later_group)


def solution(mesh):
    return jax.shard_map(
        on_device,
        mesh=mesh,
        in_specs=(
            P("seq", "tp"),
            P("seq", "tp"),
            P("seq", "tp"),
            P("seq", "tp"),
            P("tp", "seq"),
            P("tp"),
            P("tp", None),
        ),
        out_specs=P("seq", "tp"),
        check_vma=False,
    )
```

```python
import functools

import jax
import jax.numpy as jnp
from jax import lax
from jax.experimental import pallas as pl
from jax.experimental.pallas import tpu as pltpu
from jax.sharding import PartitionSpec as P

HEAD_DIM = 128
GROUP = 256
SCALE = HEAD_DIM ** (-0.5)
F32 = jnp.float32
BF16 = jnp.bfloat16
VMEM = pl.BlockSpec(memory_space=pltpu.VMEM)
HBM = pl.BlockSpec(memory_space=pltpu.HBM)
ANY = pl.BlockSpec(memory_space=pl.ANY)
DECAY_ROWS = 16
MEMBERS = 4
PARAMS = pltpu.CompilerParams(vmem_limit_bytes=24 * 1024 * 1024)


def state_rows(j):
    return slice(j * HEAD_DIM, (j + 1) * HEAD_DIM)


def place():
    return lax.rem(lax.axis_index("seq"), MEMBERS)


def side():
    return lax.rem(lax.axis_index("seq"), 2)


def half_at(owner, size):
    return pl.ds(pl.multiple_of(owner * size, size), size)


def pick(owner, values, axis):
    half = values.shape[axis] // 2
    low = lax.slice_in_dim(values, 0, half, axis=axis)
    high = lax.slice_in_dim(values, half, 2 * half, axis=axis)
    return jnp.where(owner == 0, low, high)


def contract(a, b):
    return lax.dot_general(a, b, (((1,), (1,)), ((), ())), preferred_element_type=F32)


def positions():
    shape = (GROUP, GROUP)
    return lax.broadcasted_iota(jnp.int32, shape, 0), lax.broadcasted_iota(jnp.int32, shape, 1)


def three_terms(values):
    first = values.astype(BF16).astype(F32)
    second = (values - first).astype(BF16).astype(F32)
    third = values - first - second
    return jnp.concatenate([first, second, third], axis=0).astype(BF16)


def sums_down(mask, decays):
    heads = decays.shape[0]
    terms = contract(mask, three_terms(decays))
    return terms[:, :heads] + terms[:, heads : 2 * heads] + terms[:, 2 * heads :]


def sums_across(mask, decays):
    heads = decays.shape[0]
    terms = contract(three_terms(decays), mask)
    return terms[:heads] + terms[heads : 2 * heads] + terms[2 * heads :]


def decays_to_rows(decays):
    each = DECAY_ROWS // (2 * len(decays))
    wide = jnp.concatenate([jnp.broadcast_to(d, (each, HEAD_DIM)) for d in decays], axis=0)
    coarse = wide.astype(BF16).astype(F32)
    return jnp.concatenate([coarse, wide - coarse], axis=0).astype(BF16)


def rows_to_decays(rows, count):
    rows = rows.astype(F32)
    each = DECAY_ROWS // (2 * count)
    both = rows[: DECAY_ROWS // 2] + rows[DECAY_ROWS // 2 :]
    return [both[j * each : j * each + 1] for j in range(count)]


def state_kernel(half, *refs):
    sources, outs, held, sems = refs[:5], refs[5:7], refs[7:12], refs[12]
    copies = [
        pltpu.make_async_copy(source, target, sems.at[i])
        for i, (source, target) in enumerate(zip(sources, held))
    ]
    for copy in copies:
        copy.start()
    decay_ref, key_ref, value_ref = held[:3]
    me = side()
    row, col = positions()
    later = jnp.where(col > row, 1.0, 0.0).astype(BF16)
    copies[0].wait()
    decays = decay_ref[...]
    tail = jnp.exp(sums_across(later, decays))
    whole = jnp.exp(jnp.sum(decays, axis=1, keepdims=True))
    copies[1].wait()
    copies[2].wait()
    decay_rows = decays_to_rows([whole[h : h + 1] for h in range(2 * half)])
    for owner, out_ref in zip((1 - me, me), outs):
        factors = pick(owner, tail, 0)
        for j in range(half):
            at = half_at(owner * half + j, HEAD_DIM)
            weighted = (key_ref[:, at].T.astype(F32) * factors[j : j + 1, :]).astype(BF16)
            update = jnp.dot(weighted, value_ref[:, at], preferred_element_type=F32)
            out_ref[state_rows(j), :] = update.astype(BF16)
        out_ref[half * HEAD_DIM :, :] = decay_rows
    for copy in copies[3:]:
        copy.wait()


def local_kernel(heads, decay_ref, query_ref, key_ref, value_ref, intra_ref, own_ref):
    row, col = positions()
    causal = col <= row
    upto = jnp.where(causal, 1.0, 0.0).astype(BF16)
    decays = decay_ref[...]
    down = sums_down(upto, decays)
    across = sums_across(upto, decays)
    own_ref[...] = jnp.exp(down) * SCALE
    for h in range(heads):
        at = slice(h * HEAD_DIM, (h + 1) * HEAD_DIM)
        scores = contract(query_ref[:, at], key_ref[:, at])
        gaps = down[:, h : h + 1] - across[h : h + 1, :]
        weights = jnp.where(causal, jnp.exp(gaps), 0.0)
        probs = (scores * SCALE * weights).astype(BF16)
        intra_ref[:, at] = jnp.dot(probs, value_ref[:, at], preferred_element_type=F32)


def gather_kernel(half, steps, *refs):
    received, (before_ref, sent_ref, through_ref, total_ref, again_ref, held_ref) = (
        refs[: len(steps)],
        refs[len(steps) :],
    )
    me, upper = place(), side() == 1
    for step, message_ref in zip(steps, received):
        held_ref[me ^ step] = message_ref[...]
    later_pair = me >= 2
    decays = [rows_to_decays(held_ref[m, half * HEAD_DIM :, :], 2 * half) for m in range(MEMBERS)]
    totals = []
    for j in range(2 * half):
        low, high = (j, half + j) if j < half else (j, j - half)
        decay = [jnp.where(upper, d[high], d[low]) for d in decays]
        through = [jnp.ones((1, HEAD_DIM), F32)]
        for m in range(MEMBERS):
            through.append(through[m] * decay[m])
        first, last = [jnp.where(later_pair, through[2 + i], through[i]) for i in range(2)]
        factor = jnp.where(upper, last, first)
        through_ref[j * 8 : (j + 1) * 8, :] = jnp.broadcast_to(factor, (8, HEAD_DIM))
        if j >= half:
            continue
        at = state_rows(j)
        held = [jnp.zeros((HEAD_DIM, HEAD_DIM), F32)]
        for m in range(MEMBERS):
            held.append(held[m] * decay[m] + held_ref[m, at, :].astype(F32))
        first, last = [jnp.where(later_pair, held[2 + i], held[i]) for i in range(2)]
        before_ref[at, :] = jnp.where(upper, last, first)
        sent_ref[at, :] = jnp.where(upper, first, last).astype(BF16)
        total_ref[at, :] = held[MEMBERS].astype(BF16)
        again_ref[at, :] = held[MEMBERS].astype(BF16)
        totals.append(through[MEMBERS])
    total_ref[half * HEAD_DIM :, :] = decays_to_rows(totals)


def start_kernel(half, before_ref, through_ref, inside_ref, earlier_ref, _, *outs):
    mine_ref, rest_ref, factor_ref = outs
    started = lax.axis_index("seq") >= MEMBERS
    for j in range(half):
        at = state_rows(j)
        earlier = jnp.where(started, earlier_ref[at, :].astype(F32), 0.0)
        held = before_ref[at, :] + through_ref[8 * j : 8 * j + 1, :] * earlier
        mine_ref[at, :] = held.astype(BF16)
    rest_ref[...] = inside_ref[...]
    factor_ref[...] = through_ref[8 * half :, :]


def start_other_kernel(half, rest_ref, factor_ref, earlier_ref, _, out_ref):
    for j in range(half):
        at = state_rows(j)
        earlier = factor_ref[8 * j : 8 * j + 1, :] * earlier_ref[at, :].astype(F32)
        out_ref[at, :] = (rest_ref[at, :].astype(F32) + earlier).astype(BF16)


def norm_kernel(half, halves, rows, query_ref, intra_ref, own_ref, gain_ref, *refs):
    states, out_ref = refs[: len(halves)], refs[-1]
    for i, (mine, state_ref) in enumerate(zip(halves, states)):
        owner = side() if mine else 1 - side()
        own = pick(owner, own_ref[rows, :], 1)
        for j in range(half):
            at = half_at(owner * half + j, HEAD_DIM)
            state = state_ref[state_rows(j), :]
            inter = jnp.dot(query_ref[rows, at], state, preferred_element_type=F32)
            attended = intra_ref[rows, at] + own[:, j : j + 1] * inter
            mean_square = jnp.mean(attended * attended, axis=-1, keepdims=True)
            normed = (attended * lax.rsqrt(mean_square + 1e-06) * gain_ref[:, at]).astype(BF16)
            to = (i * half + j) * HEAD_DIM
            out_ref[:, to : to + HEAD_DIM] = normed


def share(halves, pair, weights):
    rows = weights[0].shape[0] // 2
    total = None
    for i, mine in enumerate(halves):
        at = half_at(side() if mine else 1 - side(), rows)
        for normed_ref, weight_ref in zip(pair, weights):
            normed = normed_ref[:, i * rows : (i + 1) * rows]
            part = jnp.dot(normed, weight_ref[at, :], preferred_element_type=F32)
            total = part if total is None else total + part
    return total


def fetch(step, whole, held, sems):
    copies = []
    for i, (weight, ref) in enumerate(zip(whole, held)):
        at = half_at(lax.axis_index("tp") ^ step, ref.shape[1])
        copies.append(pltpu.make_async_copy(weight.at[:, at], ref, sems.at[i]))
        copies[i].start()
    return copies


def fetch_kernel(weight_hbm, other_weight_hbm, _, weight_ref, other_weight_ref, sems):
    for copy in fetch(2, (weight_hbm, other_weight_hbm), (weight_ref, other_weight_ref), sems):
        copy.wait()


def far_mine_kernel(chunks, weight_ref, other_weight_ref, *refs):
    for i, rows in enumerate(chunks):
        pair = refs[2 * i : 2 * i + 2]
        refs[-1][rows, :] = share((True,), pair, (weight_ref, other_weight_ref))


def far_kernel(rows, begun_ref, mine_ref, other_ref, weight_ref, other_weight_ref, out_ref):
    rest = share((False,), (mine_ref, other_ref), (weight_ref, other_weight_ref))
    out_ref[...] = (begun_ref[rows, :] + rest).astype(BF16)


def far_all_kernel(mine_ref, other_ref, weight_ref, other_weight_ref, out_ref):
    pair, weights = (mine_ref, other_ref), (weight_ref, other_weight_ref)
    out_ref[...] = share((True, False), pair, weights).astype(BF16)


def near_kernel(chunks, passes, residual_hbm, weight_hbm, other_weight_hbm, *refs):
    out_ref, residual_ref, *weights, sems = refs[-5:]
    copies = fetch(0, (weight_hbm, other_weight_hbm), weights, sems)
    copies.append(pltpu.make_async_copy(residual_hbm, residual_ref, sems.at[2]))
    copies[2].start()
    for copy in copies:
        copy.wait()
    pairs = iter(zip(refs[0:-5:2], refs[1:-5:2]))
    for rows in chunks:
        near = residual_ref[rows, :].astype(F32)
        for halves in passes:
            near = near + share(halves, next(pairs), weights)
        out_ref[rows, :] = near


def nothing_kernel(out_hbm):
    pass


def add_kernel(chunks, near_ref, *refs):
    far, (out_hbm, out_ref, sems) = refs[: len(chunks)], refs[-3:]
    copies = []
    for i, rows in enumerate(chunks):
        out_ref[rows, :] = (near_ref[rows, :] + far[i][...].astype(F32)).astype(BF16)
        copies.append(
            pltpu.make_async_copy(out_ref.at[rows, :], out_hbm.at[rows, :], sems.at[i])
        )
        copies[-1].start()
    for copy in copies:
        copy.wait()


def call(kernel, out_shape, in_specs, name, out_specs=None, scratch=(), cost=0, aliases={}):
    single = isinstance(out_shape, jax.ShapeDtypeStruct)
    if out_specs is None:
        out_specs = VMEM if single else (VMEM,) * len(out_shape)
    cost = pl.CostEstimate(
        flops=cost, bytes_accessed=2_000_000 if cost else 0, transcendentals=0
    )
    return pl.pallas_call(
        kernel,
        out_shape=out_shape,
        in_specs=in_specs,
        out_specs=out_specs,
        scratch_shapes=scratch,
        input_output_aliases=aliases,
        compiler_params=PARAMS,
        cost_estimate=cost,
        name=name,
    )


def earlier_groups(total, again, half, devices):
    groups = devices // MEMBERS

    def swap(message, step):
        return lax.ppermute(message, "seq", [(i, i ^ step) for i in range(devices)])

    if groups == 2:
        return swap(total, MEMBERS), swap(again, MEMBERS + 1)

    def shift(message, by):
        moves = [(i, i + by * MEMBERS) for i in range(devices - by * MEMBERS)]
        return lax.ppermute(message, "seq", moves)

    rows = half * HEAD_DIM
    held = shift(total, 1)
    by = 1
    while by < groups - 1:
        before = shift(held, by)
        decays = rows_to_decays(held[rows:], half)
        factor = jnp.concatenate([jnp.broadcast_to(d, (HEAD_DIM, HEAD_DIM)) for d in decays])
        state = held[:rows].astype(F32) + factor * before[:rows].astype(F32)
        through = [a * b for a, b in zip(decays, rows_to_decays(before[rows:], half))]
        held = jnp.concatenate([state.astype(BF16), decays_to_rows(through)], axis=0)
        by *= 2
    return held, swap(held, 1)


def on_device(
    residual, query_vectors, key_vectors, value_vectors, log_decay, norm_gain, out_weight
):
    tokens, width = residual.shape
    heads = log_decay.shape[0]
    half = heads // 2
    devices = lax.axis_size("seq")
    tp = lax.axis_size("tp")
    wide = (tokens, heads * HEAD_DIM)
    out_width = out_weight.shape[1] // tp
    states = (half * HEAD_DIM, HEAD_DIM)
    near_pairs = [(i, i ^ 1) for i in range(tp)]
    far_pairs = [(i, i ^ 2) for i in range(tp)]
    shape = jax.ShapeDtypeStruct
    message = shape((half * HEAD_DIM + DECAY_ROWS, HEAD_DIM), BF16)

    def swap(piece, step):
        return lax.ppermute(piece, "seq", [(i, i ^ step) for i in range(devices)])

    other_weight = lax.ppermute(out_weight, "tp", near_pairs)
    arguments = (log_decay, key_vectors, value_vectors, query_vectors, norm_gain.reshape(1, -1))
    theirs, mine, decays, keys, values, queries, gain = call(
        functools.partial(state_kernel, half),
        (message, message) + tuple(shape(a.shape, a.dtype) for a in arguments),
        [HBM] * 5,
        "states",
        scratch=[pltpu.SemaphoreType.DMA((5,))],
    )(*(pltpu.with_memory_space_constraint(a, pltpu.HBM) for a in arguments))
    steps = (3, 1, 2, 0)
    received = [swap(theirs, 3), swap(theirs, 1), swap(mine, 2), mine]
    state = shape(states, BF16)
    before, sent, through, total, again = call(
        functools.partial(gather_kernel, half, steps),
        (shape(states, F32), state, shape((heads * 8, HEAD_DIM), F32), message, state),
        [VMEM] * len(steps),
        "gather_states",
        scratch=[pltpu.VMEM((MEMBERS,) + message.shape, BF16)],
    )(*received)
    earlier, other_earlier = earlier_groups(total, again, half, devices)
    inside = swap(sent, 1)
    intra, own = call(
        functools.partial(local_kernel, heads),
        (shape(wide, F32), shape((tokens, heads), F32)),
        [VMEM] * 4,
        "local",
        cost=4 * tokens * tokens * heads * HEAD_DIM,
    )(decays, queries, keys, values)
    block = (out_weight.shape[0], out_width)
    weights = (out_weight, other_weight)
    far_weights = call(
        fetch_kernel,
        (shape(block, BF16),) * 2,
        [ANY] * 2 + [VMEM],
        "fetch_far",
        scratch=[pltpu.SemaphoreType.DMA((2,))],
    )(*weights, own)
    mine, rest, factor = call(
        functools.partial(start_kernel, half),
        (state, state, shape((half * 8, HEAD_DIM), F32)),
        [VMEM] * 5,
        "start_states",
    )(before, through, inside, earlier, far_weights[0])
    chunks = [slice(0, tokens // 2), slice(tokens // 2, tokens)]

    def normed(name, halves, rows, *states):
        part = call(
            functools.partial(norm_kernel, half, halves, rows),
            shape((rows.stop - rows.start, len(halves) * half * HEAD_DIM), BF16),
            [VMEM] * (4 + len(states)),
            name,
        )(queries, intra, own, gain, *states)
        return part, lax.ppermute(part, "tp", near_pairs)

    def send_far(name, kernel, rows, *operands):
        part = call(
            kernel,
            shape((rows.stop - rows.start, out_width), BF16),
            [VMEM] * (len(operands) + 2),
            name,
        )(*operands, *far_weights)
        return lax.ppermute(part, "tp", far_pairs)

    def add(passes, pairs, far, out=()):
        near = call(
            functools.partial(near_kernel, chunks, passes),
            shape((tokens, out_width), F32),
            [ANY] * 3 + [VMEM] * (2 * len(pairs)),
            "project_near",
            scratch=[
                pltpu.VMEM(residual.shape, BF16),
                pltpu.VMEM(block, BF16),
                pltpu.VMEM(block, BF16),
                pltpu.SemaphoreType.DMA((3,)),
            ],
        )(residual, *weights, *(a for pair in pairs for a in pair))
        return call(
            functools.partial(add_kernel, chunks),
            pltpu.HBM((tokens, out_width), BF16),
            [VMEM] * (1 + len(chunks)) + [HBM] * len(out),
            "add",
            out_specs=HBM,
            scratch=[
                pltpu.VMEM((tokens, out_width), BF16),
                pltpu.SemaphoreType.DMA((len(chunks),)),
            ],
            aliases={1 + len(chunks): 0} if out else {},
        )(near, *far, *out)

    def first_group():
        both = (True, False)
        pairs = [normed(f"norm_{i}", both, rows, mine, rest) for i, rows in enumerate(chunks)]
        far = [
            send_far(f"project_far_{i}", far_all_kernel, rows, *pairs[i])
            for i, rows in enumerate(chunks)
        ]
        return add((both,), pairs, far)

    def not_yet():
        return call(
            nothing_kernel, pltpu.HBM((tokens, out_width), BF16), [], "nothing", out_specs=HBM
        )()

    def later_group(out):
        begun = [normed(f"norm_mine_{i}", (True,), rows, mine) for i, rows in enumerate(chunks)]
        far_begun = call(
            functools.partial(far_mine_kernel, chunks),
            shape((tokens, out_width), F32),
            [VMEM] * (2 + 2 * len(chunks)),
            "project_far_mine",
        )(*far_weights, *(a for pair in begun for a in pair))
        other = call(functools.partial(start_other_kernel, half), state, [VMEM] * 4, "start_other")(
            rest, factor, other_earlier, far_begun
        )
        parts = [normed(f"norm_{i}", (False,), rows, other) for i, rows in enumerate(chunks)]
        far = [
            send_far(
                f"project_far_{i}", functools.partial(far_kernel, rows), rows, far_begun, *parts[i]
            )
            for i, rows in enumerate(chunks)
        ]
        pairs = [pair for i in range(len(chunks)) for pair in (begun[i], parts[i])]
        return add(((True,), (False,)), pairs, far, (out,))

    first = lax.axis_index("seq") < MEMBERS
    out = lax.cond(first, first_group, not_yet)
    return lax.cond(first, lambda out: out, later_group, out)


def solution(mesh):
    return jax.shard_map(
        on_device,
        mesh=mesh,
        in_specs=(
            P("seq", "tp"),
            P("seq", "tp"),
            P("seq", "tp"),
            P("seq", "tp"),
            P("tp", "seq"),
            P("tp"),
            P("tp", None),
        ),
        out_specs=P("seq", "tp"),
        check_vma=False,
    )
```

```python
import functools

import jax
import jax.numpy as jnp
from jax import lax
from jax.experimental import pallas as pl
from jax.experimental.pallas import tpu as pltpu
from jax.sharding import PartitionSpec as P

HEAD_DIM = 128
GROUP = 256
SCALE = HEAD_DIM ** (-0.5)
F32 = jnp.float32
BF16 = jnp.bfloat16
VMEM = pl.BlockSpec(memory_space=pltpu.VMEM)
HBM = pl.BlockSpec(memory_space=pltpu.HBM)
ANY = pl.BlockSpec(memory_space=pl.ANY)
DECAY_ROWS = 16
MEMBERS = 4
PARAMS = pltpu.CompilerParams(vmem_limit_bytes=24 * 1024 * 1024)


def state_rows(j):
    return slice(j * HEAD_DIM, (j + 1) * HEAD_DIM)


def place():
    return lax.rem(lax.axis_index("seq"), MEMBERS)


def side():
    return lax.rem(lax.axis_index("seq"), 2)


def half_at(owner, size):
    return pl.ds(pl.multiple_of(owner * size, size), size)


def pick(owner, values, axis):
    half = values.shape[axis] // 2
    low = lax.slice_in_dim(values, 0, half, axis=axis)
    high = lax.slice_in_dim(values, half, 2 * half, axis=axis)
    return jnp.where(owner == 0, low, high)


def contract(a, b):
    return lax.dot_general(a, b, (((1,), (1,)), ((), ())), preferred_element_type=F32)


def positions():
    shape = (GROUP, GROUP)
    return lax.broadcasted_iota(jnp.int32, shape, 0), lax.broadcasted_iota(jnp.int32, shape, 1)


def three_terms(values):
    first = values.astype(BF16).astype(F32)
    second = (values - first).astype(BF16).astype(F32)
    third = values - first - second
    return jnp.concatenate([first, second, third], axis=0).astype(BF16)


def sums_down(mask, decays):
    heads = decays.shape[0]
    terms = contract(mask, three_terms(decays))
    return terms[:, :heads] + terms[:, heads : 2 * heads] + terms[:, 2 * heads :]


def sums_across(mask, decays):
    heads = decays.shape[0]
    terms = contract(three_terms(decays), mask)
    return terms[:heads] + terms[heads : 2 * heads] + terms[2 * heads :]


def decays_to_rows(decays):
    each = DECAY_ROWS // (2 * len(decays))
    wide = jnp.concatenate([jnp.broadcast_to(d, (each, HEAD_DIM)) for d in decays], axis=0)
    coarse = wide.astype(BF16).astype(F32)
    return jnp.concatenate([coarse, wide - coarse], axis=0).astype(BF16)


def rows_to_decays(rows, count):
    rows = rows.astype(F32)
    each = DECAY_ROWS // (2 * count)
    both = rows[: DECAY_ROWS // 2] + rows[DECAY_ROWS // 2 :]
    return [both[j * each : j * each + 1] for j in range(count)]


def state_kernel(half, *refs):
    sources, outs, held, sems = refs[:5], refs[5:7], refs[7:12], refs[12]
    copies = [
        pltpu.make_async_copy(source, target, sems.at[i])
        for i, (source, target) in enumerate(zip(sources, held))
    ]
    for copy in copies:
        copy.start()
    decay_ref, key_ref, value_ref = held[:3]
    me = side()
    row, col = positions()
    later = jnp.where(col > row, 1.0, 0.0).astype(BF16)
    copies[0].wait()
    decays = decay_ref[...]
    tail = jnp.exp(sums_across(later, decays))
    whole = jnp.exp(jnp.sum(decays, axis=1, keepdims=True))
    copies[1].wait()
    copies[2].wait()
    decay_rows = decays_to_rows([whole[h : h + 1] for h in range(2 * half)])
    for owner, out_ref in zip((1 - me, me), outs):
        factors = pick(owner, tail, 0)
        for j in range(half):
            at = half_at(owner * half + j, HEAD_DIM)
            weighted = (key_ref[:, at].T.astype(F32) * factors[j : j + 1, :]).astype(BF16)
            update = jnp.dot(weighted, value_ref[:, at], preferred_element_type=F32)
            out_ref[state_rows(j), :] = update.astype(BF16)
        out_ref[half * HEAD_DIM :, :] = decay_rows
    for copy in copies[3:]:
        copy.wait()


def local_kernel(heads, decay_ref, query_ref, key_ref, value_ref, intra_ref, own_ref):
    row, col = positions()
    causal = col <= row
    upto = jnp.where(causal, 1.0, 0.0).astype(BF16)
    decays = decay_ref[...]
    down = sums_down(upto, decays)
    across = sums_across(upto, decays)
    own_ref[...] = jnp.exp(down) * SCALE
    for h in range(heads):
        at = slice(h * HEAD_DIM, (h + 1) * HEAD_DIM)
        scores = contract(query_ref[:, at], key_ref[:, at])
        gaps = down[:, h : h + 1] - across[h : h + 1, :]
        weights = jnp.where(causal, jnp.exp(gaps), 0.0)
        probs = (scores * SCALE * weights).astype(BF16)
        intra_ref[:, at] = jnp.dot(probs, value_ref[:, at], preferred_element_type=F32)


def gather_kernel(half, steps, *refs):
    received, (before_ref, sent_ref, through_ref, total_ref, again_ref, held_ref) = (
        refs[: len(steps)],
        refs[len(steps) :],
    )
    me, upper = place(), side() == 1
    for step, message_ref in zip(steps, received):
        held_ref[me ^ step] = message_ref[...]
    later_pair = me >= 2
    decays = [rows_to_decays(held_ref[m, half * HEAD_DIM :, :], 2 * half) for m in range(MEMBERS)]
    totals = []
    for j in range(2 * half):
        low, high = (j, half + j) if j < half else (j, j - half)
        decay = [jnp.where(upper, d[high], d[low]) for d in decays]
        through = [jnp.ones((1, HEAD_DIM), F32)]
        for m in range(MEMBERS):
            through.append(through[m] * decay[m])
        first, last = [jnp.where(later_pair, through[2 + i], through[i]) for i in range(2)]
        factor = jnp.where(upper, last, first)
        through_ref[j * 8 : (j + 1) * 8, :] = jnp.broadcast_to(factor, (8, HEAD_DIM))
        if j >= half:
            continue
        at = state_rows(j)
        held = [jnp.zeros((HEAD_DIM, HEAD_DIM), F32)]
        for m in range(MEMBERS):
            held.append(held[m] * decay[m] + held_ref[m, at, :].astype(F32))
        first, last = [jnp.where(later_pair, held[2 + i], held[i]) for i in range(2)]
        before_ref[at, :] = jnp.where(upper, last, first)
        sent_ref[at, :] = jnp.where(upper, first, last).astype(BF16)
        total_ref[at, :] = held[MEMBERS].astype(BF16)
        again_ref[at, :] = held[MEMBERS].astype(BF16)
        totals.append(through[MEMBERS])
    total_ref[half * HEAD_DIM :, :] = decays_to_rows(totals)


def start_kernel(half, before_ref, through_ref, inside_ref, earlier_ref, _, *outs):
    mine_ref, rest_ref, factor_ref = outs
    started = lax.axis_index("seq") >= MEMBERS
    for j in range(half):
        at = state_rows(j)
        earlier = jnp.where(started, earlier_ref[at, :].astype(F32), 0.0)
        held = before_ref[at, :] + through_ref[8 * j : 8 * j + 1, :] * earlier
        mine_ref[at, :] = held.astype(BF16)
    rest_ref[...] = inside_ref[...]
    factor_ref[...] = through_ref[8 * half :, :]


def start_other_kernel(half, rest_ref, factor_ref, earlier_ref, out_ref):
    for j in range(half):
        at = state_rows(j)
        earlier = factor_ref[8 * j : 8 * j + 1, :] * earlier_ref[at, :].astype(F32)
        out_ref[at, :] = (rest_ref[at, :].astype(F32) + earlier).astype(BF16)


def norm_kernel(
    half, rows, query_ref, intra_ref, own_ref, gain_ref, mine_ref, other_ref, out_ref
):
    for i, (owner, state_ref) in enumerate(zip((side(), 1 - side()), (mine_ref, other_ref))):
        own = pick(owner, own_ref[rows, :], 1)
        for j in range(half):
            at = half_at(owner * half + j, HEAD_DIM)
            state = state_ref[state_rows(j), :]
            inter = jnp.dot(query_ref[rows, at], state, preferred_element_type=F32)
            attended = intra_ref[rows, at] + own[:, j : j + 1] * inter
            mean_square = jnp.mean(attended * attended, axis=-1, keepdims=True)
            normed = (attended * lax.rsqrt(mean_square + 1e-06) * gain_ref[:, at]).astype(BF16)
            to = (i * half + j) * HEAD_DIM
            out_ref[:, to : to + HEAD_DIM] = normed


def share(pair, weights):
    rows = weights[0].shape[0] // 2
    total = None
    for i, owner in enumerate((side(), 1 - side())):
        at = half_at(owner, rows)
        for normed_ref, weight_ref in zip(pair, weights):
            normed = normed_ref[:, i * rows : (i + 1) * rows]
            part = jnp.dot(normed, weight_ref[at, :], preferred_element_type=F32)
            total = part if total is None else total + part
    return total


def fetch(step, whole, held, sems):
    copies = []
    for i, (weight, ref) in enumerate(zip(whole, held)):
        at = half_at(lax.axis_index("tp") ^ step, ref.shape[1])
        copies.append(pltpu.make_async_copy(weight.at[:, at], ref, sems.at[i]))
        copies[i].start()
    return copies


def fetch_kernel(weight_hbm, other_weight_hbm, _, weight_ref, other_weight_ref, sems):
    for copy in fetch(2, (weight_hbm, other_weight_hbm), (weight_ref, other_weight_ref), sems):
        copy.wait()


def far_kernel(mine_ref, other_ref, weight_ref, other_weight_ref, out_ref):
    out_ref[...] = share((mine_ref, other_ref), (weight_ref, other_weight_ref)).astype(BF16)


def near_kernel(chunks, residual_hbm, weight_hbm, other_weight_hbm, *refs):
    out_ref, residual_ref, *weights, sems = refs[-5:]
    copies = fetch(0, (weight_hbm, other_weight_hbm), weights, sems)
    copies.append(pltpu.make_async_copy(residual_hbm, residual_ref, sems.at[2]))
    copies[2].start()
    for copy in copies:
        copy.wait()
    for i, rows in enumerate(chunks):
        near = share(refs[2 * i : 2 * i + 2], weights)
        out_ref[rows, :] = residual_ref[rows, :].astype(F32) + near


def nothing_kernel(out_hbm):
    pass


def add_kernel(chunks, near_ref, *refs):
    far, (out_hbm, out_ref, sems) = refs[: len(chunks)], refs[-3:]
    copies = []
    for i, rows in enumerate(chunks):
        out_ref[rows, :] = (near_ref[rows, :] + far[i][...].astype(F32)).astype(BF16)
        copies.append(
            pltpu.make_async_copy(out_ref.at[rows, :], out_hbm.at[rows, :], sems.at[i])
        )
        copies[-1].start()
    for copy in copies:
        copy.wait()


def call(kernel, out_shape, in_specs, name, out_specs=None, scratch=(), cost=0, aliases={}):
    single = isinstance(out_shape, jax.ShapeDtypeStruct)
    if out_specs is None:
        out_specs = VMEM if single else (VMEM,) * len(out_shape)
    cost = pl.CostEstimate(
        flops=cost, bytes_accessed=2_000_000 if cost else 0, transcendentals=0
    )
    return pl.pallas_call(
        kernel,
        out_shape=out_shape,
        in_specs=in_specs,
        out_specs=out_specs,
        scratch_shapes=scratch,
        input_output_aliases=aliases,
        compiler_params=PARAMS,
        cost_estimate=cost,
        name=name,
    )


def earlier_groups(total, again, half, devices):
    groups = devices // MEMBERS

    def swap(message, step):
        return lax.ppermute(message, "seq", [(i, i ^ step) for i in range(devices)])

    if groups == 2:
        return swap(total, MEMBERS), swap(again, MEMBERS + 1)

    def shift(message, by):
        moves = [(i, i + by * MEMBERS) for i in range(devices - by * MEMBERS)]
        return lax.ppermute(message, "seq", moves)

    rows = half * HEAD_DIM
    held = shift(total, 1)
    by = 1
    while by < groups - 1:
        before = shift(held, by)
        decays = rows_to_decays(held[rows:], half)
        factor = jnp.concatenate([jnp.broadcast_to(d, (HEAD_DIM, HEAD_DIM)) for d in decays])
        state = held[:rows].astype(F32) + factor * before[:rows].astype(F32)
        through = [a * b for a, b in zip(decays, rows_to_decays(before[rows:], half))]
        held = jnp.concatenate([state.astype(BF16), decays_to_rows(through)], axis=0)
        by *= 2
    return held, swap(held, 1)


def on_device(
    residual, query_vectors, key_vectors, value_vectors, log_decay, norm_gain, out_weight
):
    tokens, width = residual.shape
    heads = log_decay.shape[0]
    half = heads // 2
    devices = lax.axis_size("seq")
    tp = lax.axis_size("tp")
    wide = (tokens, heads * HEAD_DIM)
    out_width = out_weight.shape[1] // tp
    states = (half * HEAD_DIM, HEAD_DIM)
    near_pairs = [(i, i ^ 1) for i in range(tp)]
    far_pairs = [(i, i ^ 2) for i in range(tp)]
    shape = jax.ShapeDtypeStruct
    message = shape((half * HEAD_DIM + DECAY_ROWS, HEAD_DIM), BF16)

    def swap(piece, step):
        return lax.ppermute(piece, "seq", [(i, i ^ step) for i in range(devices)])

    other_weight = lax.ppermute(out_weight, "tp", near_pairs)
    arguments = (log_decay, key_vectors, value_vectors, query_vectors, norm_gain.reshape(1, -1))
    theirs, mine, decays, keys, values, queries, gain = call(
        functools.partial(state_kernel, half),
        (message, message) + tuple(shape(a.shape, a.dtype) for a in arguments),
        [HBM] * 5,
        "states",
        scratch=[pltpu.SemaphoreType.DMA((5,))],
    )(*(pltpu.with_memory_space_constraint(a, pltpu.HBM) for a in arguments))
    steps = (3, 1, 2, 0)
    received = [swap(theirs, 3), swap(theirs, 1), swap(mine, 2), mine]
    state = shape(states, BF16)
    before, sent, through, total, again = call(
        functools.partial(gather_kernel, half, steps),
        (shape(states, F32), state, shape((heads * 8, HEAD_DIM), F32), message, state),
        [VMEM] * len(steps),
        "gather_states",
        scratch=[pltpu.VMEM((MEMBERS,) + message.shape, BF16)],
    )(*received)
    earlier, other_earlier = earlier_groups(total, again, half, devices)
    inside = swap(sent, 1)
    intra, own = call(
        functools.partial(local_kernel, heads),
        (shape(wide, F32), shape((tokens, heads), F32)),
        [VMEM] * 4,
        "local",
        cost=4 * tokens * tokens * heads * HEAD_DIM,
    )(decays, queries, keys, values)
    block = (out_weight.shape[0], out_width)
    weights = (out_weight, other_weight)
    far_weights = call(
        fetch_kernel,
        (shape(block, BF16),) * 2,
        [ANY] * 2 + [VMEM],
        "fetch_far",
        scratch=[pltpu.SemaphoreType.DMA((2,))],
    )(*weights, own)
    mine, rest, factor = call(
        functools.partial(start_kernel, half),
        (state, state, shape((half * 8, HEAD_DIM), F32)),
        [VMEM] * 5,
        "start_states",
    )(before, through, inside, earlier, far_weights[0])
    chunks = [slice(0, tokens // 2), slice(tokens // 2, tokens)]

    def finish(mine, other, out=()):
        pairs, far = [], []
        for i, rows in enumerate(chunks):
            part = call(
                functools.partial(norm_kernel, half, rows),
                shape((rows.stop - rows.start, heads * HEAD_DIM), BF16),
                [VMEM] * 6,
                f"norm_{i}",
            )(queries, intra, own, gain, mine, other)
            pairs.append((part, lax.ppermute(part, "tp", near_pairs)))
        for i, rows in enumerate(chunks):
            part = call(
                far_kernel,
                shape((rows.stop - rows.start, out_width), BF16),
                [VMEM] * 4,
                f"project_far_{i}",
            )(*pairs[i], *far_weights)
            far.append(lax.ppermute(part, "tp", far_pairs))
        near = call(
            functools.partial(near_kernel, chunks),
            shape((tokens, out_width), F32),
            [ANY] * 3 + [VMEM] * (2 * len(chunks)),
            "project_near",
            scratch=[
                pltpu.VMEM(residual.shape, BF16),
                pltpu.VMEM(block, BF16),
                pltpu.VMEM(block, BF16),
                pltpu.SemaphoreType.DMA((3,)),
            ],
        )(residual, *weights, *(a for pair in pairs for a in pair))
        return call(
            functools.partial(add_kernel, chunks),
            pltpu.HBM((tokens, out_width), BF16),
            [VMEM] * (1 + len(chunks)) + [HBM] * len(out),
            "add",
            out_specs=HBM,
            scratch=[
                pltpu.VMEM((tokens, out_width), BF16),
                pltpu.SemaphoreType.DMA((len(chunks),)),
            ],
            aliases={1 + len(chunks): 0} if out else {},
        )(near, *far, *out)

    def not_yet():
        return call(
            nothing_kernel, pltpu.HBM((tokens, out_width), BF16), [], "nothing", out_specs=HBM
        )()

    def later_group(out):
        other = call(functools.partial(start_other_kernel, half), state, [VMEM] * 3, "start_other")(
            rest, factor, other_earlier
        )
        return finish(mine, other, (out,))

    first = lax.axis_index("seq") < MEMBERS
    out = lax.cond(first, lambda: finish(mine, rest), not_yet)
    return lax.cond(first, lambda out: out, later_group, out)


def solution(mesh):
    return jax.shard_map(
        on_device,
        mesh=mesh,
        in_specs=(
            P("seq", "tp"),
            P("seq", "tp"),
            P("seq", "tp"),
            P("seq", "tp"),
            P("tp", "seq"),
            P("tp"),
            P("tp", None),
        ),
        out_specs=P("seq", "tp"),
        check_vma=False,
    )
```

```python
import functools

import jax
import jax.numpy as jnp
from jax import lax
from jax.experimental import pallas as pl
from jax.experimental.pallas import tpu as pltpu
from jax.sharding import PartitionSpec as P

HEAD_DIM = 128
GROUP = 256
SCALE = HEAD_DIM ** (-0.5)
F32 = jnp.float32
BF16 = jnp.bfloat16
VMEM = pl.BlockSpec(memory_space=pltpu.VMEM)
HBM = pl.BlockSpec(memory_space=pltpu.HBM)
ANY = pl.BlockSpec(memory_space=pl.ANY)
DECAY_ROWS = 16
MEMBERS = 4
PARAMS = pltpu.CompilerParams(vmem_limit_bytes=24 * 1024 * 1024)


def state_rows(j):
    return slice(j * HEAD_DIM, (j + 1) * HEAD_DIM)


def place():
    return lax.rem(lax.axis_index("seq"), MEMBERS)


def side():
    return lax.rem(lax.axis_index("seq"), 2)


def half_at(owner, size):
    return pl.ds(pl.multiple_of(owner * size, size), size)


def pick(owner, values, axis):
    half = values.shape[axis] // 2
    low = lax.slice_in_dim(values, 0, half, axis=axis)
    high = lax.slice_in_dim(values, half, 2 * half, axis=axis)
    return jnp.where(owner == 0, low, high)


def contract(a, b):
    return lax.dot_general(a, b, (((1,), (1,)), ((), ())), preferred_element_type=F32)


def positions():
    shape = (GROUP, GROUP)
    return lax.broadcasted_iota(jnp.int32, shape, 0), lax.broadcasted_iota(jnp.int32, shape, 1)


def three_terms(values):
    first = values.astype(BF16).astype(F32)
    second = (values - first).astype(BF16).astype(F32)
    third = values - first - second
    return jnp.concatenate([first, second, third], axis=0).astype(BF16)


def sums_down(mask, decays):
    heads = decays.shape[0]
    terms = contract(mask, three_terms(decays))
    return terms[:, :heads] + terms[:, heads : 2 * heads] + terms[:, 2 * heads :]


def sums_across(mask, decays):
    heads = decays.shape[0]
    terms = contract(three_terms(decays), mask)
    return terms[:heads] + terms[heads : 2 * heads] + terms[2 * heads :]


def decays_to_rows(decays):
    each = DECAY_ROWS // (2 * len(decays))
    wide = jnp.concatenate([jnp.broadcast_to(d, (each, HEAD_DIM)) for d in decays], axis=0)
    coarse = wide.astype(BF16).astype(F32)
    return jnp.concatenate([coarse, wide - coarse], axis=0).astype(BF16)


def rows_to_decays(rows, count):
    rows = rows.astype(F32)
    each = DECAY_ROWS // (2 * count)
    both = rows[: DECAY_ROWS // 2] + rows[DECAY_ROWS // 2 :]
    return [both[j * each : j * each + 1] for j in range(count)]


def state_kernel(half, *refs):
    sources, outs, held, sems = refs[:5], refs[5:7], refs[7:12], refs[12]
    copies = [
        pltpu.make_async_copy(source, target, sems.at[i])
        for i, (source, target) in enumerate(zip(sources, held))
    ]
    for copy in copies:
        copy.start()
    decay_ref, key_ref, value_ref = held[:3]
    me = side()
    row, col = positions()
    later = jnp.where(col > row, 1.0, 0.0).astype(BF16)
    copies[0].wait()
    decays = decay_ref[...]
    tail = jnp.exp(sums_across(later, decays))
    whole = jnp.exp(jnp.sum(decays, axis=1, keepdims=True))
    copies[1].wait()
    copies[2].wait()
    decay_rows = decays_to_rows([whole[h : h + 1] for h in range(2 * half)])
    for owner, out_ref in zip((1 - me, me), outs):
        factors = pick(owner, tail, 0)
        for j in range(half):
            at = half_at(owner * half + j, HEAD_DIM)
            weighted = (key_ref[:, at].T.astype(F32) * factors[j : j + 1, :]).astype(BF16)
            update = jnp.dot(weighted, value_ref[:, at], preferred_element_type=F32)
            out_ref[state_rows(j), :] = update.astype(BF16)
        out_ref[half * HEAD_DIM :, :] = decay_rows
    for copy in copies[3:]:
        copy.wait()


def local_kernel(heads, decay_ref, query_ref, key_ref, value_ref, intra_ref, scaled_ref):
    row, col = positions()
    causal = col <= row
    upto = jnp.where(causal, 1.0, 0.0).astype(BF16)
    decays = decay_ref[...]
    down = sums_down(upto, decays)
    across = sums_across(upto, decays)
    own = jnp.exp(down) * SCALE
    for h in range(heads):
        at = slice(h * HEAD_DIM, (h + 1) * HEAD_DIM)
        scaled_ref[:, at] = (query_ref[:, at].astype(F32) * own[:, h : h + 1]).astype(BF16)
        scores = contract(query_ref[:, at], key_ref[:, at])
        gaps = down[:, h : h + 1] - across[h : h + 1, :]
        weights = jnp.where(causal, jnp.exp(gaps), 0.0)
        probs = (scores * SCALE * weights).astype(BF16)
        intra = jnp.dot(probs, value_ref[:, at], preferred_element_type=F32)
        intra_ref[:, at] = intra.astype(BF16)


def gather_kernel(half, steps, *refs):
    received, (before_ref, sent_ref, through_ref, total_ref, again_ref, held_ref) = (
        refs[: len(steps)],
        refs[len(steps) :],
    )
    me, upper = place(), side() == 1
    for step, message_ref in zip(steps, received):
        held_ref[me ^ step] = message_ref[...]
    later_pair = me >= 2
    decays = [rows_to_decays(held_ref[m, half * HEAD_DIM :, :], 2 * half) for m in range(MEMBERS)]
    totals = []
    for j in range(2 * half):
        low, high = (j, half + j) if j < half else (j, j - half)
        decay = [jnp.where(upper, d[high], d[low]) for d in decays]
        through = [jnp.ones((1, HEAD_DIM), F32)]
        for m in range(MEMBERS):
            through.append(through[m] * decay[m])
        first, last = [jnp.where(later_pair, through[2 + i], through[i]) for i in range(2)]
        factor = jnp.where(upper, last, first)
        through_ref[j * 8 : (j + 1) * 8, :] = jnp.broadcast_to(factor, (8, HEAD_DIM))
        if j >= half:
            continue
        at = state_rows(j)
        held = [jnp.zeros((HEAD_DIM, HEAD_DIM), F32)]
        for m in range(MEMBERS):
            held.append(held[m] * decay[m] + held_ref[m, at, :].astype(F32))
        first, last = [jnp.where(later_pair, held[2 + i], held[i]) for i in range(2)]
        before_ref[at, :] = jnp.where(upper, last, first)
        sent_ref[at, :] = jnp.where(upper, first, last).astype(BF16)
        total_ref[at, :] = held[MEMBERS].astype(BF16)
        again_ref[at, :] = held[MEMBERS].astype(BF16)
        totals.append(through[MEMBERS])
    total_ref[half * HEAD_DIM :, :] = decays_to_rows(totals)


def start_kernel(half, before_ref, through_ref, inside_ref, earlier_ref, _, *outs):
    mine_ref, rest_ref, factor_ref = outs
    started = lax.axis_index("seq") >= MEMBERS
    for j in range(half):
        at = state_rows(j)
        earlier = jnp.where(started, earlier_ref[at, :].astype(F32), 0.0)
        held = before_ref[at, :] + through_ref[8 * j : 8 * j + 1, :] * earlier
        mine_ref[at, :] = held.astype(BF16)
    rest_ref[...] = inside_ref[...]
    factor_ref[...] = through_ref[8 * half :, :]


def start_other_kernel(half, rest_ref, factor_ref, earlier_ref, out_ref):
    for j in range(half):
        at = state_rows(j)
        earlier = factor_ref[8 * j : 8 * j + 1, :] * earlier_ref[at, :].astype(F32)
        out_ref[at, :] = (rest_ref[at, :].astype(F32) + earlier).astype(BF16)


def norm_kernel(half, rows, scaled_ref, intra_ref, gain_ref, mine_ref, other_ref, out_ref):
    for i, (owner, state_ref) in enumerate(zip((side(), 1 - side()), (mine_ref, other_ref))):
        for j in range(half):
            at = half_at(owner * half + j, HEAD_DIM)
            state = state_ref[state_rows(j), :]
            inter = jnp.dot(scaled_ref[rows, at], state, preferred_element_type=F32)
            attended = intra_ref[rows, at].astype(F32) + inter
            mean_square = jnp.mean(attended * attended, axis=-1, keepdims=True)
            normed = (attended * lax.rsqrt(mean_square + 1e-06) * gain_ref[:, at]).astype(BF16)
            to = (i * half + j) * HEAD_DIM
            out_ref[:, to : to + HEAD_DIM] = normed


def share(pair, weights):
    rows = weights[0].shape[0] // 2
    total = None
    for i, owner in enumerate((side(), 1 - side())):
        at = half_at(owner, rows)
        for normed_ref, weight_ref in zip(pair, weights):
            normed = normed_ref[:, i * rows : (i + 1) * rows]
            part = jnp.dot(normed, weight_ref[at, :], preferred_element_type=F32)
            total = part if total is None else total + part
    return total


def fetch(step, whole, held, sems):
    copies = []
    for i, (weight, ref) in enumerate(zip(whole, held)):
        at = half_at(lax.axis_index("tp") ^ step, ref.shape[1])
        copies.append(pltpu.make_async_copy(weight.at[:, at], ref, sems.at[i]))
        copies[i].start()
    return copies


def fetch_kernel(weight_hbm, other_weight_hbm, _, weight_ref, other_weight_ref, sems):
    for copy in fetch(2, (weight_hbm, other_weight_hbm), (weight_ref, other_weight_ref), sems):
        copy.wait()


def far_kernel(mine_ref, other_ref, weight_ref, other_weight_ref, out_ref):
    out_ref[...] = share((mine_ref, other_ref), (weight_ref, other_weight_ref)).astype(BF16)


def near_kernel(chunks, residual_hbm, weight_hbm, other_weight_hbm, *refs):
    out_ref, residual_ref, *weights, sems = refs[-5:]
    copies = fetch(0, (weight_hbm, other_weight_hbm), weights, sems)
    copies.append(pltpu.make_async_copy(residual_hbm, residual_ref, sems.at[2]))
    copies[2].start()
    for copy in copies:
        copy.wait()
    for i, rows in enumerate(chunks):
        near = share(refs[2 * i : 2 * i + 2], weights)
        out_ref[rows, :] = residual_ref[rows, :].astype(F32) + near


def nothing_kernel(out_hbm):
    pass


def add_kernel(chunks, near_ref, *refs):
    far, (out_hbm, out_ref, sems) = refs[: len(chunks)], refs[-3:]
    copies = []
    for i, rows in enumerate(chunks):
        out_ref[rows, :] = (near_ref[rows, :] + far[i][...].astype(F32)).astype(BF16)
        copies.append(
            pltpu.make_async_copy(out_ref.at[rows, :], out_hbm.at[rows, :], sems.at[i])
        )
        copies[-1].start()
    for copy in copies:
        copy.wait()


def call(kernel, out_shape, in_specs, name, out_specs=None, scratch=(), cost=0, aliases={}):
    single = isinstance(out_shape, jax.ShapeDtypeStruct)
    if out_specs is None:
        out_specs = VMEM if single else (VMEM,) * len(out_shape)
    cost = pl.CostEstimate(
        flops=cost, bytes_accessed=2_000_000 if cost else 0, transcendentals=0
    )
    return pl.pallas_call(
        kernel,
        out_shape=out_shape,
        in_specs=in_specs,
        out_specs=out_specs,
        scratch_shapes=scratch,
        input_output_aliases=aliases,
        compiler_params=PARAMS,
        cost_estimate=cost,
        name=name,
    )


def earlier_groups(total, again, half, devices):
    groups = devices // MEMBERS

    def swap(message, step):
        return lax.ppermute(message, "seq", [(i, i ^ step) for i in range(devices)])

    if groups == 2:
        return swap(total, MEMBERS), swap(again, MEMBERS + 1)

    def shift(message, by):
        moves = [(i, i + by * MEMBERS) for i in range(devices - by * MEMBERS)]
        return lax.ppermute(message, "seq", moves)

    rows = half * HEAD_DIM
    held = shift(total, 1)
    by = 1
    while by < groups - 1:
        before = shift(held, by)
        decays = rows_to_decays(held[rows:], half)
        factor = jnp.concatenate([jnp.broadcast_to(d, (HEAD_DIM, HEAD_DIM)) for d in decays])
        state = held[:rows].astype(F32) + factor * before[:rows].astype(F32)
        through = [a * b for a, b in zip(decays, rows_to_decays(before[rows:], half))]
        held = jnp.concatenate([state.astype(BF16), decays_to_rows(through)], axis=0)
        by *= 2
    return held, swap(held, 1)


def on_device(
    residual, query_vectors, key_vectors, value_vectors, log_decay, norm_gain, out_weight
):
    tokens, width = residual.shape
    heads = log_decay.shape[0]
    half = heads // 2
    devices = lax.axis_size("seq")
    tp = lax.axis_size("tp")
    wide = (tokens, heads * HEAD_DIM)
    out_width = out_weight.shape[1] // tp
    states = (half * HEAD_DIM, HEAD_DIM)
    near_pairs = [(i, i ^ 1) for i in range(tp)]
    far_pairs = [(i, i ^ 2) for i in range(tp)]
    shape = jax.ShapeDtypeStruct
    message = shape((half * HEAD_DIM + DECAY_ROWS, HEAD_DIM), BF16)

    def swap(piece, step):
        return lax.ppermute(piece, "seq", [(i, i ^ step) for i in range(devices)])

    other_weight = lax.ppermute(out_weight, "tp", near_pairs)
    arguments = (log_decay, key_vectors, value_vectors, query_vectors, norm_gain.reshape(1, -1))
    theirs, mine, decays, keys, values, queries, gain = call(
        functools.partial(state_kernel, half),
        (message, message) + tuple(shape(a.shape, a.dtype) for a in arguments),
        [HBM] * 5,
        "states",
        scratch=[pltpu.SemaphoreType.DMA((5,))],
    )(*(pltpu.with_memory_space_constraint(a, pltpu.HBM) for a in arguments))
    steps = (3, 1, 2, 0)
    received = [swap(theirs, 3), swap(theirs, 1), swap(mine, 2), mine]
    state = shape(states, BF16)
    before, sent, through, total, again = call(
        functools.partial(gather_kernel, half, steps),
        (shape(states, F32), state, shape((heads * 8, HEAD_DIM), F32), message, state),
        [VMEM] * len(steps),
        "gather_states",
        scratch=[pltpu.VMEM((MEMBERS,) + message.shape, BF16)],
    )(*received)
    earlier, other_earlier = earlier_groups(total, again, half, devices)
    inside = swap(sent, 1)
    intra, scaled = call(
        functools.partial(local_kernel, heads),
        (shape(wide, BF16),) * 2,
        [VMEM] * 4,
        "local",
        cost=4 * tokens * tokens * heads * HEAD_DIM,
    )(decays, queries, keys, values)
    block = (out_weight.shape[0], out_width)
    weights = (out_weight, other_weight)
    far_weights = call(
        fetch_kernel,
        (shape(block, BF16),) * 2,
        [ANY] * 2 + [VMEM],
        "fetch_far",
        scratch=[pltpu.SemaphoreType.DMA((2,))],
    )(*weights, scaled)
    mine, rest, factor = call(
        functools.partial(start_kernel, half),
        (state, state, shape((half * 8, HEAD_DIM), F32)),
        [VMEM] * 5,
        "start_states",
    )(before, through, inside, earlier, far_weights[0])
    chunks = [slice(0, tokens // 2), slice(tokens // 2, tokens)]

    def finish(mine, other, out=()):
        pairs, far = [], []
        for i, rows in enumerate(chunks):
            part = call(
                functools.partial(norm_kernel, half, rows),
                shape((rows.stop - rows.start, heads * HEAD_DIM), BF16),
                [VMEM] * 5,
                f"norm_{i}",
            )(scaled, intra, gain, mine, other)
            pairs.append((part, lax.ppermute(part, "tp", near_pairs)))
        for i, rows in enumerate(chunks):
            part = call(
                far_kernel,
                shape((rows.stop - rows.start, out_width), BF16),
                [VMEM] * 4,
                f"project_far_{i}",
            )(*pairs[i], *far_weights)
            far.append(lax.ppermute(part, "tp", far_pairs))
        near = call(
            functools.partial(near_kernel, chunks),
            shape((tokens, out_width), F32),
            [ANY] * 3 + [VMEM] * (2 * len(chunks)),
            "project_near",
            scratch=[
                pltpu.VMEM(residual.shape, BF16),
                pltpu.VMEM(block, BF16),
                pltpu.VMEM(block, BF16),
                pltpu.SemaphoreType.DMA((3,)),
            ],
        )(residual, *weights, *(a for pair in pairs for a in pair))
        return call(
            functools.partial(add_kernel, chunks),
            pltpu.HBM((tokens, out_width), BF16),
            [VMEM] * (1 + len(chunks)) + [HBM] * len(out),
            "add",
            out_specs=HBM,
            scratch=[
                pltpu.VMEM((tokens, out_width), BF16),
                pltpu.SemaphoreType.DMA((len(chunks),)),
            ],
            aliases={1 + len(chunks): 0} if out else {},
        )(near, *far, *out)

    def not_yet():
        return call(
            nothing_kernel, pltpu.HBM((tokens, out_width), BF16), [], "nothing", out_specs=HBM
        )()

    def later_group(out):
        other = call(functools.partial(start_other_kernel, half), state, [VMEM] * 3, "start_other")(
            rest, factor, other_earlier
        )
        return finish(mine, other, (out,))

    first = lax.axis_index("seq") < MEMBERS
    out = lax.cond(first, lambda: finish(mine, rest), not_yet)
    return lax.cond(first, lambda out: out, later_group, out)


def solution(mesh):
    return jax.shard_map(
        on_device,
        mesh=mesh,
        in_specs=(
            P("seq", "tp"),
            P("seq", "tp"),
            P("seq", "tp"),
            P("seq", "tp"),
            P("tp", "seq"),
            P("tp"),
            P("tp", None),
        ),
        out_specs=P("seq", "tp"),
        check_vma=False,
    )
```

```python
import functools

import jax
import jax.numpy as jnp
from jax import lax
from jax.experimental import pallas as pl
from jax.experimental.pallas import tpu as pltpu
from jax.sharding import PartitionSpec as P

HEAD_DIM = 128
GROUP = 256
SCALE = HEAD_DIM ** (-0.5)
F32 = jnp.float32
BF16 = jnp.bfloat16
VMEM = pl.BlockSpec(memory_space=pltpu.VMEM)
HBM = pl.BlockSpec(memory_space=pltpu.HBM)
ANY = pl.BlockSpec(memory_space=pl.ANY)
DECAY_ROWS = 16
MEMBERS = 4
PARAMS = pltpu.CompilerParams(vmem_limit_bytes=24 * 1024 * 1024)


def state_rows(j):
    return slice(j * HEAD_DIM, (j + 1) * HEAD_DIM)


def place():
    return lax.rem(lax.axis_index("seq"), MEMBERS)


def side():
    return lax.rem(lax.axis_index("seq"), 2)


def half_at(owner, size):
    return pl.ds(pl.multiple_of(owner * size, size), size)


def pick(owner, values, axis):
    half = values.shape[axis] // 2
    low = lax.slice_in_dim(values, 0, half, axis=axis)
    high = lax.slice_in_dim(values, half, 2 * half, axis=axis)
    return jnp.where(owner == 0, low, high)


def contract(a, b):
    return lax.dot_general(a, b, (((1,), (1,)), ((), ())), preferred_element_type=F32)


def positions():
    shape = (GROUP, GROUP)
    return lax.broadcasted_iota(jnp.int32, shape, 0), lax.broadcasted_iota(jnp.int32, shape, 1)


def three_terms(values):
    first = values.astype(BF16).astype(F32)
    second = (values - first).astype(BF16).astype(F32)
    third = values - first - second
    return jnp.concatenate([first, second, third], axis=0).astype(BF16)


def sums_down(mask, decays):
    heads = decays.shape[0]
    terms = contract(mask, three_terms(decays))
    return terms[:, :heads] + terms[:, heads : 2 * heads] + terms[:, 2 * heads :]


def sums_across(mask, decays):
    heads = decays.shape[0]
    terms = contract(three_terms(decays), mask)
    return terms[:heads] + terms[heads : 2 * heads] + terms[2 * heads :]


def decays_to_rows(decays):
    each = DECAY_ROWS // (2 * len(decays))
    wide = jnp.concatenate([jnp.broadcast_to(d, (each, HEAD_DIM)) for d in decays], axis=0)
    coarse = wide.astype(BF16).astype(F32)
    return jnp.concatenate([coarse, wide - coarse], axis=0).astype(BF16)


def rows_to_decays(rows, count):
    rows = rows.astype(F32)
    each = DECAY_ROWS // (2 * count)
    both = rows[: DECAY_ROWS // 2] + rows[DECAY_ROWS // 2 :]
    return [both[j * each : j * each + 1] for j in range(count)]


def state_kernel(half, *refs):
    sources, outs, held, sems = refs[:5], refs[5:7], refs[7:12], refs[12]
    copies = [
        pltpu.make_async_copy(source, target, sems.at[i])
        for i, (source, target) in enumerate(zip(sources, held))
    ]
    for copy in copies:
        copy.start()
    decay_ref, key_ref, value_ref = held[:3]
    me = side()
    row, col = positions()
    later = jnp.where(col > row, 1.0, 0.0).astype(BF16)
    copies[0].wait()
    decays = decay_ref[...]
    tail = jnp.exp(sums_across(later, decays))
    whole = jnp.exp(jnp.sum(decays, axis=1, keepdims=True))
    copies[1].wait()
    copies[2].wait()
    decay_rows = decays_to_rows([whole[h : h + 1] for h in range(2 * half)])
    for owner, out_ref in zip((1 - me, me), outs):
        factors = pick(owner, tail, 0)
        for j in range(half):
            at = half_at(owner * half + j, HEAD_DIM)
            weighted = (key_ref[:, at].T.astype(F32) * factors[j : j + 1, :]).astype(BF16)
            update = jnp.dot(weighted, value_ref[:, at], preferred_element_type=F32)
            out_ref[state_rows(j), :] = update.astype(BF16)
        out_ref[half * HEAD_DIM :, :] = decay_rows
    for copy in copies[3:]:
        copy.wait()


def local_kernel(heads, decay_ref, query_ref, key_ref, value_ref, intra_ref, own_ref):
    row, col = positions()
    causal = col <= row
    upto = jnp.where(causal, 1.0, 0.0).astype(BF16)
    decays = decay_ref[...]
    down = sums_down(upto, decays)
    across = sums_across(upto, decays)
    own_ref[...] = jnp.exp(down) * SCALE
    for h in range(heads):
        at = slice(h * HEAD_DIM, (h + 1) * HEAD_DIM)
        scores = contract(query_ref[:, at], key_ref[:, at])
        gaps = down[:, h : h + 1] - across[h : h + 1, :]
        weights = jnp.where(causal, jnp.exp(gaps), 0.0)
        probs = (scores * SCALE * weights).astype(BF16)
        intra_ref[:, at] = jnp.dot(probs, value_ref[:, at], preferred_element_type=F32)


def gather_kernel(half, steps, *refs):
    received, (before_ref, sent_ref, through_ref, total_ref, again_ref, held_ref) = (
        refs[: len(steps)],
        refs[len(steps) :],
    )
    me, upper = place(), side() == 1
    for step, message_ref in zip(steps, received):
        held_ref[me ^ step] = message_ref[...]
    later_pair = me >= 2
    decays = [rows_to_decays(held_ref[m, half * HEAD_DIM :, :], 2 * half) for m in range(MEMBERS)]
    totals = []
    for j in range(2 * half):
        low, high = (j, half + j) if j < half else (j, j - half)
        decay = [jnp.where(upper, d[high], d[low]) for d in decays]
        through = [jnp.ones((1, HEAD_DIM), F32)]
        for m in range(MEMBERS):
            through.append(through[m] * decay[m])
        first, last = [jnp.where(later_pair, through[2 + i], through[i]) for i in range(2)]
        factor = jnp.where(upper, last, first)
        through_ref[j * 8 : (j + 1) * 8, :] = jnp.broadcast_to(factor, (8, HEAD_DIM))
        if j >= half:
            continue
        at = state_rows(j)
        held = [jnp.zeros((HEAD_DIM, HEAD_DIM), F32)]
        for m in range(MEMBERS):
            held.append(held[m] * decay[m] + held_ref[m, at, :].astype(F32))
        first, last = [jnp.where(later_pair, held[2 + i], held[i]) for i in range(2)]
        before_ref[at, :] = jnp.where(upper, last, first)
        sent_ref[at, :] = jnp.where(upper, first, last).astype(BF16)
        total_ref[at, :] = held[MEMBERS].astype(BF16)
        again_ref[at, :] = held[MEMBERS].astype(BF16)
        totals.append(through[MEMBERS])
    total_ref[half * HEAD_DIM :, :] = decays_to_rows(totals)


def start_kernel(half, before_ref, through_ref, inside_ref, earlier_ref, _, *outs):
    mine_ref, rest_ref, factor_ref = outs
    started = lax.axis_index("seq") >= MEMBERS
    for j in range(half):
        at = state_rows(j)
        earlier = jnp.where(started, earlier_ref[at, :].astype(F32), 0.0)
        held = before_ref[at, :] + through_ref[8 * j : 8 * j + 1, :] * earlier
        mine_ref[at, :] = held.astype(BF16)
    rest_ref[...] = inside_ref[...]
    factor_ref[...] = through_ref[8 * half :, :]


def start_other_kernel(half, rest_ref, factor_ref, earlier_ref, out_ref):
    for j in range(half):
        at = state_rows(j)
        earlier = factor_ref[8 * j : 8 * j + 1, :] * earlier_ref[at, :].astype(F32)
        out_ref[at, :] = (rest_ref[at, :].astype(F32) + earlier).astype(BF16)


def norm_kernel(
    half, rows, query_ref, intra_ref, own_ref, gain_ref, mine_ref, other_ref, out_ref
):
    for i, (owner, state_ref) in enumerate(zip((side(), 1 - side()), (mine_ref, other_ref))):
        own = pick(owner, own_ref[rows, :], 1)
        for j in range(half):
            at = half_at(owner * half + j, HEAD_DIM)
            state = state_ref[state_rows(j), :]
            inter = jnp.dot(query_ref[rows, at], state, preferred_element_type=F32)
            attended = intra_ref[rows, at] + own[:, j : j + 1] * inter
            mean_square = jnp.mean(attended * attended, axis=-1, keepdims=True)
            normed = (attended * lax.rsqrt(mean_square + 1e-06) * gain_ref[:, at]).astype(BF16)
            to = (i * half + j) * HEAD_DIM
            out_ref[:, to : to + HEAD_DIM] = normed


def share(pair, weights):
    rows = weights[0].shape[0] // 2
    total = None
    for i, owner in enumerate((side(), 1 - side())):
        at = half_at(owner, rows)
        for normed_ref, weight_ref in zip(pair, weights):
            normed = normed_ref[:, i * rows : (i + 1) * rows]
            part = jnp.dot(normed, weight_ref[at, :], preferred_element_type=F32)
            total = part if total is None else total + part
    return total


def fetch(step, weight_hbm, ref, sem):
    at = half_at(lax.axis_index("tp") ^ step, ref.shape[1])
    copy = pltpu.make_async_copy(weight_hbm.at[:, at], ref, sem)
    copy.start()
    return copy


def fetch_kernel(
    weight_hbm, other_weight_hbm, _, weight_ref, other_weight_ref, near_hbm, near_ref, sems
):
    near = fetch(0, weight_hbm, near_ref, sems.at[2])
    copies = [
        fetch(2, weight_hbm, weight_ref, sems.at[0]),
        fetch(2, other_weight_hbm, other_weight_ref, sems.at[1]),
    ]
    near.wait()
    copies.append(pltpu.make_async_copy(near_ref, near_hbm, sems.at[3]))
    copies[2].start()
    for copy in copies:
        copy.wait()


def far_kernel(mine_ref, other_ref, weight_ref, other_weight_ref, out_ref):
    out_ref[...] = share((mine_ref, other_ref), (weight_ref, other_weight_ref)).astype(BF16)


def near_kernel(chunks, residual_hbm, weight_hbm, other_weight_hbm, *refs):
    out_ref, residual_ref, *weights, sems = refs[-5:]
    copies = [
        pltpu.make_async_copy(residual_hbm, residual_ref, sems.at[2]),
        pltpu.make_async_copy(weight_hbm, weights[0], sems.at[0]),
    ]
    for copy in copies:
        copy.start()
    copies.append(fetch(0, other_weight_hbm, weights[1], sems.at[1]))
    for copy in copies:
        copy.wait()
    for i, rows in enumerate(chunks):
        near = share(refs[2 * i : 2 * i + 2], weights)
        out_ref[rows, :] = residual_ref[rows, :].astype(F32) + near


def nothing_kernel(out_hbm):
    pass


def add_kernel(chunks, near_ref, *refs):
    far, (out_hbm, out_ref, sems) = refs[: len(chunks)], refs[-3:]
    copies = []
    for i, rows in enumerate(chunks):
        out_ref[rows, :] = (near_ref[rows, :] + far[i][...].astype(F32)).astype(BF16)
        copies.append(
            pltpu.make_async_copy(out_ref.at[rows, :], out_hbm.at[rows, :], sems.at[i])
        )
        copies[-1].start()
    for copy in copies:
        copy.wait()


def call(kernel, out_shape, in_specs, name, out_specs=None, scratch=(), cost=0, aliases={}):
    single = isinstance(out_shape, jax.ShapeDtypeStruct)
    if out_specs is None:
        out_specs = VMEM if single else (VMEM,) * len(out_shape)
    cost = pl.CostEstimate(
        flops=cost, bytes_accessed=2_000_000 if cost else 0, transcendentals=0
    )
    return pl.pallas_call(
        kernel,
        out_shape=out_shape,
        in_specs=in_specs,
        out_specs=out_specs,
        scratch_shapes=scratch,
        input_output_aliases=aliases,
        compiler_params=PARAMS,
        cost_estimate=cost,
        name=name,
    )


def earlier_groups(total, again, half, devices):
    groups = devices // MEMBERS

    def swap(message, step):
        return lax.ppermute(message, "seq", [(i, i ^ step) for i in range(devices)])

    if groups == 2:
        return swap(total, MEMBERS), swap(again, MEMBERS + 1)

    def shift(message, by):
        moves = [(i, i + by * MEMBERS) for i in range(devices - by * MEMBERS)]
        return lax.ppermute(message, "seq", moves)

    rows = half * HEAD_DIM
    held = shift(total, 1)
    by = 1
    while by < groups - 1:
        before = shift(held, by)
        decays = rows_to_decays(held[rows:], half)
        factor = jnp.concatenate([jnp.broadcast_to(d, (HEAD_DIM, HEAD_DIM)) for d in decays])
        state = held[:rows].astype(F32) + factor * before[:rows].astype(F32)
        through = [a * b for a, b in zip(decays, rows_to_decays(before[rows:], half))]
        held = jnp.concatenate([state.astype(BF16), decays_to_rows(through)], axis=0)
        by *= 2
    return held, swap(held, 1)


def on_device(
    residual, query_vectors, key_vectors, value_vectors, log_decay, norm_gain, out_weight
):
    tokens, width = residual.shape
    heads = log_decay.shape[0]
    half = heads // 2
    devices = lax.axis_size("seq")
    tp = lax.axis_size("tp")
    wide = (tokens, heads * HEAD_DIM)
    out_width = out_weight.shape[1] // tp
    states = (half * HEAD_DIM, HEAD_DIM)
    near_pairs = [(i, i ^ 1) for i in range(tp)]
    far_pairs = [(i, i ^ 2) for i in range(tp)]
    shape = jax.ShapeDtypeStruct
    message = shape((half * HEAD_DIM + DECAY_ROWS, HEAD_DIM), BF16)

    def swap(piece, step):
        return lax.ppermute(piece, "seq", [(i, i ^ step) for i in range(devices)])

    other_weight = lax.ppermute(out_weight, "tp", near_pairs)
    arguments = (log_decay, key_vectors, value_vectors, query_vectors, norm_gain.reshape(1, -1))
    theirs, mine, decays, keys, values, queries, gain = call(
        functools.partial(state_kernel, half),
        (message, message) + tuple(shape(a.shape, a.dtype) for a in arguments),
        [HBM] * 5,
        "states",
        scratch=[pltpu.SemaphoreType.DMA((5,))],
    )(*(pltpu.with_memory_space_constraint(a, pltpu.HBM) for a in arguments))
    steps = (3, 1, 2, 0)
    received = [swap(theirs, 3), swap(theirs, 1), swap(mine, 2), mine]
    state = shape(states, BF16)
    before, sent, through, total, again = call(
        functools.partial(gather_kernel, half, steps),
        (shape(states, F32), state, shape((heads * 8, HEAD_DIM), F32), message, state),
        [VMEM] * len(steps),
        "gather_states",
        scratch=[pltpu.VMEM((MEMBERS,) + message.shape, BF16)],
    )(*received)
    earlier, other_earlier = earlier_groups(total, again, half, devices)
    inside = swap(sent, 1)
    intra, own = call(
        functools.partial(local_kernel, heads),
        (shape(wide, F32), shape((tokens, heads), F32)),
        [VMEM] * 4,
        "local",
        cost=4 * tokens * tokens * heads * HEAD_DIM,
    )(decays, queries, keys, values)
    block = (out_weight.shape[0], out_width)
    *far_weights, near_weight = call(
        fetch_kernel,
        (shape(block, BF16),) * 2 + (pltpu.HBM(block, BF16),),
        [ANY] * 2 + [VMEM],
        "fetch_weights",
        out_specs=(VMEM, VMEM, HBM),
        scratch=[pltpu.VMEM(block, BF16), pltpu.SemaphoreType.DMA((4,))],
    )(out_weight, other_weight, own)
    mine, rest, factor = call(
        functools.partial(start_kernel, half),
        (state, state, shape((half * 8, HEAD_DIM), F32)),
        [VMEM] * 5,
        "start_states",
    )(before, through, inside, earlier, far_weights[0])
    chunks = [slice(0, tokens // 2), slice(tokens // 2, tokens)]

    def finish(mine, other, out=()):
        pairs, far = [], []
        for i, rows in enumerate(chunks):
            part = call(
                functools.partial(norm_kernel, half, rows),
                shape((rows.stop - rows.start, heads * HEAD_DIM), BF16),
                [VMEM] * 6,
                f"norm_{i}",
            )(queries, intra, own, gain, mine, other)
            pairs.append((part, lax.ppermute(part, "tp", near_pairs)))
        for i, rows in enumerate(chunks):
            part = call(
                far_kernel,
                shape((rows.stop - rows.start, out_width), BF16),
                [VMEM] * 4,
                f"project_far_{i}",
            )(*pairs[i], *far_weights)
            far.append(lax.ppermute(part, "tp", far_pairs))
        near = call(
            functools.partial(near_kernel, chunks),
            shape((tokens, out_width), F32),
            [ANY] * 3 + [VMEM] * (2 * len(chunks)),
            "project_near",
            scratch=[
                pltpu.VMEM(residual.shape, BF16),
                pltpu.VMEM(block, BF16),
                pltpu.VMEM(block, BF16),
                pltpu.SemaphoreType.DMA((3,)),
            ],
        )(residual, near_weight, other_weight, *(a for pair in pairs for a in pair))
        return call(
            functools.partial(add_kernel, chunks),
            pltpu.HBM((tokens, out_width), BF16),
            [VMEM] * (1 + len(chunks)) + [HBM] * len(out),
            "add",
            out_specs=HBM,
            scratch=[
                pltpu.VMEM((tokens, out_width), BF16),
                pltpu.SemaphoreType.DMA((len(chunks),)),
            ],
            aliases={1 + len(chunks): 0} if out else {},
        )(near, *far, *out)

    def not_yet():
        return call(
            nothing_kernel, pltpu.HBM((tokens, out_width), BF16), [], "nothing", out_specs=HBM
        )()

    def later_group(out):
        other = call(functools.partial(start_other_kernel, half), state, [VMEM] * 3, "start_other")(
            rest, factor, other_earlier
        )
        return finish(mine, other, (out,))

    first = lax.axis_index("seq") < MEMBERS
    out = lax.cond(first, lambda: finish(mine, rest), not_yet)
    return lax.cond(first, lambda out: out, later_group, out)


def solution(mesh):
    return jax.shard_map(
        on_device,
        mesh=mesh,
        in_specs=(
            P("seq", "tp"),
            P("seq", "tp"),
            P("seq", "tp"),
            P("seq", "tp"),
            P("tp", "seq"),
            P("tp"),
            P("tp", None),
        ),
        out_specs=P("seq", "tp"),
        check_vma=False,
    )
```

```python
import functools

import jax
import jax.numpy as jnp
from jax import lax
from jax.experimental import pallas as pl
from jax.experimental.pallas import tpu as pltpu
from jax.sharding import PartitionSpec as P

HEAD_DIM = 128
GROUP = 256
SCALE = HEAD_DIM ** (-0.5)
F32 = jnp.float32
BF16 = jnp.bfloat16
VMEM = pl.BlockSpec(memory_space=pltpu.VMEM)
HBM = pl.BlockSpec(memory_space=pltpu.HBM)
ANY = pl.BlockSpec(memory_space=pl.ANY)
DECAY_ROWS = 16
MEMBERS = 4
PARAMS = pltpu.CompilerParams(vmem_limit_bytes=24 * 1024 * 1024)


def state_rows(j):
    return slice(j * HEAD_DIM, (j + 1) * HEAD_DIM)


def place():
    return lax.rem(lax.axis_index("seq"), MEMBERS)


def side():
    return lax.rem(lax.axis_index("seq"), 2)


def half_at(owner, size):
    return pl.ds(pl.multiple_of(owner * size, size), size)


def pick(owner, values, axis):
    half = values.shape[axis] // 2
    low = lax.slice_in_dim(values, 0, half, axis=axis)
    high = lax.slice_in_dim(values, half, 2 * half, axis=axis)
    return jnp.where(owner == 0, low, high)


def contract(a, b):
    return lax.dot_general(a, b, (((1,), (1,)), ((), ())), preferred_element_type=F32)


def positions():
    shape = (GROUP, GROUP)
    return lax.broadcasted_iota(jnp.int32, shape, 0), lax.broadcasted_iota(jnp.int32, shape, 1)


def three_terms(values):
    first = values.astype(BF16).astype(F32)
    second = (values - first).astype(BF16).astype(F32)
    third = values - first - second
    return jnp.concatenate([first, second, third], axis=0).astype(BF16)


def sums_down(mask, decays):
    heads = decays.shape[0]
    terms = contract(mask, three_terms(decays))
    return terms[:, :heads] + terms[:, heads : 2 * heads] + terms[:, 2 * heads :]


def sums_across(mask, decays):
    heads = decays.shape[0]
    terms = contract(three_terms(decays), mask)
    return terms[:heads] + terms[heads : 2 * heads] + terms[2 * heads :]


def decays_to_rows(decays):
    each = DECAY_ROWS // (2 * len(decays))
    wide = jnp.concatenate([jnp.broadcast_to(d, (each, HEAD_DIM)) for d in decays], axis=0)
    coarse = wide.astype(BF16).astype(F32)
    return jnp.concatenate([coarse, wide - coarse], axis=0).astype(BF16)


def rows_to_decays(rows, count):
    rows = rows.astype(F32)
    each = DECAY_ROWS // (2 * count)
    both = rows[: DECAY_ROWS // 2] + rows[DECAY_ROWS // 2 :]
    return [both[j * each : j * each + 1] for j in range(count)]


def state_kernel(half, *refs):
    sources, outs, held, sems = refs[:5], refs[5:7], refs[7:12], refs[12]
    copies = [
        pltpu.make_async_copy(source, target, sems.at[i])
        for i, (source, target) in enumerate(zip(sources, held))
    ]
    for copy in copies:
        copy.start()
    decay_ref, key_ref, value_ref = held[:3]
    me = side()
    row, col = positions()
    later = jnp.where(col > row, 1.0, 0.0).astype(BF16)
    copies[0].wait()
    decays = decay_ref[...]
    tail = jnp.exp(sums_across(later, decays))
    whole = jnp.exp(jnp.sum(decays, axis=1, keepdims=True))
    copies[1].wait()
    copies[2].wait()
    decay_rows = decays_to_rows([whole[h : h + 1] for h in range(2 * half)])
    for owner, out_ref in zip((1 - me, me), outs):
        factors = pick(owner, tail, 0)
        for j in range(half):
            at = half_at(owner * half + j, HEAD_DIM)
            weighted = (key_ref[:, at].T.astype(F32) * factors[j : j + 1, :]).astype(BF16)
            update = jnp.dot(weighted, value_ref[:, at], preferred_element_type=F32)
            out_ref[state_rows(j), :] = update.astype(BF16)
        out_ref[half * HEAD_DIM :, :] = decay_rows
    for copy in copies[3:]:
        copy.wait()


def local_kernel(heads, decay_ref, query_ref, key_ref, value_ref, intra_ref, own_ref):
    row, col = positions()
    causal = col <= row
    upto = jnp.where(causal, 1.0, 0.0).astype(BF16)
    decays = decay_ref[...]
    down = sums_down(upto, decays)
    across = sums_across(upto, decays)
    own_ref[...] = jnp.exp(down) * SCALE
    for h in range(heads):
        at = slice(h * HEAD_DIM, (h + 1) * HEAD_DIM)
        scores = contract(query_ref[:, at], key_ref[:, at])
        gaps = down[:, h : h + 1] - across[h : h + 1, :]
        weights = jnp.where(causal, jnp.exp(gaps), 0.0)
        probs = (scores * SCALE * weights).astype(BF16)
        intra_ref[:, at] = jnp.dot(probs, value_ref[:, at], preferred_element_type=F32)


def gather_kernel(half, steps, *refs):
    received, (before_ref, sent_ref, through_ref, total_ref, again_ref, held_ref) = (
        refs[: len(steps)],
        refs[len(steps) :],
    )
    me, upper = place(), side() == 1
    for step, message_ref in zip(steps, received):
        held_ref[me ^ step] = message_ref[...]
    later_pair = me >= 2
    decays = [rows_to_decays(held_ref[m, half * HEAD_DIM :, :], 2 * half) for m in range(MEMBERS)]
    totals = []
    for j in range(2 * half):
        low, high = (j, half + j) if j < half else (j, j - half)
        decay = [jnp.where(upper, d[high], d[low]) for d in decays]
        through = [jnp.ones((1, HEAD_DIM), F32)]
        for m in range(MEMBERS):
            through.append(through[m] * decay[m])
        first, last = [jnp.where(later_pair, through[2 + i], through[i]) for i in range(2)]
        factor = jnp.where(upper, last, first)
        through_ref[j * 8 : (j + 1) * 8, :] = jnp.broadcast_to(factor, (8, HEAD_DIM))
        if j >= half:
            continue
        at = state_rows(j)
        held = [jnp.zeros((HEAD_DIM, HEAD_DIM), F32)]
        for m in range(MEMBERS):
            held.append(held[m] * decay[m] + held_ref[m, at, :].astype(F32))
        first, last = [jnp.where(later_pair, held[2 + i], held[i]) for i in range(2)]
        before_ref[at, :] = jnp.where(upper, last, first)
        sent_ref[at, :] = jnp.where(upper, first, last).astype(BF16)
        total_ref[at, :] = held[MEMBERS].astype(BF16)
        again_ref[at, :] = held[MEMBERS].astype(BF16)
        totals.append(through[MEMBERS])
    total_ref[half * HEAD_DIM :, :] = decays_to_rows(totals)


def start_kernel(half, before_ref, through_ref, inside_ref, earlier_ref, _, *outs):
    mine_ref, rest_ref, factor_ref = outs
    started = lax.axis_index("seq") >= MEMBERS
    for j in range(half):
        at = state_rows(j)
        earlier = jnp.where(started, earlier_ref[at, :].astype(F32), 0.0)
        held = before_ref[at, :] + through_ref[8 * j : 8 * j + 1, :] * earlier
        mine_ref[at, :] = held.astype(BF16)
    rest_ref[...] = inside_ref[...]
    factor_ref[...] = through_ref[8 * half :, :]


def start_other_kernel(half, rest_ref, factor_ref, earlier_ref, out_ref):
    for j in range(half):
        at = state_rows(j)
        earlier = factor_ref[8 * j : 8 * j + 1, :] * earlier_ref[at, :].astype(F32)
        out_ref[at, :] = (rest_ref[at, :].astype(F32) + earlier).astype(BF16)


def norm_kernel(
    half, rows, query_ref, intra_ref, own_ref, gain_ref, mine_ref, other_ref, out_ref
):
    for i, (owner, state_ref) in enumerate(zip((side(), 1 - side()), (mine_ref, other_ref))):
        own = pick(owner, own_ref[rows, :], 1)
        for j in range(half):
            at = half_at(owner * half + j, HEAD_DIM)
            state = state_ref[state_rows(j), :]
            inter = jnp.dot(query_ref[rows, at], state, preferred_element_type=F32)
            attended = intra_ref[rows, at] + own[:, j : j + 1] * inter
            mean_square = jnp.mean(attended * attended, axis=-1, keepdims=True)
            normed = (attended * lax.rsqrt(mean_square + 1e-06) * gain_ref[:, at]).astype(BF16)
            to = (i * half + j) * HEAD_DIM
            out_ref[:, to : to + HEAD_DIM] = normed


def share(pair, weights):
    rows = weights[0].shape[0] // 2
    total = None
    for i, owner in enumerate((side(), 1 - side())):
        at = half_at(owner, rows)
        for normed_ref, weight_ref in zip(pair, weights):
            normed = normed_ref[:, i * rows : (i + 1) * rows]
            part = jnp.dot(normed, weight_ref[at, :], preferred_element_type=F32)
            total = part if total is None else total + part
    return total


def fetch(step, weight_hbm, ref, sem):
    at = half_at(lax.axis_index("tp") ^ step, ref.shape[1])
    copy = pltpu.make_async_copy(weight_hbm.at[:, at], ref, sem)
    copy.start()
    return copy


def fetch_kernel(
    weight_hbm, other_weight_hbm, _, weight_ref, other_weight_ref, near_hbm, near_ref, sems
):
    near = fetch(0, weight_hbm, near_ref, sems.at[2])
    copies = [
        fetch(2, weight_hbm, weight_ref, sems.at[0]),
        fetch(2, other_weight_hbm, other_weight_ref, sems.at[1]),
    ]
    near.wait()
    copies.append(pltpu.make_async_copy(near_ref, near_hbm, sems.at[3]))
    copies[2].start()
    for copy in copies:
        copy.wait()


def far_kernel(mine_ref, other_ref, weight_ref, other_weight_ref, out_ref):
    out_ref[...] = share((mine_ref, other_ref), (weight_ref, other_weight_ref)).astype(BF16)


def near_kernel(chunks, residual_hbm, weight_hbm, other_weight_hbm, *refs):
    out_ref, residual_ref, *weights, sems = refs[-5:]
    copies = [
        pltpu.make_async_copy(residual_hbm, residual_ref, sems.at[2]),
        pltpu.make_async_copy(weight_hbm, weights[0], sems.at[0]),
    ]
    for copy in copies:
        copy.start()
    copies.append(fetch(0, other_weight_hbm, weights[1], sems.at[1]))
    for copy in copies:
        copy.wait()
    for i, rows in enumerate(chunks):
        near = share(refs[2 * i : 2 * i + 2], weights)
        out_ref[rows, :] = residual_ref[rows, :].astype(F32) + near


def nothing_kernel(out_hbm):
    pass


def add_kernel(chunks, near_ref, *refs):
    far, (out_hbm, out_ref, sems) = refs[: len(chunks)], refs[-3:]
    copies = []
    for i, rows in enumerate(chunks):
        out_ref[rows, :] = (near_ref[rows, :] + far[i][...].astype(F32)).astype(BF16)
        copies.append(
            pltpu.make_async_copy(out_ref.at[rows, :], out_hbm.at[rows, :], sems.at[i])
        )
        copies[-1].start()
    for copy in copies:
        copy.wait()


def call(kernel, out_shape, in_specs, name, out_specs=None, scratch=(), cost=0, aliases={}):
    single = isinstance(out_shape, jax.ShapeDtypeStruct)
    if out_specs is None:
        out_specs = VMEM if single else (VMEM,) * len(out_shape)
    cost = pl.CostEstimate(
        flops=cost, bytes_accessed=2_000_000 if cost else 0, transcendentals=0
    )
    return pl.pallas_call(
        kernel,
        out_shape=out_shape,
        in_specs=in_specs,
        out_specs=out_specs,
        scratch_shapes=scratch,
        input_output_aliases=aliases,
        compiler_params=PARAMS,
        cost_estimate=cost,
        name=name,
    )


def earlier_groups(total, again, half, devices):
    groups = devices // MEMBERS

    def swap(message, step):
        return lax.ppermute(message, "seq", [(i, i ^ step) for i in range(devices)])

    if groups == 2:
        return swap(total, MEMBERS), swap(again, MEMBERS + 1)

    def shift(message, by):
        moves = [(i, i + by * MEMBERS) for i in range(devices - by * MEMBERS)]
        return lax.ppermute(message, "seq", moves)

    rows = half * HEAD_DIM
    held = shift(total, 1)
    by = 1
    while by < groups - 1:
        before = shift(held, by)
        decays = rows_to_decays(held[rows:], half)
        factor = jnp.concatenate([jnp.broadcast_to(d, (HEAD_DIM, HEAD_DIM)) for d in decays])
        state = held[:rows].astype(F32) + factor * before[:rows].astype(F32)
        through = [a * b for a, b in zip(decays, rows_to_decays(before[rows:], half))]
        held = jnp.concatenate([state.astype(BF16), decays_to_rows(through)], axis=0)
        by *= 2
    return held, swap(held, 1)


def on_device(
    residual, query_vectors, key_vectors, value_vectors, log_decay, norm_gain, out_weight
):
    tokens, width = residual.shape
    heads = log_decay.shape[0]
    half = heads // 2
    devices = lax.axis_size("seq")
    tp = lax.axis_size("tp")
    wide = (tokens, heads * HEAD_DIM)
    out_width = out_weight.shape[1] // tp
    states = (half * HEAD_DIM, HEAD_DIM)
    near_pairs = [(i, i ^ 1) for i in range(tp)]
    far_pairs = [(i, i ^ 2) for i in range(tp)]
    shape = jax.ShapeDtypeStruct
    message = shape((half * HEAD_DIM + DECAY_ROWS, HEAD_DIM), BF16)

    def swap(piece, step):
        return lax.ppermute(piece, "seq", [(i, i ^ step) for i in range(devices)])

    other_weight = lax.ppermute(out_weight, "tp", near_pairs)
    arguments = (log_decay, key_vectors, value_vectors, query_vectors, norm_gain.reshape(1, -1))
    theirs, mine, decays, keys, values, queries, gain = call(
        functools.partial(state_kernel, half),
        (message, message) + tuple(shape(a.shape, a.dtype) for a in arguments),
        [HBM] * 5,
        "states",
        scratch=[pltpu.SemaphoreType.DMA((5,))],
    )(*(pltpu.with_memory_space_constraint(a, pltpu.HBM) for a in arguments))
    steps = (3, 1, 2, 0)
    received = [swap(theirs, 3), swap(theirs, 1), swap(mine, 2), mine]
    state = shape(states, BF16)
    before, sent, through, total, again = call(
        functools.partial(gather_kernel, half, steps),
        (shape(states, F32), state, shape((heads * 8, HEAD_DIM), F32), message, state),
        [VMEM] * len(steps),
        "gather_states",
        scratch=[pltpu.VMEM((MEMBERS,) + message.shape, BF16)],
    )(*received)
    earlier, other_earlier = earlier_groups(total, again, half, devices)
    inside = swap(sent, 1)
    intra, own = call(
        functools.partial(local_kernel, heads),
        (shape(wide, F32), shape((tokens, heads), F32)),
        [VMEM] * 4,
        "local",
        cost=4 * tokens * tokens * heads * HEAD_DIM,
    )(decays, queries, keys, values)
    block = (out_weight.shape[0], out_width)
    *far_weights, near_weight = call(
        fetch_kernel,
        (shape(block, BF16),) * 2 + (pltpu.HBM(block, BF16),),
        [HBM, ANY, VMEM],
        "fetch_weights",
        out_specs=(VMEM, VMEM, HBM),
        scratch=[pltpu.VMEM(block, BF16), pltpu.SemaphoreType.DMA((4,))],
    )(
        pltpu.with_memory_space_constraint(out_weight, pltpu.HBM), other_weight, own
    )
    mine, rest, factor = call(
        functools.partial(start_kernel, half),
        (state, state, shape((half * 8, HEAD_DIM), F32)),
        [VMEM] * 5,
        "start_states",
    )(before, through, inside, earlier, far_weights[0])
    chunks = [slice(0, tokens // 2), slice(tokens // 2, tokens)]

    def finish(mine, other, out=()):
        pairs, far = [], []
        for i, rows in enumerate(chunks):
            part = call(
                functools.partial(norm_kernel, half, rows),
                shape((rows.stop - rows.start, heads * HEAD_DIM), BF16),
                [VMEM] * 6,
                f"norm_{i}",
            )(queries, intra, own, gain, mine, other)
            pairs.append((part, lax.ppermute(part, "tp", near_pairs)))
        for i, rows in enumerate(chunks):
            part = call(
                far_kernel,
                shape((rows.stop - rows.start, out_width), BF16),
                [VMEM] * 4,
                f"project_far_{i}",
            )(*pairs[i], *far_weights)
            far.append(lax.ppermute(part, "tp", far_pairs))
        near = call(
            functools.partial(near_kernel, chunks),
            shape((tokens, out_width), F32),
            [ANY] * 3 + [VMEM] * (2 * len(chunks)),
            "project_near",
            scratch=[
                pltpu.VMEM(residual.shape, BF16),
                pltpu.VMEM(block, BF16),
                pltpu.VMEM(block, BF16),
                pltpu.SemaphoreType.DMA((3,)),
            ],
        )(residual, near_weight, other_weight, *(a for pair in pairs for a in pair))
        return call(
            functools.partial(add_kernel, chunks),
            pltpu.HBM((tokens, out_width), BF16),
            [VMEM] * (1 + len(chunks)) + [HBM] * len(out),
            "add",
            out_specs=HBM,
            scratch=[
                pltpu.VMEM((tokens, out_width), BF16),
                pltpu.SemaphoreType.DMA((len(chunks),)),
            ],
            aliases={1 + len(chunks): 0} if out else {},
        )(near, *far, *out)

    def not_yet():
        return call(
            nothing_kernel, pltpu.HBM((tokens, out_width), BF16), [], "nothing", out_specs=HBM
        )()

    def later_group(out):
        other = call(functools.partial(start_other_kernel, half), state, [VMEM] * 3, "start_other")(
            rest, factor, other_earlier
        )
        return finish(mine, other, (out,))

    first = lax.axis_index("seq") < MEMBERS
    out = lax.cond(first, lambda: finish(mine, rest), not_yet)
    return lax.cond(first, lambda out: out, later_group, out)


def solution(mesh):
    return jax.shard_map(
        on_device,
        mesh=mesh,
        in_specs=(
            P("seq", "tp"),
            P("seq", "tp"),
            P("seq", "tp"),
            P("seq", "tp"),
            P("tp", "seq"),
            P("tp"),
            P("tp", None),
        ),
        out_specs=P("seq", "tp"),
        check_vma=False,
    )
```

```python
import functools

import jax
import jax.numpy as jnp
from jax import lax
from jax.experimental import pallas as pl
from jax.experimental.pallas import tpu as pltpu
from jax.sharding import PartitionSpec as P

HEAD_DIM = 128
GROUP = 256
SCALE = HEAD_DIM ** (-0.5)
F32 = jnp.float32
BF16 = jnp.bfloat16
VMEM = pl.BlockSpec(memory_space=pltpu.VMEM)
HBM = pl.BlockSpec(memory_space=pltpu.HBM)
ANY = pl.BlockSpec(memory_space=pl.ANY)
DECAY_ROWS = 16
MEMBERS = 4
PARAMS = pltpu.CompilerParams(vmem_limit_bytes=24 * 1024 * 1024)


def state_rows(j):
    return slice(j * HEAD_DIM, (j + 1) * HEAD_DIM)


def place():
    return lax.rem(lax.axis_index("seq"), MEMBERS)


def side():
    return lax.rem(lax.axis_index("seq"), 2)


def half_at(owner, size):
    return pl.ds(pl.multiple_of(owner * size, size), size)


def pick(owner, values, axis):
    half = values.shape[axis] // 2
    low = lax.slice_in_dim(values, 0, half, axis=axis)
    high = lax.slice_in_dim(values, half, 2 * half, axis=axis)
    return jnp.where(owner == 0, low, high)


def contract(a, b):
    return lax.dot_general(a, b, (((1,), (1,)), ((), ())), preferred_element_type=F32)


def positions():
    shape = (GROUP, GROUP)
    return lax.broadcasted_iota(jnp.int32, shape, 0), lax.broadcasted_iota(jnp.int32, shape, 1)


def three_terms(values):
    first = values.astype(BF16).astype(F32)
    second = (values - first).astype(BF16).astype(F32)
    third = values - first - second
    return jnp.concatenate([first, second, third], axis=0).astype(BF16)


def sums_down(mask, decays):
    heads = decays.shape[0]
    terms = contract(mask, three_terms(decays))
    return terms[:, :heads] + terms[:, heads : 2 * heads] + terms[:, 2 * heads :]


def sums_across(mask, decays):
    heads = decays.shape[0]
    terms = contract(three_terms(decays), mask)
    return terms[:heads] + terms[heads : 2 * heads] + terms[2 * heads :]


def decays_to_rows(decays):
    each = DECAY_ROWS // (2 * len(decays))
    wide = jnp.concatenate([jnp.broadcast_to(d, (each, HEAD_DIM)) for d in decays], axis=0)
    coarse = wide.astype(BF16).astype(F32)
    return jnp.concatenate([coarse, wide - coarse], axis=0).astype(BF16)


def rows_to_decays(rows, count):
    rows = rows.astype(F32)
    each = DECAY_ROWS // (2 * count)
    both = rows[: DECAY_ROWS // 2] + rows[DECAY_ROWS // 2 :]
    return [both[j * each : j * each + 1] for j in range(count)]


def state_kernel(half, *refs):
    sources, outs, held, sems = refs[:5], refs[5:7], refs[7:12], refs[12]
    copies = [
        pltpu.make_async_copy(source, target, sems.at[i])
        for i, (source, target) in enumerate(zip(sources, held))
    ]
    for copy in copies:
        copy.start()
    decay_ref, key_ref, value_ref = held[:3]
    me = side()
    row, col = positions()
    later = jnp.where(col > row, 1.0, 0.0).astype(BF16)
    copies[0].wait()
    decays = decay_ref[...]
    tail = jnp.exp(sums_across(later, decays))
    whole = jnp.exp(jnp.sum(decays, axis=1, keepdims=True))
    copies[1].wait()
    copies[2].wait()
    decay_rows = decays_to_rows([whole[h : h + 1] for h in range(2 * half)])
    for owner, out_ref in zip((1 - me, me), outs):
        factors = pick(owner, tail, 0)
        for j in range(half):
            at = half_at(owner * half + j, HEAD_DIM)
            weighted = (key_ref[:, at].T.astype(F32) * factors[j : j + 1, :]).astype(BF16)
            update = jnp.dot(weighted, value_ref[:, at], preferred_element_type=F32)
            out_ref[state_rows(j), :] = update.astype(BF16)
        out_ref[half * HEAD_DIM :, :] = decay_rows
    for copy in copies[3:]:
        copy.wait()


def local_kernel(heads, decay_ref, query_ref, key_ref, value_ref, intra_ref, own_ref):
    row, col = positions()
    causal = col <= row
    upto = jnp.where(causal, 1.0, 0.0).astype(BF16)
    decays = decay_ref[...]
    down = sums_down(upto, decays)
    across = sums_across(upto, decays)
    own_ref[...] = jnp.exp(down) * SCALE
    for h in range(heads):
        at = slice(h * HEAD_DIM, (h + 1) * HEAD_DIM)
        scores = contract(query_ref[:, at], key_ref[:, at])
        gaps = down[:, h : h + 1] - across[h : h + 1, :]
        weights = jnp.where(causal, jnp.exp(gaps), 0.0)
        probs = (scores * SCALE * weights).astype(BF16)
        intra_ref[:, at] = jnp.dot(probs, value_ref[:, at], preferred_element_type=F32)


def gather_kernel(half, steps, *refs):
    received, (before_ref, sent_ref, through_ref, total_ref, again_ref, held_ref) = (
        refs[: len(steps)],
        refs[len(steps) :],
    )
    me, upper = place(), side() == 1
    for step, message_ref in zip(steps, received):
        held_ref[me ^ step] = message_ref[...]
    later_pair = me >= 2
    decays = [rows_to_decays(held_ref[m, half * HEAD_DIM :, :], 2 * half) for m in range(MEMBERS)]
    totals = []
    for j in range(2 * half):
        low, high = (j, half + j) if j < half else (j, j - half)
        decay = [jnp.where(upper, d[high], d[low]) for d in decays]
        through = [jnp.ones((1, HEAD_DIM), F32)]
        for m in range(MEMBERS):
            through.append(through[m] * decay[m])
        first, last = [jnp.where(later_pair, through[2 + i], through[i]) for i in range(2)]
        factor = jnp.where(upper, last, first)
        through_ref[j * 8 : (j + 1) * 8, :] = jnp.broadcast_to(factor, (8, HEAD_DIM))
        if j >= half:
            continue
        at = state_rows(j)
        held = [jnp.zeros((HEAD_DIM, HEAD_DIM), F32)]
        for m in range(MEMBERS):
            held.append(held[m] * decay[m] + held_ref[m, at, :].astype(F32))
        first, last = [jnp.where(later_pair, held[2 + i], held[i]) for i in range(2)]
        before_ref[at, :] = jnp.where(upper, last, first)
        sent_ref[at, :] = jnp.where(upper, first, last).astype(BF16)
        total_ref[at, :] = held[MEMBERS].astype(BF16)
        again_ref[at, :] = held[MEMBERS].astype(BF16)
        totals.append(through[MEMBERS])
    total_ref[half * HEAD_DIM :, :] = decays_to_rows(totals)


def start_kernel(half, before_ref, through_ref, inside_ref, earlier_ref, _, *outs):
    mine_ref, rest_ref, factor_ref = outs
    started = lax.axis_index("seq") >= MEMBERS
    for j in range(half):
        at = state_rows(j)
        earlier = jnp.where(started, earlier_ref[at, :].astype(F32), 0.0)
        held = before_ref[at, :] + through_ref[8 * j : 8 * j + 1, :] * earlier
        mine_ref[at, :] = held.astype(BF16)
    rest_ref[...] = inside_ref[...]
    factor_ref[...] = through_ref[8 * half :, :]


def start_other_kernel(half, rest_ref, factor_ref, earlier_ref, out_ref):
    for j in range(half):
        at = state_rows(j)
        earlier = factor_ref[8 * j : 8 * j + 1, :] * earlier_ref[at, :].astype(F32)
        out_ref[at, :] = (rest_ref[at, :].astype(F32) + earlier).astype(BF16)


def norm_kernel(
    half, rows, query_ref, intra_ref, own_ref, gain_ref, mine_ref, other_ref, out_ref
):
    for i, (owner, state_ref) in enumerate(zip((side(), 1 - side()), (mine_ref, other_ref))):
        own = pick(owner, own_ref[rows, :], 1)
        for j in range(half):
            at = half_at(owner * half + j, HEAD_DIM)
            state = state_ref[state_rows(j), :]
            inter = jnp.dot(query_ref[rows, at], state, preferred_element_type=F32)
            attended = intra_ref[rows, at] + own[:, j : j + 1] * inter
            mean_square = jnp.mean(attended * attended, axis=-1, keepdims=True)
            normed = (attended * lax.rsqrt(mean_square + 1e-06) * gain_ref[:, at]).astype(BF16)
            to = (i * half + j) * HEAD_DIM
            out_ref[:, to : to + HEAD_DIM] = normed


def share(pair, weights):
    rows = weights[0].shape[0] // 2
    total = None
    for i, owner in enumerate((side(), 1 - side())):
        at = half_at(owner, rows)
        for normed_ref, weight_ref in zip(pair, weights):
            normed = normed_ref[:, i * rows : (i + 1) * rows]
            part = jnp.dot(normed, weight_ref[at, :], preferred_element_type=F32)
            total = part if total is None else total + part
    return total


def fetch(step, whole, held, sems):
    copies = []
    for i, (weight, ref) in enumerate(zip(whole, held)):
        at = half_at(lax.axis_index("tp") ^ step, ref.shape[1])
        copies.append(pltpu.make_async_copy(weight.at[:, at], ref, sems.at[i]))
        copies[i].start()
    return copies


def fetch_kernel(weight_hbm, other_weight_hbm, _, weight_ref, other_weight_ref, sems):
    for copy in fetch(2, (weight_hbm, other_weight_hbm), (weight_ref, other_weight_ref), sems):
        copy.wait()


def far_kernel(mine_ref, other_ref, weight_ref, other_weight_ref, out_ref):
    out_ref[...] = share((mine_ref, other_ref), (weight_ref, other_weight_ref)).astype(BF16)


def near_kernel(chunks, residual_hbm, weight_hbm, other_weight_hbm, *refs):
    out_ref, residual_ref, *weights, sems = refs[-5:]
    copies = fetch(0, (weight_hbm, other_weight_hbm), weights, sems)
    copies.append(pltpu.make_async_copy(residual_hbm, residual_ref, sems.at[2]))
    copies[2].start()
    for copy in copies:
        copy.wait()
    for i, rows in enumerate(chunks):
        near = share(refs[2 * i : 2 * i + 2], weights)
        out_ref[rows, :] = residual_ref[rows, :].astype(F32) + near


def nothing_kernel(out_hbm):
    pass


def add_kernel(chunks, near_ref, *refs):
    far, (out_hbm, out_ref, sems) = refs[: len(chunks)], refs[-3:]
    copies = []
    for i, rows in enumerate(chunks):
        out_ref[rows, :] = (near_ref[rows, :] + far[i][...].astype(F32)).astype(BF16)
        copies.append(
            pltpu.make_async_copy(out_ref.at[rows, :], out_hbm.at[rows, :], sems.at[i])
        )
        copies[-1].start()
    for copy in copies:
        copy.wait()


def call(kernel, out_shape, in_specs, name, out_specs=None, scratch=(), cost=0, aliases={}):
    single = isinstance(out_shape, jax.ShapeDtypeStruct)
    if out_specs is None:
        out_specs = VMEM if single else (VMEM,) * len(out_shape)
    cost = pl.CostEstimate(
        flops=cost, bytes_accessed=2_000_000 if cost else 0, transcendentals=0
    )
    return pl.pallas_call(
        kernel,
        out_shape=out_shape,
        in_specs=in_specs,
        out_specs=out_specs,
        scratch_shapes=scratch,
        input_output_aliases=aliases,
        compiler_params=PARAMS,
        cost_estimate=cost,
        name=name,
    )


def earlier_groups(total, again, half, devices):
    groups = devices // MEMBERS

    def swap(message, step):
        return lax.ppermute(message, "seq", [(i, i ^ step) for i in range(devices)])

    if groups == 2:
        return swap(total, MEMBERS), swap(again, MEMBERS + 1)

    def shift(message, by):
        moves = [(i, i + by * MEMBERS) for i in range(devices - by * MEMBERS)]
        return lax.ppermute(message, "seq", moves)

    rows = half * HEAD_DIM
    held = shift(total, 1)
    by = 1
    while by < groups - 1:
        before = shift(held, by)
        decays = rows_to_decays(held[rows:], half)
        factor = jnp.concatenate([jnp.broadcast_to(d, (HEAD_DIM, HEAD_DIM)) for d in decays])
        state = held[:rows].astype(F32) + factor * before[:rows].astype(F32)
        through = [a * b for a, b in zip(decays, rows_to_decays(before[rows:], half))]
        held = jnp.concatenate([state.astype(BF16), decays_to_rows(through)], axis=0)
        by *= 2
    return held, swap(held, 1)


def on_device(
    residual, query_vectors, key_vectors, value_vectors, log_decay, norm_gain, out_weight
):
    tokens, width = residual.shape
    heads = log_decay.shape[0]
    half = heads // 2
    devices = lax.axis_size("seq")
    tp = lax.axis_size("tp")
    wide = (tokens, heads * HEAD_DIM)
    out_width = out_weight.shape[1] // tp
    states = (half * HEAD_DIM, HEAD_DIM)
    near_pairs = [(i, i ^ 1) for i in range(tp)]
    far_pairs = [(i, i ^ 2) for i in range(tp)]
    shape = jax.ShapeDtypeStruct
    message = shape((half * HEAD_DIM + DECAY_ROWS, HEAD_DIM), BF16)

    def swap(piece, step):
        return lax.ppermute(piece, "seq", [(i, i ^ step) for i in range(devices)])

    other_weight = lax.ppermute(out_weight, "tp", near_pairs)
    arguments = (log_decay, key_vectors, value_vectors, query_vectors, norm_gain.reshape(1, -1))
    theirs, mine, decays, keys, values, queries, gain = call(
        functools.partial(state_kernel, half),
        (message, message) + tuple(shape(a.shape, a.dtype) for a in arguments),
        [HBM] * 5,
        "states",
        scratch=[pltpu.SemaphoreType.DMA((5,))],
    )(*(pltpu.with_memory_space_constraint(a, pltpu.HBM) for a in arguments))
    steps = (3, 1, 2, 0)
    received = [swap(theirs, 3), swap(theirs, 1), swap(mine, 2), mine]
    state = shape(states, BF16)
    before, sent, through, total, again = call(
        functools.partial(gather_kernel, half, steps),
        (shape(states, F32), state, shape((heads * 8, HEAD_DIM), F32), message, state),
        [VMEM] * len(steps),
        "gather_states",
        scratch=[pltpu.VMEM((MEMBERS,) + message.shape, BF16)],
    )(*received)
    earlier, other_earlier = earlier_groups(total, again, half, devices)
    inside = swap(sent, 1)
    intra, own = call(
        functools.partial(local_kernel, heads),
        (shape(wide, F32), shape((tokens, heads), F32)),
        [VMEM] * 4,
        "local",
        cost=4 * tokens * tokens * heads * HEAD_DIM,
    )(decays, queries, keys, values)
    block = (out_weight.shape[0], out_width)
    weights = (out_weight, other_weight)
    far_weights = call(
        fetch_kernel,
        (shape(block, BF16),) * 2,
        [ANY] * 2 + [VMEM],
        "fetch_far",
        scratch=[pltpu.SemaphoreType.DMA((2,))],
    )(*weights, own)
    mine, rest, factor = call(
        functools.partial(start_kernel, half),
        (state, state, shape((half * 8, HEAD_DIM), F32)),
        [VMEM] * 5,
        "start_states",
    )(before, through, inside, earlier, far_weights[0])
    chunks = [slice(0, tokens // 2), slice(tokens // 2, tokens)]

    def finish(mine, other, out=()):
        pairs, far = [], []
        for i, rows in enumerate(chunks):
            part = call(
                functools.partial(norm_kernel, half, rows),
                shape((rows.stop - rows.start, heads * HEAD_DIM), BF16),
                [VMEM] * 6,
                f"norm_{i}",
                cost=1000000000,
            )(queries, intra, own, gain, mine, other)
            pairs.append((part, lax.ppermute(part, "tp", near_pairs)))
        for i, rows in enumerate(chunks):
            part = call(
                far_kernel,
                shape((rows.stop - rows.start, out_width), BF16),
                [VMEM] * 4,
                f"project_far_{i}",
                cost=1000000000,
            )(*pairs[i], *far_weights)
            far.append(lax.ppermute(part, "tp", far_pairs))
        near = call(
            functools.partial(near_kernel, chunks),
            shape((tokens, out_width), F32),
            [ANY] * 3 + [VMEM] * (2 * len(chunks)),
            "project_near",
            scratch=[
                pltpu.VMEM(residual.shape, BF16),
                pltpu.VMEM(block, BF16),
                pltpu.VMEM(block, BF16),
                pltpu.SemaphoreType.DMA((3,)),
            ],
        )(residual, *weights, *(a for pair in pairs for a in pair))
        return call(
            functools.partial(add_kernel, chunks),
            pltpu.HBM((tokens, out_width), BF16),
            [VMEM] * (1 + len(chunks)) + [HBM] * len(out),
            "add",
            out_specs=HBM,
            scratch=[
                pltpu.VMEM((tokens, out_width), BF16),
                pltpu.SemaphoreType.DMA((len(chunks),)),
            ],
            aliases={1 + len(chunks): 0} if out else {},
        )(near, *far, *out)

    def not_yet():
        return call(
            nothing_kernel, pltpu.HBM((tokens, out_width), BF16), [], "nothing", out_specs=HBM
        )()

    def later_group(out):
        other = call(functools.partial(start_other_kernel, half), state, [VMEM] * 3, "start_other")(
            rest, factor, other_earlier
        )
        return finish(mine, other, (out,))

    first = lax.axis_index("seq") < MEMBERS
    out = lax.cond(first, lambda: finish(mine, rest), not_yet)
    return lax.cond(first, lambda out: out, later_group, out)


def solution(mesh):
    return jax.shard_map(
        on_device,
        mesh=mesh,
        in_specs=(
            P("seq", "tp"),
            P("seq", "tp"),
            P("seq", "tp"),
            P("seq", "tp"),
            P("tp", "seq"),
            P("tp"),
            P("tp", None),
        ),
        out_specs=P("seq", "tp"),
        check_vma=False,
    )
```

```python
import functools

import jax
import jax.numpy as jnp
from jax import lax
from jax.experimental import pallas as pl
from jax.experimental.pallas import tpu as pltpu
from jax.sharding import PartitionSpec as P

HEAD_DIM = 128
GROUP = 256
SCALE = HEAD_DIM ** (-0.5)
F32 = jnp.float32
BF16 = jnp.bfloat16
VMEM = pl.BlockSpec(memory_space=pltpu.VMEM)
HBM = pl.BlockSpec(memory_space=pltpu.HBM)
DECAY_ROWS = 16
MEMBERS = 4
PARAMS = pltpu.CompilerParams(vmem_limit_bytes=24 * 1024 * 1024)


def state_rows(j):
    return slice(j * HEAD_DIM, (j + 1) * HEAD_DIM)


def place():
    return lax.rem(lax.axis_index("seq"), MEMBERS)


def side():
    return lax.rem(lax.axis_index("seq"), 2)


def half_at(owner, size):
    return pl.ds(pl.multiple_of(owner * size, size), size)


def pick(owner, values, axis):
    half = values.shape[axis] // 2
    low = lax.slice_in_dim(values, 0, half, axis=axis)
    high = lax.slice_in_dim(values, half, 2 * half, axis=axis)
    return jnp.where(owner == 0, low, high)


def contract(a, b):
    return lax.dot_general(a, b, (((1,), (1,)), ((), ())), preferred_element_type=F32)


def positions():
    shape = (GROUP, GROUP)
    return lax.broadcasted_iota(jnp.int32, shape, 0), lax.broadcasted_iota(jnp.int32, shape, 1)


def three_terms(values):
    first = values.astype(BF16).astype(F32)
    second = (values - first).astype(BF16).astype(F32)
    third = values - first - second
    return jnp.concatenate([first, second, third], axis=0).astype(BF16)


def sums_down(mask, decays):
    heads = decays.shape[0]
    terms = contract(mask, three_terms(decays))
    return terms[:, :heads] + terms[:, heads : 2 * heads] + terms[:, 2 * heads :]


def sums_across(mask, decays):
    heads = decays.shape[0]
    terms = contract(three_terms(decays), mask)
    return terms[:heads] + terms[heads : 2 * heads] + terms[2 * heads :]


def decays_to_rows(decays):
    each = DECAY_ROWS // (2 * len(decays))
    wide = jnp.concatenate([jnp.broadcast_to(d, (each, HEAD_DIM)) for d in decays], axis=0)
    coarse = wide.astype(BF16).astype(F32)
    return jnp.concatenate([coarse, wide - coarse], axis=0).astype(BF16)


def rows_to_decays(rows, count):
    rows = rows.astype(F32)
    each = DECAY_ROWS // (2 * count)
    both = rows[: DECAY_ROWS // 2] + rows[DECAY_ROWS // 2 :]
    return [both[j * each : j * each + 1] for j in range(count)]


def state_kernel(half, *refs):
    sources, outs, held, sems = refs[:5], refs[5:7], refs[7:12], refs[12]
    copies = [
        pltpu.make_async_copy(source, target, sems.at[i])
        for i, (source, target) in enumerate(zip(sources, held))
    ]
    for copy in copies:
        copy.start()
    decay_ref, key_ref, value_ref = held[:3]
    me = side()
    row, col = positions()
    later = jnp.where(col > row, 1.0, 0.0).astype(BF16)
    copies[0].wait()
    decays = decay_ref[...]
    tail = jnp.exp(sums_across(later, decays))
    whole = jnp.exp(jnp.sum(decays, axis=1, keepdims=True))
    copies[1].wait()
    copies[2].wait()
    decay_rows = decays_to_rows([whole[h : h + 1] for h in range(2 * half)])
    for owner, out_ref in zip((1 - me, me), outs):
        factors = pick(owner, tail, 0)
        for j in range(half):
            at = half_at(owner * half + j, HEAD_DIM)
            weighted = (key_ref[:, at].T.astype(F32) * factors[j : j + 1, :]).astype(BF16)
            update = jnp.dot(weighted, value_ref[:, at], preferred_element_type=F32)
            out_ref[state_rows(j), :] = update.astype(BF16)
        out_ref[half * HEAD_DIM :, :] = decay_rows
    for copy in copies[3:]:
        copy.wait()


def local_kernel(heads, decay_ref, query_ref, key_ref, value_ref, intra_ref, own_ref):
    row, col = positions()
    causal = col <= row
    upto = jnp.where(causal, 1.0, 0.0).astype(BF16)
    decays = decay_ref[...]
    down = sums_down(upto, decays)
    across = sums_across(upto, decays)
    own_ref[...] = jnp.exp(down) * SCALE
    for h in range(heads):
        at = slice(h * HEAD_DIM, (h + 1) * HEAD_DIM)
        scores = contract(query_ref[:, at], key_ref[:, at])
        gaps = down[:, h : h + 1] - across[h : h + 1, :]
        weights = jnp.where(causal, jnp.exp(gaps), 0.0)
        probs = (scores * SCALE * weights).astype(BF16)
        intra_ref[:, at] = jnp.dot(probs, value_ref[:, at], preferred_element_type=F32)


def gather_kernel(half, steps, *refs):
    received, (before_ref, sent_ref, through_ref, total_ref, held_ref) = (
        refs[: len(steps)],
        refs[len(steps) :],
    )
    me, upper = place(), side() == 1
    for step, message_ref in zip(steps, received):
        held_ref[me ^ step] = message_ref[...]
    later_pair = me >= 2
    decays = [rows_to_decays(held_ref[m, half * HEAD_DIM :, :], 2 * half) for m in range(MEMBERS)]
    totals = []
    for j in range(2 * half):
        low, high = (j, half + j) if j < half else (j, j - half)
        decay = [jnp.where(upper, d[high], d[low]) for d in decays]
        through = [jnp.ones((1, HEAD_DIM), F32)]
        for m in range(MEMBERS):
            through.append(through[m] * decay[m])
        first, last = [jnp.where(later_pair, through[2 + i], through[i]) for i in range(2)]
        factor = jnp.where(upper, last, first)
        through_ref[j * 8 : (j + 1) * 8, :] = jnp.broadcast_to(factor, (8, HEAD_DIM))
        if j >= half:
            continue
        at = state_rows(j)
        held = [jnp.zeros((HEAD_DIM, HEAD_DIM), F32)]
        for m in range(MEMBERS):
            held.append(held[m] * decay[m] + held_ref[m, at, :].astype(F32))
        first, last = [jnp.where(later_pair, held[2 + i], held[i]) for i in range(2)]
        before_ref[at, :] = jnp.where(upper, last, first)
        sent_ref[at, :] = jnp.where(upper, first, last).astype(BF16)
        total_ref[at, :] = held[MEMBERS].astype(BF16)
        totals.append(through[MEMBERS])
    total_ref[half * HEAD_DIM :, :] = decays_to_rows(totals)


def start_kernel(half, before_ref, through_ref, inside_ref, earlier_ref, _, *outs):
    mine_ref, rest_ref, factor_ref, sent_ref = outs
    started = lax.axis_index("seq") >= MEMBERS
    for j in range(half):
        at = state_rows(j)
        earlier = jnp.where(started, earlier_ref[at, :].astype(F32), 0.0)
        held = before_ref[at, :] + through_ref[8 * j : 8 * j + 1, :] * earlier
        mine_ref[at, :] = held.astype(BF16)
    rest_ref[...] = inside_ref[...]
    factor_ref[...] = through_ref[8 * half :, :]
    sent_ref[...] = earlier_ref[...]


def start_other_kernel(half, rest_ref, factor_ref, earlier_ref, _, out_ref):
    for j in range(half):
        at = state_rows(j)
        earlier = factor_ref[8 * j : 8 * j + 1, :] * earlier_ref[at, :].astype(F32)
        out_ref[at, :] = (rest_ref[at, :].astype(F32) + earlier).astype(BF16)


def norm_kernel(half, halves, rows, query_ref, intra_ref, own_ref, gain_ref, *refs):
    states, out_ref = refs[: len(halves)], refs[-1]
    for i, (mine, state_ref) in enumerate(zip(halves, states)):
        owner = side() if mine else 1 - side()
        own = pick(owner, own_ref[rows, :], 1)
        for j in range(half):
            at = half_at(owner * half + j, HEAD_DIM)
            state = state_ref[state_rows(j), :]
            inter = jnp.dot(query_ref[rows, at], state, preferred_element_type=F32)
            attended = intra_ref[rows, at] + own[:, j : j + 1] * inter
            mean_square = jnp.mean(attended * attended, axis=-1, keepdims=True)
            normed = (attended * lax.rsqrt(mean_square + 1e-06) * gain_ref[:, at]).astype(BF16)
            to = (i * half + j) * HEAD_DIM
            out_ref[:, to : to + HEAD_DIM] = normed


def share(halves, pair, weights):
    rows = weights[0].shape[0] // 2
    total = None
    for i, mine in enumerate(halves):
        at = half_at(side() if mine else 1 - side(), rows)
        for normed_ref, weight_ref in zip(pair, weights):
            normed = normed_ref[:, i * rows : (i + 1) * rows]
            part = jnp.dot(normed, weight_ref[at, :], preferred_element_type=F32)
            total = part if total is None else total + part
    return total


def fetch(step, whole, held, sems):
    copies = []
    for i, (weight, ref) in enumerate(zip(whole, held)):
        at = half_at(lax.axis_index("tp") ^ step, ref.shape[1])
        copies.append(pltpu.make_async_copy(weight.at[:, at], ref, sems.at[i]))
        copies[i].start()
    return copies


def fetch_kernel(weight_hbm, other_weight_hbm, _, weight_ref, other_weight_ref, sems):
    for copy in fetch(2, (weight_hbm, other_weight_hbm), (weight_ref, other_weight_ref), sems):
        copy.wait()


def far_mine_kernel(chunks, weight_ref, other_weight_ref, *refs):
    for i, rows in enumerate(chunks):
        pair = refs[2 * i : 2 * i + 2]
        refs[-1][rows, :] = share((True,), pair, (weight_ref, other_weight_ref))


def far_kernel(rows, begun_ref, mine_ref, other_ref, weight_ref, other_weight_ref, out_ref):
    rest = share((False,), (mine_ref, other_ref), (weight_ref, other_weight_ref))
    out_ref[...] = (begun_ref[rows, :] + rest).astype(BF16)


def far_all_kernel(mine_ref, other_ref, weight_ref, other_weight_ref, out_ref):
    pair, weights = (mine_ref, other_ref), (weight_ref, other_weight_ref)
    out_ref[...] = share((True, False), pair, weights).astype(BF16)


def near_kernel(chunks, passes, residual_hbm, weight_hbm, other_weight_hbm, *refs):
    out_ref, residual_ref, *weights, sems = refs[-5:]
    copies = fetch(0, (weight_hbm, other_weight_hbm), weights, sems)
    copies.append(pltpu.make_async_copy(residual_hbm, residual_ref, sems.at[2]))
    copies[2].start()
    for copy in copies:
        copy.wait()
    pairs = iter(zip(refs[0:-5:2], refs[1:-5:2]))
    for rows in chunks:
        near = residual_ref[rows, :].astype(F32)
        for halves in passes:
            near = near + share(halves, next(pairs), weights)
        out_ref[rows, :] = near


def add_kernel(chunks, near_ref, *refs):
    far, (out_hbm, out_ref, sems) = refs[: len(chunks)], refs[len(chunks) :]
    copies = []
    for i, rows in enumerate(chunks):
        out_ref[rows, :] = (near_ref[rows, :] + far[i][...].astype(F32)).astype(BF16)
        copies.append(
            pltpu.make_async_copy(out_ref.at[rows, :], out_hbm.at[rows, :], sems.at[i])
        )
        copies[-1].start()
    for copy in copies:
        copy.wait()


def call(kernel, out_shape, in_specs, name, out_specs=None, scratch=(), cost=0):
    single = isinstance(out_shape, jax.ShapeDtypeStruct)
    if out_specs is None:
        out_specs = VMEM if single else (VMEM,) * len(out_shape)
    cost = pl.CostEstimate(
        flops=cost, bytes_accessed=2_000_000 if cost else 0, transcendentals=0
    )
    return pl.pallas_call(
        kernel,
        out_shape=out_shape,
        in_specs=in_specs,
        out_specs=out_specs,
        scratch_shapes=scratch,
        compiler_params=PARAMS,
        cost_estimate=cost,
        name=name,
    )


def earlier_groups(total, half, devices):
    groups = devices // MEMBERS
    if groups == 2:
        return lax.ppermute(total, "seq", [(i, i ^ MEMBERS) for i in range(devices)])

    def shift(message, by):
        moves = [(i, i + by * MEMBERS) for i in range(devices - by * MEMBERS)]
        return lax.ppermute(message, "seq", moves)

    rows = half * HEAD_DIM
    held = shift(total, 1)
    by = 1
    while by < groups - 1:
        before = shift(held, by)
        decays = rows_to_decays(held[rows:], half)
        factor = jnp.concatenate([jnp.broadcast_to(d, (HEAD_DIM, HEAD_DIM)) for d in decays])
        state = held[:rows].astype(F32) + factor * before[:rows].astype(F32)
        through = [a * b for a, b in zip(decays, rows_to_decays(before[rows:], half))]
        held = jnp.concatenate([state.astype(BF16), decays_to_rows(through)], axis=0)
        by *= 2
    return held


def on_device(
    residual, query_vectors, key_vectors, value_vectors, log_decay, norm_gain, out_weight
):
    tokens, width = residual.shape
    heads = log_decay.shape[0]
    half = heads // 2
    devices = lax.axis_size("seq")
    tp = lax.axis_size("tp")
    wide = (tokens, heads * HEAD_DIM)
    out_width = out_weight.shape[1] // tp
    states = (half * HEAD_DIM, HEAD_DIM)
    near_pairs = [(i, i ^ 1) for i in range(tp)]
    far_pairs = [(i, i ^ 2) for i in range(tp)]
    shape = jax.ShapeDtypeStruct
    message = shape((half * HEAD_DIM + DECAY_ROWS, HEAD_DIM), BF16)

    def swap(piece, step):
        return lax.ppermute(piece, "seq", [(i, i ^ step) for i in range(devices)])

    other_weight = lax.ppermute(out_weight, "tp", near_pairs)
    weight = pltpu.with_memory_space_constraint(out_weight, pltpu.HBM)
    arguments = (log_decay, key_vectors, value_vectors, query_vectors, norm_gain.reshape(1, -1))
    theirs, mine, decays, keys, values, queries, gain = call(
        functools.partial(state_kernel, half),
        (message, message) + tuple(shape(a.shape, a.dtype) for a in arguments),
        [HBM] * 5,
        "states",
        scratch=[pltpu.SemaphoreType.DMA((5,))],
    )(*(pltpu.with_memory_space_constraint(a, pltpu.HBM) for a in arguments))
    steps = (3, 1, 2, 0)
    received = [swap(theirs, 3), swap(theirs, 1), swap(mine, 2), mine]
    state = shape(states, BF16)
    before, sent, through, total = call(
        functools.partial(gather_kernel, half, steps),
        (shape(states, F32), state, shape((heads * 8, HEAD_DIM), F32), message),
        [VMEM] * len(steps),
        "gather_states",
        scratch=[pltpu.VMEM((MEMBERS,) + message.shape, BF16)],
    )(*received)
    earlier = earlier_groups(total, half, devices)
    inside = swap(sent, 1)
    intra, own = call(
        functools.partial(local_kernel, heads),
        (shape(wide, F32), shape((tokens, heads), F32)),
        [VMEM] * 4,
        "local",
        cost=4 * tokens * tokens * heads * HEAD_DIM,
    )(decays, queries, keys, values)
    mine, rest, factor, sent = call(
        functools.partial(start_kernel, half),
        (state, state, shape((half * 8, HEAD_DIM), F32), message),
        [VMEM] * 5,
        "start_states",
    )(before, through, inside, earlier, own)

    chunks = [slice(0, tokens // 2), slice(tokens // 2, tokens)]
    block = (out_weight.shape[0], out_width)
    weights = (weight, other_weight)
    weight_specs = [HBM, pl.BlockSpec(memory_space=pl.ANY)]

    def normed(name, halves, rows, *states):
        part = call(
            functools.partial(norm_kernel, half, halves, rows),
            shape((rows.stop - rows.start, len(halves) * half * HEAD_DIM), BF16),
            [VMEM] * (4 + len(states)),
            name,
        )(queries, intra, own, gain, *states)
        return part, lax.ppermute(part, "tp", near_pairs)

    def far_columns(after):
        return call(
            fetch_kernel,
            (shape(block, BF16),) * 2,
            weight_specs + [VMEM],
            "fetch_far",
            scratch=[pltpu.SemaphoreType.DMA((2,))],
        )(*weights, after)

    def send_far(i, kernel, *operands):
        part = call(
            kernel,
            shape((chunks[i].stop - chunks[i].start, out_width), BF16),
            [VMEM] * len(operands),
            f"project_far_{i}",
        )(*operands)
        return lax.ppermute(part, "tp", far_pairs)

    def finish(passes, pairs, far):
        near = call(
            functools.partial(near_kernel, chunks, passes),
            shape((tokens, out_width), F32),
            [HBM] + weight_specs + [VMEM] * (2 * len(pairs)),
            "project_near",
            scratch=[
                pltpu.VMEM(residual.shape, BF16),
                pltpu.VMEM(block, BF16),
                pltpu.VMEM(block, BF16),
                pltpu.SemaphoreType.DMA((3,)),
            ],
        )(
            pltpu.with_memory_space_constraint(residual, pltpu.HBM),
            *weights,
            *(a for pair in pairs for a in pair),
        )
        return call(
            functools.partial(add_kernel, chunks),
            pltpu.HBM((tokens, out_width), BF16),
            [VMEM] * (1 + len(chunks)),
            "add",
            out_specs=HBM,
            scratch=[
                pltpu.VMEM((tokens, out_width), BF16),
                pltpu.SemaphoreType.DMA((len(chunks),)),
            ],
        )(near, *far)

    def first_group():
        both = (True, False)
        pairs = [normed(f"norm_{i}", both, rows, mine, rest) for i, rows in enumerate(chunks)]
        far_weights = far_columns(pairs[-1][0])
        far = [send_far(i, far_all_kernel, *pairs[i], *far_weights) for i in range(len(chunks))]
        return finish((both,), pairs, far)

    def later_group():
        swapped = swap(sent, 1)
        begun = [normed(f"norm_mine_{i}", (True,), rows, mine) for i, rows in enumerate(chunks)]
        far_weights = far_columns(begun[-1][0])
        far_begun = call(
            functools.partial(far_mine_kernel, chunks),
            shape((tokens, out_width), F32),
            [VMEM] * (2 + 2 * len(chunks)),
            "project_far_mine",
        )(*far_weights, *(a for pair in begun for a in pair))
        other = call(functools.partial(start_other_kernel, half), state, [VMEM] * 4, "start_other")(
            rest, factor, swapped, far_begun
        )
        parts = [normed(f"norm_{i}", (False,), rows, other) for i, rows in enumerate(chunks)]
        far = [
            send_far(i, functools.partial(far_kernel, rows), far_begun, *parts[i], *far_weights)
            for i, rows in enumerate(chunks)
        ]
        pairs = [pair for i in range(len(chunks)) for pair in (begun[i], parts[i])]
        return finish(((True,), (False,)), pairs, far)

    return lax.cond(lax.axis_index("seq") < MEMBERS, first_group, later_group)


def solution(mesh):
    return jax.shard_map(
        on_device,
        mesh=mesh,
        in_specs=(
            P("seq", "tp"),
            P("seq", "tp"),
            P("seq", "tp"),
            P("seq", "tp"),
            P("tp", "seq"),
            P("tp"),
            P("tp", None),
        ),
        out_specs=P("seq", "tp"),
        check_vma=False,
    )
```

```python
import functools

import jax
import jax.numpy as jnp
from jax import lax
from jax.experimental import pallas as pl
from jax.experimental.pallas import tpu as pltpu
from jax.sharding import PartitionSpec as P

HEAD_DIM = 128
GROUP = 256
SCALE = HEAD_DIM ** (-0.5)
F32 = jnp.float32
BF16 = jnp.bfloat16
VMEM = pl.BlockSpec(memory_space=pltpu.VMEM)
HBM = pl.BlockSpec(memory_space=pltpu.HBM)
DECAY_ROWS = 16
MEMBERS = 4
PARAMS = pltpu.CompilerParams(vmem_limit_bytes=24 * 1024 * 1024)


def state_rows(j):
    return slice(j * HEAD_DIM, (j + 1) * HEAD_DIM)


def place():
    return lax.rem(lax.axis_index("seq"), MEMBERS)


def side():
    return lax.rem(lax.axis_index("seq"), 2)


def half_at(owner, size):
    return pl.ds(pl.multiple_of(owner * size, size), size)


def pick(owner, values, axis):
    half = values.shape[axis] // 2
    low = lax.slice_in_dim(values, 0, half, axis=axis)
    high = lax.slice_in_dim(values, half, 2 * half, axis=axis)
    return jnp.where(owner == 0, low, high)


def contract(a, b):
    return lax.dot_general(a, b, (((1,), (1,)), ((), ())), preferred_element_type=F32)


def positions():
    shape = (GROUP, GROUP)
    return lax.broadcasted_iota(jnp.int32, shape, 0), lax.broadcasted_iota(jnp.int32, shape, 1)


def three_terms(values):
    first = values.astype(BF16).astype(F32)
    second = (values - first).astype(BF16).astype(F32)
    third = values - first - second
    return jnp.concatenate([first, second, third], axis=0).astype(BF16)


def sums_down(mask, decays):
    heads = decays.shape[0]
    terms = contract(mask, three_terms(decays))
    return terms[:, :heads] + terms[:, heads : 2 * heads] + terms[:, 2 * heads :]


def sums_across(mask, decays):
    heads = decays.shape[0]
    terms = contract(three_terms(decays), mask)
    return terms[:heads] + terms[heads : 2 * heads] + terms[2 * heads :]


def decays_to_rows(decays):
    each = DECAY_ROWS // (2 * len(decays))
    wide = jnp.concatenate([jnp.broadcast_to(d, (each, HEAD_DIM)) for d in decays], axis=0)
    coarse = wide.astype(BF16).astype(F32)
    return jnp.concatenate([coarse, wide - coarse], axis=0).astype(BF16)


def rows_to_decays(rows, count):
    rows = rows.astype(F32)
    each = DECAY_ROWS // (2 * count)
    both = rows[: DECAY_ROWS // 2] + rows[DECAY_ROWS // 2 :]
    return [both[j * each : j * each + 1] for j in range(count)]


def state_kernel(half, *refs):
    sources, outs, held, sems = refs[:5], refs[5:7], refs[7:12], refs[12]
    copies = [
        pltpu.make_async_copy(source, target, sems.at[i])
        for i, (source, target) in enumerate(zip(sources, held))
    ]
    for copy in copies:
        copy.start()
    decay_ref, key_ref, value_ref = held[:3]
    me = side()
    row, col = positions()
    later = jnp.where(col > row, 1.0, 0.0).astype(BF16)
    copies[0].wait()
    decays = decay_ref[...]
    tail = jnp.exp(sums_across(later, decays))
    whole = jnp.exp(jnp.sum(decays, axis=1, keepdims=True))
    copies[1].wait()
    copies[2].wait()
    decay_rows = decays_to_rows([whole[h : h + 1] for h in range(2 * half)])
    for owner, out_ref in zip((1 - me, me), outs):
        factors = pick(owner, tail, 0)
        for j in range(half):
            at = half_at(owner * half + j, HEAD_DIM)
            weighted = (key_ref[:, at].T.astype(F32) * factors[j : j + 1, :]).astype(BF16)
            update = jnp.dot(weighted, value_ref[:, at], preferred_element_type=F32)
            out_ref[state_rows(j), :] = update.astype(BF16)
        out_ref[half * HEAD_DIM :, :] = decay_rows
    for copy in copies[3:]:
        copy.wait()


def local_kernel(heads, decay_ref, query_ref, key_ref, value_ref, intra_ref, own_ref):
    row, col = positions()
    causal = col <= row
    upto = jnp.where(causal, 1.0, 0.0).astype(BF16)
    decays = decay_ref[...]
    down = sums_down(upto, decays)
    across = sums_across(upto, decays)
    own_ref[...] = jnp.exp(down) * SCALE
    for h in range(heads):
        at = slice(h * HEAD_DIM, (h + 1) * HEAD_DIM)
        scores = contract(query_ref[:, at], key_ref[:, at])
        gaps = down[:, h : h + 1] - across[h : h + 1, :]
        weights = jnp.where(causal, jnp.exp(gaps), 0.0)
        probs = (scores * SCALE * weights).astype(BF16)
        intra_ref[:, at] = jnp.dot(probs, value_ref[:, at], preferred_element_type=F32)


def gather_kernel(half, steps, *refs):
    received, (before_ref, sent_ref, through_ref, total_ref, held_ref) = (
        refs[: len(steps)],
        refs[len(steps) :],
    )
    me, upper = place(), side() == 1
    for step, message_ref in zip(steps, received):
        held_ref[me ^ step] = message_ref[...]
    later_pair = me >= 2
    decays = [rows_to_decays(held_ref[m, half * HEAD_DIM :, :], 2 * half) for m in range(MEMBERS)]
    totals = []
    for j in range(2 * half):
        low, high = (j, half + j) if j < half else (j, j - half)
        decay = [jnp.where(upper, d[high], d[low]) for d in decays]
        through = [jnp.ones((1, HEAD_DIM), F32)]
        for m in range(MEMBERS):
            through.append(through[m] * decay[m])
        first, last = [jnp.where(later_pair, through[2 + i], through[i]) for i in range(2)]
        factor = jnp.where(upper, last, first)
        through_ref[j * 8 : (j + 1) * 8, :] = jnp.broadcast_to(factor, (8, HEAD_DIM))
        if j >= half:
            continue
        at = state_rows(j)
        held = [jnp.zeros((HEAD_DIM, HEAD_DIM), F32)]
        for m in range(MEMBERS):
            held.append(held[m] * decay[m] + held_ref[m, at, :].astype(F32))
        first, last = [jnp.where(later_pair, held[2 + i], held[i]) for i in range(2)]
        before_ref[at, :] = jnp.where(upper, last, first)
        sent_ref[at, :] = jnp.where(upper, first, last).astype(BF16)
        total_ref[at, :] = held[MEMBERS].astype(BF16)
        totals.append(through[MEMBERS])
    total_ref[half * HEAD_DIM :, :] = decays_to_rows(totals)


def start_kernel(half, before_ref, through_ref, inside_ref, earlier_ref, _, *outs):
    mine_ref, rest_ref, factor_ref, sent_ref = outs
    started = lax.axis_index("seq") >= MEMBERS
    for j in range(half):
        at = state_rows(j)
        earlier = jnp.where(started, earlier_ref[at, :].astype(F32), 0.0)
        held = before_ref[at, :] + through_ref[8 * j : 8 * j + 1, :] * earlier
        mine_ref[at, :] = held.astype(BF16)
    rest_ref[...] = inside_ref[...]
    factor_ref[...] = through_ref[8 * half :, :]
    sent_ref[...] = earlier_ref[...]


def start_other_kernel(half, rest_ref, factor_ref, earlier_ref, _, out_ref):
    for j in range(half):
        at = state_rows(j)
        earlier = factor_ref[8 * j : 8 * j + 1, :] * earlier_ref[at, :].astype(F32)
        out_ref[at, :] = (rest_ref[at, :].astype(F32) + earlier).astype(BF16)


def norm_kernel(half, halves, rows, query_ref, intra_ref, own_ref, gain_ref, *refs):
    states, out_ref = refs[: len(halves)], refs[-1]
    for i, (mine, state_ref) in enumerate(zip(halves, states)):
        owner = side() if mine else 1 - side()
        own = pick(owner, own_ref[rows, :], 1)
        for j in range(half):
            at = half_at(owner * half + j, HEAD_DIM)
            state = state_ref[state_rows(j), :]
            inter = jnp.dot(query_ref[rows, at], state, preferred_element_type=F32)
            attended = intra_ref[rows, at] + own[:, j : j + 1] * inter
            mean_square = jnp.mean(attended * attended, axis=-1, keepdims=True)
            normed = (attended * lax.rsqrt(mean_square + 1e-06) * gain_ref[:, at]).astype(BF16)
            to = (i * half + j) * HEAD_DIM
            out_ref[:, to : to + HEAD_DIM] = normed


def share(halves, pair, weights):
    rows = weights[0].shape[0] // 2
    total = None
    for i, mine in enumerate(halves):
        at = half_at(side() if mine else 1 - side(), rows)
        for normed_ref, weight_ref in zip(pair, weights):
            normed = normed_ref[:, i * rows : (i + 1) * rows]
            part = jnp.dot(normed, weight_ref[at, :], preferred_element_type=F32)
            total = part if total is None else total + part
    return total


def fetch(step, whole, held, sems):
    copies = []
    for i, (weight, ref) in enumerate(zip(whole, held)):
        at = half_at(lax.axis_index("tp") ^ step, ref.shape[1])
        copies.append(pltpu.make_async_copy(weight.at[:, at], ref, sems.at[i]))
        copies[i].start()
    return copies


def fetch_kernel(weight_hbm, other_weight_hbm, _, weight_ref, other_weight_ref, sems):
    for copy in fetch(2, (weight_hbm, other_weight_hbm), (weight_ref, other_weight_ref), sems):
        copy.wait()


def far_mine_kernel(chunks, weight_ref, other_weight_ref, *refs):
    for i, rows in enumerate(chunks):
        pair = refs[2 * i : 2 * i + 2]
        refs[-1][rows, :] = share((True,), pair, (weight_ref, other_weight_ref))


def far_kernel(rows, begun_ref, mine_ref, other_ref, weight_ref, other_weight_ref, out_ref):
    rest = share((False,), (mine_ref, other_ref), (weight_ref, other_weight_ref))
    out_ref[...] = (begun_ref[rows, :] + rest).astype(BF16)


def far_all_kernel(mine_ref, other_ref, weight_ref, other_weight_ref, out_ref):
    pair, weights = (mine_ref, other_ref), (weight_ref, other_weight_ref)
    out_ref[...] = share((True, False), pair, weights).astype(BF16)


def near_kernel(chunks, passes, residual_hbm, weight_hbm, other_weight_hbm, *refs):
    out_ref, residual_ref, *weights, sems = refs[-5:]
    copies = fetch(0, (weight_hbm, other_weight_hbm), weights, sems)
    copies.append(pltpu.make_async_copy(residual_hbm, residual_ref, sems.at[2]))
    copies[2].start()
    for copy in copies:
        copy.wait()
    pairs = iter(zip(refs[0:-5:2], refs[1:-5:2]))
    for rows in chunks:
        near = residual_ref[rows, :].astype(F32)
        for halves in passes:
            near = near + share(halves, next(pairs), weights)
        out_ref[rows, :] = near


def add_kernel(chunks, near_ref, *refs):
    far, (out_hbm, out_ref, sems) = refs[: len(chunks)], refs[len(chunks) :]
    copies = []
    for i, rows in enumerate(chunks):
        out_ref[rows, :] = (near_ref[rows, :] + far[i][...].astype(F32)).astype(BF16)
        copies.append(
            pltpu.make_async_copy(out_ref.at[rows, :], out_hbm.at[rows, :], sems.at[i])
        )
        copies[-1].start()
    for copy in copies:
        copy.wait()


def call(kernel, out_shape, in_specs, name, out_specs=None, scratch=(), cost=0):
    single = isinstance(out_shape, jax.ShapeDtypeStruct)
    if out_specs is None:
        out_specs = VMEM if single else (VMEM,) * len(out_shape)
    cost = pl.CostEstimate(
        flops=cost, bytes_accessed=2_000_000 if cost else 0, transcendentals=0
    )
    return pl.pallas_call(
        kernel,
        out_shape=out_shape,
        in_specs=in_specs,
        out_specs=out_specs,
        scratch_shapes=scratch,
        compiler_params=PARAMS,
        cost_estimate=cost,
        name=name,
    )


def earlier_groups(total, half, devices):
    groups = devices // MEMBERS
    if groups == 2:
        return lax.ppermute(total, "seq", [(i, i ^ MEMBERS) for i in range(devices)])

    def shift(message, by):
        moves = [(i, i + by * MEMBERS) for i in range(devices - by * MEMBERS)]
        return lax.ppermute(message, "seq", moves)

    rows = half * HEAD_DIM
    held = shift(total, 1)
    by = 1
    while by < groups - 1:
        before = shift(held, by)
        decays = rows_to_decays(held[rows:], half)
        factor = jnp.concatenate([jnp.broadcast_to(d, (HEAD_DIM, HEAD_DIM)) for d in decays])
        state = held[:rows].astype(F32) + factor * before[:rows].astype(F32)
        through = [a * b for a, b in zip(decays, rows_to_decays(before[rows:], half))]
        held = jnp.concatenate([state.astype(BF16), decays_to_rows(through)], axis=0)
        by *= 2
    return held


def on_device(
    residual, query_vectors, key_vectors, value_vectors, log_decay, norm_gain, out_weight
):
    tokens, width = residual.shape
    heads = log_decay.shape[0]
    half = heads // 2
    devices = lax.axis_size("seq")
    tp = lax.axis_size("tp")
    wide = (tokens, heads * HEAD_DIM)
    out_width = out_weight.shape[1] // tp
    states = (half * HEAD_DIM, HEAD_DIM)
    near_pairs = [(i, i ^ 1) for i in range(tp)]
    far_pairs = [(i, i ^ 2) for i in range(tp)]
    shape = jax.ShapeDtypeStruct
    message = shape((half * HEAD_DIM + DECAY_ROWS, HEAD_DIM), BF16)

    def swap(piece, step):
        return lax.ppermute(piece, "seq", [(i, i ^ step) for i in range(devices)])

    other_weight = lax.ppermute(out_weight, "tp", near_pairs)
    weight = pltpu.with_memory_space_constraint(out_weight, pltpu.HBM)
    arguments = (log_decay, key_vectors, value_vectors, query_vectors, norm_gain.reshape(1, -1))
    theirs, mine, decays, keys, values, queries, gain = call(
        functools.partial(state_kernel, half),
        (message, message) + tuple(shape(a.shape, a.dtype) for a in arguments),
        [HBM] * 5,
        "states",
        scratch=[pltpu.SemaphoreType.DMA((5,))],
    )(*(pltpu.with_memory_space_constraint(a, pltpu.HBM) for a in arguments))
    steps = (3, 2, 1, 0)
    received = [swap(theirs, 3), swap(mine, 2), swap(theirs, 1), mine]
    state = shape(states, BF16)
    before, sent, through, total = call(
        functools.partial(gather_kernel, half, steps),
        (shape(states, F32), state, shape((heads * 8, HEAD_DIM), F32), message),
        [VMEM] * len(steps),
        "gather_states",
        scratch=[pltpu.VMEM((MEMBERS,) + message.shape, BF16)],
    )(*received)
    earlier = earlier_groups(total, half, devices)
    inside = swap(sent, 1)
    intra, own = call(
        functools.partial(local_kernel, heads),
        (shape(wide, F32), shape((tokens, heads), F32)),
        [VMEM] * 4,
        "local",
        cost=4 * tokens * tokens * heads * HEAD_DIM,
    )(decays, queries, keys, values)
    mine, rest, factor, sent = call(
        functools.partial(start_kernel, half),
        (state, state, shape((half * 8, HEAD_DIM), F32), message),
        [VMEM] * 5,
        "start_states",
    )(before, through, inside, earlier, own)

    chunks = [slice(0, tokens // 2), slice(tokens // 2, tokens)]
    block = (out_weight.shape[0], out_width)
    weights = (weight, other_weight)
    weight_specs = [HBM, pl.BlockSpec(memory_space=pl.ANY)]

    def normed(name, halves, rows, *states):
        part = call(
            functools.partial(norm_kernel, half, halves, rows),
            shape((rows.stop - rows.start, len(halves) * half * HEAD_DIM), BF16),
            [VMEM] * (4 + len(states)),
            name,
        )(queries, intra, own, gain, *states)
        return part, lax.ppermute(part, "tp", near_pairs)

    def far_columns(after):
        return call(
            fetch_kernel,
            (shape(block, BF16),) * 2,
            weight_specs + [VMEM],
            "fetch_far",
            scratch=[pltpu.SemaphoreType.DMA((2,))],
        )(*weights, after)

    def send_far(i, kernel, *operands):
        part = call(
            kernel,
            shape((chunks[i].stop - chunks[i].start, out_width), BF16),
            [VMEM] * len(operands),
            f"project_far_{i}",
        )(*operands)
        return lax.ppermute(part, "tp", far_pairs)

    def finish(passes, pairs, far):
        near = call(
            functools.partial(near_kernel, chunks, passes),
            shape((tokens, out_width), F32),
            [HBM] + weight_specs + [VMEM] * (2 * len(pairs)),
            "project_near",
            scratch=[
                pltpu.VMEM(residual.shape, BF16),
                pltpu.VMEM(block, BF16),
                pltpu.VMEM(block, BF16),
                pltpu.SemaphoreType.DMA((3,)),
            ],
        )(
            pltpu.with_memory_space_constraint(residual, pltpu.HBM),
            *weights,
            *(a for pair in pairs for a in pair),
        )
        return call(
            functools.partial(add_kernel, chunks),
            pltpu.HBM((tokens, out_width), BF16),
            [VMEM] * (1 + len(chunks)),
            "add",
            out_specs=HBM,
            scratch=[
                pltpu.VMEM((tokens, out_width), BF16),
                pltpu.SemaphoreType.DMA((len(chunks),)),
            ],
        )(near, *far)

    def first_group():
        both = (True, False)
        pairs = [normed(f"norm_{i}", both, rows, mine, rest) for i, rows in enumerate(chunks)]
        far_weights = far_columns(pairs[-1][0])
        far = [send_far(i, far_all_kernel, *pairs[i], *far_weights) for i in range(len(chunks))]
        return finish((both,), pairs, far)

    def later_group():
        swapped = swap(sent, 1)
        begun = [normed(f"norm_mine_{i}", (True,), rows, mine) for i, rows in enumerate(chunks)]
        far_weights = far_columns(begun[-1][0])
        far_begun = call(
            functools.partial(far_mine_kernel, chunks),
            shape((tokens, out_width), F32),
            [VMEM] * (2 + 2 * len(chunks)),
            "project_far_mine",
        )(*far_weights, *(a for pair in begun for a in pair))
        other = call(functools.partial(start_other_kernel, half), state, [VMEM] * 4, "start_other")(
            rest, factor, swapped, far_begun
        )
        parts = [normed(f"norm_{i}", (False,), rows, other) for i, rows in enumerate(chunks)]
        far = [
            send_far(i, functools.partial(far_kernel, rows), far_begun, *parts[i], *far_weights)
            for i, rows in enumerate(chunks)
        ]
        pairs = [pair for i in range(len(chunks)) for pair in (begun[i], parts[i])]
        return finish(((True,), (False,)), pairs, far)

    return lax.cond(lax.axis_index("seq") < MEMBERS, first_group, later_group)


def solution(mesh):
    return jax.shard_map(
        on_device,
        mesh=mesh,
        in_specs=(
            P("seq", "tp"),
            P("seq", "tp"),
            P("seq", "tp"),
            P("seq", "tp"),
            P("tp", "seq"),
            P("tp"),
            P("tp", None),
        ),
        out_specs=P("seq", "tp"),
        check_vma=False,
    )
```

```python
import functools

import jax
import jax.numpy as jnp
from jax import lax
from jax.experimental import pallas as pl
from jax.experimental.pallas import tpu as pltpu
from jax.sharding import PartitionSpec as P

HEAD_DIM = 128
GROUP = 256
SCALE = HEAD_DIM ** (-0.5)
F32 = jnp.float32
BF16 = jnp.bfloat16
VMEM = pl.BlockSpec(memory_space=pltpu.VMEM)
HBM = pl.BlockSpec(memory_space=pltpu.HBM)
DECAY_ROWS = 16
MEMBERS = 4
PARAMS = pltpu.CompilerParams(vmem_limit_bytes=24 * 1024 * 1024)


def state_rows(j):
    return slice(j * HEAD_DIM, (j + 1) * HEAD_DIM)


def place():
    return lax.rem(lax.axis_index("seq"), MEMBERS)


def side():
    return lax.rem(lax.axis_index("seq"), 2)


def half_at(owner, size):
    return pl.ds(pl.multiple_of(owner * size, size), size)


def pick(owner, values, axis):
    half = values.shape[axis] // 2
    low = lax.slice_in_dim(values, 0, half, axis=axis)
    high = lax.slice_in_dim(values, half, 2 * half, axis=axis)
    return jnp.where(owner == 0, low, high)


def contract(a, b):
    return lax.dot_general(a, b, (((1,), (1,)), ((), ())), preferred_element_type=F32)


def positions():
    shape = (GROUP, GROUP)
    return lax.broadcasted_iota(jnp.int32, shape, 0), lax.broadcasted_iota(jnp.int32, shape, 1)


def three_terms(values):
    first = values.astype(BF16).astype(F32)
    second = (values - first).astype(BF16).astype(F32)
    third = values - first - second
    return jnp.concatenate([first, second, third], axis=0).astype(BF16)


def sums_down(mask, decays):
    heads = decays.shape[0]
    terms = contract(mask, three_terms(decays))
    return terms[:, :heads] + terms[:, heads : 2 * heads] + terms[:, 2 * heads :]


def sums_across(mask, decays):
    heads = decays.shape[0]
    terms = contract(three_terms(decays), mask)
    return terms[:heads] + terms[heads : 2 * heads] + terms[2 * heads :]


def decays_to_rows(decays):
    each = DECAY_ROWS // (2 * len(decays))
    wide = jnp.concatenate([jnp.broadcast_to(d, (each, HEAD_DIM)) for d in decays], axis=0)
    coarse = wide.astype(BF16).astype(F32)
    return jnp.concatenate([coarse, wide - coarse], axis=0).astype(BF16)


def rows_to_decays(rows, count):
    rows = rows.astype(F32)
    each = DECAY_ROWS // (2 * count)
    both = rows[: DECAY_ROWS // 2] + rows[DECAY_ROWS // 2 :]
    return [both[j * each : j * each + 1] for j in range(count)]


def state_kernel(half, *refs):
    sources, outs, held, sems = refs[:5], refs[5:7], refs[7:12], refs[12]
    moves = [(sources[0], held[0])]
    for i in (1, 2):
        middle = sources[i].shape[0] // 2
        for rows in (slice(0, middle), slice(middle, 2 * middle)):
            moves.append((sources[i].at[rows, :], held[i].at[rows, :]))
    moves += list(zip(sources[3:], held[3:]))
    copies = [
        pltpu.make_async_copy(source, target, sems.at[i])
        for i, (source, target) in enumerate(moves)
    ]
    for copy in copies:
        copy.start()
    decay_ref, key_ref, value_ref = held[:3]
    me = side()
    row, col = positions()
    later = jnp.where(col > row, 1.0, 0.0).astype(BF16)
    copies[0].wait()
    decays = decay_ref[...]
    tail = jnp.exp(sums_across(later, decays))
    whole = jnp.exp(jnp.sum(decays, axis=1, keepdims=True))
    for copy in copies[1:5]:
        copy.wait()
    decay_rows = decays_to_rows([whole[h : h + 1] for h in range(2 * half)])
    for owner, out_ref in zip((1 - me, me), outs):
        factors = pick(owner, tail, 0)
        for j in range(half):
            at = half_at(owner * half + j, HEAD_DIM)
            weighted = (key_ref[:, at].T.astype(F32) * factors[j : j + 1, :]).astype(BF16)
            update = jnp.dot(weighted, value_ref[:, at], preferred_element_type=F32)
            out_ref[state_rows(j), :] = update.astype(BF16)
        out_ref[half * HEAD_DIM :, :] = decay_rows
    for copy in copies[5:]:
        copy.wait()


def local_kernel(heads, decay_ref, query_ref, key_ref, value_ref, intra_ref, own_ref):
    row, col = positions()
    causal = col <= row
    upto = jnp.where(causal, 1.0, 0.0).astype(BF16)
    decays = decay_ref[...]
    down = sums_down(upto, decays)
    across = sums_across(upto, decays)
    own_ref[...] = jnp.exp(down) * SCALE
    for h in range(heads):
        at = slice(h * HEAD_DIM, (h + 1) * HEAD_DIM)
        scores = contract(query_ref[:, at], key_ref[:, at])
        gaps = down[:, h : h + 1] - across[h : h + 1, :]
        weights = jnp.where(causal, jnp.exp(gaps), 0.0)
        probs = (scores * SCALE * weights).astype(BF16)
        intra_ref[:, at] = jnp.dot(probs, value_ref[:, at], preferred_element_type=F32)


def gather_kernel(half, steps, *refs):
    received, (before_ref, sent_ref, through_ref, total_ref, held_ref) = (
        refs[: len(steps)],
        refs[len(steps) :],
    )
    me, upper = place(), side() == 1
    for step, message_ref in zip(steps, received):
        held_ref[me ^ step] = message_ref[...]
    later_pair = me >= 2
    decays = [rows_to_decays(held_ref[m, half * HEAD_DIM :, :], 2 * half) for m in range(MEMBERS)]
    totals = []
    for j in range(2 * half):
        low, high = (j, half + j) if j < half else (j, j - half)
        decay = [jnp.where(upper, d[high], d[low]) for d in decays]
        through = [jnp.ones((1, HEAD_DIM), F32)]
        for m in range(MEMBERS):
            through.append(through[m] * decay[m])
        first, last = [jnp.where(later_pair, through[2 + i], through[i]) for i in range(2)]
        factor = jnp.where(upper, last, first)
        through_ref[j * 8 : (j + 1) * 8, :] = jnp.broadcast_to(factor, (8, HEAD_DIM))
        if j >= half:
            continue
        at = state_rows(j)
        held = [jnp.zeros((HEAD_DIM, HEAD_DIM), F32)]
        for m in range(MEMBERS):
            held.append(held[m] * decay[m] + held_ref[m, at, :].astype(F32))
        first, last = [jnp.where(later_pair, held[2 + i], held[i]) for i in range(2)]
        before_ref[at, :] = jnp.where(upper, last, first)
        sent_ref[at, :] = jnp.where(upper, first, last).astype(BF16)
        total_ref[at, :] = held[MEMBERS].astype(BF16)
        totals.append(through[MEMBERS])
    total_ref[half * HEAD_DIM :, :] = decays_to_rows(totals)


def start_kernel(half, before_ref, through_ref, inside_ref, earlier_ref, _, *outs):
    mine_ref, rest_ref, factor_ref, sent_ref = outs
    started = lax.axis_index("seq") >= MEMBERS
    for j in range(half):
        at = state_rows(j)
        earlier = jnp.where(started, earlier_ref[at, :].astype(F32), 0.0)
        held = before_ref[at, :] + through_ref[8 * j : 8 * j + 1, :] * earlier
        mine_ref[at, :] = held.astype(BF16)
    rest_ref[...] = inside_ref[...]
    factor_ref[...] = through_ref[8 * half :, :]
    sent_ref[...] = earlier_ref[...]


def start_other_kernel(half, rest_ref, factor_ref, earlier_ref, _, out_ref):
    for j in range(half):
        at = state_rows(j)
        earlier = factor_ref[8 * j : 8 * j + 1, :] * earlier_ref[at, :].astype(F32)
        out_ref[at, :] = (rest_ref[at, :].astype(F32) + earlier).astype(BF16)


def norm_kernel(half, halves, rows, query_ref, intra_ref, own_ref, gain_ref, *refs):
    states, out_ref = refs[: len(halves)], refs[-1]
    for i, (mine, state_ref) in enumerate(zip(halves, states)):
        owner = side() if mine else 1 - side()
        own = pick(owner, own_ref[rows, :], 1)
        for j in range(half):
            at = half_at(owner * half + j, HEAD_DIM)
            state = state_ref[state_rows(j), :]
            inter = jnp.dot(query_ref[rows, at], state, preferred_element_type=F32)
            attended = intra_ref[rows, at] + own[:, j : j + 1] * inter
            mean_square = jnp.mean(attended * attended, axis=-1, keepdims=True)
            normed = (attended * lax.rsqrt(mean_square + 1e-06) * gain_ref[:, at]).astype(BF16)
            to = (i * half + j) * HEAD_DIM
            out_ref[:, to : to + HEAD_DIM] = normed


def share(halves, pair, weights):
    rows = weights[0].shape[0] // 2
    total = None
    for i, mine in enumerate(halves):
        at = half_at(side() if mine else 1 - side(), rows)
        for normed_ref, weight_ref in zip(pair, weights):
            normed = normed_ref[:, i * rows : (i + 1) * rows]
            part = jnp.dot(normed, weight_ref[at, :], preferred_element_type=F32)
            total = part if total is None else total + part
    return total


def fetch(step, whole, held, sems):
    copies = []
    for i, (weight, ref) in enumerate(zip(whole, held)):
        at = half_at(lax.axis_index("tp") ^ step, ref.shape[1])
        middle = ref.shape[0] // 2
        for j, rows in enumerate((slice(0, middle), slice(middle, 2 * middle))):
            source = weight.at[rows, at]
            copies.append(pltpu.make_async_copy(source, ref.at[rows, :], sems.at[2 * i + j]))
            copies[-1].start()
    return copies


def fetch_kernel(weight_hbm, other_weight_hbm, _, weight_ref, other_weight_ref, sems):
    for copy in fetch(2, (weight_hbm, other_weight_hbm), (weight_ref, other_weight_ref), sems):
        copy.wait()


def far_mine_kernel(chunks, weight_ref, other_weight_ref, *refs):
    for i, rows in enumerate(chunks):
        pair = refs[2 * i : 2 * i + 2]
        refs[-1][rows, :] = share((True,), pair, (weight_ref, other_weight_ref))


def far_kernel(rows, begun_ref, mine_ref, other_ref, weight_ref, other_weight_ref, out_ref):
    rest = share((False,), (mine_ref, other_ref), (weight_ref, other_weight_ref))
    out_ref[...] = (begun_ref[rows, :] + rest).astype(BF16)


def far_all_kernel(mine_ref, other_ref, weight_ref, other_weight_ref, out_ref):
    pair, weights = (mine_ref, other_ref), (weight_ref, other_weight_ref)
    out_ref[...] = share((True, False), pair, weights).astype(BF16)


def near_kernel(chunks, passes, residual_hbm, weight_hbm, other_weight_hbm, *refs):
    out_ref, residual_ref, *weights, sems = refs[-5:]
    copies = fetch(0, (weight_hbm, other_weight_hbm), weights, sems)
    copies.append(pltpu.make_async_copy(residual_hbm, residual_ref, sems.at[4]))
    copies[4].start()
    for copy in copies:
        copy.wait()
    pairs = iter(zip(refs[0:-5:2], refs[1:-5:2]))
    for rows in chunks:
        near = residual_ref[rows, :].astype(F32)
        for halves in passes:
            near = near + share(halves, next(pairs), weights)
        out_ref[rows, :] = near


def add_kernel(chunks, near_ref, *refs):
    far, (out_hbm, out_ref, sems) = refs[: len(chunks)], refs[len(chunks) :]
    copies = []
    for i, rows in enumerate(chunks):
        out_ref[rows, :] = (near_ref[rows, :] + far[i][...].astype(F32)).astype(BF16)
        copies.append(
            pltpu.make_async_copy(out_ref.at[rows, :], out_hbm.at[rows, :], sems.at[i])
        )
        copies[-1].start()
    for copy in copies:
        copy.wait()


def call(kernel, out_shape, in_specs, name, out_specs=None, scratch=(), cost=0):
    single = isinstance(out_shape, jax.ShapeDtypeStruct)
    if out_specs is None:
        out_specs = VMEM if single else (VMEM,) * len(out_shape)
    cost = pl.CostEstimate(
        flops=cost, bytes_accessed=2_000_000 if cost else 0, transcendentals=0
    )
    return pl.pallas_call(
        kernel,
        out_shape=out_shape,
        in_specs=in_specs,
        out_specs=out_specs,
        scratch_shapes=scratch,
        compiler_params=PARAMS,
        cost_estimate=cost,
        name=name,
    )


def earlier_groups(total, half, devices):
    groups = devices // MEMBERS
    if groups == 2:
        return lax.ppermute(total, "seq", [(i, i ^ MEMBERS) for i in range(devices)])

    def shift(message, by):
        moves = [(i, i + by * MEMBERS) for i in range(devices - by * MEMBERS)]
        return lax.ppermute(message, "seq", moves)

    rows = half * HEAD_DIM
    held = shift(total, 1)
    by = 1
    while by < groups - 1:
        before = shift(held, by)
        decays = rows_to_decays(held[rows:], half)
        factor = jnp.concatenate([jnp.broadcast_to(d, (HEAD_DIM, HEAD_DIM)) for d in decays])
        state = held[:rows].astype(F32) + factor * before[:rows].astype(F32)
        through = [a * b for a, b in zip(decays, rows_to_decays(before[rows:], half))]
        held = jnp.concatenate([state.astype(BF16), decays_to_rows(through)], axis=0)
        by *= 2
    return held


def on_device(
    residual, query_vectors, key_vectors, value_vectors, log_decay, norm_gain, out_weight
):
    tokens, width = residual.shape
    heads = log_decay.shape[0]
    half = heads // 2
    devices = lax.axis_size("seq")
    tp = lax.axis_size("tp")
    wide = (tokens, heads * HEAD_DIM)
    out_width = out_weight.shape[1] // tp
    states = (half * HEAD_DIM, HEAD_DIM)
    near_pairs = [(i, i ^ 1) for i in range(tp)]
    far_pairs = [(i, i ^ 2) for i in range(tp)]
    shape = jax.ShapeDtypeStruct
    message = shape((half * HEAD_DIM + DECAY_ROWS, HEAD_DIM), BF16)

    def swap(piece, step):
        return lax.ppermute(piece, "seq", [(i, i ^ step) for i in range(devices)])

    other_weight = lax.ppermute(out_weight, "tp", near_pairs)
    weight = pltpu.with_memory_space_constraint(out_weight, pltpu.HBM)
    arguments = (log_decay, key_vectors, value_vectors, query_vectors, norm_gain.reshape(1, -1))
    theirs, mine, decays, keys, values, queries, gain = call(
        functools.partial(state_kernel, half),
        (message, message) + tuple(shape(a.shape, a.dtype) for a in arguments),
        [HBM] * 5,
        "states",
        scratch=[pltpu.SemaphoreType.DMA((7,))],
    )(*(pltpu.with_memory_space_constraint(a, pltpu.HBM) for a in arguments))
    steps = (3, 1, 2, 0)
    received = [swap(theirs, 3), swap(theirs, 1), swap(mine, 2), mine]
    state = shape(states, BF16)
    before, sent, through, total = call(
        functools.partial(gather_kernel, half, steps),
        (shape(states, F32), state, shape((heads * 8, HEAD_DIM), F32), message),
        [VMEM] * len(steps),
        "gather_states",
        scratch=[pltpu.VMEM((MEMBERS,) + message.shape, BF16)],
    )(*received)
    earlier = earlier_groups(total, half, devices)
    inside = swap(sent, 1)
    intra, own = call(
        functools.partial(local_kernel, heads),
        (shape(wide, F32), shape((tokens, heads), F32)),
        [VMEM] * 4,
        "local",
        cost=4 * tokens * tokens * heads * HEAD_DIM,
    )(decays, queries, keys, values)
    mine, rest, factor, sent = call(
        functools.partial(start_kernel, half),
        (state, state, shape((half * 8, HEAD_DIM), F32), message),
        [VMEM] * 5,
        "start_states",
    )(before, through, inside, earlier, own)

    chunks = [slice(0, tokens // 2), slice(tokens // 2, tokens)]
    block = (out_weight.shape[0], out_width)
    weights = (weight, other_weight)
    weight_specs = [HBM, pl.BlockSpec(memory_space=pl.ANY)]

    def normed(name, halves, rows, *states):
        part = call(
            functools.partial(norm_kernel, half, halves, rows),
            shape((rows.stop - rows.start, len(halves) * half * HEAD_DIM), BF16),
            [VMEM] * (4 + len(states)),
            name,
        )(queries, intra, own, gain, *states)
        return part, lax.ppermute(part, "tp", near_pairs)

    def far_columns(after):
        return call(
            fetch_kernel,
            (shape(block, BF16),) * 2,
            weight_specs + [VMEM],
            "fetch_far",
            scratch=[pltpu.SemaphoreType.DMA((4,))],
        )(*weights, after)

    def send_far(i, kernel, *operands):
        part = call(
            kernel,
            shape((chunks[i].stop - chunks[i].start, out_width), BF16),
            [VMEM] * len(operands),
            f"project_far_{i}",
        )(*operands)
        return lax.ppermute(part, "tp", far_pairs)

    def finish(passes, pairs, far):
        near = call(
            functools.partial(near_kernel, chunks, passes),
            shape((tokens, out_width), F32),
            [HBM] + weight_specs + [VMEM] * (2 * len(pairs)),
            "project_near",
            scratch=[
                pltpu.VMEM(residual.shape, BF16),
                pltpu.VMEM(block, BF16),
                pltpu.VMEM(block, BF16),
                pltpu.SemaphoreType.DMA((5,)),
            ],
        )(
            pltpu.with_memory_space_constraint(residual, pltpu.HBM),
            *weights,
            *(a for pair in pairs for a in pair),
        )
        return call(
            functools.partial(add_kernel, chunks),
            pltpu.HBM((tokens, out_width), BF16),
            [VMEM] * (1 + len(chunks)),
            "add",
            out_specs=HBM,
            scratch=[
                pltpu.VMEM((tokens, out_width), BF16),
                pltpu.SemaphoreType.DMA((len(chunks),)),
            ],
        )(near, *far)

    def first_group():
        both = (True, False)
        pairs = [normed(f"norm_{i}", both, rows, mine, rest) for i, rows in enumerate(chunks)]
        far_weights = far_columns(pairs[-1][0])
        far = [send_far(i, far_all_kernel, *pairs[i], *far_weights) for i in range(len(chunks))]
        return finish((both,), pairs, far)

    def later_group():
        swapped = swap(sent, 1)
        begun = [normed(f"norm_mine_{i}", (True,), rows, mine) for i, rows in enumerate(chunks)]
        far_weights = far_columns(begun[-1][0])
        far_begun = call(
            functools.partial(far_mine_kernel, chunks),
            shape((tokens, out_width), F32),
            [VMEM] * (2 + 2 * len(chunks)),
            "project_far_mine",
        )(*far_weights, *(a for pair in begun for a in pair))
        other = call(functools.partial(start_other_kernel, half), state, [VMEM] * 4, "start_other")(
            rest, factor, swapped, far_begun
        )
        parts = [normed(f"norm_{i}", (False,), rows, other) for i, rows in enumerate(chunks)]
        far = [
            send_far(i, functools.partial(far_kernel, rows), far_begun, *parts[i], *far_weights)
            for i, rows in enumerate(chunks)
        ]
        pairs = [pair for i in range(len(chunks)) for pair in (begun[i], parts[i])]
        return finish(((True,), (False,)), pairs, far)

    return lax.cond(lax.axis_index("seq") < MEMBERS, first_group, later_group)


def solution(mesh):
    return jax.shard_map(
        on_device,
        mesh=mesh,
        in_specs=(
            P("seq", "tp"),
            P("seq", "tp"),
            P("seq", "tp"),
            P("seq", "tp"),
            P("tp", "seq"),
            P("tp"),
            P("tp", None),
        ),
        out_specs=P("seq", "tp"),
        check_vma=False,
    )
```

```python
import functools

import jax
import jax.numpy as jnp
from jax import lax
from jax.experimental import pallas as pl
from jax.experimental.pallas import tpu as pltpu
from jax.sharding import PartitionSpec as P

HEAD_DIM = 128
GROUP = 256
SCALE = HEAD_DIM ** (-0.5)
F32 = jnp.float32
BF16 = jnp.bfloat16
VMEM = pl.BlockSpec(memory_space=pltpu.VMEM)
HBM = pl.BlockSpec(memory_space=pltpu.HBM)
DECAY_ROWS = 16
MEMBERS = 4
PARAMS = pltpu.CompilerParams(vmem_limit_bytes=24 * 1024 * 1024)


def state_rows(j):
    return slice(j * HEAD_DIM, (j + 1) * HEAD_DIM)


def place():
    return lax.rem(lax.axis_index("seq"), MEMBERS)


def side():
    return lax.rem(lax.axis_index("seq"), 2)


def half_at(owner, size):
    return pl.ds(pl.multiple_of(owner * size, size), size)


def pick(owner, values, axis):
    half = values.shape[axis] // 2
    low = lax.slice_in_dim(values, 0, half, axis=axis)
    high = lax.slice_in_dim(values, half, 2 * half, axis=axis)
    return jnp.where(owner == 0, low, high)


def contract(a, b):
    return lax.dot_general(a, b, (((1,), (1,)), ((), ())), preferred_element_type=F32)


def positions():
    shape = (GROUP, GROUP)
    return lax.broadcasted_iota(jnp.int32, shape, 0), lax.broadcasted_iota(jnp.int32, shape, 1)


def three_terms(values):
    first = values.astype(BF16).astype(F32)
    second = (values - first).astype(BF16).astype(F32)
    third = values - first - second
    return jnp.concatenate([first, second, third], axis=0).astype(BF16)


def sums_down(mask, decays):
    heads = decays.shape[0]
    terms = contract(mask, three_terms(decays))
    return terms[:, :heads] + terms[:, heads : 2 * heads] + terms[:, 2 * heads :]


def sums_across(mask, decays):
    heads = decays.shape[0]
    terms = contract(three_terms(decays), mask)
    return terms[:heads] + terms[heads : 2 * heads] + terms[2 * heads :]


def decays_to_rows(decays):
    each = DECAY_ROWS // (2 * len(decays))
    wide = jnp.concatenate([jnp.broadcast_to(d, (each, HEAD_DIM)) for d in decays], axis=0)
    coarse = wide.astype(BF16).astype(F32)
    return jnp.concatenate([coarse, wide - coarse], axis=0).astype(BF16)


def rows_to_decays(rows, count):
    rows = rows.astype(F32)
    each = DECAY_ROWS // (2 * count)
    both = rows[: DECAY_ROWS // 2] + rows[DECAY_ROWS // 2 :]
    return [both[j * each : j * each + 1] for j in range(count)]


def state_kernel(half, *refs):
    sources, outs, held, sems = refs[:5], refs[5:7], refs[7:12], refs[12]
    copies = [
        pltpu.make_async_copy(source, target, sems.at[i])
        for i, (source, target) in enumerate(zip(sources, held))
    ]
    for copy in copies:
        copy.start()
    decay_ref, key_ref, value_ref = held[:3]
    me = side()
    row, col = positions()
    later = jnp.where(col > row, 1.0, 0.0).astype(BF16)
    copies[0].wait()
    decays = decay_ref[...]
    tail = jnp.exp(sums_across(later, decays))
    whole = jnp.exp(jnp.sum(decays, axis=1, keepdims=True))
    copies[1].wait()
    copies[2].wait()
    decay_rows = decays_to_rows([whole[h : h + 1] for h in range(2 * half)])
    for owner, out_ref in zip((1 - me, me), outs):
        factors = pick(owner, tail, 0)
        for j in range(half):
            at = half_at(owner * half + j, HEAD_DIM)
            weighted = (key_ref[:, at].T.astype(F32) * factors[j : j + 1, :]).astype(BF16)
            update = jnp.dot(weighted, value_ref[:, at], preferred_element_type=F32)
            out_ref[state_rows(j), :] = update.astype(BF16)
        out_ref[half * HEAD_DIM :, :] = decay_rows
    for copy in copies[3:]:
        copy.wait()


def local_kernel(heads, decay_ref, query_ref, key_ref, value_ref, intra_ref, own_ref):
    row, col = positions()
    causal = col <= row
    upto = jnp.where(causal, 1.0, 0.0).astype(BF16)
    decays = decay_ref[...]
    down = sums_down(upto, decays)
    across = sums_across(upto, decays)
    own_ref[...] = jnp.exp(down) * SCALE
    for h in range(heads):
        at = slice(h * HEAD_DIM, (h + 1) * HEAD_DIM)
        scores = contract(query_ref[:, at], key_ref[:, at])
        gaps = down[:, h : h + 1] - across[h : h + 1, :]
        weights = jnp.where(causal, jnp.exp(gaps), 0.0)
        probs = (scores * SCALE * weights).astype(BF16)
        intra_ref[:, at] = jnp.dot(probs, value_ref[:, at], preferred_element_type=F32)


def gather_kernel(half, steps, wanted, *refs):
    received, (before_ref, *outs, held_ref) = refs[: len(steps)], refs[len(steps) :]
    through_ref = outs[0] if wanted[0] else None
    total_ref = outs[-1] if wanted[1] else None
    me, upper = place(), side() == 1
    for step, message_ref in zip(steps, received):
        held_ref[me ^ step] = message_ref[...]
    later_pair = me >= 2
    decays = [rows_to_decays(held_ref[m, half * HEAD_DIM :, :], 2 * half) for m in range(MEMBERS)]
    totals = []
    for j in range(half):
        at = state_rows(j)
        decay = [jnp.where(upper, d[half + j], d[j]) for d in decays]
        held = [jnp.zeros((HEAD_DIM, HEAD_DIM), F32)]
        through = [jnp.ones((1, HEAD_DIM), F32)]
        for m in range(MEMBERS):
            held.append(held[m] * decay[m] + held_ref[m, at, :].astype(F32))
            through.append(through[m] * decay[m])
        first, last = [jnp.where(later_pair, held[2 + i], held[i]) for i in range(2)]
        before_ref[0, at, :] = jnp.where(upper, last, first)
        before_ref[1, at, :] = jnp.where(upper, first, last)
        first, last = [jnp.where(later_pair, through[2 + i], through[i]) for i in range(2)]
        for i, factor in enumerate((jnp.where(upper, last, first), jnp.where(upper, first, last))):
            rows = slice((i * half + j) * 8, (i * half + j + 1) * 8)
            if wanted[0]:
                through_ref[rows, :] = jnp.broadcast_to(factor, (8, HEAD_DIM))
        if wanted[1]:
            total_ref[at, :] = held[MEMBERS].astype(BF16)
        totals.append(through[MEMBERS])
    if wanted[1]:
        total_ref[half * HEAD_DIM :, :] = decays_to_rows(totals)


def inside_kernel(before_ref, mine_ref, sent_ref):
    mine_ref[...] = before_ref[0].astype(BF16)
    sent_ref[...] = before_ref[1].astype(BF16)


def hand_on_kernel(mine_ref, rest_ref, mine_out_ref, rest_out_ref):
    mine_out_ref[...] = mine_ref[...]
    rest_out_ref[...] = rest_ref[...]


def start_kernel(half, before_ref, through_ref, earlier_ref, mine_ref, sent_ref):
    for j in range(half):
        at = state_rows(j)
        earlier = earlier_ref[at, :].astype(F32)
        for i, out_ref in enumerate((mine_ref, sent_ref)):
            row = (i * half + j) * 8
            held = before_ref[i, at, :] + through_ref[row : row + 1, :] * earlier
            out_ref[at, :] = held.astype(BF16)
    sent_ref[half * HEAD_DIM :, :] = jnp.zeros((DECAY_ROWS, HEAD_DIM), BF16)


def nothing_kernel(*refs):
    pass


def norm_kernel(half, halves, rows, query_ref, intra_ref, own_ref, gain_ref, *refs):
    states, out_ref = refs[: len(halves)], refs[-1]
    for i, (mine, state_ref) in enumerate(zip(halves, states)):
        owner = side() if mine else 1 - side()
        own = pick(owner, own_ref[rows, :], 1)
        for j in range(half):
            at = half_at(owner * half + j, HEAD_DIM)
            state = state_ref[state_rows(j), :]
            inter = jnp.dot(query_ref[rows, at], state, preferred_element_type=F32)
            attended = intra_ref[rows, at] + own[:, j : j + 1] * inter
            mean_square = jnp.mean(attended * attended, axis=-1, keepdims=True)
            normed = (attended * lax.rsqrt(mean_square + 1e-06) * gain_ref[:, at]).astype(BF16)
            to = (i * half + j) * HEAD_DIM
            out_ref[:, to : to + HEAD_DIM] = normed


def share(halves, pair, weights):
    rows = weights[0].shape[0] // 2
    total = None
    for i, mine in enumerate(halves):
        at = half_at(side() if mine else 1 - side(), rows)
        for normed_ref, weight_ref in zip(pair, weights):
            normed = normed_ref[:, i * rows : (i + 1) * rows]
            part = jnp.dot(normed, weight_ref[at, :], preferred_element_type=F32)
            total = part if total is None else total + part
    return total


def fetch(step, whole, held, sems):
    copies = []
    for i, (weight, ref) in enumerate(zip(whole, held)):
        at = half_at(lax.axis_index("tp") ^ step, ref.shape[1])
        copies.append(pltpu.make_async_copy(weight.at[:, at], ref, sems.at[i]))
        copies[i].start()
    return copies


def fetch_kernel(weight_hbm, other_weight_hbm, _, weight_ref, other_weight_ref, sems):
    for copy in fetch(2, (weight_hbm, other_weight_hbm), (weight_ref, other_weight_ref), sems):
        copy.wait()


def far_mine_kernel(chunks, weight_ref, other_weight_ref, *refs):
    for i, rows in enumerate(chunks):
        pair = refs[2 * i : 2 * i + 2]
        refs[-1][rows, :] = share((True,), pair, (weight_ref, other_weight_ref))


def far_kernel(rows, begun_ref, mine_ref, other_ref, weight_ref, other_weight_ref, out_ref):
    rest = share((False,), (mine_ref, other_ref), (weight_ref, other_weight_ref))
    out_ref[...] = (begun_ref[rows, :] + rest).astype(BF16)


def far_all_kernel(mine_ref, other_ref, weight_ref, other_weight_ref, out_ref):
    pair, weights = (mine_ref, other_ref), (weight_ref, other_weight_ref)
    out_ref[...] = share((True, False), pair, weights).astype(BF16)


def near_kernel(chunks, passes, residual_hbm, weight_hbm, other_weight_hbm, *refs):
    out_ref, residual_ref, *weights, sems = refs[-5:]
    copies = fetch(0, (weight_hbm, other_weight_hbm), weights, sems)
    copies.append(pltpu.make_async_copy(residual_hbm, residual_ref, sems.at[2]))
    copies[2].start()
    for copy in copies:
        copy.wait()
    pairs = iter(zip(refs[0:-5:2], refs[1:-5:2]))
    for rows in chunks:
        near = residual_ref[rows, :].astype(F32)
        for halves in passes:
            near = near + share(halves, next(pairs), weights)
        out_ref[rows, :] = near


def add_kernel(chunks, near_ref, *refs):
    far, (out_hbm, out_ref, sems) = refs[: len(chunks)], refs[len(chunks) :]
    copies = []
    for i, rows in enumerate(chunks):
        out_ref[rows, :] = (near_ref[rows, :] + far[i][...].astype(F32)).astype(BF16)
        copies.append(
            pltpu.make_async_copy(out_ref.at[rows, :], out_hbm.at[rows, :], sems.at[i])
        )
        copies[-1].start()
    for copy in copies:
        copy.wait()


def call(kernel, out_shape, in_specs, name, out_specs=None, scratch=(), cost=0):
    single = isinstance(out_shape, jax.ShapeDtypeStruct)
    if out_specs is None:
        out_specs = VMEM if single else (VMEM,) * len(out_shape)
    cost = pl.CostEstimate(
        flops=cost, bytes_accessed=2_000_000 if cost else 0, transcendentals=0
    )
    return pl.pallas_call(
        kernel,
        out_shape=out_shape,
        in_specs=in_specs,
        out_specs=out_specs,
        scratch_shapes=scratch,
        compiler_params=PARAMS,
        cost_estimate=cost,
        name=name,
    )


def earlier_groups(total, half, devices):
    groups = devices // MEMBERS
    def shift(message, by):
        moves = [(i, i + by * MEMBERS) for i in range(devices - by * MEMBERS)]
        return lax.ppermute(message, "seq", moves)

    rows = half * HEAD_DIM
    held = shift(total, 1)
    by = 1
    while by < groups - 1:
        before = shift(held, by)
        decays = rows_to_decays(held[rows:], half)
        factor = jnp.concatenate([jnp.broadcast_to(d, (HEAD_DIM, HEAD_DIM)) for d in decays])
        state = held[:rows].astype(F32) + factor * before[:rows].astype(F32)
        through = [a * b for a, b in zip(decays, rows_to_decays(before[rows:], half))]
        held = jnp.concatenate([state.astype(BF16), decays_to_rows(through)], axis=0)
        by *= 2
    return held


def on_device(
    residual, query_vectors, key_vectors, value_vectors, log_decay, norm_gain, out_weight
):
    tokens, width = residual.shape
    heads = log_decay.shape[0]
    half = heads // 2
    devices = lax.axis_size("seq")
    tp = lax.axis_size("tp")
    wide = (tokens, heads * HEAD_DIM)
    out_width = out_weight.shape[1] // tp
    states = (half * HEAD_DIM, HEAD_DIM)
    near_pairs = [(i, i ^ 1) for i in range(tp)]
    far_pairs = [(i, i ^ 2) for i in range(tp)]
    shape = jax.ShapeDtypeStruct
    message = shape((half * HEAD_DIM + DECAY_ROWS, HEAD_DIM), BF16)

    def swap(piece, step):
        return lax.ppermute(piece, "seq", [(i, i ^ step) for i in range(devices)])

    other_weight = lax.ppermute(out_weight, "tp", near_pairs)
    weight = pltpu.with_memory_space_constraint(out_weight, pltpu.HBM)
    arguments = (log_decay, key_vectors, value_vectors, query_vectors, norm_gain.reshape(1, -1))
    theirs, own_message, decays, keys, values, queries, gain = call(
        functools.partial(state_kernel, half),
        (message, message) + tuple(shape(a.shape, a.dtype) for a in arguments),
        [HBM] * 5,
        "states",
        scratch=[pltpu.SemaphoreType.DMA((5,))],
    )(*(pltpu.with_memory_space_constraint(a, pltpu.HBM) for a in arguments))
    steps = (3, 1, 2, 0)
    state = shape(states, BF16)
    before_shape = shape((2,) + states, F32)
    through_shape = shape((2 * half * 8, HEAD_DIM), F32)

    def nothing(*shapes):
        return call(nothing_kernel, shapes, [], "nothing")()

    def gathered(wanted=(True, True)):
        received = [swap(theirs, 3), swap(theirs, 1), swap(own_message, 2), own_message]
        return call(
            functools.partial(gather_kernel, half, steps, wanted),
            (before_shape,) + (through_shape,) * wanted[0] + (message,) * wanted[1],
            [VMEM] * len(steps),
            "gather_states",
            scratch=[pltpu.VMEM((MEMBERS,) + message.shape, BF16)],
        )(*received)

    def local():
        return call(
            functools.partial(local_kernel, heads),
            (shape(wide, F32), shape((tokens, heads), F32)),
            [VMEM] * 4,
            "local",
            cost=4 * tokens * tokens * heads * HEAD_DIM,
        )(decays, queries, keys, values)

    def start_inside(before):
        mine, sent = call(inside_kernel, (state, state), [VMEM], "start_inside")(before)
        return call(hand_on_kernel, (state, state), [VMEM] * 2, "hand_on")(mine, swap(sent, 1))

    first = lax.axis_index("seq") < MEMBERS
    if devices == 2 * MEMBERS:
        first_before, total = lax.cond(
            first, lambda: tuple(gathered((False, True))), lambda: tuple(nothing(before_shape, message))
        )
        earlier = lax.ppermute(total, "seq", [(i, i + MEMBERS) for i in range(MEMBERS)])

        def first_inside():
            return (*nothing(before_shape, through_shape), *start_inside(first_before), *local())

        def later_inside():
            return (*gathered((True, False)), *nothing(state, state), *local())

        before, through, mine, rest, intra, own = lax.cond(first, first_inside, later_inside)
    else:
        before, through, total = gathered()
        earlier = earlier_groups(total, half, devices)
        mine, rest = start_inside(before)
        intra, own = local()
    chunks = [slice(0, tokens // 2), slice(tokens // 2, tokens)]
    block = (out_weight.shape[0], out_width)
    weights = (weight, other_weight)
    weight_specs = [HBM, pl.BlockSpec(memory_space=pl.ANY)]

    def normed(name, halves, rows, *states):
        part = call(
            functools.partial(norm_kernel, half, halves, rows),
            shape((rows.stop - rows.start, len(halves) * half * HEAD_DIM), BF16),
            [VMEM] * (4 + len(states)),
            name,
        )(queries, intra, own, gain, *states)
        return part, lax.ppermute(part, "tp", near_pairs)

    def far_columns(after):
        return call(
            fetch_kernel,
            (shape(block, BF16),) * 2,
            weight_specs + [VMEM],
            "fetch_far",
            scratch=[pltpu.SemaphoreType.DMA((2,))],
        )(*weights, after)

    def send_far(i, kernel, *operands):
        part = call(
            kernel,
            shape((chunks[i].stop - chunks[i].start, out_width), BF16),
            [VMEM] * len(operands),
            f"project_far_{i}",
        )(*operands)
        return lax.ppermute(part, "tp", far_pairs)

    def finish(passes, pairs, far):
        near = call(
            functools.partial(near_kernel, chunks, passes),
            shape((tokens, out_width), F32),
            [HBM] + weight_specs + [VMEM] * (2 * len(pairs)),
            "project_near",
            scratch=[
                pltpu.VMEM(residual.shape, BF16),
                pltpu.VMEM(block, BF16),
                pltpu.VMEM(block, BF16),
                pltpu.SemaphoreType.DMA((3,)),
            ],
        )(
            pltpu.with_memory_space_constraint(residual, pltpu.HBM),
            *weights,
            *(a for pair in pairs for a in pair),
        )
        return call(
            functools.partial(add_kernel, chunks),
            pltpu.HBM((tokens, out_width), BF16),
            [VMEM] * (1 + len(chunks)),
            "add",
            out_specs=HBM,
            scratch=[
                pltpu.VMEM((tokens, out_width), BF16),
                pltpu.SemaphoreType.DMA((len(chunks),)),
            ],
        )(near, *far)

    def first_group():
        both = (True, False)
        pairs = [normed(f"norm_{i}", both, rows, mine, rest) for i, rows in enumerate(chunks)]
        far_weights = far_columns(pairs[-1][0])
        far = [send_far(i, far_all_kernel, *pairs[i], *far_weights) for i in range(len(chunks))]
        return finish((both,), pairs, far)

    def later_group():
        my_start, sent = call(
            functools.partial(start_kernel, half), (state, message), [VMEM] * 3, "start_states"
        )(before, through, earlier)
        other = swap(sent, 1)
        begun = [normed(f"norm_mine_{i}", (True,), rows, my_start) for i, rows in enumerate(chunks)]
        far_weights = far_columns(begun[-1][0])
        far_begun = call(
            functools.partial(far_mine_kernel, chunks),
            shape((tokens, out_width), F32),
            [VMEM] * (2 + 2 * len(chunks)),
            "project_far_mine",
        )(*far_weights, *(a for pair in begun for a in pair))
        parts = [
            normed(f"norm_{i}", (False,), rows, other, far_begun) for i, rows in enumerate(chunks)
        ]
        far = [
            send_far(i, functools.partial(far_kernel, rows), far_begun, *parts[i], *far_weights)
            for i, rows in enumerate(chunks)
        ]
        pairs = [pair for i in range(len(chunks)) for pair in (begun[i], parts[i])]
        return finish(((True,), (False,)), pairs, far)

    return lax.cond(first, first_group, later_group)


def solution(mesh):
    return jax.shard_map(
        on_device,
        mesh=mesh,
        in_specs=(
            P("seq", "tp"),
            P("seq", "tp"),
            P("seq", "tp"),
            P("seq", "tp"),
            P("tp", "seq"),
            P("tp"),
            P("tp", None),
        ),
        out_specs=P("seq", "tp"),
        check_vma=False,
    )
```

```python
import functools

import jax
import jax.numpy as jnp
from jax import lax
from jax.experimental import pallas as pl
from jax.experimental.pallas import tpu as pltpu
from jax.sharding import PartitionSpec as P

HEAD_DIM = 128
GROUP = 256
SCALE = HEAD_DIM ** (-0.5)
F32 = jnp.float32
BF16 = jnp.bfloat16
VMEM = pl.BlockSpec(memory_space=pltpu.VMEM)
HBM = pl.BlockSpec(memory_space=pltpu.HBM)
DECAY_ROWS = 16
MEMBERS = 4
PARAMS = pltpu.CompilerParams(vmem_limit_bytes=24 * 1024 * 1024)


def state_rows(j):
    return slice(j * HEAD_DIM, (j + 1) * HEAD_DIM)


def place():
    return lax.rem(lax.axis_index("seq"), MEMBERS)


def side():
    return lax.rem(lax.axis_index("seq"), 2)


def half_at(owner, size):
    return pl.ds(pl.multiple_of(owner * size, size), size)


def pick(owner, values, axis):
    half = values.shape[axis] // 2
    low = lax.slice_in_dim(values, 0, half, axis=axis)
    high = lax.slice_in_dim(values, half, 2 * half, axis=axis)
    return jnp.where(owner == 0, low, high)


def contract(a, b):
    return lax.dot_general(a, b, (((1,), (1,)), ((), ())), preferred_element_type=F32)


def positions():
    shape = (GROUP, GROUP)
    return lax.broadcasted_iota(jnp.int32, shape, 0), lax.broadcasted_iota(jnp.int32, shape, 1)


def three_terms(values):
    first = values.astype(BF16).astype(F32)
    second = (values - first).astype(BF16).astype(F32)
    third = values - first - second
    return jnp.concatenate([first, second, third], axis=0).astype(BF16)


def sums_down(mask, decays):
    heads = decays.shape[0]
    terms = contract(mask, three_terms(decays))
    return terms[:, :heads] + terms[:, heads : 2 * heads] + terms[:, 2 * heads :]


def sums_across(mask, decays):
    heads = decays.shape[0]
    terms = contract(three_terms(decays), mask)
    return terms[:heads] + terms[heads : 2 * heads] + terms[2 * heads :]


def decays_to_rows(decays):
    each = DECAY_ROWS // (2 * len(decays))
    wide = jnp.concatenate([jnp.broadcast_to(d, (each, HEAD_DIM)) for d in decays], axis=0)
    coarse = wide.astype(BF16).astype(F32)
    return jnp.concatenate([coarse, wide - coarse], axis=0).astype(BF16)


def rows_to_decays(rows, count):
    rows = rows.astype(F32)
    each = DECAY_ROWS // (2 * count)
    both = rows[: DECAY_ROWS // 2] + rows[DECAY_ROWS // 2 :]
    return [both[j * each : j * each + 1] for j in range(count)]


def state_kernel(half, *refs):
    sources, outs, held, sems = refs[:5], refs[5:7], refs[7:12], refs[12]
    copies = [
        pltpu.make_async_copy(source, target, sems.at[i])
        for i, (source, target) in enumerate(zip(sources, held))
    ]
    for copy in copies:
        copy.start()
    decay_ref, key_ref, value_ref = held[:3]
    me = side()
    row, col = positions()
    later = jnp.where(col > row, 1.0, 0.0).astype(BF16)
    copies[0].wait()
    decays = decay_ref[...]
    tail = jnp.exp(sums_across(later, decays))
    whole = jnp.exp(jnp.sum(decays, axis=1, keepdims=True))
    copies[1].wait()
    copies[2].wait()
    decay_rows = decays_to_rows([whole[h : h + 1] for h in range(2 * half)])
    for owner, out_ref in zip((1 - me, me), outs):
        factors = pick(owner, tail, 0)
        for j in range(half):
            at = half_at(owner * half + j, HEAD_DIM)
            weighted = (key_ref[:, at].T.astype(F32) * factors[j : j + 1, :]).astype(BF16)
            update = jnp.dot(weighted, value_ref[:, at], preferred_element_type=F32)
            out_ref[state_rows(j), :] = update.astype(BF16)
        out_ref[half * HEAD_DIM :, :] = decay_rows
    for copy in copies[3:]:
        copy.wait()


def local_kernel(heads, decay_ref, query_ref, key_ref, value_ref, intra_ref, own_ref):
    row, col = positions()
    causal = col <= row
    upto = jnp.where(causal, 1.0, 0.0).astype(BF16)
    decays = decay_ref[...]
    down = sums_down(upto, decays)
    across = sums_across(upto, decays)
    own_ref[...] = jnp.exp(down) * SCALE
    for h in range(heads):
        at = slice(h * HEAD_DIM, (h + 1) * HEAD_DIM)
        scores = contract(query_ref[:, at], key_ref[:, at])
        gaps = down[:, h : h + 1] - across[h : h + 1, :]
        weights = jnp.where(causal, jnp.exp(gaps), 0.0)
        probs = (scores * SCALE * weights).astype(BF16)
        intra_ref[:, at] = jnp.dot(probs, value_ref[:, at], preferred_element_type=F32)


def gather_kernel(half, steps, *refs):
    received, (before_ref, sent_ref, through_ref, total_ref, held_ref) = (
        refs[: len(steps)],
        refs[len(steps) :],
    )
    me, upper = place(), side() == 1
    for step, message_ref in zip(steps, received):
        held_ref[me ^ step] = message_ref[...]
    later_pair = me >= 2
    decays = [rows_to_decays(held_ref[m, half * HEAD_DIM :, :], 2 * half) for m in range(MEMBERS)]
    totals = []
    for j in range(2 * half):
        low, high = (j, half + j) if j < half else (j, j - half)
        decay = [jnp.where(upper, d[high], d[low]) for d in decays]
        through = [jnp.ones((1, HEAD_DIM), F32)]
        for m in range(MEMBERS):
            through.append(through[m] * decay[m])
        first, last = [jnp.where(later_pair, through[2 + i], through[i]) for i in range(2)]
        factor = jnp.where(upper, last, first)
        through_ref[j * 8 : (j + 1) * 8, :] = jnp.broadcast_to(factor, (8, HEAD_DIM))
        if j >= half:
            continue
        at = state_rows(j)
        held = [jnp.zeros((HEAD_DIM, HEAD_DIM), F32)]
        for m in range(MEMBERS):
            held.append(held[m] * decay[m] + held_ref[m, at, :].astype(F32))
        first, last = [jnp.where(later_pair, held[2 + i], held[i]) for i in range(2)]
        before_ref[at, :] = jnp.where(upper, last, first)
        sent_ref[at, :] = jnp.where(upper, first, last).astype(BF16)
        total_ref[at, :] = held[MEMBERS].astype(BF16)
        totals.append(through[MEMBERS])
    total_ref[half * HEAD_DIM :, :] = decays_to_rows(totals)


def start_kernel(half, before_ref, through_ref, inside_ref, earlier_ref, _, *outs):
    mine_ref, rest_ref, factor_ref, sent_ref = outs
    started = lax.axis_index("seq") >= MEMBERS
    for j in range(half):
        at = state_rows(j)
        earlier = jnp.where(started, earlier_ref[at, :].astype(F32), 0.0)
        held = before_ref[at, :] + through_ref[8 * j : 8 * j + 1, :] * earlier
        mine_ref[at, :] = held.astype(BF16)
    rest_ref[...] = inside_ref[...]
    factor_ref[...] = through_ref[8 * half :, :]
    sent_ref[...] = earlier_ref[...]


def start_other_kernel(half, rest_ref, factor_ref, earlier_ref, _, out_ref):
    for j in range(half):
        at = state_rows(j)
        earlier = factor_ref[8 * j : 8 * j + 1, :] * earlier_ref[at, :].astype(F32)
        out_ref[at, :] = (rest_ref[at, :].astype(F32) + earlier).astype(BF16)


def norm_kernel(half, halves, rows, query_ref, intra_ref, own_ref, gain_ref, *refs):
    states, out_ref = refs[: len(halves)], refs[-1]
    for i, (mine, state_ref) in enumerate(zip(halves, states)):
        owner = side() if mine else 1 - side()
        own = pick(owner, own_ref[rows, :], 1)
        for j in range(half):
            at = half_at(owner * half + j, HEAD_DIM)
            state = state_ref[state_rows(j), :]
            inter = jnp.dot(query_ref[rows, at], state, preferred_element_type=F32)
            attended = intra_ref[rows, at] + own[:, j : j + 1] * inter
            mean_square = jnp.mean(attended * attended, axis=-1, keepdims=True)
            normed = (attended * lax.rsqrt(mean_square + 1e-06) * gain_ref[:, at]).astype(BF16)
            to = (i * half + j) * HEAD_DIM
            out_ref[:, to : to + HEAD_DIM] = normed


def share(halves, pair, weights):
    rows = weights[0].shape[0] // 2
    total = None
    for i, mine in enumerate(halves):
        at = half_at(side() if mine else 1 - side(), rows)
        for normed_ref, weight_ref in zip(pair, weights):
            normed = normed_ref[:, i * rows : (i + 1) * rows]
            part = jnp.dot(normed, weight_ref[at, :], preferred_element_type=F32)
            total = part if total is None else total + part
    return total


def fetch(step, whole, held, sems):
    copies = []
    for i, (weight, ref) in enumerate(zip(whole, held)):
        at = half_at(lax.axis_index("tp") ^ step, ref.shape[1])
        copies.append(pltpu.make_async_copy(weight.at[:, at], ref, sems.at[i]))
        copies[i].start()
    return copies


def fetch_kernel(weight_hbm, other_weight_hbm, _, weight_ref, other_weight_ref, sems):
    for copy in fetch(3, (weight_hbm, other_weight_hbm), (weight_ref, other_weight_ref), sems):
        copy.wait()


def far_mine_kernel(chunks, weight_ref, other_weight_ref, *refs):
    for i, rows in enumerate(chunks):
        pair = refs[2 * i : 2 * i + 2]
        refs[-1][rows, :] = share((True,), pair, (weight_ref, other_weight_ref))


def far_kernel(rows, begun_ref, mine_ref, other_ref, weight_ref, other_weight_ref, out_ref):
    rest = share((False,), (mine_ref, other_ref), (weight_ref, other_weight_ref))
    out_ref[...] = (begun_ref[rows, :] + rest).astype(BF16)


def far_all_kernel(mine_ref, other_ref, weight_ref, other_weight_ref, out_ref):
    pair, weights = (mine_ref, other_ref), (weight_ref, other_weight_ref)
    out_ref[...] = share((True, False), pair, weights).astype(BF16)


def near_kernel(chunks, passes, residual_hbm, weight_hbm, other_weight_hbm, *refs):
    out_ref, residual_ref, *weights, sems = refs[-5:]
    copies = fetch(0, (weight_hbm, other_weight_hbm), weights, sems)
    copies.append(pltpu.make_async_copy(residual_hbm, residual_ref, sems.at[2]))
    copies[2].start()
    for copy in copies:
        copy.wait()
    pairs = iter(zip(refs[0:-5:2], refs[1:-5:2]))
    for rows in chunks:
        near = residual_ref[rows, :].astype(F32)
        for halves in passes:
            near = near + share(halves, next(pairs), weights)
        out_ref[rows, :] = near


def add_kernel(chunks, near_ref, *refs):
    far, (out_hbm, out_ref, sems) = refs[: len(chunks)], refs[len(chunks) :]
    copies = []
    for i, rows in enumerate(chunks):
        out_ref[rows, :] = (near_ref[rows, :] + far[i][...].astype(F32)).astype(BF16)
        copies.append(
            pltpu.make_async_copy(out_ref.at[rows, :], out_hbm.at[rows, :], sems.at[i])
        )
        copies[-1].start()
    for copy in copies:
        copy.wait()


def call(kernel, out_shape, in_specs, name, out_specs=None, scratch=(), cost=0):
    single = isinstance(out_shape, jax.ShapeDtypeStruct)
    if out_specs is None:
        out_specs = VMEM if single else (VMEM,) * len(out_shape)
    cost = pl.CostEstimate(
        flops=cost, bytes_accessed=2_000_000 if cost else 0, transcendentals=0
    )
    return pl.pallas_call(
        kernel,
        out_shape=out_shape,
        in_specs=in_specs,
        out_specs=out_specs,
        scratch_shapes=scratch,
        compiler_params=PARAMS,
        cost_estimate=cost,
        name=name,
    )


def earlier_groups(total, half, devices):
    groups = devices // MEMBERS
    if groups == 2:
        return lax.ppermute(total, "seq", [(i, i ^ MEMBERS) for i in range(devices)])

    def shift(message, by):
        moves = [(i, i + by * MEMBERS) for i in range(devices - by * MEMBERS)]
        return lax.ppermute(message, "seq", moves)

    rows = half * HEAD_DIM
    held = shift(total, 1)
    by = 1
    while by < groups - 1:
        before = shift(held, by)
        decays = rows_to_decays(held[rows:], half)
        factor = jnp.concatenate([jnp.broadcast_to(d, (HEAD_DIM, HEAD_DIM)) for d in decays])
        state = held[:rows].astype(F32) + factor * before[:rows].astype(F32)
        through = [a * b for a, b in zip(decays, rows_to_decays(before[rows:], half))]
        held = jnp.concatenate([state.astype(BF16), decays_to_rows(through)], axis=0)
        by *= 2
    return held


def on_device(
    residual, query_vectors, key_vectors, value_vectors, log_decay, norm_gain, out_weight
):
    tokens, width = residual.shape
    heads = log_decay.shape[0]
    half = heads // 2
    devices = lax.axis_size("seq")
    tp = lax.axis_size("tp")
    wide = (tokens, heads * HEAD_DIM)
    out_width = out_weight.shape[1] // tp
    states = (half * HEAD_DIM, HEAD_DIM)
    near_pairs = [(i, i ^ 1) for i in range(tp)]
    far_pairs = [(i, i ^ 3) for i in range(tp)]
    shape = jax.ShapeDtypeStruct
    message = shape((half * HEAD_DIM + DECAY_ROWS, HEAD_DIM), BF16)

    def swap(piece, step):
        return lax.ppermute(piece, "seq", [(i, i ^ step) for i in range(devices)])

    other_weight = lax.ppermute(out_weight, "tp", near_pairs)
    weight = pltpu.with_memory_space_constraint(out_weight, pltpu.HBM)
    arguments = (log_decay, key_vectors, value_vectors, query_vectors, norm_gain.reshape(1, -1))
    theirs, mine, decays, keys, values, queries, gain = call(
        functools.partial(state_kernel, half),
        (message, message) + tuple(shape(a.shape, a.dtype) for a in arguments),
        [HBM] * 5,
        "states",
        scratch=[pltpu.SemaphoreType.DMA((5,))],
    )(*(pltpu.with_memory_space_constraint(a, pltpu.HBM) for a in arguments))
    steps = (3, 1, 2, 0)
    received = [swap(theirs, 3), swap(theirs, 1), swap(mine, 2), mine]
    state = shape(states, BF16)
    before, sent, through, total = call(
        functools.partial(gather_kernel, half, steps),
        (shape(states, F32), state, shape((heads * 8, HEAD_DIM), F32), message),
        [VMEM] * len(steps),
        "gather_states",
        scratch=[pltpu.VMEM((MEMBERS,) + message.shape, BF16)],
    )(*received)
    earlier = earlier_groups(total, half, devices)
    inside = swap(sent, 1)
    intra, own = call(
        functools.partial(local_kernel, heads),
        (shape(wide, F32), shape((tokens, heads), F32)),
        [VMEM] * 4,
        "local",
        cost=4 * tokens * tokens * heads * HEAD_DIM,
    )(decays, queries, keys, values)
    mine, rest, factor, sent = call(
        functools.partial(start_kernel, half),
        (state, state, shape((half * 8, HEAD_DIM), F32), message),
        [VMEM] * 5,
        "start_states",
    )(before, through, inside, earlier, own)

    chunks = [slice(0, tokens // 2), slice(tokens // 2, tokens)]
    block = (out_weight.shape[0], out_width)
    weights = (weight, other_weight)
    weight_specs = [HBM, pl.BlockSpec(memory_space=pl.ANY)]

    def normed(name, halves, rows, *states):
        part = call(
            functools.partial(norm_kernel, half, halves, rows),
            shape((rows.stop - rows.start, len(halves) * half * HEAD_DIM), BF16),
            [VMEM] * (4 + len(states)),
            name,
        )(queries, intra, own, gain, *states)
        return part, lax.ppermute(part, "tp", near_pairs)

    def far_columns(after):
        return call(
            fetch_kernel,
            (shape(block, BF16),) * 2,
            weight_specs + [VMEM],
            "fetch_far",
            scratch=[pltpu.SemaphoreType.DMA((2,))],
        )(*weights, after)

    def send_far(i, kernel, *operands):
        part = call(
            kernel,
            shape((chunks[i].stop - chunks[i].start, out_width), BF16),
            [VMEM] * len(operands),
            f"project_far_{i}",
        )(*operands)
        return lax.ppermute(part, "tp", far_pairs)

    def finish(passes, pairs, far):
        near = call(
            functools.partial(near_kernel, chunks, passes),
            shape((tokens, out_width), F32),
            [HBM] + weight_specs + [VMEM] * (2 * len(pairs)),
            "project_near",
            scratch=[
                pltpu.VMEM(residual.shape, BF16),
                pltpu.VMEM(block, BF16),
                pltpu.VMEM(block, BF16),
                pltpu.SemaphoreType.DMA((3,)),
            ],
        )(
            pltpu.with_memory_space_constraint(residual, pltpu.HBM),
            *weights,
            *(a for pair in pairs for a in pair),
        )
        return call(
            functools.partial(add_kernel, chunks),
            pltpu.HBM((tokens, out_width), BF16),
            [VMEM] * (1 + len(chunks)),
            "add",
            out_specs=HBM,
            scratch=[
                pltpu.VMEM((tokens, out_width), BF16),
                pltpu.SemaphoreType.DMA((len(chunks),)),
            ],
        )(near, *far)

    def first_group():
        both = (True, False)
        pairs = [normed(f"norm_{i}", both, rows, mine, rest) for i, rows in enumerate(chunks)]
        far_weights = far_columns(pairs[-1][0])
        far = [send_far(i, far_all_kernel, *pairs[i], *far_weights) for i in range(len(chunks))]
        return finish((both,), pairs, far)

    def later_group():
        swapped = swap(sent, 1)
        begun = [normed(f"norm_mine_{i}", (True,), rows, mine) for i, rows in enumerate(chunks)]
        far_weights = far_columns(begun[-1][0])
        far_begun = call(
            functools.partial(far_mine_kernel, chunks),
            shape((tokens, out_width), F32),
            [VMEM] * (2 + 2 * len(chunks)),
            "project_far_mine",
        )(*far_weights, *(a for pair in begun for a in pair))
        other = call(functools.partial(start_other_kernel, half), state, [VMEM] * 4, "start_other")(
            rest, factor, swapped, far_begun
        )
        parts = [normed(f"norm_{i}", (False,), rows, other) for i, rows in enumerate(chunks)]
        far = [
            send_far(i, functools.partial(far_kernel, rows), far_begun, *parts[i], *far_weights)
            for i, rows in enumerate(chunks)
        ]
        pairs = [pair for i in range(len(chunks)) for pair in (begun[i], parts[i])]
        return finish(((True,), (False,)), pairs, far)

    return lax.cond(lax.axis_index("seq") < MEMBERS, first_group, later_group)


def solution(mesh):
    return jax.shard_map(
        on_device,
        mesh=mesh,
        in_specs=(
            P("seq", "tp"),
            P("seq", "tp"),
            P("seq", "tp"),
            P("seq", "tp"),
            P("tp", "seq"),
            P("tp"),
            P("tp", None),
        ),
        out_specs=P("seq", "tp"),
        check_vma=False,
    )
```

```python
import functools

import jax
import jax.numpy as jnp
from jax import lax
from jax.experimental import pallas as pl
from jax.experimental.pallas import tpu as pltpu
from jax.sharding import PartitionSpec as P

HEAD_DIM = 128
GROUP = 256
SCALE = HEAD_DIM ** (-0.5)
F32 = jnp.float32
BF16 = jnp.bfloat16
VMEM = pl.BlockSpec(memory_space=pltpu.VMEM)
HBM = pl.BlockSpec(memory_space=pltpu.HBM)
DECAY_ROWS = 16
MEMBERS = 4
PARAMS = pltpu.CompilerParams(vmem_limit_bytes=24 * 1024 * 1024)


def state_rows(j):
    return slice(j * HEAD_DIM, (j + 1) * HEAD_DIM)


def place():
    return lax.rem(lax.axis_index("seq"), MEMBERS)


def side():
    return lax.rem(lax.axis_index("seq"), 2)


def half_at(owner, size):
    return pl.ds(pl.multiple_of(owner * size, size), size)


def pick(owner, values, axis):
    half = values.shape[axis] // 2
    low = lax.slice_in_dim(values, 0, half, axis=axis)
    high = lax.slice_in_dim(values, half, 2 * half, axis=axis)
    return jnp.where(owner == 0, low, high)


def contract(a, b):
    return lax.dot_general(a, b, (((1,), (1,)), ((), ())), preferred_element_type=F32)


def positions():
    shape = (GROUP, GROUP)
    return lax.broadcasted_iota(jnp.int32, shape, 0), lax.broadcasted_iota(jnp.int32, shape, 1)


def three_terms(values):
    first = values.astype(BF16).astype(F32)
    second = (values - first).astype(BF16).astype(F32)
    third = values - first - second
    return jnp.concatenate([first, second, third], axis=0).astype(BF16)


def sums_down(mask, decays):
    heads = decays.shape[0]
    terms = contract(mask, three_terms(decays))
    return terms[:, :heads] + terms[:, heads : 2 * heads] + terms[:, 2 * heads :]


def sums_across(mask, decays):
    heads = decays.shape[0]
    terms = contract(three_terms(decays), mask)
    return terms[:heads] + terms[heads : 2 * heads] + terms[2 * heads :]


def decays_to_rows(decays):
    each = DECAY_ROWS // (2 * len(decays))
    wide = jnp.concatenate([jnp.broadcast_to(d, (each, HEAD_DIM)) for d in decays], axis=0)
    coarse = wide.astype(BF16).astype(F32)
    return jnp.concatenate([coarse, wide - coarse], axis=0).astype(BF16)


def rows_to_decays(rows, count):
    rows = rows.astype(F32)
    each = DECAY_ROWS // (2 * count)
    both = rows[: DECAY_ROWS // 2] + rows[DECAY_ROWS // 2 :]
    return [both[j * each : j * each + 1] for j in range(count)]


def state_kernel(half, *refs):
    sources, outs, held, sems = refs[:5], refs[5:7], refs[7:12], refs[12]
    copies = [
        pltpu.make_async_copy(source, target, sems.at[i])
        for i, (source, target) in enumerate(zip(sources, held))
    ]
    for copy in copies:
        copy.start()
    decay_ref, key_ref, value_ref = held[:3]
    me = side()
    row, col = positions()
    later = jnp.where(col > row, 1.0, 0.0).astype(BF16)
    copies[0].wait()
    decays = decay_ref[...]
    tail = jnp.exp(sums_across(later, decays))
    whole = jnp.exp(jnp.sum(decays, axis=1, keepdims=True))
    copies[1].wait()
    copies[2].wait()
    decay_rows = decays_to_rows([whole[h : h + 1] for h in range(2 * half)])
    for owner, out_ref in zip((1 - me, me), outs):
        factors = pick(owner, tail, 0)
        for j in range(half):
            at = half_at(owner * half + j, HEAD_DIM)
            weighted = (key_ref[:, at].T.astype(F32) * factors[j : j + 1, :]).astype(BF16)
            update = jnp.dot(weighted, value_ref[:, at], preferred_element_type=F32)
            out_ref[state_rows(j), :] = update.astype(BF16)
        out_ref[half * HEAD_DIM :, :] = decay_rows
    for copy in copies[3:]:
        copy.wait()


def local_kernel(heads, decay_ref, query_ref, key_ref, value_ref, intra_ref, own_ref):
    row, col = positions()
    causal = col <= row
    upto = jnp.where(causal, 1.0, 0.0).astype(BF16)
    decays = decay_ref[...]
    down = sums_down(upto, decays)
    across = sums_across(upto, decays)
    own_ref[...] = jnp.exp(down) * SCALE
    for h in range(heads):
        at = slice(h * HEAD_DIM, (h + 1) * HEAD_DIM)
        scores = contract(query_ref[:, at], key_ref[:, at])
        gaps = down[:, h : h + 1] - across[h : h + 1, :]
        weights = jnp.where(causal, jnp.exp(gaps), 0.0)
        probs = (scores * SCALE * weights).astype(BF16)
        intra_ref[:, at] = jnp.dot(probs, value_ref[:, at], preferred_element_type=F32)


def gather_kernel(half, steps, *refs):
    received, (before_ref, sent_ref, through_ref, total_ref, held_ref) = (
        refs[: len(steps)],
        refs[len(steps) :],
    )
    me, upper = place(), side() == 1
    for step, message_ref in zip(steps, received):
        held_ref[me ^ step] = message_ref[...]
    later_pair = me >= 2
    decays = [rows_to_decays(held_ref[m, half * HEAD_DIM :, :], 2 * half) for m in range(MEMBERS)]
    totals = []
    for j in range(2 * half):
        low, high = (j, half + j) if j < half else (j, j - half)
        decay = [jnp.where(upper, d[high], d[low]) for d in decays]
        through = [jnp.ones((1, HEAD_DIM), F32)]
        for m in range(MEMBERS):
            through.append(through[m] * decay[m])
        first, last = [jnp.where(later_pair, through[2 + i], through[i]) for i in range(2)]
        factor = jnp.where(upper, last, first)
        through_ref[j * 8 : (j + 1) * 8, :] = jnp.broadcast_to(factor, (8, HEAD_DIM))
        if j >= half:
            continue
        at = state_rows(j)
        held = [jnp.zeros((HEAD_DIM, HEAD_DIM), F32)]
        for m in range(MEMBERS):
            held.append(held[m] * decay[m] + held_ref[m, at, :].astype(F32))
        first, last = [jnp.where(later_pair, held[2 + i], held[i]) for i in range(2)]
        before_ref[at, :] = jnp.where(upper, last, first)
        sent_ref[at, :] = jnp.where(upper, first, last).astype(BF16)
        total_ref[at, :] = held[MEMBERS].astype(BF16)
        totals.append(through[MEMBERS])
    total_ref[half * HEAD_DIM :, :] = decays_to_rows(totals)


def start_kernel(half, before_ref, through_ref, inside_ref, earlier_ref, _, *outs):
    mine_ref, rest_ref, factor_ref, sent_ref = outs
    started = lax.axis_index("seq") >= MEMBERS
    for j in range(half):
        at = state_rows(j)
        earlier = jnp.where(started, earlier_ref[at, :].astype(F32), 0.0)
        held = before_ref[at, :] + through_ref[8 * j : 8 * j + 1, :] * earlier
        mine_ref[at, :] = held.astype(BF16)
    rest_ref[...] = inside_ref[...]
    factor_ref[...] = through_ref[8 * half :, :]
    sent_ref[...] = earlier_ref[...]


def start_other_kernel(half, rest_ref, factor_ref, earlier_ref, _, out_ref):
    for j in range(half):
        at = state_rows(j)
        earlier = factor_ref[8 * j : 8 * j + 1, :] * earlier_ref[at, :].astype(F32)
        out_ref[at, :] = (rest_ref[at, :].astype(F32) + earlier).astype(BF16)


def nothing_kernel(out_ref):
    pass


def norm_kernel(half, halves, rows, query_ref, intra_ref, own_ref, gain_ref, *refs):
    states, out_ref = refs[: len(halves)], refs[-1]
    for i, (mine, state_ref) in enumerate(zip(halves, states)):
        owner = side() if mine else 1 - side()
        own = pick(owner, own_ref[rows, :], 1)
        for j in range(half):
            at = half_at(owner * half + j, HEAD_DIM)
            state = state_ref[state_rows(j), :]
            inter = jnp.dot(query_ref[rows, at], state, preferred_element_type=F32)
            attended = intra_ref[rows, at] + own[:, j : j + 1] * inter
            mean_square = jnp.mean(attended * attended, axis=-1, keepdims=True)
            normed = (attended * lax.rsqrt(mean_square + 1e-06) * gain_ref[:, at]).astype(BF16)
            to = (i * half + j) * HEAD_DIM
            out_ref[:, to : to + HEAD_DIM] = normed


def share(halves, pair, weights):
    rows = weights[0].shape[0] // 2
    total = None
    for i, mine in enumerate(halves):
        at = half_at(side() if mine else 1 - side(), rows)
        for normed_ref, weight_ref in zip(pair, weights):
            normed = normed_ref[:, i * rows : (i + 1) * rows]
            part = jnp.dot(normed, weight_ref[at, :], preferred_element_type=F32)
            total = part if total is None else total + part
    return total


def fetch(step, whole, held, sems):
    copies = []
    for i, (weight, ref) in enumerate(zip(whole, held)):
        at = half_at(lax.axis_index("tp") ^ step, ref.shape[1])
        copies.append(pltpu.make_async_copy(weight.at[:, at], ref, sems.at[i]))
        copies[i].start()
    return copies


def fetch_kernel(weight_hbm, other_weight_hbm, _, weight_ref, other_weight_ref, sems):
    for copy in fetch(2, (weight_hbm, other_weight_hbm), (weight_ref, other_weight_ref), sems):
        copy.wait()


def far_mine_kernel(chunks, weight_ref, other_weight_ref, *refs):
    for i, rows in enumerate(chunks):
        pair = refs[2 * i : 2 * i + 2]
        refs[-1][rows, :] = share((True,), pair, (weight_ref, other_weight_ref))


def far_kernel(rows, begun_ref, mine_ref, other_ref, weight_ref, other_weight_ref, out_ref):
    rest = share((False,), (mine_ref, other_ref), (weight_ref, other_weight_ref))
    out_ref[...] = (begun_ref[rows, :] + rest).astype(BF16)


def far_all_kernel(mine_ref, other_ref, weight_ref, other_weight_ref, out_ref):
    pair, weights = (mine_ref, other_ref), (weight_ref, other_weight_ref)
    out_ref[...] = share((True, False), pair, weights).astype(BF16)


def near_kernel(chunks, passes, residual_hbm, weight_hbm, other_weight_hbm, *refs):
    out_ref, residual_ref, *weights, sems = refs[-5:]
    copies = fetch(0, (weight_hbm, other_weight_hbm), weights, sems)
    copies.append(pltpu.make_async_copy(residual_hbm, residual_ref, sems.at[2]))
    copies[2].start()
    for copy in copies:
        copy.wait()
    pairs = iter(zip(refs[0:-5:2], refs[1:-5:2]))
    for rows in chunks:
        near = residual_ref[rows, :].astype(F32)
        for halves in passes:
            near = near + share(halves, next(pairs), weights)
        out_ref[rows, :] = near


def add_kernel(chunks, near_ref, *refs):
    far, (out_hbm, out_ref, sems) = refs[: len(chunks)], refs[len(chunks) :]
    copies = []
    for i, rows in enumerate(chunks):
        out_ref[rows, :] = (near_ref[rows, :] + far[i][...].astype(F32)).astype(BF16)
        copies.append(
            pltpu.make_async_copy(out_ref.at[rows, :], out_hbm.at[rows, :], sems.at[i])
        )
        copies[-1].start()
    for copy in copies:
        copy.wait()


def call(kernel, out_shape, in_specs, name, out_specs=None, scratch=(), cost=0):
    single = isinstance(out_shape, jax.ShapeDtypeStruct)
    if out_specs is None:
        out_specs = VMEM if single else (VMEM,) * len(out_shape)
    cost = pl.CostEstimate(
        flops=cost, bytes_accessed=2_000_000 if cost else 0, transcendentals=0
    )
    return pl.pallas_call(
        kernel,
        out_shape=out_shape,
        in_specs=in_specs,
        out_specs=out_specs,
        scratch_shapes=scratch,
        compiler_params=PARAMS,
        cost_estimate=cost,
        name=name,
    )


def earlier_groups(total, half, devices, first_alone):
    groups = devices // MEMBERS
    if groups == 2:
        tp = lax.axis_size("tp")
        swapped = first_alone(
            lambda: lax.ppermute(total, "tp", [(i, i ^ 1) for i in range(tp)]), total
        )
        pairs = [
            (i * tp + j, (i ^ MEMBERS) * tp + (j ^ 1)) for i in range(devices) for j in range(tp)
        ]
        return lax.ppermute(swapped, ("seq", "tp"), pairs)

    def shift(message, by):
        moves = [(i, i + by * MEMBERS) for i in range(devices - by * MEMBERS)]
        return lax.ppermute(message, "seq", moves)

    rows = half * HEAD_DIM
    held = shift(total, 1)
    by = 1
    while by < groups - 1:
        before = shift(held, by)
        decays = rows_to_decays(held[rows:], half)
        factor = jnp.concatenate([jnp.broadcast_to(d, (HEAD_DIM, HEAD_DIM)) for d in decays])
        state = held[:rows].astype(F32) + factor * before[:rows].astype(F32)
        through = [a * b for a, b in zip(decays, rows_to_decays(before[rows:], half))]
        held = jnp.concatenate([state.astype(BF16), decays_to_rows(through)], axis=0)
        by *= 2
    return held


def on_device(
    residual, query_vectors, key_vectors, value_vectors, log_decay, norm_gain, out_weight
):
    tokens, width = residual.shape
    heads = log_decay.shape[0]
    half = heads // 2
    devices = lax.axis_size("seq")
    tp = lax.axis_size("tp")
    wide = (tokens, heads * HEAD_DIM)
    out_width = out_weight.shape[1] // tp
    states = (half * HEAD_DIM, HEAD_DIM)
    near_pairs = [(i, i ^ 1) for i in range(tp)]
    far_pairs = [(i, i ^ 2) for i in range(tp)]
    shape = jax.ShapeDtypeStruct
    message = shape((half * HEAD_DIM + DECAY_ROWS, HEAD_DIM), BF16)

    def swap(piece, step):
        return lax.ppermute(piece, "seq", [(i, i ^ step) for i in range(devices)])

    other_weight = lax.ppermute(out_weight, "tp", near_pairs)
    weight = pltpu.with_memory_space_constraint(out_weight, pltpu.HBM)
    arguments = (log_decay, key_vectors, value_vectors, query_vectors, norm_gain.reshape(1, -1))
    theirs, mine, decays, keys, values, queries, gain = call(
        functools.partial(state_kernel, half),
        (message, message) + tuple(shape(a.shape, a.dtype) for a in arguments),
        [HBM] * 5,
        "states",
        scratch=[pltpu.SemaphoreType.DMA((5,))],
    )(*(pltpu.with_memory_space_constraint(a, pltpu.HBM) for a in arguments))
    steps = (3, 1, 2, 0)
    received = [swap(theirs, 3), swap(theirs, 1), swap(mine, 2), mine]
    state = shape(states, BF16)
    before, sent, through, total = call(
        functools.partial(gather_kernel, half, steps),
        (shape(states, F32), state, shape((heads * 8, HEAD_DIM), F32), message),
        [VMEM] * len(steps),
        "gather_states",
        scratch=[pltpu.VMEM((MEMBERS,) + message.shape, BF16)],
    )(*received)
    first = lax.axis_index("seq") < MEMBERS

    def first_alone(work, like):
        def nothing():
            return call(nothing_kernel, shape(like.shape, like.dtype), [], "nothing")()

        return lax.cond(first, work, nothing)

    earlier = earlier_groups(total, half, devices, first_alone)
    inside = swap(sent, 1)
    intra, own = call(
        functools.partial(local_kernel, heads),
        (shape(wide, F32), shape((tokens, heads), F32)),
        [VMEM] * 4,
        "local",
        cost=4 * tokens * tokens * heads * HEAD_DIM,
    )(decays, queries, keys, values)
    mine, rest, factor, sent = call(
        functools.partial(start_kernel, half),
        (state, state, shape((half * 8, HEAD_DIM), F32), message),
        [VMEM] * 5,
        "start_states",
    )(before, through, inside, earlier, own)

    chunks = [slice(0, tokens // 2), slice(tokens // 2, tokens)]
    block = (out_weight.shape[0], out_width)
    weights = (weight, other_weight)
    weight_specs = [HBM, pl.BlockSpec(memory_space=pl.ANY)]

    def normed(name, halves, rows, *states):
        part = call(
            functools.partial(norm_kernel, half, halves, rows),
            shape((rows.stop - rows.start, len(halves) * half * HEAD_DIM), BF16),
            [VMEM] * (4 + len(states)),
            name,
        )(queries, intra, own, gain, *states)
        return part, lax.ppermute(part, "tp", near_pairs)

    def far_columns(after):
        return call(
            fetch_kernel,
            (shape(block, BF16),) * 2,
            weight_specs + [VMEM],
            "fetch_far",
            scratch=[pltpu.SemaphoreType.DMA((2,))],
        )(*weights, after)

    def send_far(i, kernel, *operands):
        part = call(
            kernel,
            shape((chunks[i].stop - chunks[i].start, out_width), BF16),
            [VMEM] * len(operands),
            f"project_far_{i}",
        )(*operands)
        return lax.ppermute(part, "tp", far_pairs)

    def finish(passes, pairs, far):
        near = call(
            functools.partial(near_kernel, chunks, passes),
            shape((tokens, out_width), F32),
            [HBM] + weight_specs + [VMEM] * (2 * len(pairs)),
            "project_near",
            scratch=[
                pltpu.VMEM(residual.shape, BF16),
                pltpu.VMEM(block, BF16),
                pltpu.VMEM(block, BF16),
                pltpu.SemaphoreType.DMA((3,)),
            ],
        )(
            pltpu.with_memory_space_constraint(residual, pltpu.HBM),
            *weights,
            *(a for pair in pairs for a in pair),
        )
        return call(
            functools.partial(add_kernel, chunks),
            pltpu.HBM((tokens, out_width), BF16),
            [VMEM] * (1 + len(chunks)),
            "add",
            out_specs=HBM,
            scratch=[
                pltpu.VMEM((tokens, out_width), BF16),
                pltpu.SemaphoreType.DMA((len(chunks),)),
            ],
        )(near, *far)

    def first_group():
        both = (True, False)
        pairs = [normed(f"norm_{i}", both, rows, mine, rest) for i, rows in enumerate(chunks)]
        far_weights = far_columns(pairs[-1][0])
        far = [send_far(i, far_all_kernel, *pairs[i], *far_weights) for i in range(len(chunks))]
        return finish((both,), pairs, far)

    def later_group():
        swapped = swap(sent, 1)
        begun = [normed(f"norm_mine_{i}", (True,), rows, mine) for i, rows in enumerate(chunks)]
        far_weights = far_columns(begun[-1][0])
        far_begun = call(
            functools.partial(far_mine_kernel, chunks),
            shape((tokens, out_width), F32),
            [VMEM] * (2 + 2 * len(chunks)),
            "project_far_mine",
        )(*far_weights, *(a for pair in begun for a in pair))
        other = call(functools.partial(start_other_kernel, half), state, [VMEM] * 4, "start_other")(
            rest, factor, swapped, far_begun
        )
        parts = [normed(f"norm_{i}", (False,), rows, other) for i, rows in enumerate(chunks)]
        far = [
            send_far(i, functools.partial(far_kernel, rows), far_begun, *parts[i], *far_weights)
            for i, rows in enumerate(chunks)
        ]
        pairs = [pair for i in range(len(chunks)) for pair in (begun[i], parts[i])]
        return finish(((True,), (False,)), pairs, far)

    return lax.cond(first, first_group, later_group)


def solution(mesh):
    return jax.shard_map(
        on_device,
        mesh=mesh,
        in_specs=(
            P("seq", "tp"),
            P("seq", "tp"),
            P("seq", "tp"),
            P("seq", "tp"),
            P("tp", "seq"),
            P("tp"),
            P("tp", None),
        ),
        out_specs=P("seq", "tp"),
        check_vma=False,
    )
```

```python
import functools

import jax
import jax.numpy as jnp
from jax import lax
from jax.experimental import pallas as pl
from jax.experimental.pallas import tpu as pltpu
from jax.sharding import PartitionSpec as P

HEAD_DIM = 128
GROUP = 256
SCALE = HEAD_DIM ** (-0.5)
F32 = jnp.float32
BF16 = jnp.bfloat16
VMEM = pl.BlockSpec(memory_space=pltpu.VMEM)
HBM = pl.BlockSpec(memory_space=pltpu.HBM)
DECAY_ROWS = 16
MEMBERS = 4
PARAMS = pltpu.CompilerParams(vmem_limit_bytes=24 * 1024 * 1024)


def state_rows(j):
    return slice(j * HEAD_DIM, (j + 1) * HEAD_DIM)


def place():
    return lax.rem(lax.axis_index("seq"), MEMBERS)


def side():
    return lax.rem(lax.axis_index("seq"), 2)


def half_at(owner, size):
    return pl.ds(pl.multiple_of(owner * size, size), size)


def pick(owner, values, axis):
    half = values.shape[axis] // 2
    low = lax.slice_in_dim(values, 0, half, axis=axis)
    high = lax.slice_in_dim(values, half, 2 * half, axis=axis)
    return jnp.where(owner == 0, low, high)


def contract(a, b):
    return lax.dot_general(a, b, (((1,), (1,)), ((), ())), preferred_element_type=F32)


def positions():
    shape = (GROUP, GROUP)
    return lax.broadcasted_iota(jnp.int32, shape, 0), lax.broadcasted_iota(jnp.int32, shape, 1)


def three_terms(values):
    first = values.astype(BF16).astype(F32)
    second = (values - first).astype(BF16).astype(F32)
    third = values - first - second
    return jnp.concatenate([first, second, third], axis=0).astype(BF16)


def sums_down(mask, decays):
    heads = decays.shape[0]
    terms = contract(mask, three_terms(decays))
    return terms[:, :heads] + terms[:, heads : 2 * heads] + terms[:, 2 * heads :]


def sums_across(mask, decays):
    heads = decays.shape[0]
    terms = contract(three_terms(decays), mask)
    return terms[:heads] + terms[heads : 2 * heads] + terms[2 * heads :]


def decays_to_rows(decays):
    each = DECAY_ROWS // (2 * len(decays))
    wide = jnp.concatenate([jnp.broadcast_to(d, (each, HEAD_DIM)) for d in decays], axis=0)
    coarse = wide.astype(BF16).astype(F32)
    return jnp.concatenate([coarse, wide - coarse], axis=0).astype(BF16)


def rows_to_decays(rows, count):
    rows = rows.astype(F32)
    each = DECAY_ROWS // (2 * count)
    both = rows[: DECAY_ROWS // 2] + rows[DECAY_ROWS // 2 :]
    return [both[j * each : j * each + 1] for j in range(count)]


def state_kernel(half, *refs):
    sources, outs, held, sems = refs[:5], refs[5:7], refs[7:12], refs[12]
    copies = [
        pltpu.make_async_copy(source, target, sems.at[i])
        for i, (source, target) in enumerate(zip(sources, held))
    ]
    for copy in copies:
        copy.start()
    decay_ref, key_ref, value_ref = held[:3]
    me = side()
    row, col = positions()
    later = jnp.where(col > row, 1.0, 0.0).astype(BF16)
    copies[0].wait()
    decays = decay_ref[...]
    tail = jnp.exp(sums_across(later, decays))
    whole = jnp.exp(jnp.sum(decays, axis=1, keepdims=True))
    copies[1].wait()
    copies[2].wait()
    decay_rows = decays_to_rows([whole[h : h + 1] for h in range(2 * half)])
    for owner, out_ref in zip((1 - me, me), outs):
        factors = pick(owner, tail, 0)
        for j in range(half):
            at = half_at(owner * half + j, HEAD_DIM)
            weighted = (key_ref[:, at].T.astype(F32) * factors[j : j + 1, :]).astype(BF16)
            update = jnp.dot(weighted, value_ref[:, at], preferred_element_type=F32)
            out_ref[state_rows(j), :] = update.astype(BF16)
        out_ref[half * HEAD_DIM :, :] = decay_rows
    for copy in copies[3:]:
        copy.wait()


def local_kernel(heads, decay_ref, query_ref, key_ref, value_ref, intra_ref, own_ref):
    row, col = positions()
    causal = col <= row
    upto = jnp.where(causal, 1.0, 0.0).astype(BF16)
    decays = decay_ref[...]
    down = sums_down(upto, decays)
    across = sums_across(upto, decays)
    own_ref[...] = jnp.exp(down) * SCALE
    for h in range(heads):
        at = slice(h * HEAD_DIM, (h + 1) * HEAD_DIM)
        scores = contract(query_ref[:, at], key_ref[:, at])
        gaps = down[:, h : h + 1] - across[h : h + 1, :]
        weights = jnp.where(causal, jnp.exp(gaps), 0.0)
        probs = (scores * SCALE * weights).astype(BF16)
        intra_ref[:, at] = jnp.dot(probs, value_ref[:, at], preferred_element_type=F32)


def gather_kernel(half, steps, *refs):
    received, (before_ref, sent_ref, through_ref, total_ref, held_ref) = (
        refs[: len(steps)],
        refs[len(steps) :],
    )
    me, upper = place(), side() == 1
    for step, message_ref in zip(steps, received):
        held_ref[me ^ step] = message_ref[...]
    later_pair = me >= 2
    decays = [rows_to_decays(held_ref[m, half * HEAD_DIM :, :], 2 * half) for m in range(MEMBERS)]
    totals = []
    for j in range(2 * half):
        low, high = (j, half + j) if j < half else (j, j - half)
        decay = [jnp.where(upper, d[high], d[low]) for d in decays]
        through = [jnp.ones((1, HEAD_DIM), F32)]
        for m in range(MEMBERS):
            through.append(through[m] * decay[m])
        first, last = [jnp.where(later_pair, through[2 + i], through[i]) for i in range(2)]
        factor = jnp.where(upper, last, first)
        through_ref[j * 8 : (j + 1) * 8, :] = jnp.broadcast_to(factor, (8, HEAD_DIM))
        if j >= half:
            continue
        at = state_rows(j)
        held = [jnp.zeros((HEAD_DIM, HEAD_DIM), F32)]
        for m in range(MEMBERS):
            held.append(held[m] * decay[m] + held_ref[m, at, :].astype(F32))
        first, last = [jnp.where(later_pair, held[2 + i], held[i]) for i in range(2)]
        before_ref[at, :] = jnp.where(upper, last, first)
        sent_ref[at, :] = jnp.where(upper, first, last).astype(BF16)
        total_ref[at, :] = held[MEMBERS].astype(BF16)
        totals.append(through[MEMBERS])
    if total_ref.shape[0] > half * HEAD_DIM:
        total_ref[half * HEAD_DIM :, :] = decays_to_rows(totals)


def start_kernel(half, before_ref, through_ref, earlier_ref, inside_ref, _, *outs):
    mine_ref, rest_ref, factor_ref, sent_ref = outs
    started = lax.axis_index("seq") >= MEMBERS
    for j in range(half):
        at = state_rows(j)
        earlier = jnp.where(started, earlier_ref[at, :].astype(F32), 0.0)
        held = before_ref[at, :] + through_ref[8 * j : 8 * j + 1, :] * earlier
        mine_ref[at, :] = held.astype(BF16)
    rest_ref[...] = inside_ref[...]
    factor_ref[...] = through_ref[8 * half :, :]
    rows = half * HEAD_DIM
    sent_ref[:rows, :] = earlier_ref[:rows, :]
    sent_ref[rows:, :] = jnp.zeros((DECAY_ROWS, HEAD_DIM), BF16)


def start_other_kernel(half, rest_ref, factor_ref, earlier_ref, _, out_ref):
    for j in range(half):
        at = state_rows(j)
        earlier = factor_ref[8 * j : 8 * j + 1, :] * earlier_ref[at, :].astype(F32)
        out_ref[at, :] = (rest_ref[at, :].astype(F32) + earlier).astype(BF16)


def norm_kernel(half, halves, rows, query_ref, intra_ref, own_ref, gain_ref, *refs):
    states, out_ref = refs[: len(halves)], refs[-1]
    for i, (mine, state_ref) in enumerate(zip(halves, states)):
        owner = side() if mine else 1 - side()
        own = pick(owner, own_ref[rows, :], 1)
        for j in range(half):
            at = half_at(owner * half + j, HEAD_DIM)
            state = state_ref[state_rows(j), :]
            inter = jnp.dot(query_ref[rows, at], state, preferred_element_type=F32)
            attended = intra_ref[rows, at] + own[:, j : j + 1] * inter
            mean_square = jnp.mean(attended * attended, axis=-1, keepdims=True)
            normed = (attended * lax.rsqrt(mean_square + 1e-06) * gain_ref[:, at]).astype(BF16)
            to = (i * half + j) * HEAD_DIM
            out_ref[:, to : to + HEAD_DIM] = normed


def share(halves, pair, weights):
    rows = weights[0].shape[0] // 2
    total = None
    for i, mine in enumerate(halves):
        at = half_at(side() if mine else 1 - side(), rows)
        for normed_ref, weight_ref in zip(pair, weights):
            normed = normed_ref[:, i * rows : (i + 1) * rows]
            part = jnp.dot(normed, weight_ref[at, :], preferred_element_type=F32)
            total = part if total is None else total + part
    return total


def fetch(step, whole, held, sems):
    copies = []
    for i, (weight, ref) in enumerate(zip(whole, held)):
        at = half_at(lax.axis_index("tp") ^ step, ref.shape[1])
        copies.append(pltpu.make_async_copy(weight.at[:, at], ref, sems.at[i]))
        copies[i].start()
    return copies


def fetch_kernel(weight_hbm, other_weight_hbm, _, weight_ref, other_weight_ref, sems):
    for copy in fetch(2, (weight_hbm, other_weight_hbm), (weight_ref, other_weight_ref), sems):
        copy.wait()


def far_mine_kernel(chunks, weight_ref, other_weight_ref, *refs):
    for i, rows in enumerate(chunks):
        pair = refs[2 * i : 2 * i + 2]
        refs[-1][rows, :] = share((True,), pair, (weight_ref, other_weight_ref))


def far_kernel(rows, begun_ref, mine_ref, other_ref, weight_ref, other_weight_ref, out_ref):
    rest = share((False,), (mine_ref, other_ref), (weight_ref, other_weight_ref))
    out_ref[...] = (begun_ref[rows, :] + rest).astype(BF16)


def far_all_kernel(mine_ref, other_ref, weight_ref, other_weight_ref, out_ref):
    pair, weights = (mine_ref, other_ref), (weight_ref, other_weight_ref)
    out_ref[...] = share((True, False), pair, weights).astype(BF16)


def near_kernel(chunks, passes, residual_hbm, weight_hbm, other_weight_hbm, *refs):
    out_ref, residual_ref, *weights, sems = refs[-5:]
    copies = fetch(0, (weight_hbm, other_weight_hbm), weights, sems)
    copies.append(pltpu.make_async_copy(residual_hbm, residual_ref, sems.at[2]))
    copies[2].start()
    for copy in copies:
        copy.wait()
    pairs = iter(zip(refs[0:-5:2], refs[1:-5:2]))
    for rows in chunks:
        near = residual_ref[rows, :].astype(F32)
        for halves in passes:
            near = near + share(halves, next(pairs), weights)
        out_ref[rows, :] = near


def add_kernel(chunks, near_ref, *refs):
    far, (out_hbm, out_ref, sems) = refs[: len(chunks)], refs[len(chunks) :]
    copies = []
    for i, rows in enumerate(chunks):
        out_ref[rows, :] = (near_ref[rows, :] + far[i][...].astype(F32)).astype(BF16)
        copies.append(
            pltpu.make_async_copy(out_ref.at[rows, :], out_hbm.at[rows, :], sems.at[i])
        )
        copies[-1].start()
    for copy in copies:
        copy.wait()


def call(kernel, out_shape, in_specs, name, out_specs=None, scratch=(), cost=0):
    single = isinstance(out_shape, jax.ShapeDtypeStruct)
    if out_specs is None:
        out_specs = VMEM if single else (VMEM,) * len(out_shape)
    cost = pl.CostEstimate(
        flops=cost, bytes_accessed=2_000_000 if cost else 0, transcendentals=0
    )
    return pl.pallas_call(
        kernel,
        out_shape=out_shape,
        in_specs=in_specs,
        out_specs=out_specs,
        scratch_shapes=scratch,
        compiler_params=PARAMS,
        cost_estimate=cost,
        name=name,
    )


def earlier_groups(total, half, devices):
    groups = devices // MEMBERS
    if groups == 2:
        return lax.ppermute(total, "seq", [(i, i ^ MEMBERS) for i in range(devices)])

    def shift(message, by):
        moves = [(i, i + by * MEMBERS) for i in range(devices - by * MEMBERS)]
        return lax.ppermute(message, "seq", moves)

    rows = half * HEAD_DIM
    held = shift(total, 1)
    by = 1
    while by < groups - 1:
        before = shift(held, by)
        decays = rows_to_decays(held[rows:], half)
        factor = jnp.concatenate([jnp.broadcast_to(d, (HEAD_DIM, HEAD_DIM)) for d in decays])
        state = held[:rows].astype(F32) + factor * before[:rows].astype(F32)
        through = [a * b for a, b in zip(decays, rows_to_decays(before[rows:], half))]
        held = jnp.concatenate([state.astype(BF16), decays_to_rows(through)], axis=0)
        by *= 2
    return held


def on_device(
    residual, query_vectors, key_vectors, value_vectors, log_decay, norm_gain, out_weight
):
    tokens, width = residual.shape
    heads = log_decay.shape[0]
    half = heads // 2
    devices = lax.axis_size("seq")
    tp = lax.axis_size("tp")
    wide = (tokens, heads * HEAD_DIM)
    out_width = out_weight.shape[1] // tp
    states = (half * HEAD_DIM, HEAD_DIM)
    near_pairs = [(i, i ^ 1) for i in range(tp)]
    far_pairs = [(i, i ^ 2) for i in range(tp)]
    shape = jax.ShapeDtypeStruct
    message = shape((half * HEAD_DIM + DECAY_ROWS, HEAD_DIM), BF16)

    def swap(piece, step):
        return lax.ppermute(piece, "seq", [(i, i ^ step) for i in range(devices)])

    other_weight = lax.ppermute(out_weight, "tp", near_pairs)
    weight = pltpu.with_memory_space_constraint(out_weight, pltpu.HBM)
    arguments = (log_decay, key_vectors, value_vectors, query_vectors, norm_gain.reshape(1, -1))
    theirs, mine, decays, keys, values, queries, gain = call(
        functools.partial(state_kernel, half),
        (message, message) + tuple(shape(a.shape, a.dtype) for a in arguments),
        [HBM] * 5,
        "states",
        scratch=[pltpu.SemaphoreType.DMA((5,))],
    )(*(pltpu.with_memory_space_constraint(a, pltpu.HBM) for a in arguments))
    steps = (3, 1, 2, 0)
    received = [swap(theirs, 3), swap(theirs, 1), swap(mine, 2), mine]
    state = shape(states, BF16)
    before, sent, through, total = call(
        functools.partial(gather_kernel, half, steps),
        (
            shape(states, F32),
            state,
            shape((heads * 8, HEAD_DIM), F32),
            state if devices == 2 * MEMBERS else message,
        ),
        [VMEM] * len(steps),
        "gather_states",
        scratch=[pltpu.VMEM((MEMBERS,) + message.shape, BF16)],
    )(*received)
    earlier = earlier_groups(total, half, devices)
    inside = swap(sent, 1)
    intra, own = call(
        functools.partial(local_kernel, heads),
        (shape(wide, F32), shape((tokens, heads), F32)),
        [VMEM] * 4,
        "local",
        cost=4 * tokens * tokens * heads * HEAD_DIM,
    )(decays, queries, keys, values)
    mine, rest, factor, sent = call(
        functools.partial(start_kernel, half),
        (state, state, shape((half * 8, HEAD_DIM), F32), message),
        [VMEM] * 5,
        "start_states",
    )(before, through, earlier, inside, own)

    chunks = [slice(0, tokens // 2), slice(tokens // 2, tokens)]
    block = (out_weight.shape[0], out_width)
    weights = (weight, other_weight)
    weight_specs = [HBM, pl.BlockSpec(memory_space=pl.ANY)]

    def normed(name, halves, rows, *states):
        part = call(
            functools.partial(norm_kernel, half, halves, rows),
            shape((rows.stop - rows.start, len(halves) * half * HEAD_DIM), BF16),
            [VMEM] * (4 + len(states)),
            name,
        )(queries, intra, own, gain, *states)
        return part, lax.ppermute(part, "tp", near_pairs)

    def far_columns(after):
        return call(
            fetch_kernel,
            (shape(block, BF16),) * 2,
            weight_specs + [VMEM],
            "fetch_far",
            scratch=[pltpu.SemaphoreType.DMA((2,))],
        )(*weights, after)

    def send_far(i, kernel, *operands):
        part = call(
            kernel,
            shape((chunks[i].stop - chunks[i].start, out_width), BF16),
            [VMEM] * len(operands),
            f"project_far_{i}",
        )(*operands)
        return lax.ppermute(part, "tp", far_pairs)

    def finish(passes, pairs, far):
        near = call(
            functools.partial(near_kernel, chunks, passes),
            shape((tokens, out_width), F32),
            [HBM] + weight_specs + [VMEM] * (2 * len(pairs)),
            "project_near",
            scratch=[
                pltpu.VMEM(residual.shape, BF16),
                pltpu.VMEM(block, BF16),
                pltpu.VMEM(block, BF16),
                pltpu.SemaphoreType.DMA((3,)),
            ],
        )(
            pltpu.with_memory_space_constraint(residual, pltpu.HBM),
            *weights,
            *(a for pair in pairs for a in pair),
        )
        return call(
            functools.partial(add_kernel, chunks),
            pltpu.HBM((tokens, out_width), BF16),
            [VMEM] * (1 + len(chunks)),
            "add",
            out_specs=HBM,
            scratch=[
                pltpu.VMEM((tokens, out_width), BF16),
                pltpu.SemaphoreType.DMA((len(chunks),)),
            ],
        )(near, *far)

    def first_group():
        both = (True, False)
        pairs = [normed(f"norm_{i}", both, rows, mine, rest) for i, rows in enumerate(chunks)]
        far_weights = far_columns(pairs[-1][0])
        far = [send_far(i, far_all_kernel, *pairs[i], *far_weights) for i in range(len(chunks))]
        return finish((both,), pairs, far)

    def later_group():
        swapped = swap(sent, 1)
        begun = [normed(f"norm_mine_{i}", (True,), rows, mine) for i, rows in enumerate(chunks)]
        far_weights = far_columns(begun[-1][0])
        far_begun = call(
            functools.partial(far_mine_kernel, chunks),
            shape((tokens, out_width), F32),
            [VMEM] * (2 + 2 * len(chunks)),
            "project_far_mine",
        )(*far_weights, *(a for pair in begun for a in pair))
        other = call(functools.partial(start_other_kernel, half), state, [VMEM] * 4, "start_other")(
            rest, factor, swapped, far_begun
        )
        parts = [normed(f"norm_{i}", (False,), rows, other) for i, rows in enumerate(chunks)]
        far = [
            send_far(i, functools.partial(far_kernel, rows), far_begun, *parts[i], *far_weights)
            for i, rows in enumerate(chunks)
        ]
        pairs = [pair for i in range(len(chunks)) for pair in (begun[i], parts[i])]
        return finish(((True,), (False,)), pairs, far)

    return lax.cond(lax.axis_index("seq") < MEMBERS, first_group, later_group)


def solution(mesh):
    return jax.shard_map(
        on_device,
        mesh=mesh,
        in_specs=(
            P("seq", "tp"),
            P("seq", "tp"),
            P("seq", "tp"),
            P("seq", "tp"),
            P("tp", "seq"),
            P("tp"),
            P("tp", None),
        ),
        out_specs=P("seq", "tp"),
        check_vma=False,
    )
```

```python
import functools

import jax
import jax.numpy as jnp
from jax import lax
from jax.experimental import pallas as pl
from jax.experimental.pallas import tpu as pltpu
from jax.sharding import PartitionSpec as P

HEAD_DIM = 128
GROUP = 256
SCALE = HEAD_DIM ** (-0.5)
F32 = jnp.float32
BF16 = jnp.bfloat16
VMEM = pl.BlockSpec(memory_space=pltpu.VMEM)
HBM = pl.BlockSpec(memory_space=pltpu.HBM)
DECAY_ROWS = 16
MEMBERS = 4
PARAMS = pltpu.CompilerParams(vmem_limit_bytes=24 * 1024 * 1024)


def state_rows(j):
    return slice(j * HEAD_DIM, (j + 1) * HEAD_DIM)


def place():
    return lax.rem(lax.axis_index("seq"), MEMBERS)


def side():
    return lax.rem(lax.axis_index("seq"), 2)


def half_at(owner, size):
    return pl.ds(pl.multiple_of(owner * size, size), size)


def pick(owner, values, axis):
    half = values.shape[axis] // 2
    low = lax.slice_in_dim(values, 0, half, axis=axis)
    high = lax.slice_in_dim(values, half, 2 * half, axis=axis)
    return jnp.where(owner == 0, low, high)


def contract(a, b):
    return lax.dot_general(a, b, (((1,), (1,)), ((), ())), preferred_element_type=F32)


def positions():
    shape = (GROUP, GROUP)
    return lax.broadcasted_iota(jnp.int32, shape, 0), lax.broadcasted_iota(jnp.int32, shape, 1)


def three_terms(values):
    first = values.astype(BF16).astype(F32)
    second = (values - first).astype(BF16).astype(F32)
    third = values - first - second
    return jnp.concatenate([first, second, third], axis=0).astype(BF16)


def sums_down(mask, decays):
    heads = decays.shape[0]
    terms = contract(mask, three_terms(decays))
    return terms[:, :heads] + terms[:, heads : 2 * heads] + terms[:, 2 * heads :]


def sums_across(mask, decays):
    heads = decays.shape[0]
    terms = contract(three_terms(decays), mask)
    return terms[:heads] + terms[heads : 2 * heads] + terms[2 * heads :]


def decays_to_rows(decays):
    each = DECAY_ROWS // (2 * len(decays))
    wide = jnp.concatenate([jnp.broadcast_to(d, (each, HEAD_DIM)) for d in decays], axis=0)
    coarse = wide.astype(BF16).astype(F32)
    return jnp.concatenate([coarse, wide - coarse], axis=0).astype(BF16)


def rows_to_decays(rows, count):
    rows = rows.astype(F32)
    each = DECAY_ROWS // (2 * count)
    both = rows[: DECAY_ROWS // 2] + rows[DECAY_ROWS // 2 :]
    return [both[j * each : j * each + 1] for j in range(count)]


def state_kernel(half, *refs):
    sources, outs, held, sems = refs[:5], refs[5:7], refs[7:12], refs[12]
    copies = [
        pltpu.make_async_copy(source, target, sems.at[i])
        for i, (source, target) in enumerate(zip(sources, held))
    ]
    for copy in copies:
        copy.start()
    decay_ref, key_ref, value_ref = held[:3]
    me = side()
    row, col = positions()
    later = jnp.where(col > row, 1.0, 0.0).astype(BF16)
    copies[0].wait()
    decays = decay_ref[...]
    tail = jnp.exp(sums_across(later, decays))
    whole = jnp.exp(jnp.sum(decays, axis=1, keepdims=True))
    copies[1].wait()
    copies[2].wait()
    decay_rows = decays_to_rows([whole[h : h + 1] for h in range(2 * half)])
    for owner, out_ref in zip((1 - me, me), outs):
        factors = pick(owner, tail, 0)
        for j in range(half):
            at = half_at(owner * half + j, HEAD_DIM)
            weighted = (key_ref[:, at].T.astype(F32) * factors[j : j + 1, :]).astype(BF16)
            update = jnp.dot(weighted, value_ref[:, at], preferred_element_type=F32)
            out_ref[state_rows(j), :] = update.astype(BF16)
        out_ref[half * HEAD_DIM :, :] = decay_rows
    for copy in copies[3:]:
        copy.wait()


def local_kernel(heads, decay_ref, query_ref, key_ref, value_ref, intra_ref, own_ref):
    row, col = positions()
    causal = col <= row
    upto = jnp.where(causal, 1.0, 0.0).astype(BF16)
    decays = decay_ref[...]
    down = sums_down(upto, decays)
    across = sums_across(upto, decays)
    own_ref[...] = jnp.exp(down) * SCALE
    for h in range(heads):
        at = slice(h * HEAD_DIM, (h + 1) * HEAD_DIM)
        scores = contract(query_ref[:, at], key_ref[:, at])
        gaps = down[:, h : h + 1] - across[h : h + 1, :]
        weights = jnp.where(causal, jnp.exp(gaps), 0.0)
        probs = (scores * SCALE * weights).astype(BF16)
        intra_ref[:, at] = jnp.dot(probs, value_ref[:, at], preferred_element_type=F32)


def gather_kernel(half, steps, *refs):
    received, (before_ref, sent_ref, through_ref, total_ref, held_ref) = (
        refs[: len(steps)],
        refs[len(steps) :],
    )
    me, upper = place(), side() == 1
    for step, message_ref in zip(steps, received):
        held_ref[me ^ step] = message_ref[...]
    later_pair = me >= 2
    decays = [rows_to_decays(held_ref[m, half * HEAD_DIM :, :], 2 * half) for m in range(MEMBERS)]
    totals = []
    for j in range(2 * half):
        low, high = (j, half + j) if j < half else (j, j - half)
        decay = [jnp.where(upper, d[high], d[low]) for d in decays]
        through = [jnp.ones((1, HEAD_DIM), F32)]
        for m in range(MEMBERS):
            through.append(through[m] * decay[m])
        first, last = [jnp.where(later_pair, through[2 + i], through[i]) for i in range(2)]
        factor = jnp.where(upper, last, first)
        through_ref[j * 8 : (j + 1) * 8, :] = jnp.broadcast_to(factor, (8, HEAD_DIM))
        if j >= half:
            continue
        at = state_rows(j)
        held = [jnp.zeros((HEAD_DIM, HEAD_DIM), F32)]
        for m in range(MEMBERS):
            held.append(held[m] * decay[m] + held_ref[m, at, :].astype(F32))
        first, last = [jnp.where(later_pair, held[2 + i], held[i]) for i in range(2)]
        before_ref[at, :] = jnp.where(upper, last, first)
        sent_ref[at, :] = jnp.where(upper, first, last).astype(BF16)
        total_ref[at, :] = held[MEMBERS].astype(BF16)
        totals.append(through[MEMBERS])
    if total_ref.shape[0] > half * HEAD_DIM:
        total_ref[half * HEAD_DIM :, :] = decays_to_rows(totals)


def start_kernel(half, before_ref, through_ref, earlier_ref, inside_ref, _, *outs):
    mine_ref, rest_ref, factor_ref, sent_ref = outs
    started = lax.axis_index("seq") >= MEMBERS
    for j in range(half):
        at = state_rows(j)
        earlier = jnp.where(started, earlier_ref[at, :].astype(F32), 0.0)
        held = before_ref[at, :] + through_ref[8 * j : 8 * j + 1, :] * earlier
        mine_ref[at, :] = held.astype(BF16)
    rest_ref[...] = inside_ref[...]
    factor_ref[...] = through_ref[8 * half :, :]
    rows = half * HEAD_DIM
    sent_ref[:rows, :] = earlier_ref[:rows, :]
    sent_ref[rows:, :] = jnp.zeros((DECAY_ROWS, HEAD_DIM), BF16)


def start_other_kernel(half, rest_ref, factor_ref, earlier_ref, _, out_ref):
    for j in range(half):
        at = state_rows(j)
        earlier = factor_ref[8 * j : 8 * j + 1, :] * earlier_ref[at, :].astype(F32)
        out_ref[at, :] = (rest_ref[at, :].astype(F32) + earlier).astype(BF16)


def norm_kernel(half, halves, rows, query_ref, intra_ref, own_ref, gain_ref, *refs):
    states, out_ref = refs[: len(halves)], refs[-1]
    for i, (mine, state_ref) in enumerate(zip(halves, states)):
        owner = side() if mine else 1 - side()
        own = pick(owner, own_ref[rows, :], 1)
        for j in range(half):
            at = half_at(owner * half + j, HEAD_DIM)
            state = state_ref[state_rows(j), :]
            inter = jnp.dot(query_ref[rows, at], state, preferred_element_type=F32)
            attended = intra_ref[rows, at] + own[:, j : j + 1] * inter
            mean_square = jnp.mean(attended * attended, axis=-1, keepdims=True)
            normed = (attended * lax.rsqrt(mean_square + 1e-06) * gain_ref[:, at]).astype(BF16)
            to = (i * half + j) * HEAD_DIM
            out_ref[:, to : to + HEAD_DIM] = normed


def share(halves, pair, weights):
    rows = weights[0].shape[0] // 2
    total = None
    for i, mine in enumerate(halves):
        at = half_at(side() if mine else 1 - side(), rows)
        for normed_ref, weight_ref in zip(pair, weights):
            normed = normed_ref[:, i * rows : (i + 1) * rows]
            part = jnp.dot(normed, weight_ref[at, :], preferred_element_type=F32)
            total = part if total is None else total + part
    return total


def fetch(step, whole, held, sems):
    copies = []
    for i, (weight, ref) in enumerate(zip(whole, held)):
        at = half_at(lax.axis_index("tp") ^ step, ref.shape[1])
        copies.append(pltpu.make_async_copy(weight.at[:, at], ref, sems.at[i]))
        copies[i].start()
    return copies


def fetch_kernel(weight_hbm, other_weight_hbm, _, weight_ref, other_weight_ref, sems):
    for copy in fetch(2, (weight_hbm, other_weight_hbm), (weight_ref, other_weight_ref), sems):
        copy.wait()


def far_mine_kernel(chunks, weight_ref, other_weight_ref, *refs):
    for i, rows in enumerate(chunks):
        pair = refs[2 * i : 2 * i + 2]
        refs[-1][rows, :] = share((True,), pair, (weight_ref, other_weight_ref))


def far_kernel(rows, begun_ref, mine_ref, other_ref, weight_ref, other_weight_ref, out_ref):
    rest = share((False,), (mine_ref, other_ref), (weight_ref, other_weight_ref))
    out_ref[...] = (begun_ref[rows, :] + rest).astype(BF16)


def far_all_kernel(mine_ref, other_ref, weight_ref, other_weight_ref, out_ref):
    pair, weights = (mine_ref, other_ref), (weight_ref, other_weight_ref)
    out_ref[...] = share((True, False), pair, weights).astype(BF16)


def near_kernel(chunks, passes, residual_hbm, weight_hbm, other_weight_hbm, *refs):
    out_ref, residual_ref, *weights, sems = refs[-5:]
    copies = fetch(0, (weight_hbm, other_weight_hbm), weights, sems)
    copies.append(pltpu.make_async_copy(residual_hbm, residual_ref, sems.at[2]))
    copies[2].start()
    for copy in copies:
        copy.wait()
    pairs = iter(zip(refs[0:-5:2], refs[1:-5:2]))
    for rows in chunks:
        near = residual_ref[rows, :].astype(F32)
        for halves in passes:
            near = near + share(halves, next(pairs), weights)
        out_ref[rows, :] = near


def add_kernel(chunks, near_ref, *refs):
    far, (out_hbm, out_ref, sems) = refs[: len(chunks)], refs[len(chunks) :]
    copies = []
    for i, rows in enumerate(chunks):
        out_ref[rows, :] = (near_ref[rows, :] + far[i][...].astype(F32)).astype(BF16)
        copies.append(
            pltpu.make_async_copy(out_ref.at[rows, :], out_hbm.at[rows, :], sems.at[i])
        )
        copies[-1].start()
    for copy in copies:
        copy.wait()


def call(kernel, out_shape, in_specs, name, out_specs=None, scratch=(), cost=0):
    single = isinstance(out_shape, jax.ShapeDtypeStruct)
    if out_specs is None:
        out_specs = VMEM if single else (VMEM,) * len(out_shape)
    cost = pl.CostEstimate(
        flops=cost, bytes_accessed=2_000_000 if cost else 0, transcendentals=0
    )
    return pl.pallas_call(
        kernel,
        out_shape=out_shape,
        in_specs=in_specs,
        out_specs=out_specs,
        scratch_shapes=scratch,
        compiler_params=PARAMS,
        cost_estimate=cost,
        name=name,
    )


def earlier_groups(total, half, devices):
    groups = devices // MEMBERS
    if groups == 2:
        return lax.ppermute(total, "seq", [(i, i ^ MEMBERS) for i in range(devices)])

    def shift(message, by):
        moves = [(i, i + by * MEMBERS) for i in range(devices - by * MEMBERS)]
        return lax.ppermute(message, "seq", moves)

    rows = half * HEAD_DIM
    held = shift(total, 1)
    by = 1
    while by < groups - 1:
        before = shift(held, by)
        decays = rows_to_decays(held[rows:], half)
        factor = jnp.concatenate([jnp.broadcast_to(d, (HEAD_DIM, HEAD_DIM)) for d in decays])
        state = held[:rows].astype(F32) + factor * before[:rows].astype(F32)
        through = [a * b for a, b in zip(decays, rows_to_decays(before[rows:], half))]
        held = jnp.concatenate([state.astype(BF16), decays_to_rows(through)], axis=0)
        by *= 2
    return held


def on_device(
    residual, query_vectors, key_vectors, value_vectors, log_decay, norm_gain, out_weight
):
    tokens, width = residual.shape
    heads = log_decay.shape[0]
    half = heads // 2
    devices = lax.axis_size("seq")
    tp = lax.axis_size("tp")
    wide = (tokens, heads * HEAD_DIM)
    out_width = out_weight.shape[1] // tp
    states = (half * HEAD_DIM, HEAD_DIM)
    near_pairs = [(i, i ^ 1) for i in range(tp)]
    far_pairs = [(i, i ^ 2) for i in range(tp)]
    shape = jax.ShapeDtypeStruct
    message = shape((half * HEAD_DIM + DECAY_ROWS, HEAD_DIM), BF16)

    def swap(piece, step):
        return lax.ppermute(piece, "seq", [(i, i ^ step) for i in range(devices)])

    other_weight = lax.ppermute(out_weight, "tp", near_pairs)
    weight = pltpu.with_memory_space_constraint(out_weight, pltpu.HBM)
    arguments = (log_decay, key_vectors, value_vectors, query_vectors, norm_gain.reshape(1, -1))
    theirs, mine, decays, keys, values, queries, gain = call(
        functools.partial(state_kernel, half),
        (message, message) + tuple(shape(a.shape, a.dtype) for a in arguments),
        [HBM] * 5,
        "states",
        scratch=[pltpu.SemaphoreType.DMA((5,))],
    )(*(pltpu.with_memory_space_constraint(a, pltpu.HBM) for a in arguments))
    steps = (2, 3, 1, 0)
    received = [swap(mine, 2), swap(theirs, 3), swap(theirs, 1), mine]
    state = shape(states, BF16)
    before, sent, through, total = call(
        functools.partial(gather_kernel, half, steps),
        (
            shape(states, F32),
            state,
            shape((heads * 8, HEAD_DIM), F32),
            state if devices == 2 * MEMBERS else message,
        ),
        [VMEM] * len(steps),
        "gather_states",
        scratch=[pltpu.VMEM((MEMBERS,) + message.shape, BF16)],
    )(*received)
    earlier = earlier_groups(total, half, devices)
    inside = swap(sent, 1)
    intra, own = call(
        functools.partial(local_kernel, heads),
        (shape(wide, F32), shape((tokens, heads), F32)),
        [VMEM] * 4,
        "local",
        cost=4 * tokens * tokens * heads * HEAD_DIM,
    )(decays, queries, keys, values)
    mine, rest, factor, sent = call(
        functools.partial(start_kernel, half),
        (state, state, shape((half * 8, HEAD_DIM), F32), message),
        [VMEM] * 5,
        "start_states",
    )(before, through, earlier, inside, own)

    chunks = [slice(0, tokens // 2), slice(tokens // 2, tokens)]
    block = (out_weight.shape[0], out_width)
    weights = (weight, other_weight)
    weight_specs = [HBM, pl.BlockSpec(memory_space=pl.ANY)]

    def normed(name, halves, rows, *states):
        part = call(
            functools.partial(norm_kernel, half, halves, rows),
            shape((rows.stop - rows.start, len(halves) * half * HEAD_DIM), BF16),
            [VMEM] * (4 + len(states)),
            name,
        )(queries, intra, own, gain, *states)
        return part, lax.ppermute(part, "tp", near_pairs)

    def far_columns(after):
        return call(
            fetch_kernel,
            (shape(block, BF16),) * 2,
            weight_specs + [VMEM],
            "fetch_far",
            scratch=[pltpu.SemaphoreType.DMA((2,))],
        )(*weights, after)

    def send_far(i, kernel, *operands):
        part = call(
            kernel,
            shape((chunks[i].stop - chunks[i].start, out_width), BF16),
            [VMEM] * len(operands),
            f"project_far_{i}",
        )(*operands)
        return lax.ppermute(part, "tp", far_pairs)

    def finish(passes, pairs, far):
        near = call(
            functools.partial(near_kernel, chunks, passes),
            shape((tokens, out_width), F32),
            [HBM] + weight_specs + [VMEM] * (2 * len(pairs)),
            "project_near",
            scratch=[
                pltpu.VMEM(residual.shape, BF16),
                pltpu.VMEM(block, BF16),
                pltpu.VMEM(block, BF16),
                pltpu.SemaphoreType.DMA((3,)),
            ],
        )(
            pltpu.with_memory_space_constraint(residual, pltpu.HBM),
            *weights,
            *(a for pair in pairs for a in pair),
        )
        return call(
            functools.partial(add_kernel, chunks),
            pltpu.HBM((tokens, out_width), BF16),
            [VMEM] * (1 + len(chunks)),
            "add",
            out_specs=HBM,
            scratch=[
                pltpu.VMEM((tokens, out_width), BF16),
                pltpu.SemaphoreType.DMA((len(chunks),)),
            ],
        )(near, *far)

    def first_group():
        both = (True, False)
        pairs = [normed(f"norm_{i}", both, rows, mine, rest) for i, rows in enumerate(chunks)]
        far_weights = far_columns(pairs[-1][0])
        far = [send_far(i, far_all_kernel, *pairs[i], *far_weights) for i in range(len(chunks))]
        return finish((both,), pairs, far)

    def later_group():
        swapped = swap(sent, 1)
        begun = [normed(f"norm_mine_{i}", (True,), rows, mine) for i, rows in enumerate(chunks)]
        far_weights = far_columns(begun[-1][0])
        far_begun = call(
            functools.partial(far_mine_kernel, chunks),
            shape((tokens, out_width), F32),
            [VMEM] * (2 + 2 * len(chunks)),
            "project_far_mine",
        )(*far_weights, *(a for pair in begun for a in pair))
        other = call(functools.partial(start_other_kernel, half), state, [VMEM] * 4, "start_other")(
            rest, factor, swapped, far_begun
        )
        parts = [normed(f"norm_{i}", (False,), rows, other) for i, rows in enumerate(chunks)]
        far = [
            send_far(i, functools.partial(far_kernel, rows), far_begun, *parts[i], *far_weights)
            for i, rows in enumerate(chunks)
        ]
        pairs = [pair for i in range(len(chunks)) for pair in (begun[i], parts[i])]
        return finish(((True,), (False,)), pairs, far)

    return lax.cond(lax.axis_index("seq") < MEMBERS, first_group, later_group)


def solution(mesh):
    return jax.shard_map(
        on_device,
        mesh=mesh,
        in_specs=(
            P("seq", "tp"),
            P("seq", "tp"),
            P("seq", "tp"),
            P("seq", "tp"),
            P("tp", "seq"),
            P("tp"),
            P("tp", None),
        ),
        out_specs=P("seq", "tp"),
        check_vma=False,
    )
```

```python
import functools

import jax
import jax.numpy as jnp
from jax import lax
from jax.experimental import pallas as pl
from jax.experimental.pallas import tpu as pltpu
from jax.sharding import PartitionSpec as P

HEAD_DIM = 128
GROUP = 256
SCALE = HEAD_DIM ** (-0.5)
F32 = jnp.float32
BF16 = jnp.bfloat16
VMEM = pl.BlockSpec(memory_space=pltpu.VMEM)
HBM = pl.BlockSpec(memory_space=pltpu.HBM)
DECAY_ROWS = 16
MEMBERS = 4
PARAMS = pltpu.CompilerParams(vmem_limit_bytes=24 * 1024 * 1024)


def state_rows(j):
    return slice(j * HEAD_DIM, (j + 1) * HEAD_DIM)


def place():
    return lax.rem(lax.axis_index("seq"), MEMBERS)


def side():
    return lax.rem(lax.axis_index("seq"), 2)


def half_at(owner, size):
    return pl.ds(pl.multiple_of(owner * size, size), size)


def pick(owner, values, axis):
    half = values.shape[axis] // 2
    low = lax.slice_in_dim(values, 0, half, axis=axis)
    high = lax.slice_in_dim(values, half, 2 * half, axis=axis)
    return jnp.where(owner == 0, low, high)


def contract(a, b):
    return lax.dot_general(a, b, (((1,), (1,)), ((), ())), preferred_element_type=F32)


def positions():
    shape = (GROUP, GROUP)
    return lax.broadcasted_iota(jnp.int32, shape, 0), lax.broadcasted_iota(jnp.int32, shape, 1)


def three_terms(values):
    first = values.astype(BF16).astype(F32)
    second = (values - first).astype(BF16).astype(F32)
    third = values - first - second
    return jnp.concatenate([first, second, third], axis=0).astype(BF16)


def sums_down(mask, decays):
    heads = decays.shape[0]
    terms = contract(mask, three_terms(decays))
    return terms[:, :heads] + terms[:, heads : 2 * heads] + terms[:, 2 * heads :]


def sums_across(mask, decays):
    heads = decays.shape[0]
    terms = contract(three_terms(decays), mask)
    return terms[:heads] + terms[heads : 2 * heads] + terms[2 * heads :]


def decays_to_rows(decays):
    each = DECAY_ROWS // (2 * len(decays))
    wide = jnp.concatenate([jnp.broadcast_to(d, (each, HEAD_DIM)) for d in decays], axis=0)
    coarse = wide.astype(BF16).astype(F32)
    return jnp.concatenate([coarse, wide - coarse], axis=0).astype(BF16)


def rows_to_decays(rows, count):
    rows = rows.astype(F32)
    each = DECAY_ROWS // (2 * count)
    both = rows[: DECAY_ROWS // 2] + rows[DECAY_ROWS // 2 :]
    return [both[j * each : j * each + 1] for j in range(count)]


def state_kernel(half, *refs):
    sources, outs, held, sems = refs[:5], refs[5:7], refs[7:12], refs[12]
    copies = [
        pltpu.make_async_copy(source, target, sems.at[i])
        for i, (source, target) in enumerate(zip(sources, held))
    ]
    for copy in copies:
        copy.start()
    decay_ref, key_ref, value_ref = held[:3]
    me = side()
    row, col = positions()
    later = jnp.where(col > row, 1.0, 0.0).astype(BF16)
    copies[0].wait()
    decays = decay_ref[...]
    tail = jnp.exp(sums_across(later, decays))
    whole = jnp.exp(jnp.sum(decays, axis=1, keepdims=True))
    copies[1].wait()
    copies[2].wait()
    decay_rows = decays_to_rows([whole[h : h + 1] for h in range(2 * half)])
    for owner, out_ref in zip((1 - me, me), outs):
        factors = pick(owner, tail, 0)
        for j in range(half):
            at = half_at(owner * half + j, HEAD_DIM)
            weighted = (key_ref[:, at].T.astype(F32) * factors[j : j + 1, :]).astype(BF16)
            update = jnp.dot(weighted, value_ref[:, at], preferred_element_type=F32)
            out_ref[state_rows(j), :] = update.astype(BF16)
        out_ref[half * HEAD_DIM :, :] = decay_rows
    for copy in copies[3:]:
        copy.wait()


def local_kernel(heads, decay_ref, query_ref, key_ref, value_ref, intra_ref, own_ref):
    row, col = positions()
    causal = col <= row
    upto = jnp.where(causal, 1.0, 0.0).astype(BF16)
    decays = decay_ref[...]
    down = sums_down(upto, decays)
    across = sums_across(upto, decays)
    own_ref[...] = jnp.exp(down) * SCALE
    for h in range(heads):
        at = slice(h * HEAD_DIM, (h + 1) * HEAD_DIM)
        scores = contract(query_ref[:, at], key_ref[:, at])
        gaps = down[:, h : h + 1] - across[h : h + 1, :]
        weights = jnp.where(causal, jnp.exp(gaps), 0.0)
        probs = (scores * SCALE * weights).astype(BF16)
        intra_ref[:, at] = jnp.dot(probs, value_ref[:, at], preferred_element_type=F32)


def gather_kernel(half, steps, *refs):
    received, (before_ref, sent_ref, through_ref, total_ref, held_ref) = (
        refs[: len(steps)],
        refs[len(steps) :],
    )
    me, upper = place(), side() == 1
    for step, message_ref in zip(steps, received):
        held_ref[me ^ step] = message_ref[...]
    later_pair = me >= 2
    decays = [rows_to_decays(held_ref[m, half * HEAD_DIM :, :], 2 * half) for m in range(MEMBERS)]
    totals = []
    for j in range(2 * half):
        low, high = (j, half + j) if j < half else (j, j - half)
        decay = [jnp.where(upper, d[high], d[low]) for d in decays]
        through = [jnp.ones((1, HEAD_DIM), F32)]
        for m in range(MEMBERS):
            through.append(through[m] * decay[m])
        first, last = [jnp.where(later_pair, through[2 + i], through[i]) for i in range(2)]
        factor = jnp.where(upper, last, first)
        through_ref[j * 8 : (j + 1) * 8, :] = jnp.broadcast_to(factor, (8, HEAD_DIM))
        if j >= half:
            continue
        at = state_rows(j)
        held = [jnp.zeros((HEAD_DIM, HEAD_DIM), F32)]
        for m in range(MEMBERS):
            held.append(held[m] * decay[m] + held_ref[m, at, :].astype(F32))
        first, last = [jnp.where(later_pair, held[2 + i], held[i]) for i in range(2)]
        before_ref[at, :] = jnp.where(upper, last, first)
        sent_ref[at, :] = jnp.where(upper, first, last).astype(BF16)
        total_ref[at, :] = held[MEMBERS].astype(BF16)
        totals.append(through[MEMBERS])
    if total_ref.shape[0] > half * HEAD_DIM:
        total_ref[half * HEAD_DIM :, :] = decays_to_rows(totals)


def start_kernel(half, before_ref, through_ref, earlier_ref, inside_ref, _, *outs):
    mine_ref, rest_ref, factor_ref, sent_ref = outs
    started = lax.axis_index("seq") >= MEMBERS
    for j in range(half):
        at = state_rows(j)
        earlier = jnp.where(started, earlier_ref[at, :].astype(F32), 0.0)
        held = before_ref[at, :] + through_ref[8 * j : 8 * j + 1, :] * earlier
        mine_ref[at, :] = held.astype(BF16)
    rest_ref[...] = inside_ref[...]
    factor_ref[...] = through_ref[8 * half :, :]
    rows = half * HEAD_DIM
    sent_ref[:rows, :] = earlier_ref[:rows, :]
    sent_ref[rows:, :] = jnp.zeros((DECAY_ROWS, HEAD_DIM), BF16)


def start_other_kernel(half, rest_ref, factor_ref, earlier_ref, _, out_ref):
    for j in range(half):
        at = state_rows(j)
        earlier = factor_ref[8 * j : 8 * j + 1, :] * earlier_ref[at, :].astype(F32)
        out_ref[at, :] = (rest_ref[at, :].astype(F32) + earlier).astype(BF16)


def norm_kernel(half, halves, rows, query_ref, intra_ref, own_ref, gain_ref, *refs):
    states, out_ref = refs[: len(halves)], refs[-1]
    for i, (mine, state_ref) in enumerate(zip(halves, states)):
        owner = side() if mine else 1 - side()
        own = pick(owner, own_ref[rows, :], 1)
        for j in range(half):
            at = half_at(owner * half + j, HEAD_DIM)
            state = state_ref[state_rows(j), :]
            inter = jnp.dot(query_ref[rows, at], state, preferred_element_type=F32)
            attended = intra_ref[rows, at] + own[:, j : j + 1] * inter
            mean_square = jnp.mean(attended * attended, axis=-1, keepdims=True)
            normed = (attended * lax.rsqrt(mean_square + 1e-06) * gain_ref[:, at]).astype(BF16)
            to = (i * half + j) * HEAD_DIM
            out_ref[:, to : to + HEAD_DIM] = normed


def share(halves, pair, weights):
    rows = weights[0].shape[0] // 2
    total = None
    for i, mine in enumerate(halves):
        at = half_at(side() if mine else 1 - side(), rows)
        for normed_ref, weight_ref in zip(pair, weights):
            normed = normed_ref[:, i * rows : (i + 1) * rows]
            part = jnp.dot(normed, weight_ref[at, :], preferred_element_type=F32)
            total = part if total is None else total + part
    return total


def fetch(step, whole, held, sems):
    copies = []
    for i, (weight, ref) in enumerate(zip(whole, held)):
        at = half_at(lax.axis_index("tp") ^ step, ref.shape[1])
        copies.append(pltpu.make_async_copy(weight.at[:, at], ref, sems.at[i]))
        copies[i].start()
    return copies


def fetch_kernel(weight_hbm, other_weight_hbm, _, weight_ref, other_weight_ref, sems):
    for copy in fetch(2, (weight_hbm, other_weight_hbm), (weight_ref, other_weight_ref), sems):
        copy.wait()


def far_mine_kernel(chunks, weight_ref, other_weight_ref, *refs):
    for i, rows in enumerate(chunks):
        pair = refs[2 * i : 2 * i + 2]
        refs[-1][rows, :] = share((True,), pair, (weight_ref, other_weight_ref))


def far_kernel(rows, begun_ref, mine_ref, other_ref, weight_ref, other_weight_ref, out_ref):
    rest = share((False,), (mine_ref, other_ref), (weight_ref, other_weight_ref))
    out_ref[...] = (begun_ref[rows, :] + rest).astype(BF16)


def far_all_kernel(mine_ref, other_ref, weight_ref, other_weight_ref, out_ref):
    pair, weights = (mine_ref, other_ref), (weight_ref, other_weight_ref)
    out_ref[...] = share((True, False), pair, weights).astype(BF16)


def near_kernel(chunks, passes, residual_hbm, weight_hbm, other_weight_hbm, *refs):
    out_ref, residual_ref, *weights, sems = refs[-5:]
    copies = fetch(0, (weight_hbm, other_weight_hbm), weights, sems)
    copies.append(pltpu.make_async_copy(residual_hbm, residual_ref, sems.at[2]))
    copies[2].start()
    for copy in copies:
        copy.wait()
    pairs = iter(zip(refs[0:-5:2], refs[1:-5:2]))
    for rows in chunks:
        near = residual_ref[rows, :].astype(F32)
        for halves in passes:
            near = near + share(halves, next(pairs), weights)
        out_ref[rows, :] = near


def add_kernel(chunks, near_ref, *refs):
    far, (out_hbm, out_ref, sems) = refs[: len(chunks)], refs[len(chunks) :]
    copies = []
    for i, rows in enumerate(chunks):
        out_ref[rows, :] = (near_ref[rows, :] + far[i][...].astype(F32)).astype(BF16)
        copies.append(
            pltpu.make_async_copy(out_ref.at[rows, :], out_hbm.at[rows, :], sems.at[i])
        )
        copies[-1].start()
    for copy in copies:
        copy.wait()


def call(kernel, out_shape, in_specs, name, out_specs=None, scratch=(), cost=0):
    single = isinstance(out_shape, jax.ShapeDtypeStruct)
    if out_specs is None:
        out_specs = VMEM if single else (VMEM,) * len(out_shape)
    cost = pl.CostEstimate(
        flops=cost, bytes_accessed=2_000_000 if cost else 0, transcendentals=0
    )
    return pl.pallas_call(
        kernel,
        out_shape=out_shape,
        in_specs=in_specs,
        out_specs=out_specs,
        scratch_shapes=scratch,
        compiler_params=PARAMS,
        cost_estimate=cost,
        name=name,
    )


def earlier_groups(total, half, devices):
    groups = devices // MEMBERS
    if groups == 2:
        return lax.ppermute(total, "seq", [(i, i ^ MEMBERS) for i in range(devices)])

    def shift(message, by):
        moves = [(i, i + by * MEMBERS) for i in range(devices - by * MEMBERS)]
        return lax.ppermute(message, "seq", moves)

    rows = half * HEAD_DIM
    held = shift(total, 1)
    by = 1
    while by < groups - 1:
        before = shift(held, by)
        decays = rows_to_decays(held[rows:], half)
        factor = jnp.concatenate([jnp.broadcast_to(d, (HEAD_DIM, HEAD_DIM)) for d in decays])
        state = held[:rows].astype(F32) + factor * before[:rows].astype(F32)
        through = [a * b for a, b in zip(decays, rows_to_decays(before[rows:], half))]
        held = jnp.concatenate([state.astype(BF16), decays_to_rows(through)], axis=0)
        by *= 2
    return held


def on_device(
    residual, query_vectors, key_vectors, value_vectors, log_decay, norm_gain, out_weight
):
    tokens, width = residual.shape
    heads = log_decay.shape[0]
    half = heads // 2
    devices = lax.axis_size("seq")
    tp = lax.axis_size("tp")
    wide = (tokens, heads * HEAD_DIM)
    out_width = out_weight.shape[1] // tp
    states = (half * HEAD_DIM, HEAD_DIM)
    near_pairs = [(i, i ^ 1) for i in range(tp)]
    far_pairs = [(i, i ^ 2) for i in range(tp)]
    shape = jax.ShapeDtypeStruct
    message = shape((half * HEAD_DIM + DECAY_ROWS, HEAD_DIM), BF16)

    def swap(piece, step):
        return lax.ppermute(piece, "seq", [(i, i ^ step) for i in range(devices)])

    other_weight = lax.ppermute(out_weight, "tp", near_pairs)
    weight = pltpu.with_memory_space_constraint(out_weight, pltpu.HBM)
    arguments = (log_decay, key_vectors, value_vectors, query_vectors, norm_gain.reshape(1, -1))
    theirs, mine, decays, keys, values, queries, gain = call(
        functools.partial(state_kernel, half),
        (message, message) + tuple(shape(a.shape, a.dtype) for a in arguments),
        [HBM] * 5,
        "states",
        scratch=[pltpu.SemaphoreType.DMA((5,))],
    )(*(pltpu.with_memory_space_constraint(a, pltpu.HBM) for a in arguments))
    steps = (1, 2, 3, 0)
    received = [swap(theirs, 1), swap(mine, 2), swap(theirs, 3), mine]
    state = shape(states, BF16)
    before, sent, through, total = call(
        functools.partial(gather_kernel, half, steps),
        (
            shape(states, F32),
            state,
            shape((heads * 8, HEAD_DIM), F32),
            state if devices == 2 * MEMBERS else message,
        ),
        [VMEM] * len(steps),
        "gather_states",
        scratch=[pltpu.VMEM((MEMBERS,) + message.shape, BF16)],
    )(*received)
    earlier = earlier_groups(total, half, devices)
    inside = swap(sent, 1)
    intra, own = call(
        functools.partial(local_kernel, heads),
        (shape(wide, F32), shape((tokens, heads), F32)),
        [VMEM] * 4,
        "local",
        cost=4 * tokens * tokens * heads * HEAD_DIM,
    )(decays, queries, keys, values)
    mine, rest, factor, sent = call(
        functools.partial(start_kernel, half),
        (state, state, shape((half * 8, HEAD_DIM), F32), message),
        [VMEM] * 5,
        "start_states",
    )(before, through, earlier, inside, own)

    chunks = [slice(0, tokens // 2), slice(tokens // 2, tokens)]
    block = (out_weight.shape[0], out_width)
    weights = (weight, other_weight)
    weight_specs = [HBM, pl.BlockSpec(memory_space=pl.ANY)]

    def normed(name, halves, rows, *states):
        part = call(
            functools.partial(norm_kernel, half, halves, rows),
            shape((rows.stop - rows.start, len(halves) * half * HEAD_DIM), BF16),
            [VMEM] * (4 + len(states)),
            name,
        )(queries, intra, own, gain, *states)
        return part, lax.ppermute(part, "tp", near_pairs)

    def far_columns(after):
        return call(
            fetch_kernel,
            (shape(block, BF16),) * 2,
            weight_specs + [VMEM],
            "fetch_far",
            scratch=[pltpu.SemaphoreType.DMA((2,))],
        )(*weights, after)

    def send_far(i, kernel, *operands):
        part = call(
            kernel,
            shape((chunks[i].stop - chunks[i].start, out_width), BF16),
            [VMEM] * len(operands),
            f"project_far_{i}",
        )(*operands)
        return lax.ppermute(part, "tp", far_pairs)

    def finish(passes, pairs, far):
        near = call(
            functools.partial(near_kernel, chunks, passes),
            shape((tokens, out_width), F32),
            [HBM] + weight_specs + [VMEM] * (2 * len(pairs)),
            "project_near",
            scratch=[
                pltpu.VMEM(residual.shape, BF16),
                pltpu.VMEM(block, BF16),
                pltpu.VMEM(block, BF16),
                pltpu.SemaphoreType.DMA((3,)),
            ],
        )(
            pltpu.with_memory_space_constraint(residual, pltpu.HBM),
            *weights,
            *(a for pair in pairs for a in pair),
        )
        return call(
            functools.partial(add_kernel, chunks),
            pltpu.HBM((tokens, out_width), BF16),
            [VMEM] * (1 + len(chunks)),
            "add",
            out_specs=HBM,
            scratch=[
                pltpu.VMEM((tokens, out_width), BF16),
                pltpu.SemaphoreType.DMA((len(chunks),)),
            ],
        )(near, *far)

    def first_group():
        both = (True, False)
        pairs = [normed(f"norm_{i}", both, rows, mine, rest) for i, rows in enumerate(chunks)]
        far_weights = far_columns(pairs[-1][0])
        far = [send_far(i, far_all_kernel, *pairs[i], *far_weights) for i in range(len(chunks))]
        return finish((both,), pairs, far)

    def later_group():
        swapped = swap(sent, 1)
        begun = [normed(f"norm_mine_{i}", (True,), rows, mine) for i, rows in enumerate(chunks)]
        far_weights = far_columns(begun[-1][0])
        far_begun = call(
            functools.partial(far_mine_kernel, chunks),
            shape((tokens, out_width), F32),
            [VMEM] * (2 + 2 * len(chunks)),
            "project_far_mine",
        )(*far_weights, *(a for pair in begun for a in pair))
        other = call(functools.partial(start_other_kernel, half), state, [VMEM] * 4, "start_other")(
            rest, factor, swapped, far_begun
        )
        parts = [normed(f"norm_{i}", (False,), rows, other) for i, rows in enumerate(chunks)]
        far = [
            send_far(i, functools.partial(far_kernel, rows), far_begun, *parts[i], *far_weights)
            for i, rows in enumerate(chunks)
        ]
        pairs = [pair for i in range(len(chunks)) for pair in (begun[i], parts[i])]
        return finish(((True,), (False,)), pairs, far)

    return lax.cond(lax.axis_index("seq") < MEMBERS, first_group, later_group)


def solution(mesh):
    return jax.shard_map(
        on_device,
        mesh=mesh,
        in_specs=(
            P("seq", "tp"),
            P("seq", "tp"),
            P("seq", "tp"),
            P("seq", "tp"),
            P("tp", "seq"),
            P("tp"),
            P("tp", None),
        ),
        out_specs=P("seq", "tp"),
        check_vma=False,
    )
```
